128 devices in a mesh: ctx: 32 (over x_lo, z, y), fsdp: 4 (over x_hi, core).
Axes of the slice: x: 4 (x_hi: 2, x_lo: 2; x = x_hi * 2 + x_lo), y: 4, z: 4, core: 2. Of those that a mesh axis runs over, the one named last changes fastest.
Arguments:
- tokens: bfloat16 [4, 8192, 960], P('fsdp', 'ctx'), may hold values from -6 to 6
- block_order: int32 [64], replicated, may hold values from 0 to 63, each once
- gain_attn: bfloat16 [960], P('fsdp'), may hold values from 0.5 to 1.5
- w_query: bfloat16 [960, 960], P('fsdp'), may hold values from -0.1875 to 0.1875
- w_key: bfloat16 [960, 320], P('fsdp'), may hold values from -0.1875 to 0.1875
- w_value: bfloat16 [960, 320], P('fsdp'), may hold values from -0.1875 to 0.1875
- w_out: bfloat16 [960, 960], P('fsdp'), may hold values from -6 to 6
- gain_mlp: bfloat16 [960], P('fsdp'), may hold values from 0.5 to 1.5
- w_gate: bfloat16 [960, 2560], P('fsdp'), may hold values from -0.1875 to 0.1875
- w_up: bfloat16 [960, 2560], P('fsdp'), may hold values from -0.1875 to 0.1875
- w_down: bfloat16 [2560, 960], P('fsdp'), may hold values from -0.125 to 0.125
- cotangent: bfloat16 [4, 8192, 960], P('fsdp', 'ctx'), may hold values from -6 to 6
Outputs:
- block_out: bfloat16 [4, 8192, 960], P('fsdp', 'ctx')
- grad_tokens: float32 [4, 8192, 960], P('fsdp', 'ctx')
- grad_gain_attn: float32 [960], P('fsdp')
- grad_query: float32 [960, 960], P('fsdp')
- grad_key: float32 [960, 320], P('fsdp')
- grad_value: float32 [960, 320], P('fsdp')
- grad_out: float32 [960, 960], P('fsdp')
- grad_gain_mlp: float32 [960], P('fsdp')
- grad_gate: float32 [960, 2560], P('fsdp')
- grad_up: float32 [960, 2560], P('fsdp')
- grad_down: float32 [2560, 960], P('fsdp')
The draws below stay inside these ranges and needn't reach their ends.
Inputs may be any that keep to these rules, and one draw needn't show every extreme that they name: `block_order`: each block number appears once.
All inputs are finite; a program needn't handle non-finite values.
Results may differ from the reference program's by a relative error of at most 0.03.
Values may be sent and summed in bfloat16 or wider, within the bound.
No kernel may reach another device: no remote copies, remote signals or barrier semaphores. Data moves between devices by JAX's collectives and lax.ppermute only.
A program may use at most 192 MiB of HBM per device.

```python
import math
import jax
import jax.numpy as jnp
from jax import lax

D = 960
HEADS = 15
KV_HEADS = 5
HEAD = 64
FF = 2560
TOK_DEV = 256
SEQ = 8192
SEQS = 4
QW = 960
KW = 320
N_CTX = 32


def block_scale(rng, extent, split, low, high):
    level, own = 1.0, jax.random.fold_in(rng, 6)
    for axis_at, shards_of in split:
        steps = jnp.exp(jax.random.uniform(jax.random.fold_in(own, axis_at), (shards_of,), jnp.float32, low / len(split), high / len(split)))
        level = level * jnp.repeat(steps, extent[axis_at] // shards_of).reshape([-1 if axis == axis_at else 1 for axis in range(len(extent))])
    return level


def normal_values(stream_key, shape, deviation, limit, split=(), held_as=jnp.bfloat16):
    drawn = jax.random.normal(stream_key, shape, jnp.float32) * deviation
    if len(split) > 0:
        drawn = block_scale(stream_key, shape, split, -0.22, 0.18) * drawn
    return jnp.clip(drawn, min=-limit, max=limit).astype(held_as)


def setup_inputs(seed: int = 0) -> dict:
    key_of = jax.random.split(jax.random.key(seed), 13)
    tokens = normal_values(key_of[0], (SEQS, SEQ, D), 1.0, 6.0, ((0, 4), (1, 32)))
    block_order = jax.random.permutation(key_of[1], 2 * N_CTX).astype(jnp.int32)
    gain_attn = jnp.clip(1.0 + 0.1 * jax.random.normal(key_of[2], (D,), jnp.float32), 0.5, 1.5).astype(jnp.bfloat16)
    w_query = normal_values(key_of[3], (D, QW), D ** -0.5, 0.1875, ((0, 4),))
    w_key = normal_values(key_of[4], (D, KW), D ** -0.5, 0.1875, ((0, 4),))
    w_value = normal_values(key_of[5], (D, KW), D ** -0.5, 0.1875, ((0, 4),))
    w_out = normal_values(key_of[6], (QW, D), (max(1, 4 * HEADS * HEAD // (TOK_DEV * N_CTX))) ** -0.5, 6.0, ((0, 4),))
    gain_mlp = jnp.clip(1.0 + 0.1 * jax.random.normal(key_of[7], (D,), jnp.float32), 0.5, 1.5).astype(jnp.bfloat16)
    w_gate = normal_values(key_of[8], (D, FF), D ** -0.5, 0.1875, ((0, 4),))
    w_up = normal_values(key_of[9], (D, FF), D ** -0.5, 0.1875, ((0, 4),))
    w_down = normal_values(key_of[10], (FF, D), FF ** -0.5, 0.125, ((0, 4),))
    cotangent = normal_values(key_of[11], (SEQS, SEQ, D), 1.0, 6.0, ((0, 4), (1, 32)))
    return {"tokens": tokens, "block_order": block_order, "gain_attn": gain_attn, "w_query": w_query, "w_key": w_key, "w_value": w_value, "w_out": w_out, "gain_mlp": gain_mlp, "w_gate": w_gate, "w_up": w_up, "w_down": w_down, "cotangent": cotangent}


EPSILON = 1e-05
THETA = 100000.0

@jax.custom_vjp
def low(v):
    return lax.optimization_barrier(v.astype(jnp.bfloat16)).astype(jnp.float32)

@jax.custom_vjp
def low_back(v):
    return v

def low_keep(v):
    return (low(v), None)

def low_pass(kept, grad):
    return (grad,)

def back_keep(v):
    return (v, None)

def back_low(kept, grad):
    return (low(grad),)
low.defvjp(low_keep, low_pass)
low_back.defvjp(back_keep, back_low)

def places(block_order, first_row, row_total, block_len):
    row_ids = first_row + jnp.arange(row_total, dtype=jnp.int32)
    owners = row_ids // block_len
    picked = owners[:, None] == jnp.arange(block_order.shape[0], dtype=jnp.int32)[None, :]
    chosen = lax.optimization_barrier(jnp.sum(jnp.where(picked, block_order[None, :], 0), axis=1)).astype(jnp.int32)
    return chosen * block_len + row_ids % block_len

def rotary(positions, half_dim):
    inverse_freq = THETA ** (-jnp.arange(half_dim, dtype=jnp.float32) / half_dim)
    angles = positions.astype(jnp.float32)[:, None] * inverse_freq[None, :]
    return (jnp.cos(angles)[:, None, :], jnp.sin(angles)[:, None, :])

def rotate(vector, cos_table, sin_table):
    half_dim = vector.shape[-1] // 2
    front = vector[..., :half_dim]
    behind = vector[..., half_dim:]
    return jnp.concatenate([front * cos_table - behind * sin_table, behind * cos_table + front * sin_table], axis=-1)

def forward(hidden_in, gain_one, w_query, w_key, w_value, w_out, gain_two, w_gate, w_up, w_down, cos_table, sin_table, positions):
    highest = lax.Precision.HIGHEST
    seq_len = hidden_in.shape[0]
    group_size = HEADS // KV_HEADS
    scale_factor = 1.0 / math.sqrt(HEAD)
    first_rms = lax.rsqrt(lax.optimization_barrier(jnp.mean(hidden_in * hidden_in, axis=-1, keepdims=True)) + EPSILON)
    normed_one = low(hidden_in * first_rms * gain_one)
    queries = low(rotate(low_back(jnp.dot(normed_one, w_query, precision=highest)).reshape(seq_len, HEADS, HEAD), cos_table, sin_table))
    keys_all = low(rotate(low_back(jnp.dot(normed_one, w_key, precision=highest)).reshape(seq_len, KV_HEADS, HEAD), cos_table, sin_table))
    values_all = low(low_back(jnp.dot(normed_one, w_value, precision=highest))).reshape(seq_len, KV_HEADS, HEAD)
    block_rows = math.gcd(seq_len, 512)
    block_count = seq_len // block_rows
    grouped = queries.reshape(block_count, block_rows, KV_HEADS, group_size, HEAD)
    query_pos = positions.reshape(block_count, block_rows)

    def attend(query_pair):
        query_block, pos_block = query_pair
        raw_scores = low_back(jnp.einsum('bkgd,skd->kgbs', query_block, keys_all, precision=highest))
        visible = positions[None, None, None, :] <= pos_block[None, None, :, None]
        scores = jnp.where(visible, raw_scores * scale_factor, -1e+30)
        top_score = lax.optimization_barrier(jnp.max(scores, axis=-1, keepdims=True))
        weights = jnp.where(visible, jnp.exp(scores - top_score), 0.0)
        weights = weights / lax.optimization_barrier(jnp.sum(weights, axis=-1, keepdims=True))
        return jnp.einsum('kgbs,skd->bkgd', low(weights), values_all, precision=highest)
    attended = lax.map(jax.checkpoint(attend), (grouped, query_pos))
    attn_rows = low(low_back(attended.reshape(seq_len, HEADS * HEAD)))
    mid_state = hidden_in + low_back(jnp.dot(attn_rows, w_out, precision=highest))
    second_rms = lax.rsqrt(lax.optimization_barrier(jnp.mean(mid_state * mid_state, axis=-1, keepdims=True)) + EPSILON)
    normed_two = low(mid_state * second_rms * gain_two)
    gate_lin = low_back(jnp.dot(normed_two, w_gate, precision=highest))
    up_lin = low_back(jnp.dot(normed_two, w_up, precision=highest))
    hidden_act = low(low_back(jax.nn.silu(gate_lin) * up_lin))
    return mid_state + low_back(jnp.dot(hidden_act, w_down, precision=highest))

def reference(tokens, block_order, gain_attn, w_query, w_key, w_value, w_out, gain_mlp, w_gate, w_up, w_down, cotangent):
    seq_len = tokens.shape[1]
    positions = places(block_order, 0, seq_len, seq_len // block_order.shape[0])
    cos_table, sin_table = rotary(positions, HEAD // 2)
    floats = [item.astype(jnp.float32) for item in (tokens, gain_attn, w_query, w_key, w_value, w_out, gain_mlp, w_gate, w_up, w_down)]

    def whole_layer(batch_in, *weight_list):

        def run_one(sequence):
            return forward(sequence, *weight_list, cos_table, sin_table, positions)
        return lax.map(run_one, batch_in)
    result, pull_back = jax.vjp(whole_layer, *floats)
    gradients = pull_back(cotangent.astype(jnp.float32))
    return (result.astype(jnp.bfloat16), gradients[0], gradients[1], gradients[2], gradients[3], gradients[4], gradients[5], gradients[6], gradients[7], gradients[8], gradients[9])
```

```python
import functools
import math

import jax
import jax.numpy as jnp
from jax import lax
from jax.experimental import pallas as pl
from jax.experimental.pallas import tpu as pltpu
from jax.sharding import Mesh
from jax.sharding import PartitionSpec as P

HEADS = 15
KV_HEADS = 5
EPSILON = 1e-05
THETA = 100000.0
BLK = 128
HEAD = 64
EXP_SCALE = math.log2(math.e) / 8.0
MASKED = -1e30


def attend_kernel(key_pos, query_rank, sorted_pos, sorted_id, own_in, other_in, send_ref, out_ref, lse_ref, kv_ref, kvt_ref, ones_v, q_sorted, *, big, small, edge_size, blocks):
    groups, width = own_in.shape[0], HEAD
    rows = blocks * BLK
    eye = (lax.broadcasted_iota(jnp.int32, (BLK, BLK), 0) == lax.broadcasted_iota(jnp.int32, (BLK, BLK), 1)).astype(jnp.bfloat16)
    is_key = lax.broadcasted_iota(jnp.int32, (BLK, 2 * width), 1) < width

    def place(index, _):
        for side, source in enumerate((own_in, other_in)):
            for half in range(2):
                where = pl.multiple_of(key_pos[side * 2 * groups + 2 * index + half] * BLK, BLK)
                piece = source[index, width:, half * BLK:(half + 1) * BLK]
                kvt_ref[:, pl.ds(where, BLK)] = piece
                turned = lax.dot_general(eye, piece, (((1,), (1,)), ((), ())), preferred_element_type=jnp.float32)
                kv_ref[pl.ds(where, BLK), :] = turned.astype(jnp.bfloat16)
                ones_v[pl.ds(where, BLK), :] = jnp.where(is_key, 1.0, turned).astype(jnp.bfloat16)
        for half in range(2):
            query = own_in[index, :width, half * BLK:(half + 1) * BLK]
            query = jnp.concatenate([query, jnp.zeros_like(query)], axis=0)
            q_sorted[pl.ds(pl.multiple_of(query_rank[2 * index + half] * BLK, BLK), BLK), :] = query.T
        return 0

    lax.fori_loop(0, groups, place, 0)

    def tile(index, _):
        low, high = sorted_pos[blocks * index], sorted_pos[blocks * index + blocks - 1]
        query = q_sorted[pl.ds(pl.multiple_of(index * rows, rows), rows), :]
        row = lax.broadcasted_iota(jnp.int32, (rows, 1), 0)
        place_of = row + low * BLK
        for part in range(1, blocks):
            place_of = jnp.where(row >= part * BLK, row + (sorted_pos[blocks * index + part] - part) * BLK, place_of)

        def step(start, carry, size, masked):
            top, total = carry
            scores = lax.dot_general(query, kv_ref[pl.ds(start, size), :], (((1,), (1,)), ((), ())), preferred_element_type=jnp.float32)
            if masked:
                column = start + lax.broadcasted_iota(jnp.int32, scores.shape, 1)
                scores = jnp.where(column <= place_of, scores, MASKED)
            new_top = jnp.maximum(top, jnp.max(scores, axis=1, keepdims=True))
            weights = jnp.exp2((scores - new_top) * EXP_SCALE).astype(jnp.bfloat16)
            factor = jnp.exp2((top - new_top) * EXP_SCALE)
            added = jnp.dot(weights, ones_v[pl.ds(start, size), :], preferred_element_type=jnp.float32)
            return new_top, total * factor + added

        def full(count, carry):
            for part in range(big // small):
                carry = step(pl.multiple_of(count * big + part * small, small), carry, small, False)
            return carry

        def edge(count, carry):
            return step(pl.multiple_of(count * edge_size, edge_size), carry, edge_size, True)

        carry = (jnp.full((rows, 1), MASKED, jnp.float32), jnp.zeros((rows, 2 * width), jnp.float32))
        done = low * BLK // big
        carry = lax.fori_loop(0, done, full, carry)
        top, total = lax.fori_loop(done * (big // edge_size), (high * BLK + BLK + edge_size - 1) // edge_size, edge, carry)
        lse = (top * EXP_SCALE + jnp.log2(total)).T
        total = total.T
        result = total[width:] / total[:1]
        for part in range(blocks):
            ident = sorted_id[blocks * index + part]
            piece = result[:, part * BLK:(part + 1) * BLK]
            out_ref[ident] = piece
            send_ref[ident // 2, :, pl.ds(pl.multiple_of(ident % 2 * BLK, BLK), BLK)] = piece.astype(jnp.bfloat16)
            lse_ref[ident] = lse[:8, part * BLK:(part + 1) * BLK]
        return 0

    lax.fori_loop(0, 2 * groups // blocks, tile, 0)


def attend(key_pos, query_rank, sorted_pos, sorted_id, own_in, other_in, big=1024, small=1024, edge_size=512, blocks=4):
    groups, width = own_in.shape[0], HEAD
    total = 4 * groups * BLK
    vm = pl.BlockSpec(memory_space=pltpu.VMEM)
    sm = pl.BlockSpec(memory_space=pltpu.SMEM)
    return pl.pallas_call(
        functools.partial(attend_kernel, big=big, small=small, edge_size=edge_size, blocks=blocks),
        out_shape=(
            jax.ShapeDtypeStruct((groups, width, 2 * BLK), jnp.bfloat16),
            jax.ShapeDtypeStruct((2 * groups, width, BLK), jnp.float32),
            jax.ShapeDtypeStruct((2 * groups, 8, BLK), jnp.float32),
            jax.ShapeDtypeStruct((total, 2 * width), jnp.bfloat16),
            jax.ShapeDtypeStruct((2 * width, total), jnp.bfloat16),
        ),
        in_specs=[sm] * 4 + [vm] * 2,
        out_specs=(vm,) * 5,
        scratch_shapes=[
            pltpu.VMEM((total, 2 * width), jnp.bfloat16),
            pltpu.VMEM((2 * groups * BLK, 2 * width), jnp.bfloat16),
        ],
        compiler_params=pltpu.CompilerParams(vmem_limit_bytes=48 * 2**20),
        cost_estimate=pl.CostEstimate(flops=40 * 10**9, bytes_accessed=10**7, transcendentals=2 * 10**7),
        name="attend",
    )(key_pos, query_rank, sorted_pos, sorted_id, own_in, other_in)


def back_kernel(key_pos, query_rank, sorted_pos, sorted_id, own_in, da_ref, out_ref, lse_ref, kv_ref, kvt_ref, dq_ref, own_ref, other_ref, dkv, q_sorted, da_sorted, *, big, small, edge_size, flip):
    groups, width = own_in.shape[0], HEAD

    def place(index, _):
        for half in range(2):
            rank = query_rank[2 * index + half]
            q_sorted[rank] = own_in[index, :width, half * BLK:(half + 1) * BLK]
            da_sorted[rank] = da_ref[index, :, half * BLK:(half + 1) * BLK]
        return 0

    lax.fori_loop(0, groups, place, 0)

    def clear(index, _):
        dkv[pl.ds(pl.multiple_of(index * BLK, BLK), BLK), :] = jnp.zeros((BLK, 2 * width), jnp.float32)
        return 0

    lax.fori_loop(0, 4 * groups, clear, 0)

    def tile(index, _):
        low, high = sorted_pos[2 * index], sorted_pos[2 * index + 1]
        first_id, second_id = sorted_id[2 * index], sorted_id[2 * index + 1]
        query = jnp.concatenate([q_sorted[2 * index], q_sorted[2 * index + 1]], axis=1)
        grad = jnp.concatenate([da_sorted[2 * index], da_sorted[2 * index + 1]], axis=1)
        value = jnp.concatenate([out_ref[first_id], out_ref[second_id]], axis=1)
        lse = jnp.concatenate([lse_ref[first_id][:1], lse_ref[second_id][:1]], axis=1)
        delta = jnp.sum(grad.astype(jnp.float32) * value, axis=0, keepdims=True)
        none = jnp.zeros_like(query)
        both = jnp.concatenate([jnp.concatenate([query, none], axis=1), jnp.concatenate([none, grad], axis=1)], axis=0)
        both_t = both.T
        lane = lax.broadcasted_iota(jnp.int32, (1, 2 * BLK), 1)
        place_of = jnp.where(lane < BLK, low * BLK + lane, (high - 1) * BLK + lane)

        def step(start, total, size, masked):
            keys = kv_ref[pl.ds(start, size), :]
            pair = jnp.dot(keys, both, preferred_element_type=jnp.float32)
            weights = jnp.exp2(pair[:, :2 * BLK] * EXP_SCALE - lse)
            if masked:
                row = start + lax.broadcasted_iota(jnp.int32, weights.shape, 0)
                weights = jnp.where(row <= place_of, weights, 0.0)
            grad_scores = (weights * (pair[:, 2 * BLK:] - delta)).astype(jnp.bfloat16)
            weights = weights.astype(jnp.bfloat16)
            dkv[pl.ds(start, size), :] += jnp.dot(jnp.concatenate([grad_scores, weights], axis=1), both_t, preferred_element_type=jnp.float32)
            if flip:
                return total + lax.dot_general(grad_scores, keys, (((0,), (0,)), ((), ())), preferred_element_type=jnp.float32)
            return total + jnp.dot(kvt_ref[:width, pl.ds(start, size)], grad_scores, preferred_element_type=jnp.float32)

        def full(count, carry):
            for part in range(big // small):
                carry = step(pl.multiple_of(count * big + part * small, small), carry, small, False)
            return carry

        def edge(count, carry):
            return step(pl.multiple_of(count * edge_size, edge_size), carry, edge_size, True)

        done = low * BLK // big
        total = jnp.zeros((2 * BLK, 2 * width) if flip else (width, 2 * BLK), jnp.float32)
        total = lax.fori_loop(0, done, full, total)
        total = lax.fori_loop(done * (big // edge_size), (high * BLK + BLK + edge_size - 1) // edge_size, edge, total) * 0.125
        if flip:
            total = total.T[:width]
        for half, ident in enumerate((first_id, second_id)):
            dq_ref[ident // 2, :, pl.ds(pl.multiple_of(ident % 2 * BLK, BLK), BLK)] = total[:, half * BLK:(half + 1) * BLK].astype(jnp.bfloat16)
        return 0

    lax.fori_loop(0, groups, tile, 0)
    factor = jnp.where(lax.broadcasted_iota(jnp.int32, (1, 2 * width), 1) < width, 0.125, 1.0)

    def spread(index, _):
        for side, target in enumerate((own_ref, other_ref)):
            for half in range(2):
                where = pl.multiple_of(key_pos[side * 2 * groups + 2 * index + half] * BLK, BLK)
                target[index, :, half * BLK:(half + 1) * BLK] = (dkv[pl.ds(where, BLK), :] * factor).astype(target.dtype)
        return 0

    lax.fori_loop(0, groups, spread, 0)


def attend_back(key_pos, query_rank, sorted_pos, sorted_id, own_in, da, out, lse, kv, kvt, big=1024, small=1024, edge_size=512, flip=False):
    groups, width = own_in.shape[0], HEAD
    total = 4 * groups * BLK
    vm = pl.BlockSpec(memory_space=pltpu.VMEM)
    sm = pl.BlockSpec(memory_space=pltpu.SMEM)
    return pl.pallas_call(
        functools.partial(back_kernel, big=big, small=small, edge_size=edge_size, flip=flip),
        out_shape=(
            jax.ShapeDtypeStruct((groups, width, 2 * BLK), jnp.bfloat16),
            jax.ShapeDtypeStruct((groups, 2 * width, 2 * BLK), jnp.float32),
            jax.ShapeDtypeStruct((groups, 2 * width, 2 * BLK), jnp.bfloat16),
        ),
        in_specs=[sm] * 4 + [vm] * 6,
        out_specs=(vm,) * 3,
        scratch_shapes=[
            pltpu.VMEM((total, 2 * width), jnp.float32),
            pltpu.VMEM((2 * groups, width, BLK), jnp.bfloat16),
            pltpu.VMEM((2 * groups, width, BLK), jnp.bfloat16),
        ],
        compiler_params=pltpu.CompilerParams(vmem_limit_bytes=48 * 2**20),
        cost_estimate=pl.CostEstimate(flops=60 * 10**9, bytes_accessed=10**7, transcendentals=2 * 10**7),
        name="attend_back",
    )(key_pos, query_rank, sorted_pos, sorted_id, own_in, da, out, lse, kv, kvt)


def turn_project_kernel(mine, x_ref, own, near, far, far_near, cos_ref, sin_ref, hat_ref, send_ref, w_ref):
    shard = own.shape[0]
    for step, piece in enumerate((own, near, far, far_near)):
        w_ref[pl.ds(pl.multiple_of((mine[0] ^ step) * shard, 16), shard), :] = piece[...]
    hidden = x_ref[...].astype(jnp.float32)
    hat = hidden * lax.rsqrt(jnp.mean(hidden * hidden, axis=-1, keepdims=True) + EPSILON)
    hat = hat.astype(jnp.bfloat16)
    hat_ref[...] = hat
    half = HEAD // 2
    cos, sin = cos_ref[...], sin_ref[...]

    def turn(pair):
        front, behind = pair[:half], pair[half:]
        return jnp.concatenate([front * cos - behind * sin, behind * cos + front * sin], axis=0).astype(jnp.bfloat16)

    key_width = KV_HEADS * HEAD
    per = HEADS // KV_HEADS
    lin = jnp.dot(hat, w_ref[:, : 2 * key_width], preferred_element_type=jnp.float32).T
    for head in range(KV_HEADS):
        key = turn(lin[head * HEAD:(head + 1) * HEAD])
        value = lin[key_width + head * HEAD:key_width + (head + 1) * HEAD].astype(jnp.bfloat16)
        for query in range(per):
            send_ref[head * per + query, HEAD:2 * HEAD] = key
            send_ref[head * per + query, 2 * HEAD:] = value
    for head in range(KV_HEADS):
        start = 2 * key_width + head * per * HEAD
        lin = jnp.dot(hat, w_ref[:, start:start + per * HEAD], preferred_element_type=jnp.float32).T
        for query in range(per):
            send_ref[head * per + query, :HEAD] = turn(lin[query * HEAD:(query + 1) * HEAD])
    send_ref[HEADS] = jnp.zeros(send_ref.shape[1:], jnp.bfloat16)


def project(mine, x, pieces, cos, sin, groups):
    shard, columns = pieces[0].shape
    rows, width = x.shape
    vm = pl.BlockSpec(memory_space=pltpu.VMEM)
    return pl.pallas_call(
        turn_project_kernel,
        out_shape=(
            jax.ShapeDtypeStruct((rows, width), jnp.bfloat16),
            jax.ShapeDtypeStruct((groups, 3 * HEAD, rows), jnp.bfloat16),
            jax.ShapeDtypeStruct((width, columns), jnp.bfloat16),
        ),
        in_specs=[pl.BlockSpec(memory_space=pltpu.SMEM)] + [vm] * 7,
        out_specs=(vm,) * 3,
        compiler_params=pltpu.CompilerParams(vmem_limit_bytes=40 * 2**20),
        cost_estimate=pl.CostEstimate(flops=10**9, bytes_accessed=10**7, transcendentals=0),
        name="project",
    )(mine, x, *pieces, cos, sin)


def finish_kernel(mine, home, x_ref, hat_ref, w_ref, mid_ref, cos_ref, sin_ref, keep_ref, give_ref, tokens_ref, turned, hat_t):
    shard = w_ref.shape[0] // 4
    half = HEAD // 2
    cos, sin = cos_ref[...], sin_ref[...]
    key_width = KV_HEADS * HEAD
    per = HEADS // KV_HEADS

    def turn_back(pair):
        front, behind = pair[:half], pair[half:]
        return jnp.concatenate([front * cos + behind * sin, behind * cos - front * sin], axis=0).astype(jnp.bfloat16)

    for head in range(KV_HEADS):
        total = sum(home[head * per + query, HEAD:, :].astype(jnp.float32) for query in range(per))
        total = jnp.concatenate([total[:, :BLK].T, total[:, BLK:].T], axis=1)
        turned[head * HEAD:(head + 1) * HEAD, :] = turn_back(total[:HEAD])
        turned[key_width + head * HEAD:key_width + (head + 1) * HEAD, :] = total[HEAD:].astype(jnp.bfloat16)
        for query in range(per):
            start = 2 * key_width + (head * per + query) * HEAD
            turned[start:start + HEAD, :] = turn_back(home[head * per + query, :HEAD, :].astype(jnp.float32))
    hat_t[...] = hat_ref[...].T
    core = mine[0] & 1
    for target, at in ((keep_ref, core), (give_ref, 1 - core)):
        for part in range(2):
            rows = hat_t[pl.ds(pl.multiple_of((2 * part + at) * shard, 16), shard), :]
            grads = lax.dot_general(rows, turned[...], (((1,), (1,)), ((), ())), preferred_element_type=jnp.float32)
            target[part, :shard, :] = grads.astype(jnp.bfloat16)
            target[part, shard:, :] = jnp.zeros((target.shape[1] - shard, target.shape[2]), jnp.bfloat16)
    scaled = jnp.dot(w_ref[...], turned[...], preferred_element_type=jnp.float32).T
    hidden = x_ref[...].astype(jnp.float32)
    rms = lax.rsqrt(jnp.mean(hidden * hidden, axis=-1, keepdims=True) + EPSILON)
    hat = hidden * rms
    tokens_ref[...] = (mid_ref[...] + rms * (scaled - hat * jnp.mean(scaled * hat, axis=-1, keepdims=True))).astype(jnp.bfloat16)


def finish(mine, home, x, hat, w, mid, cos, sin):
    width, columns = w.shape
    rows = x.shape[0]
    vm = pl.BlockSpec(memory_space=pltpu.VMEM)
    return pl.pallas_call(
        finish_kernel,
        out_shape=(
            jax.ShapeDtypeStruct((2, 256, columns), jnp.bfloat16),
            jax.ShapeDtypeStruct((2, 256, columns), jnp.bfloat16),
            jax.ShapeDtypeStruct((rows, width), jnp.bfloat16),
        ),
        in_specs=[pl.BlockSpec(memory_space=pltpu.SMEM)] + [vm] * 7,
        out_specs=(vm,) * 3,
        scratch_shapes=[pltpu.VMEM((columns, rows), jnp.bfloat16), pltpu.VMEM((width, rows), jnp.bfloat16)],
        compiler_params=pltpu.CompilerParams(vmem_limit_bytes=40 * 2**20),
        cost_estimate=pl.CostEstimate(flops=10**9, bytes_accessed=10**7, transcendentals=0),
        name="finish",
    )(mine, home, x, hat, w, mid, cos, sin)
SEQ_AXES = ("xl", "z", "yh")
CTX_AXES = ("xl", "z", "yh", "yl")
RING_AXES = ("z", "yh", "yl")
CHIP_AXES = ("xh", "xl", "z", "yh", "yl")
FSDP_AXES = ("xh", "core")
SWAP = ((0, 1), (1, 0))
STRIP = 16


def over_core(value):
    return lax.ppermute(value, "core", SWAP)


def over_chip(value):
    return lax.ppermute(value, "xh", SWAP)


def over_both(value):
    return lax.ppermute(value, FSDP_AXES, ((0, 3), (3, 0), (1, 2), (2, 1)))


def trade(value):
    return lax.ppermute(value, ("yl", "core"), ((0, 0), (1, 2), (2, 1), (3, 3)))


def arrange(pieces, xh, core):
    low = jnp.where(core == 1, pieces[1], pieces[0]), jnp.where(core == 1, pieces[0], pieces[1])
    high = jnp.where(core == 1, pieces[3], pieces[2]), jnp.where(core == 1, pieces[2], pieces[3])
    return jnp.stack([jnp.where(xh == 1, h, l) for l, h in zip(low, high)] + [jnp.where(xh == 1, l, h) for l, h in zip(low, high)])


def gather_tokens(rows):
    far = over_chip(rows)
    return jnp.concatenate([rows, over_core(rows), far, over_core(far)])


def scatter_tokens(partial):
    parts = partial.reshape(4, -1, partial.shape[-1])
    received = over_core(jnp.stack([parts[1], parts[3]]).astype(jnp.bfloat16))
    far = over_chip((parts[2] + received[1].astype(jnp.float32)).astype(jnp.bfloat16))
    return parts[0] + received[0].astype(jnp.float32) + far.astype(jnp.float32)


def exchange(value, axes):
    return lax.all_to_all(value, axes, split_axis=0, concat_axis=0, tiled=True)


def pad_heads(value):
    return jnp.concatenate([value, jnp.zeros((1,) + value.shape[1:], value.dtype)])


def per_device(
    tokens,
    block_order,
    gain_attn,
    w_query,
    w_key,
    w_value,
    w_out,
    gain_mlp,
    w_gate,
    w_up,
    w_down,
    cotangent,
):
    f32, bf16 = jnp.float32, jnp.bfloat16
    xh, core = lax.axis_index("xh"), lax.axis_index("core")
    mine = 2 * xh + core
    row_total, width = tokens.shape[1:]
    shard = w_query.shape[0]
    ff_part = w_down.shape[0]
    groups = lax.axis_size(SEQ_AXES)
    key_width = KV_HEADS * HEAD
    gain_one = gain_attn.astype(f32)[:, None]
    gain_two = gain_mlp.astype(f32)[:, None]

    qkv_plain = jnp.concatenate([w_key, w_value, w_query], axis=1).astype(f32)
    qkv_shard = (qkv_plain * gain_one).astype(bf16)
    far_shard = over_chip(qkv_shard)
    near_shard = over_core(qkv_shard)
    hidden_low = trade(tokens[0])
    far_near_shard = over_core(far_shard)

    order = block_order.reshape(groups, 2, 2)
    own_order = jnp.where(core == 0, order[:, 0], order[:, 1]).reshape(-1)
    other_order = jnp.where(core == 0, order[:, 1], order[:, 0]).reshape(-1)
    key_pos = jnp.concatenate([own_order, other_order])
    query_rank = jnp.sum((own_order[None, :] < own_order[:, None]).astype(jnp.int32), axis=1)
    hit = query_rank[None, :] == jnp.arange(2 * groups, dtype=jnp.int32)[:, None]
    sorted_pos = jnp.sum(jnp.where(hit, own_order[None, :], 0), axis=1)
    sorted_id = jnp.sum(jnp.where(hit, jnp.arange(2 * groups, dtype=jnp.int32)[None, :], 0), axis=1)
    here = lax.axis_index(SEQ_AXES)
    own_blocks = lax.dynamic_slice_in_dim(own_order, 2 * here, 2)
    row = jnp.arange(row_total, dtype=jnp.int32)
    own_pos = jnp.where(row < BLK, own_blocks[0] * BLK + row, own_blocks[1] * BLK + row - BLK)
    inverse_freq = THETA ** (-jnp.arange(HEAD // 2, dtype=f32) / (HEAD // 2))
    angles = inverse_freq[:, None] * own_pos.astype(f32)[None, :]
    cos_table, sin_table = jnp.cos(angles), jnp.sin(angles)

    normed_one, group_send, qkv_full = project(
        mine.reshape(1), hidden_low, (qkv_shard, near_shard, far_shard, far_near_shard), cos_table, sin_table, groups
    )
    group_own = exchange(group_send, SEQ_AXES)
    group_other = over_core(group_own)

    normed_one, w_out, w_gate, w_up, upstream = lax.optimization_barrier((normed_one, w_out, w_gate, w_up, cotangent[0]))
    upstream = trade(upstream)
    far_out = over_chip(w_out)
    out_full = arrange([w_out, over_core(w_out), far_out, over_core(far_out)], xh, core).reshape(width, width)

    def gate_up(step):
        start = (mine ^ step) * ff_part
        both = [lax.dynamic_slice_in_dim(w, start, ff_part, 1).astype(f32) * gain_two for w in (w_gate, w_up)]
        return jnp.stack(both).astype(bf16)

    gate_part, up_part = (
        arrange([gate_up(0), over_core(gate_up(1)), over_chip(gate_up(2)), over_both(gate_up(3))], xh, core).transpose(1, 0, 2, 3).reshape(2, width, ff_part)
    )
    upstream_all = gather_tokens(upstream)

    out_send, out_blocks, lse, kv_sorted, kv_turned = attend(key_pos, query_rank, sorted_pos, sorted_id, group_own, group_other)
    attn_turned = exchange(out_send, SEQ_AXES)[:HEADS].reshape(HEADS * HEAD, row_total)

    hidden_in = hidden_low.astype(f32)
    mid_state = hidden_in + lax.dot_general(attn_turned, out_full, (((0,), (0,)), ((), ())), preferred_element_type=f32)
    second_rms = lax.rsqrt(jnp.mean(mid_state * mid_state, axis=-1, keepdims=True) + EPSILON)
    second_hat = mid_state * second_rms

    normed_all = gather_tokens(second_hat.astype(bf16))
    gate_lin = jnp.dot(normed_all, gate_part, preferred_element_type=f32)
    up_lin = jnp.dot(normed_all, up_part, preferred_element_type=f32)
    sigmoid_gate = jax.nn.sigmoid(gate_lin)
    activated = gate_lin * sigmoid_gate
    hidden_act = (activated * up_lin).astype(bf16)
    grad_act = lax.dot_general(upstream_all, w_down, (((1,), (1,)), ((), ())), preferred_element_type=f32).astype(bf16).astype(f32)
    grad_gate_lin = (grad_act * up_lin * sigmoid_gate * (1.0 + gate_lin * (1.0 - sigmoid_gate))).astype(bf16)
    grad_up_lin = (grad_act * activated).astype(bf16)
    scaled_part = lax.dot_general(grad_gate_lin, gate_part, (((1,), (1,)), ((), ())), preferred_element_type=f32) + lax.dot_general(
        grad_up_lin, up_part, (((1,), (1,)), ((), ())), preferred_element_type=f32
    )
    scaled_two = scatter_tokens(scaled_part)
    grad_mid = upstream.astype(f32) + second_rms * (scaled_two - second_hat * jnp.mean(scaled_two * second_hat, axis=-1, keepdims=True))
    mid_low = grad_mid.astype(bf16)
    grad_attn = lax.dot_general(out_full, mid_low, (((1,), (1,)), ((), ())), preferred_element_type=f32).astype(bf16)
    grad_group = exchange(pad_heads(grad_attn.reshape(HEADS, HEAD, row_total)), SEQ_AXES)

    turned = (((0,), (0,)), ((), ()))
    ring = lax.axis_size(RING_AXES)
    strips = shard // STRIP
    stacked = jnp.stack(
        [
            lax.dot_general(normed_all, grad_gate_lin, turned, preferred_element_type=f32).astype(bf16),
            lax.dot_general(normed_all, grad_up_lin, turned, preferred_element_type=f32).astype(bf16),
            lax.dot_general(upstream_all, hidden_act, turned, preferred_element_type=f32).astype(bf16),
        ]
    ).reshape(12, strips, STRIP, ff_part)
    stacked = jnp.pad(stacked.transpose(1, 0, 2, 3), ((0, ring - strips), (0, 0), (0, 0), (0, 0)))
    reduced = lax.psum_scatter(stacked.reshape(ring, 12 * STRIP, ff_part), RING_AXES, scatter_dimension=0, tiled=True)[0]

    result = mid_state + scatter_tokens(jnp.dot(hidden_act, w_down, preferred_element_type=f32))
    block_out = trade(result.astype(bf16))[None]

    ctx = lax.axis_size(CTX_AXES)
    slab = 8
    by_core = lambda value, at: lax.dynamic_index_in_dim(value, at, 1, keepdims=False)
    grad_out = jnp.dot(attn_turned, mid_low, preferred_element_type=f32).reshape(2, 2, shard, width)
    grad_out = by_core(grad_out, core) + over_core(by_core(grad_out, 1 - core).astype(bf16)).astype(f32)
    grad_out = jnp.pad(grad_out.astype(bf16), ((0, 0), (0, ctx * slab - shard), (0, 0))).reshape(2 * ctx, slab, width)
    grad_out, grad_group = lax.optimization_barrier((grad_out, grad_group))
    out_sum = jnp.sum(exchange(grad_out, CHIP_AXES).astype(f32), axis=0).astype(bf16)

    dq, dkv_own, dkv_other = attend_back(key_pos, query_rank, sorted_pos, sorted_id, group_own, grad_group, out_blocks, lse, kv_sorted, kv_turned)
    dkv_other, reduced = lax.optimization_barrier((dkv_other, reduced))
    dkv = (dkv_own + over_core(dkv_other).astype(f32)).astype(bf16)
    home = exchange(jnp.concatenate([dq, dkv], axis=1), SEQ_AXES)

    reduced = (reduced.astype(f32) + lax.ppermute(reduced, "xl", SWAP).astype(f32)).astype(bf16).reshape(3, 4, STRIP, ff_part)
    part = lambda step: lax.dynamic_index_in_dim(reduced[:2], mine ^ step, 1, keepdims=False)
    pieces = arrange([part(0), over_core(part(1)), over_chip(part(2)), over_both(part(3))], xh, core).transpose(1, 0, 2, 3)
    whole = lax.all_gather(jnp.concatenate([pieces, reduced[2:]]), RING_AXES, axis=0, tiled=False)
    whole = whole[:strips].transpose(1, 2, 0, 3, 4).reshape(3, 4, shard, ff_part).astype(f32)
    gate_sum = whole[0].transpose(1, 0, 2).reshape(shard, 4 * ff_part)
    up_sum = whole[1].transpose(1, 0, 2).reshape(shard, 4 * ff_part)
    down_shard = whole[2].reshape(width, ff_part).T
    gain_two_shard = jnp.sum(gate_sum * w_gate.astype(f32) + up_sum * w_up.astype(f32), axis=1)

    keep, give, grad_tokens = finish(mine.reshape(1), home, hidden_low, normed_one, qkv_full, grad_mid, cos_table, sin_table)
    grad_tokens = trade(grad_tokens).astype(f32)[None]
    columns = keep.shape[-1]
    chip_sum = (keep.astype(f32) + over_core(give).astype(f32)).astype(bf16).reshape(2 * ctx, slab, columns)
    qkv_sum = jnp.sum(exchange(chip_sum, CHIP_AXES).astype(f32), axis=0).astype(bf16)
    summed = jnp.concatenate([qkv_sum, out_sum], axis=1)
    final = exchange(jnp.broadcast_to(summed[None], (ctx,) + summed.shape), CTX_AXES).reshape(ctx * slab, -1)[:shard].astype(f32)
    qkv_final, out_shard = final[:, :columns], final[:, columns:]
    gain_one_shard = jnp.sum(qkv_final * qkv_plain, axis=1)
    qkv_final = qkv_final * gain_one
    return (
        block_out,
        grad_tokens,
        gain_one_shard,
        qkv_final[:, 2 * key_width :],
        qkv_final[:, :key_width],
        qkv_final[:, key_width : 2 * key_width],
        out_shard,
        gain_two_shard,
        gate_sum * gain_two,
        up_sum * gain_two,
        down_shard,
    )


def solution(mesh):
    fine = Mesh(mesh.devices.reshape(2, 4, 2, 2, 2, 2), ("xl", "z", "yh", "yl", "xh", "core"))
    rows = P(FSDP_AXES, CTX_AXES, None)
    gain = P(FSDP_AXES)
    weight = P(FSDP_AXES, None)
    return jax.shard_map(
        per_device,
        mesh=fine,
        in_specs=(rows, P(), gain, weight, weight, weight, weight, gain, weight, weight, weight, rows),
        out_specs=(rows, rows, gain, weight, weight, weight, weight, gain, weight, weight, weight),
        check_vma=False,
    )
```

```python
import functools
import math

import jax
import jax.numpy as jnp
from jax import lax
from jax.experimental import pallas as pl
from jax.experimental.pallas import tpu as pltpu
from jax.sharding import Mesh
from jax.sharding import PartitionSpec as P

HEADS = 15
KV_HEADS = 5
EPSILON = 1e-05
THETA = 100000.0
SEQ_AXES = ("xl", "z", "yh")
CTX_AXES = ("xl", "z", "yh", "yl")
RING_AXES = ("z", "yh", "yl")
CHIP_AXES = ("xh", "xl", "z", "yh", "yl")
FSDP_AXES = ("xh", "core")
SWAP = ((0, 1), (1, 0))
STRIP = 16


BLK = 128
HEAD = 64
EXP_SCALE = math.log2(math.e) / 8.0
MASKED = -1e30


def attend_kernel(key_pos, query_rank, sorted_pos, sorted_id, own_in, other_in, send_ref, out_ref, lse_ref, kv_ref, kvt_ref, ones_v, q_sorted, *, big, small, edge_size, blocks):
    groups, width = own_in.shape[0], HEAD
    rows = blocks * BLK
    eye = (lax.broadcasted_iota(jnp.int32, (BLK, BLK), 0) == lax.broadcasted_iota(jnp.int32, (BLK, BLK), 1)).astype(jnp.bfloat16)
    is_key = lax.broadcasted_iota(jnp.int32, (BLK, 2 * width), 1) < width

    def place(index, _):
        for side, source in enumerate((own_in, other_in)):
            for half in range(2):
                where = pl.multiple_of(key_pos[side * 2 * groups + 2 * index + half] * BLK, BLK)
                piece = source[index, width:, half * BLK:(half + 1) * BLK]
                kvt_ref[:, pl.ds(where, BLK)] = piece
                turned = lax.dot_general(eye, piece, (((1,), (1,)), ((), ())), preferred_element_type=jnp.float32)
                kv_ref[pl.ds(where, BLK), :] = turned.astype(jnp.bfloat16)
                ones_v[pl.ds(where, BLK), :] = jnp.where(is_key, 1.0, turned).astype(jnp.bfloat16)
        for half in range(2):
            query = own_in[index, :width, half * BLK:(half + 1) * BLK]
            query = jnp.concatenate([query, jnp.zeros_like(query)], axis=0)
            q_sorted[pl.ds(pl.multiple_of(query_rank[2 * index + half] * BLK, BLK), BLK), :] = query.T
        return 0

    lax.fori_loop(0, groups, place, 0)

    def tile(index, _):
        low, high = sorted_pos[blocks * index], sorted_pos[blocks * index + blocks - 1]
        query = q_sorted[pl.ds(pl.multiple_of(index * rows, rows), rows), :]
        row = lax.broadcasted_iota(jnp.int32, (rows, 1), 0)
        place_of = row + low * BLK
        for part in range(1, blocks):
            place_of = jnp.where(row >= part * BLK, row + (sorted_pos[blocks * index + part] - part) * BLK, place_of)

        def step(start, carry, size, masked):
            top, total = carry
            scores = lax.dot_general(query, kv_ref[pl.ds(start, size), :], (((1,), (1,)), ((), ())), preferred_element_type=jnp.float32)
            if masked:
                column = start + lax.broadcasted_iota(jnp.int32, scores.shape, 1)
                scores = jnp.where(column <= place_of, scores, MASKED)
            new_top = jnp.maximum(top, jnp.max(scores, axis=1, keepdims=True))
            weights = jnp.exp2((scores - new_top) * EXP_SCALE).astype(jnp.bfloat16)
            factor = jnp.exp2((top - new_top) * EXP_SCALE)
            added = jnp.dot(weights, ones_v[pl.ds(start, size), :], preferred_element_type=jnp.float32)
            return new_top, total * factor + added

        def full(count, carry):
            for part in range(big // small):
                carry = step(pl.multiple_of(count * big + part * small, small), carry, small, False)
            return carry

        def edge(count, carry):
            return step(pl.multiple_of(count * edge_size, edge_size), carry, edge_size, True)

        carry = (jnp.full((rows, 1), MASKED, jnp.float32), jnp.zeros((rows, 2 * width), jnp.float32))
        done = low * BLK // big
        carry = lax.fori_loop(0, done, full, carry)
        top, total = lax.fori_loop(done * (big // edge_size), (high * BLK + BLK + edge_size - 1) // edge_size, edge, carry)
        lse = (top * EXP_SCALE + jnp.log2(total)).T
        total = total.T
        result = total[width:] / total[:1]
        for part in range(blocks):
            ident = sorted_id[blocks * index + part]
            piece = result[:, part * BLK:(part + 1) * BLK]
            out_ref[ident] = piece
            send_ref[ident // 2, :, pl.ds(pl.multiple_of(ident % 2 * BLK, BLK), BLK)] = piece.astype(jnp.bfloat16)
            lse_ref[ident] = lse[:8, part * BLK:(part + 1) * BLK]
        return 0

    lax.fori_loop(0, 2 * groups // blocks, tile, 0)


def attend(key_pos, query_rank, sorted_pos, sorted_id, own_in, other_in, big=1024, small=1024, edge_size=512, blocks=4):
    groups, width = own_in.shape[0], HEAD
    total = 4 * groups * BLK
    vm = pl.BlockSpec(memory_space=pltpu.VMEM)
    sm = pl.BlockSpec(memory_space=pltpu.SMEM)
    return pl.pallas_call(
        functools.partial(attend_kernel, big=big, small=small, edge_size=edge_size, blocks=blocks),
        out_shape=(
            jax.ShapeDtypeStruct((groups, width, 2 * BLK), jnp.bfloat16),
            jax.ShapeDtypeStruct((2 * groups, width, BLK), jnp.float32),
            jax.ShapeDtypeStruct((2 * groups, 8, BLK), jnp.float32),
            jax.ShapeDtypeStruct((total, 2 * width), jnp.bfloat16),
            jax.ShapeDtypeStruct((2 * width, total), jnp.bfloat16),
        ),
        in_specs=[sm] * 4 + [vm] * 2,
        out_specs=(vm,) * 5,
        scratch_shapes=[
            pltpu.VMEM((total, 2 * width), jnp.bfloat16),
            pltpu.VMEM((2 * groups * BLK, 2 * width), jnp.bfloat16),
        ],
        compiler_params=pltpu.CompilerParams(vmem_limit_bytes=48 * 2**20),
        cost_estimate=pl.CostEstimate(flops=40 * 10**9, bytes_accessed=10**7, transcendentals=2 * 10**7),
        name="attend",
    )(key_pos, query_rank, sorted_pos, sorted_id, own_in, other_in)


def back_kernel(key_pos, query_rank, sorted_pos, sorted_id, own_in, da_ref, out_ref, lse_ref, kv_ref, kvt_ref, dq_ref, own_ref, other_ref, dkv, q_sorted, da_sorted, *, big, small, edge_size, flip):
    groups, width = own_in.shape[0], HEAD

    def place(index, _):
        for half in range(2):
            rank = query_rank[2 * index + half]
            q_sorted[rank] = own_in[index, :width, half * BLK:(half + 1) * BLK]
            da_sorted[rank] = da_ref[index, :, half * BLK:(half + 1) * BLK]
        return 0

    lax.fori_loop(0, groups, place, 0)

    def clear(index, _):
        dkv[pl.ds(pl.multiple_of(index * BLK, BLK), BLK), :] = jnp.zeros((BLK, 2 * width), jnp.float32)
        return 0

    lax.fori_loop(0, 4 * groups, clear, 0)

    def tile(index, _):
        low, high = sorted_pos[2 * index], sorted_pos[2 * index + 1]
        first_id, second_id = sorted_id[2 * index], sorted_id[2 * index + 1]
        query = jnp.concatenate([q_sorted[2 * index], q_sorted[2 * index + 1]], axis=1)
        grad = jnp.concatenate([da_sorted[2 * index], da_sorted[2 * index + 1]], axis=1)
        value = jnp.concatenate([out_ref[first_id], out_ref[second_id]], axis=1)
        lse = jnp.concatenate([lse_ref[first_id][:1], lse_ref[second_id][:1]], axis=1)
        delta = jnp.sum(grad.astype(jnp.float32) * value, axis=0, keepdims=True)
        none = jnp.zeros_like(query)
        both = jnp.concatenate([jnp.concatenate([query, none], axis=1), jnp.concatenate([none, grad], axis=1)], axis=0)
        both_t = both.T
        lane = lax.broadcasted_iota(jnp.int32, (1, 2 * BLK), 1)
        place_of = jnp.where(lane < BLK, low * BLK + lane, (high - 1) * BLK + lane)

        def step(start, total, size, masked):
            keys = kv_ref[pl.ds(start, size), :]
            pair = jnp.dot(keys, both, preferred_element_type=jnp.float32)
            weights = jnp.exp2(pair[:, :2 * BLK] * EXP_SCALE - lse)
            if masked:
                row = start + lax.broadcasted_iota(jnp.int32, weights.shape, 0)
                weights = jnp.where(row <= place_of, weights, 0.0)
            grad_scores = (weights * (pair[:, 2 * BLK:] - delta)).astype(jnp.bfloat16)
            weights = weights.astype(jnp.bfloat16)
            dkv[pl.ds(start, size), :] += jnp.dot(jnp.concatenate([grad_scores, weights], axis=1), both_t, preferred_element_type=jnp.float32)
            if flip:
                return total + lax.dot_general(grad_scores, keys, (((0,), (0,)), ((), ())), preferred_element_type=jnp.float32)
            return total + jnp.dot(kvt_ref[:width, pl.ds(start, size)], grad_scores, preferred_element_type=jnp.float32)

        def full(count, carry):
            for part in range(big // small):
                carry = step(pl.multiple_of(count * big + part * small, small), carry, small, False)
            return carry

        def edge(count, carry):
            return step(pl.multiple_of(count * edge_size, edge_size), carry, edge_size, True)

        done = low * BLK // big
        total = jnp.zeros((2 * BLK, 2 * width) if flip else (width, 2 * BLK), jnp.float32)
        total = lax.fori_loop(0, done, full, total)
        total = lax.fori_loop(done * (big // edge_size), (high * BLK + BLK + edge_size - 1) // edge_size, edge, total) * 0.125
        if flip:
            total = total.T[:width]
        for half, ident in enumerate((first_id, second_id)):
            dq_ref[ident // 2, :, pl.ds(pl.multiple_of(ident % 2 * BLK, BLK), BLK)] = total[:, half * BLK:(half + 1) * BLK].astype(jnp.bfloat16)
        return 0

    lax.fori_loop(0, groups, tile, 0)
    factor = jnp.where(lax.broadcasted_iota(jnp.int32, (1, 2 * width), 1) < width, 0.125, 1.0)

    def spread(index, _):
        for side, target in enumerate((own_ref, other_ref)):
            for half in range(2):
                where = pl.multiple_of(key_pos[side * 2 * groups + 2 * index + half] * BLK, BLK)
                target[index, :, half * BLK:(half + 1) * BLK] = (dkv[pl.ds(where, BLK), :] * factor).astype(target.dtype)
        return 0

    lax.fori_loop(0, groups, spread, 0)


def attend_back(key_pos, query_rank, sorted_pos, sorted_id, own_in, da, out, lse, kv, kvt, big=1024, small=1024, edge_size=512, flip=False):
    groups, width = own_in.shape[0], HEAD
    total = 4 * groups * BLK
    vm = pl.BlockSpec(memory_space=pltpu.VMEM)
    sm = pl.BlockSpec(memory_space=pltpu.SMEM)
    return pl.pallas_call(
        functools.partial(back_kernel, big=big, small=small, edge_size=edge_size, flip=flip),
        out_shape=(
            jax.ShapeDtypeStruct((groups, width, 2 * BLK), jnp.bfloat16),
            jax.ShapeDtypeStruct((groups, 2 * width, 2 * BLK), jnp.float32),
            jax.ShapeDtypeStruct((groups, 2 * width, 2 * BLK), jnp.bfloat16),
        ),
        in_specs=[sm] * 4 + [vm] * 6,
        out_specs=(vm,) * 3,
        scratch_shapes=[
            pltpu.VMEM((total, 2 * width), jnp.float32),
            pltpu.VMEM((2 * groups, width, BLK), jnp.bfloat16),
            pltpu.VMEM((2 * groups, width, BLK), jnp.bfloat16),
        ],
        compiler_params=pltpu.CompilerParams(vmem_limit_bytes=48 * 2**20),
        cost_estimate=pl.CostEstimate(flops=60 * 10**9, bytes_accessed=10**7, transcendentals=2 * 10**7),
        name="attend_back",
    )(key_pos, query_rank, sorted_pos, sorted_id, own_in, da, out, lse, kv, kvt)


def turn_project_kernel(mine, x_ref, own, near, far, far_near, cos_ref, sin_ref, hat_ref, send_ref, w_ref):
    shard = own.shape[0]
    for step, piece in enumerate((own, near, far, far_near)):
        w_ref[pl.ds(pl.multiple_of((mine[0] ^ step) * shard, 16), shard), :] = piece[...]
    hidden = x_ref[...].astype(jnp.float32)
    hat = hidden * lax.rsqrt(jnp.mean(hidden * hidden, axis=-1, keepdims=True) + EPSILON)
    hat = hat.astype(jnp.bfloat16)
    hat_ref[...] = hat
    half = HEAD // 2
    cos, sin = cos_ref[...], sin_ref[...]

    def turn(pair):
        front, behind = pair[:half], pair[half:]
        return jnp.concatenate([front * cos - behind * sin, behind * cos + front * sin], axis=0).astype(jnp.bfloat16)

    key_width = KV_HEADS * HEAD
    per = HEADS // KV_HEADS
    lin = jnp.dot(hat, w_ref[:, : 2 * key_width], preferred_element_type=jnp.float32).T
    for head in range(KV_HEADS):
        key = turn(lin[head * HEAD:(head + 1) * HEAD])
        value = lin[key_width + head * HEAD:key_width + (head + 1) * HEAD].astype(jnp.bfloat16)
        for query in range(per):
            send_ref[head * per + query, HEAD:2 * HEAD] = key
            send_ref[head * per + query, 2 * HEAD:] = value
    for head in range(KV_HEADS):
        start = 2 * key_width + head * per * HEAD
        lin = jnp.dot(hat, w_ref[:, start:start + per * HEAD], preferred_element_type=jnp.float32).T
        for query in range(per):
            send_ref[head * per + query, :HEAD] = turn(lin[query * HEAD:(query + 1) * HEAD])
    send_ref[HEADS] = jnp.zeros(send_ref.shape[1:], jnp.bfloat16)


def project(mine, x, pieces, cos, sin, groups):
    shard, columns = pieces[0].shape
    rows, width = x.shape
    vm = pl.BlockSpec(memory_space=pltpu.VMEM)
    return pl.pallas_call(
        turn_project_kernel,
        out_shape=(
            jax.ShapeDtypeStruct((rows, width), jnp.bfloat16),
            jax.ShapeDtypeStruct((groups, 3 * HEAD, rows), jnp.bfloat16),
            jax.ShapeDtypeStruct((width, columns), jnp.bfloat16),
        ),
        in_specs=[pl.BlockSpec(memory_space=pltpu.SMEM)] + [vm] * 7,
        out_specs=(vm,) * 3,
        compiler_params=pltpu.CompilerParams(vmem_limit_bytes=40 * 2**20),
        cost_estimate=pl.CostEstimate(flops=10**9, bytes_accessed=10**7, transcendentals=0),
        name="project",
    )(mine, x, *pieces, cos, sin)


def finish_kernel(mine, home, x_ref, hat_ref, w_ref, mid_ref, cos_ref, sin_ref, keep_ref, give_ref, tokens_ref, turned, hat_t):
    shard = w_ref.shape[0] // 4
    half = HEAD // 2
    cos, sin = cos_ref[...], sin_ref[...]
    key_width = KV_HEADS * HEAD
    per = HEADS // KV_HEADS

    def turn_back(pair):
        front, behind = pair[:half], pair[half:]
        return jnp.concatenate([front * cos + behind * sin, behind * cos - front * sin], axis=0).astype(jnp.bfloat16)

    for head in range(KV_HEADS):
        total = sum(home[head * per + query, HEAD:, :].astype(jnp.float32) for query in range(per))
        total = jnp.concatenate([total[:, :BLK].T, total[:, BLK:].T], axis=1)
        turned[head * HEAD:(head + 1) * HEAD, :] = turn_back(total[:HEAD])
        turned[key_width + head * HEAD:key_width + (head + 1) * HEAD, :] = total[HEAD:].astype(jnp.bfloat16)
        for query in range(per):
            start = 2 * key_width + (head * per + query) * HEAD
            turned[start:start + HEAD, :] = turn_back(home[head * per + query, :HEAD, :].astype(jnp.float32))
    hat_t[...] = hat_ref[...].T
    core = mine[0] & 1
    for target, at in ((keep_ref, core), (give_ref, 1 - core)):
        target[...] = jnp.zeros(target.shape, target.dtype)
        for part in range(2):
            rows = hat_t[pl.ds(pl.multiple_of((2 * part + at) * shard, 16), shard), :]
            grads = lax.dot_general(rows, turned[...], (((1,), (1,)), ((), ())), preferred_element_type=jnp.float32)
            target[part, :shard, : grads.shape[1]] = grads.astype(jnp.bfloat16)
    scaled = jnp.dot(w_ref[...], turned[...], preferred_element_type=jnp.float32).T
    hidden = x_ref[...].astype(jnp.float32)
    rms = lax.rsqrt(jnp.mean(hidden * hidden, axis=-1, keepdims=True) + EPSILON)
    hat = hidden * rms
    tokens_ref[...] = (mid_ref[...] + rms * (scaled - hat * jnp.mean(scaled * hat, axis=-1, keepdims=True))).astype(jnp.bfloat16)


def finish(mine, home, x, hat, w, mid, cos, sin):
    width, columns = w.shape
    rows = x.shape[0]
    vm = pl.BlockSpec(memory_space=pltpu.VMEM)
    return pl.pallas_call(
        finish_kernel,
        out_shape=(
            jax.ShapeDtypeStruct((2, 256, -(-columns // BLK) * BLK), jnp.bfloat16),
            jax.ShapeDtypeStruct((2, 256, -(-columns // BLK) * BLK), jnp.bfloat16),
            jax.ShapeDtypeStruct((rows, width), jnp.bfloat16),
        ),
        in_specs=[pl.BlockSpec(memory_space=pltpu.SMEM)] + [vm] * 7,
        out_specs=(vm,) * 3,
        scratch_shapes=[pltpu.VMEM((columns, rows), jnp.bfloat16), pltpu.VMEM((width, rows), jnp.bfloat16)],
        compiler_params=pltpu.CompilerParams(vmem_limit_bytes=40 * 2**20),
        cost_estimate=pl.CostEstimate(flops=10**9, bytes_accessed=10**7, transcendentals=0),
        name="finish",
    )(mine, home, x, hat, w, mid, cos, sin)


def in_vmem(kernel, out_shape, scalars, arrays, scratch=(), flops=10**9, name=None):
    vm = pl.BlockSpec(memory_space=pltpu.VMEM)
    return pl.pallas_call(
        kernel,
        out_shape=tuple(jax.ShapeDtypeStruct(shape, dtype) for shape, dtype in out_shape),
        in_specs=[pl.BlockSpec(memory_space=pltpu.SMEM)] * len(scalars) + [vm] * len(arrays),
        out_specs=(vm,) * len(out_shape),
        scratch_shapes=[pltpu.VMEM(shape, dtype) for shape, dtype in scratch],
        compiler_params=pltpu.CompilerParams(vmem_limit_bytes=48 * 2**20),
        cost_estimate=pl.CostEstimate(flops=flops, bytes_accessed=10**7, transcendentals=0),
        name=name,
    )(*scalars, *arrays)


def across(left, right):
    return lax.dot_general(left, right, (((1,), (1,)), ((), ())), preferred_element_type=jnp.float32)


def unit_rms(value):
    return lax.rsqrt(jnp.mean(value * value, axis=-1, keepdims=True) + EPSILON)


def norm_back(value, grad):
    rms = unit_rms(value)
    hat = value * rms
    return rms * (grad - hat * jnp.mean(grad * hat, axis=-1, keepdims=True))


def out_kernel(mine, attn, x_ref, own, near, far, far_near, mid_ref, hat_ref, w_ref):
    shard = own.shape[0]
    for step, piece in enumerate((own, near, far, far_near)):
        w_ref[pl.ds(pl.multiple_of((mine[0] ^ step) * shard, 16), shard), :] = piece[...]
    rows = attn[:HEADS].reshape(HEADS * HEAD, attn.shape[2]).T
    mid = x_ref[...].astype(jnp.float32) + jnp.dot(rows, w_ref[...], preferred_element_type=jnp.float32)
    mid_ref[...] = mid
    hat_ref[...] = (mid * unit_rms(mid)).astype(jnp.bfloat16)


def project_out(mine, attn, x, pieces):
    shape = x.shape
    width = shape[1]
    return in_vmem(
        out_kernel, ((shape, jnp.float32), (shape, jnp.bfloat16), ((width, width), jnp.bfloat16)), (mine,), (attn, x, *pieces), name="project_out"
    )


def feed_kernel(mine, *refs):
    hats, grads, weights, (w_down,) = refs[:4], refs[4:8], refs[8:12], refs[12:13]
    scaled_keep, scaled_send, out_keep, out_send, act_ref, gate_grad_ref, up_grad_ref, w_gate, w_up = refs[13:]
    shard = weights[0].shape[1]
    for step, piece in enumerate(weights):
        where = pl.ds(pl.multiple_of((mine[0] ^ step) * shard, 16), shard)
        w_gate[where, :] = piece[0]
        w_up[where, :] = piece[1]
    rows = hats[0].shape[0]
    for step in range(4):
        here = slice(step * rows, (step + 1) * rows)
        hat = hats[step][...]
        gate = jnp.dot(hat, w_gate[...], preferred_element_type=jnp.float32)
        up = jnp.dot(hat, w_up[...], preferred_element_type=jnp.float32)
        sigmoid = jax.nn.sigmoid(gate)
        silu = gate * sigmoid
        act = (silu * up).astype(jnp.bfloat16)
        act_ref[here, :] = act
        grad_act = across(grads[step][...], w_down[...]).astype(jnp.bfloat16).astype(jnp.float32)
        gate_grad = (grad_act * up * sigmoid * (1.0 + gate * (1.0 - sigmoid))).astype(jnp.bfloat16)
        up_grad = (grad_act * silu).astype(jnp.bfloat16)
        gate_grad_ref[here, :] = gate_grad
        up_grad_ref[here, :] = up_grad
        scaled = across(gate_grad, w_gate[...]) + across(up_grad, w_up[...])
        out = jnp.dot(act, w_down[...], preferred_element_type=jnp.float32)
        if step % 2:
            scaled_send[step // 2, :, : scaled.shape[1]] = scaled.astype(jnp.bfloat16)
            out_send[step // 2, :, : out.shape[1]] = out.astype(jnp.bfloat16)
            for target in (scaled_send, out_send):
                target[step // 2, :, scaled.shape[1]:] = jnp.zeros((rows, target.shape[2] - scaled.shape[1]), jnp.bfloat16)
        else:
            scaled_keep[step // 2] = scaled
            out_keep[step // 2] = out


def feed(mine, hats, grads, weights, w_down):
    rows, width = hats[0].shape
    part = w_down.shape[0]
    pair = (2, rows, width)
    sent = (2, rows, -(-width // 256) * 256)
    hidden = ((4 * rows, part), jnp.bfloat16)
    return in_vmem(
        feed_kernel,
        ((pair, jnp.float32), (sent, jnp.bfloat16), (pair, jnp.float32), (sent, jnp.bfloat16), hidden, hidden, hidden),
        (mine,),
        (*hats, *grads, *weights, w_down),
        scratch=(((width, part), jnp.bfloat16),) * 2,
        flops=10**10,
        name="feed",
    )


def feed_grads_kernel(*refs):
    hats, grads, (act, gate_grad, up_grad), (out_ref, hat_t, grad_t) = refs[:4], refs[4:8], refs[8:11], refs[11:]
    rows = hats[0].shape[0]
    for step in range(4):
        here = slice(step * rows, (step + 1) * rows)
        hat_t[:, here] = hats[step][...].T
        grad_t[:, here] = grads[step][...].T
    shard = hat_t.shape[0] // 4
    strips = shard // STRIP
    for index, (left, right) in enumerate(((hat_t, gate_grad), (hat_t, up_grad), (grad_t, act))):
        for part in range(4):
            product = jnp.dot(left[part * shard:(part + 1) * shard, :], right[...], preferred_element_type=jnp.float32)
            out_ref[:strips, 4 * index + part] = product.astype(jnp.bfloat16).reshape(strips, STRIP, product.shape[1])
    out_ref[strips:] = jnp.zeros((out_ref.shape[0] - strips,) + out_ref.shape[1:], jnp.bfloat16)


def feed_grads(hats, grads, act, gate_grad, up_grad, ring):
    rows, width = hats[0].shape
    turned = ((width, 4 * rows), jnp.bfloat16)
    return in_vmem(
        feed_grads_kernel,
        (((ring, 12, STRIP, act.shape[1]), jnp.bfloat16),),
        (),
        (*hats, *grads, act, gate_grad, up_grad),
        scratch=(turned, turned),
        flops=8 * 10**9,
        name="feed_grads",
    )[0]


def mid_kernel(keep, received, far, mid_ref, grad_ref, w_ref, total_ref, low_ref, send_ref):
    scaled = keep[0] + received[0, :, : keep.shape[2]].astype(jnp.float32) + far[...].astype(jnp.float32)
    total = grad_ref[...].astype(jnp.float32) + norm_back(mid_ref[...], scaled)
    total_ref[...] = total
    low = total.astype(jnp.bfloat16)
    low_ref[...] = low
    send_ref[:HEADS] = across(w_ref[...], low).astype(jnp.bfloat16).reshape(HEADS, HEAD, low.shape[0])
    send_ref[HEADS:] = jnp.zeros((send_ref.shape[0] - HEADS,) + send_ref.shape[1:], jnp.bfloat16)


def mid_back(keep, received, far, mid, grad, w_out, groups):
    shape = mid.shape
    return in_vmem(
        mid_kernel,
        ((shape, jnp.float32), (shape, jnp.bfloat16), ((groups, HEAD, shape[0]), jnp.bfloat16)),
        (),
        (keep, received, far, mid, grad, w_out),
        name="mid_back",
    )


def out_grad_kernel(mine, attn, low, keep_ref, give_ref, rows_ref):
    width = low.shape[1]
    shard = width // 4
    rows_ref[...] = attn[:HEADS].reshape(HEADS * HEAD, attn.shape[2])
    core = mine[0] & 1
    for target, at in ((keep_ref, core), (give_ref, 1 - core)):
        target[...] = jnp.zeros(target.shape, target.dtype)
        for part in range(2):
            rows = rows_ref[pl.ds(pl.multiple_of((2 * part + at) * shard, 16), shard), :]
            target[part, :shard, :width] = jnp.dot(rows, low[...], preferred_element_type=jnp.float32).astype(target.dtype)


def out_grad(mine, attn, low):
    rows, width = low.shape
    shape = (2, 256, 1024)
    return in_vmem(
        out_grad_kernel, ((shape, jnp.bfloat16), (shape, jnp.bfloat16)), (mine,), (attn, low), scratch=(((width, rows), jnp.bfloat16),), name="out_grad"
    )


def pack_kernel(key_t, value_t, query, gain, out_ref):
    width = key_t.shape[0]
    scale = gain[...]
    for index, piece in enumerate((key_t, value_t)):
        out_ref[:, index * width:(index + 1) * width] = (piece[...].astype(jnp.float32).T * scale).astype(jnp.bfloat16)
    out_ref[:, 2 * width:] = (query[...].astype(jnp.float32) * scale).astype(jnp.bfloat16)


def pack(w_key, w_value, w_query, gain):
    shape = (w_key.shape[0], 2 * w_key.shape[1] + w_query.shape[1])
    return in_vmem(pack_kernel, ((shape, jnp.bfloat16),), (), (w_key.T, w_value.T, w_query, gain), name="pack")[0]


def as_row(column):
    return jnp.broadcast_to(column, (column.shape[0], BLK)).T[:1]


def last_kernel(total, weights, gain, query_ref, key_ref, value_ref, out_ref, gain_ref):
    shard, columns = weights.shape
    padded = -(-columns // BLK) * BLK
    width = query_ref.shape[1]
    key_width = key_ref.shape[0]
    rows = total[...].reshape(total.shape[0] * total.shape[1], total.shape[2])[:shard].astype(jnp.float32)
    grads = rows[:, :columns]
    scale = gain[...]
    gain_ref[...] = as_row(jnp.sum(grads * weights[...].astype(jnp.float32), axis=1, keepdims=True) / scale)
    grads = grads * scale
    key_ref[...] = grads[:, :key_width].T
    value_ref[...] = grads[:, key_width:2 * key_width].T
    query_ref[...] = grads[:, 2 * key_width:]
    out_ref[...] = rows[:, padded:padded + width]


def last(total, weights, gain, width, key_width):
    shard = weights.shape[0]
    query, key, value, out, gain_grad = in_vmem(
        last_kernel,
        (((shard, width), jnp.float32), ((key_width, shard), jnp.float32), ((key_width, shard), jnp.float32), ((shard, width), jnp.float32), ((1, shard), jnp.float32)),
        (),
        (total, weights, gain),
        name="last",
    )
    return gain_grad.reshape(shard), query, key.T, value.T, out


def unpack_kernel(total, w_gate, w_up, gain, gate_ref, up_ref, down_ref, gain_ref):
    shard, part = w_gate.shape[0], total.shape[3]
    strips = shard // STRIP
    scale = gain[...]
    gain_sum = jnp.zeros((shard, 1), jnp.float32)
    for index, (weight, target) in enumerate(((w_gate, gate_ref), (w_up, up_ref))):
        for step in range(4):
            columns = slice(step * part, (step + 1) * part)
            grads = total[:strips, 4 * index + step].reshape(shard, part).astype(jnp.float32)
            gain_sum = gain_sum + jnp.sum(grads * weight[:, columns].astype(jnp.float32), axis=1, keepdims=True)
            target[:, columns] = grads * scale
    for step in range(4):
        down_ref[step * shard:(step + 1) * shard, :] = total[:strips, 8 + step].reshape(shard, part).astype(jnp.float32)
    gain_ref[...] = as_row(gain_sum)


def unpack(total, w_gate, w_up, gain):
    shard, columns = w_gate.shape
    part = total.shape[3]
    full = ((shard, columns), jnp.float32)
    gate, up, down, gain_grad = in_vmem(
        unpack_kernel, (full, full, ((4 * shard, part), jnp.float32), ((1, shard), jnp.float32)), (), (total, w_gate, w_up, gain), name="unpack"
    )
    return gain_grad.reshape(shard), gate, up, down.T


def over_core(value):
    return lax.ppermute(value, "core", SWAP)


def over_chip(value):
    return lax.ppermute(value, "xh", SWAP)


def over_both(value):
    return lax.ppermute(value, FSDP_AXES, ((0, 3), (3, 0), (1, 2), (2, 1)))


def trade(value):
    return lax.ppermute(value, ("yl", "core"), ((0, 0), (1, 2), (2, 1), (3, 3)))


def arrange(pieces, xh, core):
    low = jnp.where(core == 1, pieces[1], pieces[0]), jnp.where(core == 1, pieces[0], pieces[1])
    high = jnp.where(core == 1, pieces[3], pieces[2]), jnp.where(core == 1, pieces[2], pieces[3])
    return jnp.stack([jnp.where(xh == 1, h, l) for l, h in zip(low, high)] + [jnp.where(xh == 1, l, h) for l, h in zip(low, high)])


def gather_tokens(rows):
    far = over_chip(rows)
    return rows, over_core(rows), far, over_core(far)


def exchange(value, axes):
    return lax.all_to_all(value, axes, split_axis=0, concat_axis=0, tiled=True)


def per_device(
    tokens,
    block_order,
    gain_attn,
    w_query,
    w_key,
    w_value,
    w_out,
    gain_mlp,
    w_gate,
    w_up,
    w_down,
    cotangent,
):
    f32, bf16 = jnp.float32, jnp.bfloat16
    xh, core = lax.axis_index("xh"), lax.axis_index("core")
    mine = 2 * xh + core
    own_id = mine.reshape(1)
    row_total, width = tokens.shape[1:]
    shard = w_query.shape[0]
    ff_part = w_down.shape[0]
    groups = lax.axis_size(SEQ_AXES)
    key_width = KV_HEADS * HEAD
    gain_one = gain_attn.astype(f32)[:, None]
    gain_two = gain_mlp.astype(f32)[:, None]

    qkv_shard = pack(w_key, w_value, w_query, gain_one)
    far_shard = over_chip(qkv_shard)
    near_shard = over_core(qkv_shard)
    hidden_low = trade(tokens[0])

    def gate_up(step):
        start = (mine ^ step) * ff_part
        both = [lax.dynamic_slice_in_dim(w, start, ff_part, 1).astype(f32) * gain_two for w in (w_gate, w_up)]
        return jnp.stack(both).astype(bf16)

    gate_up_parts = [gate_up(step) for step in range(4)]
    far_shard, w_out, upstream, gate_up_parts = lax.optimization_barrier((far_shard, w_out, cotangent[0], gate_up_parts))
    far_near_shard = over_core(far_shard)

    order = block_order.reshape(groups, 2, 2)
    own_order = jnp.where(core == 0, order[:, 0], order[:, 1]).reshape(-1)
    other_order = jnp.where(core == 0, order[:, 1], order[:, 0]).reshape(-1)
    key_pos = jnp.concatenate([own_order, other_order])
    query_rank = jnp.sum((own_order[None, :] < own_order[:, None]).astype(jnp.int32), axis=1)
    hit = query_rank[None, :] == jnp.arange(2 * groups, dtype=jnp.int32)[:, None]
    sorted_pos = jnp.sum(jnp.where(hit, own_order[None, :], 0), axis=1)
    sorted_id = jnp.sum(jnp.where(hit, jnp.arange(2 * groups, dtype=jnp.int32)[None, :], 0), axis=1)
    here = lax.axis_index(SEQ_AXES)
    own_blocks = lax.dynamic_slice_in_dim(own_order, 2 * here, 2)
    row = jnp.arange(row_total, dtype=jnp.int32)
    own_pos = jnp.where(row < BLK, own_blocks[0] * BLK + row, own_blocks[1] * BLK + row - BLK)
    inverse_freq = THETA ** (-jnp.arange(HEAD // 2, dtype=f32) / (HEAD // 2))
    angles = inverse_freq[:, None] * own_pos.astype(f32)[None, :]
    cos_table, sin_table = jnp.cos(angles), jnp.sin(angles)

    normed_one, group_send, qkv_full = project(
        own_id, hidden_low, (qkv_shard, near_shard, far_shard, far_near_shard), cos_table, sin_table, groups
    )
    group_own = exchange(group_send, SEQ_AXES)
    group_other = over_core(group_own)

    upstream = trade(upstream)
    far_out = over_chip(w_out)
    out_pieces = (w_out, over_core(w_out), far_out, over_core(far_out))
    weights = (gate_up_parts[0], over_core(gate_up_parts[1]), over_chip(gate_up_parts[2]), over_both(gate_up_parts[3]))
    upstream_all = gather_tokens(upstream)

    out_send, out_blocks, lse, kv_sorted, kv_turned = attend(key_pos, query_rank, sorted_pos, sorted_id, group_own, group_other)
    attn = exchange(out_send, SEQ_AXES)
    mid_state, second_hat, out_full = project_out(own_id, attn, hidden_low, out_pieces)
    normed_all = gather_tokens(second_hat)
    scaled_keep, scaled_send, result_keep, result_send, hidden_act, grad_gate_lin, grad_up_lin = feed(own_id, normed_all, upstream_all, weights, w_down)
    scaled_received = over_core(scaled_send)
    far_send = (scaled_keep[1] + scaled_received[1, :, :width].astype(f32)).astype(bf16)
    far_send, normed_all, hidden_act = lax.optimization_barrier((far_send, normed_all, hidden_act))
    scaled_far = over_chip(far_send)
    ring = lax.axis_size(RING_AXES)
    stacked = feed_grads(normed_all, upstream_all, hidden_act, grad_gate_lin, grad_up_lin, ring)
    scaled_far, stacked = lax.optimization_barrier((scaled_far, stacked))
    reduced = lax.psum_scatter(stacked.reshape(ring, 12 * STRIP, ff_part), RING_AXES, scatter_dimension=0, tiled=True)[0]

    grad_mid, mid_low, grad_send = mid_back(scaled_keep, scaled_received, scaled_far, mid_state, upstream, out_full, groups)
    grad_group = exchange(grad_send, SEQ_AXES)
    ctx = lax.axis_size(CTX_AXES)
    slab = 8
    out_grad_keep, out_grad_give = out_grad(own_id, attn, mid_low)
    out_chip = (out_grad_keep.astype(f32) + over_core(out_grad_give).astype(f32)).astype(bf16).reshape(2 * ctx, slab, -1)
    grad_group, result_send, out_chip = lax.optimization_barrier((grad_group, result_send, out_chip))

    out_chips = exchange(out_chip, CHIP_AXES)
    result_received = over_core(result_send)[:, :, :width]
    result_far = over_chip((result_keep[1] + result_received[1].astype(f32)).astype(bf16))
    result = mid_state + result_keep[0] + result_received[0].astype(f32) + result_far.astype(f32)
    block_out = trade(result.astype(bf16))[None]

    dq, dkv_own, dkv_other = attend_back(key_pos, query_rank, sorted_pos, sorted_id, group_own, grad_group, out_blocks, lse, kv_sorted, kv_turned)
    dkv_other, reduced, out_chips = lax.optimization_barrier((dkv_other, reduced, out_chips))
    out_sum = jnp.sum(out_chips.astype(f32), axis=0).astype(bf16)
    reduced = (reduced.astype(f32) + lax.ppermute(reduced, "xl", SWAP).astype(f32)).astype(bf16).reshape(3, 4, STRIP, ff_part)
    dkv = (dkv_own + over_core(dkv_other).astype(f32)).astype(bf16)
    dkv, reduced = lax.optimization_barrier((dkv, reduced))
    home = exchange(jnp.concatenate([dq, dkv], axis=1), SEQ_AXES)

    part = lambda step: lax.dynamic_index_in_dim(reduced[:2], mine ^ step, 1, keepdims=False)
    pieces = arrange([part(0), over_core(part(1)), over_chip(part(2)), over_both(part(3))], xh, core).transpose(1, 0, 2, 3)
    pieces = jnp.concatenate([pieces, reduced[2:]]).reshape(12, STRIP, ff_part)
    home, pieces = lax.optimization_barrier((home, pieces))
    whole = lax.all_gather(pieces, RING_AXES, axis=0, tiled=False)
    gain_two_shard, gate_shard, up_shard, down_shard = unpack(whole, w_gate, w_up, gain_two)

    keep, give, grad_tokens = finish(own_id, home, hidden_low, normed_one, qkv_full, grad_mid, cos_table, sin_table)
    grad_tokens = trade(grad_tokens).astype(f32)[None]
    columns = keep.shape[-1]
    chip_sum = (keep.astype(f32) + over_core(give).astype(f32)).astype(bf16).reshape(2 * ctx, slab, columns)
    qkv_sum = jnp.sum(exchange(chip_sum, CHIP_AXES).astype(f32), axis=0).astype(bf16)
    summed = jnp.concatenate([qkv_sum, out_sum], axis=1)
    final = exchange(jnp.broadcast_to(summed[None], (ctx,) + summed.shape), CTX_AXES)
    gain_one_shard, query_shard, key_shard, value_shard, out_shard = last(final, qkv_shard, gain_one, width, key_width)
    return (
        block_out,
        grad_tokens,
        gain_one_shard,
        query_shard,
        key_shard,
        value_shard,
        out_shard,
        gain_two_shard,
        gate_shard,
        up_shard,
        down_shard,
    )


def solution(mesh):
    fine = Mesh(mesh.devices.reshape(2, 4, 2, 2, 2, 2), ("xl", "z", "yh", "yl", "xh", "core"))
    rows = P(FSDP_AXES, CTX_AXES, None)
    gain = P(FSDP_AXES)
    weight = P(FSDP_AXES, None)
    return jax.shard_map(
        per_device,
        mesh=fine,
        in_specs=(rows, P(), gain, weight, weight, weight, weight, gain, weight, weight, weight, rows),
        out_specs=(rows, rows, gain, weight, weight, weight, weight, gain, weight, weight, weight),
        check_vma=False,
    )
```

```python
import functools
import math

import jax
import jax.numpy as jnp
from jax import lax
from jax.experimental import pallas as pl
from jax.experimental.pallas import tpu as pltpu
from jax.sharding import Mesh
from jax.sharding import PartitionSpec as P

HEADS = 15
KV_HEADS = 5
EPSILON = 1e-05
THETA = 100000.0
SEQ_AXES = ("xl", "z", "yh")
CTX_AXES = ("xl", "z", "yh", "yl")
RING_AXES = ("z", "yh", "yl")
CHIP_AXES = ("xh", "xl", "z", "yh", "yl")
FSDP_AXES = ("xh", "core")
SWAP = ((0, 1), (1, 0))
STRIP = 16


BLK = 128
HEAD = 64
EXP_SCALE = math.log2(math.e) / 8.0
MASKED = -1e30


def attend_kernel(key_pos, query_rank, sorted_pos, sorted_id, own_in, other_in, send_ref, out_ref, lse_ref, kv_ref, kvt_ref, ones_v, q_sorted, *, big, small, edge_size, blocks):
    groups, width = own_in.shape[0], HEAD
    rows = blocks * BLK
    is_key = lax.broadcasted_iota(jnp.int32, (BLK, 2 * width), 1) < width

    def place(index, _):
        for side, source in enumerate((own_in, other_in)):
            for half in range(2):
                where = pl.multiple_of(key_pos[side * 2 * groups + 2 * index + half] * BLK, BLK)
                piece = source[index, width:, half * BLK:(half + 1) * BLK]
                kvt_ref[:, pl.ds(where, BLK)] = piece
                turned = piece.T
                kv_ref[pl.ds(where, BLK), :] = turned
                ones_v[pl.ds(where, BLK), :] = jnp.where(is_key, jnp.ones_like(turned), turned)
        for half in range(2):
            query = own_in[index, :width, half * BLK:(half + 1) * BLK]
            query = jnp.concatenate([query, jnp.zeros_like(query)], axis=0)
            q_sorted[pl.ds(pl.multiple_of(query_rank[2 * index + half] * BLK, BLK), BLK), :] = query.T
        return 0

    lax.fori_loop(0, groups, place, 0, unroll=4)

    def tile(index, _):
        low, high = sorted_pos[blocks * index], sorted_pos[blocks * index + blocks - 1]
        query = q_sorted[pl.ds(pl.multiple_of(index * rows, rows), rows), :]
        row = lax.broadcasted_iota(jnp.int32, (rows, 1), 0)
        place_of = row + low * BLK
        for part in range(1, blocks):
            place_of = jnp.where(row >= part * BLK, row + (sorted_pos[blocks * index + part] - part) * BLK, place_of)

        def step(start, carry, size, masked):
            top, total = carry
            scores = lax.dot_general(query, kv_ref[pl.ds(start, size), :], (((1,), (1,)), ((), ())), preferred_element_type=jnp.float32)
            if masked:
                column = start + lax.broadcasted_iota(jnp.int32, scores.shape, 1)
                scores = jnp.where(column <= place_of, scores, MASKED)
            new_top = jnp.maximum(top, jnp.max(scores, axis=1, keepdims=True))
            weights = jnp.exp2((scores - new_top) * EXP_SCALE).astype(jnp.bfloat16)
            factor = jnp.exp2((top - new_top) * EXP_SCALE)
            added = jnp.dot(weights, ones_v[pl.ds(start, size), :], preferred_element_type=jnp.float32)
            return new_top, total * factor + added

        def full(count, carry):
            for part in range(big // small):
                carry = step(pl.multiple_of(count * big + part * small, small), carry, small, False)
            return carry

        def edge(count, carry):
            return step(pl.multiple_of(count * edge_size, edge_size), carry, edge_size, True)

        carry = (jnp.full((rows, 1), MASKED, jnp.float32), jnp.zeros((rows, 2 * width), jnp.float32))
        done = low * BLK // big
        carry = lax.fori_loop(0, done, full, carry)
        top, total = lax.fori_loop(done * (big // edge_size), (high * BLK + BLK + edge_size - 1) // edge_size, edge, carry)
        lse = (top * EXP_SCALE + jnp.log2(total)).T
        total = total.T
        result = total[width:] / total[:1]
        for part in range(blocks):
            ident = sorted_id[blocks * index + part]
            piece = result[:, part * BLK:(part + 1) * BLK]
            out_ref[ident] = piece
            send_ref[ident // 2, :, pl.ds(pl.multiple_of(ident % 2 * BLK, BLK), BLK)] = piece.astype(jnp.bfloat16)
            lse_ref[ident] = lse[:8, part * BLK:(part + 1) * BLK]
        return 0

    lax.fori_loop(0, 2 * groups // blocks, tile, 0)


def attend(key_pos, query_rank, sorted_pos, sorted_id, own_in, other_in, big=1024, small=1024, edge_size=512, blocks=4):
    groups, width = own_in.shape[0], HEAD
    total = 4 * groups * BLK
    vm = pl.BlockSpec(memory_space=pltpu.VMEM)
    sm = pl.BlockSpec(memory_space=pltpu.SMEM)
    return pl.pallas_call(
        functools.partial(attend_kernel, big=big, small=small, edge_size=edge_size, blocks=blocks),
        out_shape=(
            jax.ShapeDtypeStruct((groups, width, 2 * BLK), jnp.bfloat16),
            jax.ShapeDtypeStruct((2 * groups, width, BLK), jnp.float32),
            jax.ShapeDtypeStruct((2 * groups, 8, BLK), jnp.float32),
            jax.ShapeDtypeStruct((total, 2 * width), jnp.bfloat16),
            jax.ShapeDtypeStruct((2 * width, total), jnp.bfloat16),
        ),
        in_specs=[sm] * 4 + [vm] * 2,
        out_specs=(vm,) * 5,
        scratch_shapes=[
            pltpu.VMEM((total, 2 * width), jnp.bfloat16),
            pltpu.VMEM((2 * groups * BLK, 2 * width), jnp.bfloat16),
        ],
        compiler_params=pltpu.CompilerParams(vmem_limit_bytes=48 * 2**20),
        cost_estimate=pl.CostEstimate(flops=40 * 10**9, bytes_accessed=10**7, transcendentals=2 * 10**7),
        name="attend",
    )(key_pos, query_rank, sorted_pos, sorted_id, own_in, other_in)


def back_kernel(key_pos, query_rank, sorted_pos, sorted_id, own_in, da_ref, out_ref, lse_ref, kv_ref, kvt_ref, dq_ref, own_ref, other_ref, dkv, q_sorted, da_sorted, *, big, small, edge_size, flip):
    groups, width = own_in.shape[0], HEAD

    def place(index, _):
        for half in range(2):
            rank = query_rank[2 * index + half]
            q_sorted[rank] = own_in[index, :width, half * BLK:(half + 1) * BLK]
            da_sorted[rank] = da_ref[index, :, half * BLK:(half + 1) * BLK]
        return 0

    lax.fori_loop(0, groups, place, 0)

    def clear(index, _):
        dkv[pl.ds(pl.multiple_of(index * BLK, BLK), BLK), :] = jnp.zeros((BLK, 2 * width), jnp.float32)
        return 0

    lax.fori_loop(0, 4 * groups, clear, 0)

    def tile(index, _):
        low, high = sorted_pos[2 * index], sorted_pos[2 * index + 1]
        first_id, second_id = sorted_id[2 * index], sorted_id[2 * index + 1]
        query = jnp.concatenate([q_sorted[2 * index], q_sorted[2 * index + 1]], axis=1)
        grad = jnp.concatenate([da_sorted[2 * index], da_sorted[2 * index + 1]], axis=1)
        value = jnp.concatenate([out_ref[first_id], out_ref[second_id]], axis=1)
        lse = jnp.concatenate([lse_ref[first_id][:1], lse_ref[second_id][:1]], axis=1)
        delta = jnp.sum(grad.astype(jnp.float32) * value, axis=0, keepdims=True)
        none = jnp.zeros_like(query)
        both = jnp.concatenate([jnp.concatenate([query, none], axis=1), jnp.concatenate([none, grad], axis=1)], axis=0)
        both_t = both.T
        lane = lax.broadcasted_iota(jnp.int32, (1, 2 * BLK), 1)
        place_of = jnp.where(lane < BLK, low * BLK + lane, (high - 1) * BLK + lane)

        def step(start, total, size, masked):
            keys = kv_ref[pl.ds(start, size), :]
            pair = jnp.dot(keys, both, preferred_element_type=jnp.float32)
            weights = jnp.exp2(pair[:, :2 * BLK] * EXP_SCALE - lse)
            if masked:
                row = start + lax.broadcasted_iota(jnp.int32, weights.shape, 0)
                weights = jnp.where(row <= place_of, weights, 0.0)
            grad_scores = (weights * (pair[:, 2 * BLK:] - delta)).astype(jnp.bfloat16)
            weights = weights.astype(jnp.bfloat16)
            dkv[pl.ds(start, size), :] += jnp.dot(jnp.concatenate([grad_scores, weights], axis=1), both_t, preferred_element_type=jnp.float32)
            if flip:
                return total + lax.dot_general(grad_scores, keys, (((0,), (0,)), ((), ())), preferred_element_type=jnp.float32)
            return total + jnp.dot(kvt_ref[:width, pl.ds(start, size)], grad_scores, preferred_element_type=jnp.float32)

        def full(count, carry):
            for part in range(big // small):
                carry = step(pl.multiple_of(count * big + part * small, small), carry, small, False)
            return carry

        def edge(count, carry):
            return step(pl.multiple_of(count * edge_size, edge_size), carry, edge_size, True)

        done = low * BLK // big
        total = jnp.zeros((2 * BLK, 2 * width) if flip else (width, 2 * BLK), jnp.float32)
        total = lax.fori_loop(0, done, full, total)
        total = lax.fori_loop(done * (big // edge_size), (high * BLK + BLK + edge_size - 1) // edge_size, edge, total) * 0.125
        if flip:
            total = total.T[:width]
        for half, ident in enumerate((first_id, second_id)):
            dq_ref[ident // 2, :, pl.ds(pl.multiple_of(ident % 2 * BLK, BLK), BLK)] = total[:, half * BLK:(half + 1) * BLK].astype(jnp.bfloat16)
        return 0

    lax.fori_loop(0, groups, tile, 0)
    factor = jnp.where(lax.broadcasted_iota(jnp.int32, (1, 2 * width), 1) < width, 0.125, 1.0)

    def spread(index, _):
        for side, target in enumerate((own_ref, other_ref)):
            for half in range(2):
                where = pl.multiple_of(key_pos[side * 2 * groups + 2 * index + half] * BLK, BLK)
                target[index, :, half * BLK:(half + 1) * BLK] = (dkv[pl.ds(where, BLK), :] * factor).astype(target.dtype)
        return 0

    lax.fori_loop(0, groups, spread, 0)


def attend_back(key_pos, query_rank, sorted_pos, sorted_id, own_in, da, out, lse, kv, kvt, big=1024, small=1024, edge_size=512, flip=False):
    groups, width = own_in.shape[0], HEAD
    total = 4 * groups * BLK
    vm = pl.BlockSpec(memory_space=pltpu.VMEM)
    sm = pl.BlockSpec(memory_space=pltpu.SMEM)
    return pl.pallas_call(
        functools.partial(back_kernel, big=big, small=small, edge_size=edge_size, flip=flip),
        out_shape=(
            jax.ShapeDtypeStruct((groups, width, 2 * BLK), jnp.bfloat16),
            jax.ShapeDtypeStruct((groups, 2 * width, 2 * BLK), jnp.float32),
            jax.ShapeDtypeStruct((groups, 2 * width, 2 * BLK), jnp.bfloat16),
        ),
        in_specs=[sm] * 4 + [vm] * 6,
        out_specs=(vm,) * 3,
        scratch_shapes=[
            pltpu.VMEM((total, 2 * width), jnp.float32),
            pltpu.VMEM((2 * groups, width, BLK), jnp.bfloat16),
            pltpu.VMEM((2 * groups, width, BLK), jnp.bfloat16),
        ],
        compiler_params=pltpu.CompilerParams(vmem_limit_bytes=48 * 2**20),
        cost_estimate=pl.CostEstimate(flops=60 * 10**9, bytes_accessed=10**7, transcendentals=2 * 10**7),
        name="attend_back",
    )(key_pos, query_rank, sorted_pos, sorted_id, own_in, da, out, lse, kv, kvt)


def turn_project_kernel(mine, x_ref, own, near, far, far_near, cos_ref, sin_ref, hat_ref, send_ref, w_ref):
    shard = own.shape[0]
    for step, piece in enumerate((own, near, far, far_near)):
        w_ref[pl.ds(pl.multiple_of((mine[0] ^ step) * shard, 16), shard), :] = piece[...]
    hidden = x_ref[...].astype(jnp.float32)
    hat = hidden * lax.rsqrt(jnp.mean(hidden * hidden, axis=-1, keepdims=True) + EPSILON)
    hat = hat.astype(jnp.bfloat16)
    hat_ref[...] = hat
    half = HEAD // 2
    cos, sin = cos_ref[...], sin_ref[...]

    def turn(pair):
        front, behind = pair[:half], pair[half:]
        return jnp.concatenate([front * cos - behind * sin, behind * cos + front * sin], axis=0).astype(jnp.bfloat16)

    key_width = KV_HEADS * HEAD
    per = HEADS // KV_HEADS
    lin = jnp.dot(hat, w_ref[:, : 2 * key_width], preferred_element_type=jnp.float32).T
    for head in range(KV_HEADS):
        key = turn(lin[head * HEAD:(head + 1) * HEAD])
        value = lin[key_width + head * HEAD:key_width + (head + 1) * HEAD].astype(jnp.bfloat16)
        for query in range(per):
            send_ref[head * per + query, HEAD:2 * HEAD] = key
            send_ref[head * per + query, 2 * HEAD:] = value
    for head in range(KV_HEADS):
        start = 2 * key_width + head * per * HEAD
        lin = jnp.dot(hat, w_ref[:, start:start + per * HEAD], preferred_element_type=jnp.float32).T
        for query in range(per):
            send_ref[head * per + query, :HEAD] = turn(lin[query * HEAD:(query + 1) * HEAD])
    send_ref[HEADS] = jnp.zeros(send_ref.shape[1:], jnp.bfloat16)


def project(mine, x, pieces, cos, sin, groups):
    shard, columns = pieces[0].shape
    rows, width = x.shape
    vm = pl.BlockSpec(memory_space=pltpu.VMEM)
    return pl.pallas_call(
        turn_project_kernel,
        out_shape=(
            jax.ShapeDtypeStruct((rows, width), jnp.bfloat16),
            jax.ShapeDtypeStruct((groups, 3 * HEAD, rows), jnp.bfloat16),
            jax.ShapeDtypeStruct((width, columns), jnp.bfloat16),
        ),
        in_specs=[pl.BlockSpec(memory_space=pltpu.SMEM)] + [vm] * 7,
        out_specs=(vm,) * 3,
        compiler_params=pltpu.CompilerParams(vmem_limit_bytes=40 * 2**20),
        cost_estimate=pl.CostEstimate(flops=10**9, bytes_accessed=10**7, transcendentals=0),
        name="project",
    )(mine, x, *pieces, cos, sin)


def finish_kernel(mine, home, x_ref, hat_ref, w_ref, mid_ref, cos_ref, sin_ref, keep_ref, give_ref, tokens_ref, turned, hat_t):
    shard = w_ref.shape[0] // 4
    half = HEAD // 2
    cos, sin = cos_ref[...], sin_ref[...]
    key_width = KV_HEADS * HEAD
    per = HEADS // KV_HEADS

    def turn_back(pair):
        front, behind = pair[:half], pair[half:]
        return jnp.concatenate([front * cos + behind * sin, behind * cos - front * sin], axis=0).astype(jnp.bfloat16)

    for head in range(KV_HEADS):
        total = sum(home[head * per + query, HEAD:, :].astype(jnp.float32) for query in range(per))
        total = jnp.concatenate([total[:, :BLK].T, total[:, BLK:].T], axis=1)
        turned[head * HEAD:(head + 1) * HEAD, :] = turn_back(total[:HEAD])
        turned[key_width + head * HEAD:key_width + (head + 1) * HEAD, :] = total[HEAD:].astype(jnp.bfloat16)
        for query in range(per):
            start = 2 * key_width + (head * per + query) * HEAD
            turned[start:start + HEAD, :] = turn_back(home[head * per + query, :HEAD, :].astype(jnp.float32))
    hat_t[...] = hat_ref[...].T
    core = mine[0] & 1
    for target, at in ((keep_ref, core), (give_ref, 1 - core)):
        target[...] = jnp.zeros(target.shape, target.dtype)
        for part in range(2):
            rows = hat_t[pl.ds(pl.multiple_of((2 * part + at) * shard, 16), shard), :]
            grads = lax.dot_general(rows, turned[...], (((1,), (1,)), ((), ())), preferred_element_type=jnp.float32)
            target[part, :shard, : grads.shape[1]] = grads.astype(jnp.bfloat16)
    scaled = jnp.dot(w_ref[...], turned[...], preferred_element_type=jnp.float32).T
    hidden = x_ref[...].astype(jnp.float32)
    rms = lax.rsqrt(jnp.mean(hidden * hidden, axis=-1, keepdims=True) + EPSILON)
    hat = hidden * rms
    tokens_ref[...] = (mid_ref[...] + rms * (scaled - hat * jnp.mean(scaled * hat, axis=-1, keepdims=True))).astype(jnp.bfloat16)


def finish(mine, home, x, hat, w, mid, cos, sin):
    width, columns = w.shape
    rows = x.shape[0]
    vm = pl.BlockSpec(memory_space=pltpu.VMEM)
    return pl.pallas_call(
        finish_kernel,
        out_shape=(
            jax.ShapeDtypeStruct((2, 256, -(-columns // BLK) * BLK), jnp.bfloat16),
            jax.ShapeDtypeStruct((2, 256, -(-columns // BLK) * BLK), jnp.bfloat16),
            jax.ShapeDtypeStruct((rows, width), jnp.bfloat16),
        ),
        in_specs=[pl.BlockSpec(memory_space=pltpu.SMEM)] + [vm] * 7,
        out_specs=(vm,) * 3,
        scratch_shapes=[pltpu.VMEM((columns, rows), jnp.bfloat16), pltpu.VMEM((width, rows), jnp.bfloat16)],
        compiler_params=pltpu.CompilerParams(vmem_limit_bytes=40 * 2**20),
        cost_estimate=pl.CostEstimate(flops=10**9, bytes_accessed=10**7, transcendentals=0),
        name="finish",
    )(mine, home, x, hat, w, mid, cos, sin)


def in_vmem(kernel, out_shape, scalars, arrays, scratch=(), flops=10**9, name=None):
    vm = pl.BlockSpec(memory_space=pltpu.VMEM)
    return pl.pallas_call(
        kernel,
        out_shape=tuple(jax.ShapeDtypeStruct(shape, dtype) for shape, dtype in out_shape),
        in_specs=[pl.BlockSpec(memory_space=pltpu.SMEM)] * len(scalars) + [vm] * len(arrays),
        out_specs=(vm,) * len(out_shape),
        scratch_shapes=[pltpu.VMEM(shape, dtype) for shape, dtype in scratch],
        compiler_params=pltpu.CompilerParams(vmem_limit_bytes=48 * 2**20),
        cost_estimate=pl.CostEstimate(flops=flops, bytes_accessed=10**7, transcendentals=0),
        name=name,
    )(*scalars, *arrays)


def across(left, right):
    return lax.dot_general(left, right, (((1,), (1,)), ((), ())), preferred_element_type=jnp.float32)


def unit_rms(value):
    return lax.rsqrt(jnp.mean(value * value, axis=-1, keepdims=True) + EPSILON)


def norm_back(value, grad):
    rms = unit_rms(value)
    hat = value * rms
    return rms * (grad - hat * jnp.mean(grad * hat, axis=-1, keepdims=True))


def out_kernel(mine, attn, x_ref, own, near, far, far_near, mid_ref, hat_ref, w_ref):
    shard = own.shape[0]
    for step, piece in enumerate((own, near, far, far_near)):
        w_ref[pl.ds(pl.multiple_of((mine[0] ^ step) * shard, 16), shard), :] = piece[...]
    rows = attn[:HEADS].reshape(HEADS * HEAD, attn.shape[2]).T
    mid = x_ref[...].astype(jnp.float32) + jnp.dot(rows, w_ref[...], preferred_element_type=jnp.float32)
    mid_ref[...] = mid
    hat_ref[...] = (mid * unit_rms(mid)).astype(jnp.bfloat16)


def project_out(mine, attn, x, pieces):
    shape = x.shape
    width = shape[1]
    return in_vmem(
        out_kernel, ((shape, jnp.float32), (shape, jnp.bfloat16), ((width, width), jnp.bfloat16)), (mine,), (attn, x, *pieces), name="project_out"
    )


def feed_kernel(mine, *refs):
    hats, grads, weights, (w_down,) = refs[:4], refs[4:8], refs[8:12], refs[12:13]
    scaled_keep, scaled_send, out_keep, out_send, act_ref, gate_grad_ref, up_grad_ref, w_gate, w_up = refs[13:]
    shard = weights[0].shape[1]
    for step, piece in enumerate(weights):
        where = pl.ds(pl.multiple_of((mine[0] ^ step) * shard, 16), shard)
        w_gate[where, :] = piece[0]
        w_up[where, :] = piece[1]
    rows = hats[0].shape[0]
    for step in range(4):
        here = slice(step * rows, (step + 1) * rows)
        hat = hats[step][...]
        gate = jnp.dot(hat, w_gate[...], preferred_element_type=jnp.float32)
        up = jnp.dot(hat, w_up[...], preferred_element_type=jnp.float32)
        sigmoid = jax.nn.sigmoid(gate)
        silu = gate * sigmoid
        act = (silu * up).astype(jnp.bfloat16)
        act_ref[here, :] = act
        grad_act = across(grads[step][...], w_down[...]).astype(jnp.bfloat16).astype(jnp.float32)
        gate_grad = (grad_act * up * sigmoid * (1.0 + gate * (1.0 - sigmoid))).astype(jnp.bfloat16)
        up_grad = (grad_act * silu).astype(jnp.bfloat16)
        gate_grad_ref[here, :] = gate_grad
        up_grad_ref[here, :] = up_grad
        scaled = across(gate_grad, w_gate[...]) + across(up_grad, w_up[...])
        out = jnp.dot(act, w_down[...], preferred_element_type=jnp.float32)
        if step % 2:
            scaled_send[step // 2, :, : scaled.shape[1]] = scaled.astype(jnp.bfloat16)
            out_send[step // 2, :, : out.shape[1]] = out.astype(jnp.bfloat16)
            for target in (scaled_send, out_send):
                target[step // 2, :, scaled.shape[1]:] = jnp.zeros((rows, target.shape[2] - scaled.shape[1]), jnp.bfloat16)
        else:
            scaled_keep[step // 2] = scaled
            out_keep[step // 2] = out


def feed(mine, hats, grads, weights, w_down):
    rows, width = hats[0].shape
    part = w_down.shape[0]
    pair = (2, rows, width)
    sent = (2, rows, -(-width // 256) * 256)
    hidden = ((4 * rows, part), jnp.bfloat16)
    return in_vmem(
        feed_kernel,
        ((pair, jnp.float32), (sent, jnp.bfloat16), (pair, jnp.float32), (sent, jnp.bfloat16), hidden, hidden, hidden),
        (mine,),
        (*hats, *grads, *weights, w_down),
        scratch=(((width, part), jnp.bfloat16),) * 2,
        flops=10**10,
        name="feed",
    )


def feed_grads_kernel(*refs):
    hats, grads, (act, gate_grad, up_grad), (out_ref, hat_t, grad_t) = refs[:4], refs[4:8], refs[8:11], refs[11:]
    rows = hats[0].shape[0]
    for step in range(4):
        here = slice(step * rows, (step + 1) * rows)
        hat_t[:, here] = hats[step][...].T
        grad_t[:, here] = grads[step][...].T
    shard = hat_t.shape[0] // 4
    strips = shard // STRIP
    for index, (left, right) in enumerate(((hat_t, gate_grad), (hat_t, up_grad), (grad_t, act))):
        for part in range(4):
            product = jnp.dot(left[part * shard:(part + 1) * shard, :], right[...], preferred_element_type=jnp.float32)
            out_ref[:strips, 4 * index + part] = product.astype(jnp.bfloat16).reshape(strips, STRIP, product.shape[1])
    out_ref[strips:] = jnp.zeros((out_ref.shape[0] - strips,) + out_ref.shape[1:], jnp.bfloat16)


def feed_grads(hats, grads, act, gate_grad, up_grad, ring):
    rows, width = hats[0].shape
    turned = ((width, 4 * rows), jnp.bfloat16)
    return in_vmem(
        feed_grads_kernel,
        (((ring, 12, STRIP, act.shape[1]), jnp.bfloat16),),
        (),
        (*hats, *grads, act, gate_grad, up_grad),
        scratch=(turned, turned),
        flops=8 * 10**9,
        name="feed_grads",
    )[0]


def mid_kernel(keep, received, far, mid_ref, grad_ref, w_ref, total_ref, low_ref, send_ref):
    scaled = keep[0] + received[0, :, : keep.shape[2]].astype(jnp.float32) + far[...].astype(jnp.float32)
    total = grad_ref[...].astype(jnp.float32) + norm_back(mid_ref[...], scaled)
    total_ref[...] = total
    low = total.astype(jnp.bfloat16)
    low_ref[...] = low
    send_ref[:HEADS] = across(w_ref[...], low).astype(jnp.bfloat16).reshape(HEADS, HEAD, low.shape[0])
    send_ref[HEADS:] = jnp.zeros((send_ref.shape[0] - HEADS,) + send_ref.shape[1:], jnp.bfloat16)


def mid_back(keep, received, far, mid, grad, w_out, groups):
    shape = mid.shape
    return in_vmem(
        mid_kernel,
        ((shape, jnp.float32), (shape, jnp.bfloat16), ((groups, HEAD, shape[0]), jnp.bfloat16)),
        (),
        (keep, received, far, mid, grad, w_out),
        name="mid_back",
    )


def out_grad_kernel(mine, attn, low, keep_ref, give_ref, rows_ref):
    width = low.shape[1]
    shard = width // 4
    rows_ref[...] = attn[:HEADS].reshape(HEADS * HEAD, attn.shape[2])
    core = mine[0] & 1
    for target, at in ((keep_ref, core), (give_ref, 1 - core)):
        target[...] = jnp.zeros(target.shape, target.dtype)
        for part in range(2):
            rows = rows_ref[pl.ds(pl.multiple_of((2 * part + at) * shard, 16), shard), :]
            target[part, :shard, :width] = jnp.dot(rows, low[...], preferred_element_type=jnp.float32).astype(target.dtype)


def out_grad(mine, attn, low):
    rows, width = low.shape
    shape = (2, 256, 1024)
    return in_vmem(
        out_grad_kernel, ((shape, jnp.bfloat16), (shape, jnp.bfloat16)), (mine,), (attn, low), scratch=(((width, rows), jnp.bfloat16),), name="out_grad"
    )


def pack_kernel(key_t, value_t, query, gain, out_ref):
    width = key_t.shape[0]
    scale = gain[...]
    for index, piece in enumerate((key_t, value_t)):
        out_ref[:, index * width:(index + 1) * width] = (piece[...].astype(jnp.float32).T * scale).astype(jnp.bfloat16)
    out_ref[:, 2 * width:] = (query[...].astype(jnp.float32) * scale).astype(jnp.bfloat16)


def pack(w_key, w_value, w_query, gain):
    shape = (w_key.shape[0], 2 * w_key.shape[1] + w_query.shape[1])
    return in_vmem(pack_kernel, ((shape, jnp.bfloat16),), (), (w_key.T, w_value.T, w_query, gain), name="pack")[0]


def as_row(column):
    return jnp.broadcast_to(column, (column.shape[0], BLK)).T[:1]


def last_kernel(total, weights, gain, query_ref, key_ref, value_ref, out_ref, gain_ref):
    shard, columns = weights.shape
    padded = -(-columns // BLK) * BLK
    width = query_ref.shape[1]
    key_width = key_ref.shape[0]
    rows = total[...].reshape(total.shape[0] * total.shape[1], total.shape[2])[:shard].astype(jnp.float32)
    grads = rows[:, :columns]
    scale = gain[...]
    gain_ref[...] = as_row(jnp.sum(grads * weights[...].astype(jnp.float32), axis=1, keepdims=True) / scale)
    grads = grads * scale
    key_ref[...] = grads[:, :key_width].T
    value_ref[...] = grads[:, key_width:2 * key_width].T
    query_ref[...] = grads[:, 2 * key_width:]
    out_ref[...] = rows[:, padded:padded + width]


def last(total, weights, gain, width, key_width):
    shard = weights.shape[0]
    query, key, value, out, gain_grad = in_vmem(
        last_kernel,
        (((shard, width), jnp.float32), ((key_width, shard), jnp.float32), ((key_width, shard), jnp.float32), ((shard, width), jnp.float32), ((1, shard), jnp.float32)),
        (),
        (total, weights, gain),
        name="last",
    )
    return gain_grad.reshape(shard), query, key.T, value.T, out


def unpack_kernel(total, w_gate, w_up, gain, gate_ref, up_ref, down_ref, gain_ref):
    shard, part = w_gate.shape[0], total.shape[3]
    strips = shard // STRIP
    scale = gain[...]
    gain_sum = jnp.zeros((shard, 1), jnp.float32)
    for index, (weight, target) in enumerate(((w_gate, gate_ref), (w_up, up_ref))):
        for step in range(4):
            columns = slice(step * part, (step + 1) * part)
            grads = total[:strips, 4 * index + step].reshape(shard, part).astype(jnp.float32)
            gain_sum = gain_sum + jnp.sum(grads * weight[:, columns].astype(jnp.float32), axis=1, keepdims=True)
            target[:, columns] = grads * scale
    for step in range(4):
        down_ref[step * shard:(step + 1) * shard, :] = total[:strips, 8 + step].reshape(shard, part).astype(jnp.float32)
    gain_ref[...] = as_row(gain_sum)


def unpack(total, w_gate, w_up, gain):
    shard, columns = w_gate.shape
    part = total.shape[3]
    full = ((shard, columns), jnp.float32)
    gate, up, down, gain_grad = in_vmem(
        unpack_kernel, (full, full, ((4 * shard, part), jnp.float32), ((1, shard), jnp.float32)), (), (total, w_gate, w_up, gain), name="unpack"
    )
    return gain_grad.reshape(shard), gate, up, down.T


def over_core(value):
    return lax.ppermute(value, "core", SWAP)


def over_chip(value):
    return lax.ppermute(value, "xh", SWAP)


def over_both(value):
    return lax.ppermute(value, FSDP_AXES, ((0, 3), (3, 0), (1, 2), (2, 1)))


def trade(value):
    return lax.ppermute(value, ("yl", "core"), ((0, 0), (1, 2), (2, 1), (3, 3)))


def arrange(pieces, xh, core):
    low = jnp.where(core == 1, pieces[1], pieces[0]), jnp.where(core == 1, pieces[0], pieces[1])
    high = jnp.where(core == 1, pieces[3], pieces[2]), jnp.where(core == 1, pieces[2], pieces[3])
    return jnp.stack([jnp.where(xh == 1, h, l) for l, h in zip(low, high)] + [jnp.where(xh == 1, l, h) for l, h in zip(low, high)])


def gather_tokens(rows):
    far = over_chip(rows)
    return rows, over_core(rows), far, over_core(far)


def exchange(value, axes):
    return lax.all_to_all(value, axes, split_axis=0, concat_axis=0, tiled=True)


def per_device(
    tokens,
    block_order,
    gain_attn,
    w_query,
    w_key,
    w_value,
    w_out,
    gain_mlp,
    w_gate,
    w_up,
    w_down,
    cotangent,
):
    f32, bf16 = jnp.float32, jnp.bfloat16
    xh, core = lax.axis_index("xh"), lax.axis_index("core")
    mine = 2 * xh + core
    own_id = mine.reshape(1)
    row_total, width = tokens.shape[1:]
    shard = w_query.shape[0]
    ff_part = w_down.shape[0]
    groups = lax.axis_size(SEQ_AXES)
    key_width = KV_HEADS * HEAD
    gain_one = gain_attn.astype(f32)[:, None]
    gain_two = gain_mlp.astype(f32)[:, None]

    qkv_shard = pack(w_key, w_value, w_query, gain_one)
    far_shard = over_chip(qkv_shard)
    near_shard = over_core(qkv_shard)
    hidden_low = trade(tokens[0])

    def gate_up(step):
        start = (mine ^ step) * ff_part
        both = [lax.dynamic_slice_in_dim(w, start, ff_part, 1).astype(f32) * gain_two for w in (w_gate, w_up)]
        return jnp.stack(both).astype(bf16)

    gate_up_parts = [gate_up(step) for step in range(4)]
    far_shard, hidden_low, gate_up_parts = lax.optimization_barrier((far_shard, hidden_low, gate_up_parts))
    far_near_shard = over_core(far_shard)

    order = block_order.reshape(groups, 2, 2)
    own_order = jnp.where(core == 0, order[:, 0], order[:, 1]).reshape(-1)
    other_order = jnp.where(core == 0, order[:, 1], order[:, 0]).reshape(-1)
    key_pos = jnp.concatenate([own_order, other_order])
    query_rank = jnp.sum((own_order[None, :] < own_order[:, None]).astype(jnp.int32), axis=1)
    hit = query_rank[None, :] == jnp.arange(2 * groups, dtype=jnp.int32)[:, None]
    sorted_pos = jnp.sum(jnp.where(hit, own_order[None, :], 0), axis=1)
    sorted_id = jnp.sum(jnp.where(hit, jnp.arange(2 * groups, dtype=jnp.int32)[None, :], 0), axis=1)
    here = lax.axis_index(SEQ_AXES)
    own_blocks = lax.dynamic_slice_in_dim(own_order, 2 * here, 2)
    row = jnp.arange(row_total, dtype=jnp.int32)
    own_pos = jnp.where(row < BLK, own_blocks[0] * BLK + row, own_blocks[1] * BLK + row - BLK)
    inverse_freq = THETA ** (-jnp.arange(HEAD // 2, dtype=f32) / (HEAD // 2))
    angles = inverse_freq[:, None] * own_pos.astype(f32)[None, :]
    cos_table, sin_table = jnp.cos(angles), jnp.sin(angles)

    normed_one, group_send, qkv_full = project(
        own_id, hidden_low, (qkv_shard, near_shard, far_shard, far_near_shard), cos_table, sin_table, groups
    )
    group_send, upstream = lax.optimization_barrier((group_send, trade(cotangent[0])))
    group_own = exchange(group_send, SEQ_AXES)
    group_other = over_core(group_own)

    group_own, w_out, upstream, gate_up_parts = lax.optimization_barrier((group_own, w_out, upstream, gate_up_parts))
    far_out, far_upstream = over_chip(w_out), over_chip(upstream)
    far_weights = over_chip(gate_up_parts[2]), over_both(gate_up_parts[3])
    out_send, out_blocks, lse, kv_sorted, kv_turned = attend(key_pos, query_rank, sorted_pos, sorted_id, group_own, group_other)
    out_send, far_out, far_upstream, far_weights = lax.optimization_barrier((out_send, far_out, far_upstream, far_weights))
    out_pieces = (w_out, over_core(w_out), far_out, over_core(far_out))
    weights = (gate_up_parts[0], over_core(gate_up_parts[1])) + far_weights
    upstream_all = (upstream, over_core(upstream), far_upstream, over_core(far_upstream))

    attn = exchange(out_send, SEQ_AXES)
    mid_state, second_hat, out_full = project_out(own_id, attn, hidden_low, out_pieces)
    normed_all = gather_tokens(second_hat)
    scaled_keep, scaled_send, result_keep, result_send, hidden_act, grad_gate_lin, grad_up_lin = feed(own_id, normed_all, upstream_all, weights, w_down)
    scaled_received = over_core(scaled_send)
    far_send = (scaled_keep[1] + scaled_received[1, :, :width].astype(f32)).astype(bf16)
    far_send, normed_all, hidden_act = lax.optimization_barrier((far_send, normed_all, hidden_act))
    scaled_far = over_chip(far_send)
    ring = lax.axis_size(RING_AXES)
    stacked = feed_grads(normed_all, upstream_all, hidden_act, grad_gate_lin, grad_up_lin, ring)
    scaled_far, stacked = lax.optimization_barrier((scaled_far, stacked))
    reduced = lax.psum_scatter(stacked.reshape(ring, 12 * STRIP, ff_part), RING_AXES, scatter_dimension=0, tiled=True)[0]

    grad_mid, mid_low, grad_send = mid_back(scaled_keep, scaled_received, scaled_far, mid_state, upstream, out_full, groups)
    grad_group = exchange(grad_send, SEQ_AXES)
    ctx = lax.axis_size(CTX_AXES)
    slab = 8
    out_grad_keep, out_grad_give = out_grad(own_id, attn, mid_low)
    out_chip = (out_grad_keep.astype(f32) + over_core(out_grad_give).astype(f32)).astype(bf16).reshape(2 * ctx, slab, -1)
    result_received = over_core(result_send)[:, :, :width]
    result_send = (result_keep[1] + result_received[1].astype(f32)).astype(bf16)
    grad_group, result_send, out_chip = lax.optimization_barrier((grad_group, result_send, out_chip))

    out_chips = exchange(out_chip, CHIP_AXES)
    result_far = over_chip(result_send)

    dq, dkv_own, dkv_other = attend_back(key_pos, query_rank, sorted_pos, sorted_id, group_own, grad_group, out_blocks, lse, kv_sorted, kv_turned)
    dkv_other, reduced, out_chips, result_far = lax.optimization_barrier((dkv_other, reduced, out_chips, result_far))
    result = mid_state + result_keep[0] + result_received[0].astype(f32) + result_far.astype(f32)
    block_out = trade(result.astype(bf16))
    out_sum = jnp.sum(out_chips.astype(f32), axis=0).astype(bf16)
    reduced = (reduced.astype(f32) + lax.ppermute(reduced, "xl", SWAP).astype(f32)).astype(bf16).reshape(3, 4, STRIP, ff_part)
    dkv = (dkv_own + over_core(dkv_other).astype(f32)).astype(bf16)
    dkv, reduced = lax.optimization_barrier((dkv, reduced))
    home = exchange(jnp.concatenate([dq, dkv], axis=1), SEQ_AXES)

    part = lambda step: lax.dynamic_index_in_dim(reduced[:2], mine ^ step, 1, keepdims=False)
    pieces = arrange([part(0), over_core(part(1)), over_chip(part(2)), over_both(part(3))], xh, core).transpose(1, 0, 2, 3)
    pieces = jnp.concatenate([pieces, reduced[2:]]).reshape(12, STRIP, ff_part)
    home, pieces, block_out = lax.optimization_barrier((home, pieces, block_out))
    whole = lax.all_gather(pieces, RING_AXES, axis=0, tiled=False)
    gain_two_shard, gate_shard, up_shard, down_shard = unpack(whole, w_gate, w_up, gain_two)

    keep, give, grad_tokens = finish(own_id, home, hidden_low, normed_one, qkv_full, grad_mid, cos_table, sin_table)
    grad_tokens = trade(grad_tokens)
    columns = keep.shape[-1]
    chip_sum = (keep.astype(f32) + over_core(give).astype(f32)).astype(bf16).reshape(2 * ctx, slab, columns)
    qkv_chips, grad_tokens = lax.optimization_barrier((exchange(chip_sum, CHIP_AXES), grad_tokens))
    qkv_sum = jnp.sum(qkv_chips.astype(f32), axis=0).astype(bf16)
    summed = jnp.concatenate([qkv_sum, out_sum], axis=1)
    final = exchange(jnp.broadcast_to(summed[None], (ctx,) + summed.shape), CTX_AXES)
    final, gate_shard = lax.optimization_barrier((final, gate_shard))
    gain_one_shard, query_shard, key_shard, value_shard, out_shard = last(final, qkv_shard, gain_one, width, key_width)
    return (
        block_out[None],
        grad_tokens.astype(f32)[None],
        gain_one_shard,
        query_shard,
        key_shard,
        value_shard,
        out_shard,
        gain_two_shard,
        gate_shard,
        up_shard,
        down_shard,
    )


def solution(mesh):
    fine = Mesh(mesh.devices.reshape(2, 4, 2, 2, 2, 2), ("xl", "z", "yh", "yl", "xh", "core"))
    rows = P(FSDP_AXES, CTX_AXES, None)
    gain = P(FSDP_AXES)
    weight = P(FSDP_AXES, None)
    return jax.shard_map(
        per_device,
        mesh=fine,
        in_specs=(rows, P(), gain, weight, weight, weight, weight, gain, weight, weight, weight, rows),
        out_specs=(rows, rows, gain, weight, weight, weight, weight, gain, weight, weight, weight),
        check_vma=False,
    )
```

```python
import functools
import math

import jax
import jax.numpy as jnp
from jax import lax
from jax.experimental import pallas as pl
from jax.experimental.pallas import tpu as pltpu
from jax.sharding import Mesh
from jax.sharding import PartitionSpec as P

HEADS = 15
KV_HEADS = 5
EPSILON = 1e-05
THETA = 100000.0
SEQ_AXES = ("z", "y")
CTX_AXES = ("xl", "z", "y")
CHIP_AXES = ("xh", "xl", "z", "y")
FSDP_AXES = ("xh", "core")
CUBE_AXES = ("xl", "xh", "core")
SWAP = ((0, 1), (1, 0))
STRIP = 16
BLK = 128
HEAD = 64
EXP_SCALE = math.log2(math.e) / 8.0
MASKED = -1e30


def attend_kernel(key_pos, query_rank, sorted_pos, sorted_id, q_ref, own_in, other_in, send_ref, out_ref, lse_ref, kv_ref, kvt_ref, ones_v, q_sorted, *, big, small, edge_size, blocks):
    groups, width = own_in.shape[0], HEAD
    rows = blocks * BLK
    is_key = lax.broadcasted_iota(jnp.int32, (BLK, 2 * width), 1) < width

    def place(index, _):
        for side, source in enumerate((own_in, other_in)):
            for half in range(2):
                where = pl.multiple_of(key_pos[side * 2 * groups + 2 * index + half] * BLK, BLK)
                piece = source[index, :, half * BLK:(half + 1) * BLK]
                kvt_ref[:, pl.ds(where, BLK)] = piece
                turned = piece.T
                kv_ref[pl.ds(where, BLK), :] = turned
                ones_v[pl.ds(where, BLK), :] = jnp.where(is_key, jnp.ones_like(turned), turned)
        for half in range(2):
            query = q_ref[index, :, half * BLK:(half + 1) * BLK]
            query = jnp.concatenate([query, jnp.zeros_like(query)], axis=0)
            q_sorted[pl.ds(pl.multiple_of(query_rank[2 * index + half] * BLK, BLK), BLK), :] = query.T
        return 0

    lax.fori_loop(0, groups, place, 0, unroll=4)

    def tile(index, _):
        low, high = sorted_pos[blocks * index], sorted_pos[blocks * index + blocks - 1]
        query = q_sorted[pl.ds(pl.multiple_of(index * rows, rows), rows), :]
        row = lax.broadcasted_iota(jnp.int32, (rows, 1), 0)
        place_of = row + low * BLK
        for part in range(1, blocks):
            place_of = jnp.where(row >= part * BLK, row + (sorted_pos[blocks * index + part] - part) * BLK, place_of)

        def step(start, carry, size, masked):
            top, total = carry
            scores = lax.dot_general(query, kv_ref[pl.ds(start, size), :], (((1,), (1,)), ((), ())), preferred_element_type=jnp.float32)
            if masked:
                column = start + lax.broadcasted_iota(jnp.int32, scores.shape, 1)
                scores = jnp.where(column <= place_of, scores, MASKED)
            new_top = jnp.maximum(top, jnp.max(scores, axis=1, keepdims=True))
            weights = jnp.exp2((scores - new_top) * EXP_SCALE).astype(jnp.bfloat16)
            factor = jnp.exp2((top - new_top) * EXP_SCALE)
            added = jnp.dot(weights, ones_v[pl.ds(start, size), :], preferred_element_type=jnp.float32)
            return new_top, total * factor + added

        def full(count, carry):
            for part in range(big // small):
                carry = step(pl.multiple_of(count * big + part * small, small), carry, small, False)
            return carry

        def edge(count, carry):
            return step(pl.multiple_of(count * edge_size, edge_size), carry, edge_size, True)

        carry = (jnp.full((rows, 1), MASKED, jnp.float32), jnp.zeros((rows, 2 * width), jnp.float32))
        done = low * BLK // big
        carry = lax.fori_loop(0, done, full, carry)
        top, total = lax.fori_loop(done * (big // edge_size), (high * BLK + BLK + edge_size - 1) // edge_size, edge, carry)
        lse = (top * EXP_SCALE + jnp.log2(total)).T
        total = total.T
        result = total[width:] / total[:1]
        for part in range(blocks):
            ident = sorted_id[blocks * index + part]
            piece = result[:, part * BLK:(part + 1) * BLK]
            out_ref[ident] = piece
            send_ref[ident // 2, :, pl.ds(pl.multiple_of(ident % 2 * BLK, BLK), BLK)] = piece.astype(jnp.bfloat16)
            lse_ref[ident] = lse[:8, part * BLK:(part + 1) * BLK]
        return 0

    lax.fori_loop(0, 2 * groups // blocks, tile, 0)


def attend(key_pos, query_rank, sorted_pos, sorted_id, q, own_in, other_in, big=1024, small=1024, edge_size=512, blocks=4):
    groups, width = own_in.shape[0], HEAD
    total = 4 * groups * BLK
    vm = pl.BlockSpec(memory_space=pltpu.VMEM)
    sm = pl.BlockSpec(memory_space=pltpu.SMEM)
    return pl.pallas_call(
        functools.partial(attend_kernel, big=big, small=small, edge_size=edge_size, blocks=blocks),
        out_shape=(
            jax.ShapeDtypeStruct((groups, width, 2 * BLK), jnp.bfloat16),
            jax.ShapeDtypeStruct((2 * groups, width, BLK), jnp.float32),
            jax.ShapeDtypeStruct((2 * groups, 8, BLK), jnp.float32),
            jax.ShapeDtypeStruct((total, 2 * width), jnp.bfloat16),
            jax.ShapeDtypeStruct((2 * width, total), jnp.bfloat16),
        ),
        in_specs=[sm] * 4 + [vm] * 3,
        out_specs=(vm,) * 5,
        scratch_shapes=[
            pltpu.VMEM((total, 2 * width), jnp.bfloat16),
            pltpu.VMEM((2 * groups * BLK, 2 * width), jnp.bfloat16),
        ],
        compiler_params=pltpu.CompilerParams(vmem_limit_bytes=48 * 2**20),
        cost_estimate=pl.CostEstimate(flops=40 * 10**9, bytes_accessed=10**7, transcendentals=2 * 10**7),
        name="attend",
    )(key_pos, query_rank, sorted_pos, sorted_id, q, own_in, other_in)


def back_kernel(key_pos, query_rank, sorted_pos, sorted_id, q_ref, da_ref, out_ref, lse_ref, kv_ref, kvt_ref, dq_ref, own_ref, other_ref, dkv, q_sorted, da_sorted, *, big, small, edge_size, flip):
    groups, width = q_ref.shape[0], HEAD

    def place(index, _):
        for half in range(2):
            rank = query_rank[2 * index + half]
            q_sorted[rank] = q_ref[index, :, half * BLK:(half + 1) * BLK]
            da_sorted[rank] = da_ref[index, :, half * BLK:(half + 1) * BLK]
        return 0

    lax.fori_loop(0, groups, place, 0)

    def clear(index, _):
        dkv[pl.ds(pl.multiple_of(index * BLK, BLK), BLK), :] = jnp.zeros((BLK, 2 * width), jnp.float32)
        return 0

    lax.fori_loop(0, 4 * groups, clear, 0)

    def tile(index, _):
        low, high = sorted_pos[2 * index], sorted_pos[2 * index + 1]
        first_id, second_id = sorted_id[2 * index], sorted_id[2 * index + 1]
        query = jnp.concatenate([q_sorted[2 * index], q_sorted[2 * index + 1]], axis=1)
        grad = jnp.concatenate([da_sorted[2 * index], da_sorted[2 * index + 1]], axis=1)
        value = jnp.concatenate([out_ref[first_id], out_ref[second_id]], axis=1)
        lse = jnp.concatenate([lse_ref[first_id][:1], lse_ref[second_id][:1]], axis=1)
        delta = jnp.sum(grad.astype(jnp.float32) * value, axis=0, keepdims=True)
        none = jnp.zeros_like(query)
        both = jnp.concatenate([jnp.concatenate([query, none], axis=1), jnp.concatenate([none, grad], axis=1)], axis=0)
        both_t = both.T
        lane = lax.broadcasted_iota(jnp.int32, (1, 2 * BLK), 1)
        place_of = jnp.where(lane < BLK, low * BLK + lane, (high - 1) * BLK + lane)

        def step(start, total, size, masked):
            keys = kv_ref[pl.ds(start, size), :]
            pair = jnp.dot(keys, both, preferred_element_type=jnp.float32)
            weights = jnp.exp2(pair[:, :2 * BLK] * EXP_SCALE - lse)
            if masked:
                row = start + lax.broadcasted_iota(jnp.int32, weights.shape, 0)
                weights = jnp.where(row <= place_of, weights, 0.0)
            grad_scores = (weights * (pair[:, 2 * BLK:] - delta)).astype(jnp.bfloat16)
            weights = weights.astype(jnp.bfloat16)
            dkv[pl.ds(start, size), :] += jnp.dot(jnp.concatenate([grad_scores, weights], axis=1), both_t, preferred_element_type=jnp.float32)
            if flip:
                return total + lax.dot_general(grad_scores, keys, (((0,), (0,)), ((), ())), preferred_element_type=jnp.float32)
            return total + jnp.dot(kvt_ref[:width, pl.ds(start, size)], grad_scores, preferred_element_type=jnp.float32)

        def full(count, carry):
            for part in range(big // small):
                carry = step(pl.multiple_of(count * big + part * small, small), carry, small, False)
            return carry

        def edge(count, carry):
            return step(pl.multiple_of(count * edge_size, edge_size), carry, edge_size, True)

        done = low * BLK // big
        total = jnp.zeros((2 * BLK, 2 * width) if flip else (width, 2 * BLK), jnp.float32)
        total = lax.fori_loop(0, done, full, total)
        total = lax.fori_loop(done * (big // edge_size), (high * BLK + BLK + edge_size - 1) // edge_size, edge, total) * 0.125
        if flip:
            total = total.T[:width]
        for half, ident in enumerate((first_id, second_id)):
            dq_ref[ident // 2, :, pl.ds(pl.multiple_of(ident % 2 * BLK, BLK), BLK)] = total[:, half * BLK:(half + 1) * BLK].astype(jnp.bfloat16)
        return 0

    lax.fori_loop(0, groups, tile, 0)
    factor = jnp.where(lax.broadcasted_iota(jnp.int32, (1, 2 * width), 1) < width, 0.125, 1.0)

    def spread(index, _):
        for side, target in enumerate((own_ref, other_ref)):
            for half in range(2):
                where = pl.multiple_of(key_pos[side * 2 * groups + 2 * index + half] * BLK, BLK)
                target[index, :, half * BLK:(half + 1) * BLK] = (dkv[pl.ds(where, BLK), :] * factor).astype(target.dtype)
        return 0

    lax.fori_loop(0, groups, spread, 0)


def attend_back(key_pos, query_rank, sorted_pos, sorted_id, q, da, out, lse, kv, kvt, big=1024, small=1024, edge_size=512, flip=False):
    groups, width = q.shape[0], HEAD
    total = 4 * groups * BLK
    vm = pl.BlockSpec(memory_space=pltpu.VMEM)
    sm = pl.BlockSpec(memory_space=pltpu.SMEM)
    return pl.pallas_call(
        functools.partial(back_kernel, big=big, small=small, edge_size=edge_size, flip=flip),
        out_shape=(
            jax.ShapeDtypeStruct((groups, width, 2 * BLK), jnp.bfloat16),
            jax.ShapeDtypeStruct((groups, 2 * width, 2 * BLK), jnp.float32),
            jax.ShapeDtypeStruct((groups, 2 * width, 2 * BLK), jnp.bfloat16),
        ),
        in_specs=[sm] * 4 + [vm] * 6,
        out_specs=(vm,) * 3,
        scratch_shapes=[
            pltpu.VMEM((total, 2 * width), jnp.float32),
            pltpu.VMEM((2 * groups, width, BLK), jnp.bfloat16),
            pltpu.VMEM((2 * groups, width, BLK), jnp.bfloat16),
        ],
        compiler_params=pltpu.CompilerParams(vmem_limit_bytes=48 * 2**20),
        cost_estimate=pl.CostEstimate(flops=60 * 10**9, bytes_accessed=10**7, transcendentals=2 * 10**7),
        name="attend_back",
    )(key_pos, query_rank, sorted_pos, sorted_id, q, da, out, lse, kv, kvt)


def in_vmem(kernel, out_shape, scalars, arrays, scratch=(), flops=10**9, name=None):
    vm = pl.BlockSpec(memory_space=pltpu.VMEM)
    return pl.pallas_call(
        kernel,
        out_shape=tuple(jax.ShapeDtypeStruct(shape, dtype) for shape, dtype in out_shape),
        in_specs=[pl.BlockSpec(memory_space=pltpu.SMEM)] * len(scalars) + [vm] * len(arrays),
        out_specs=(vm,) * len(out_shape),
        scratch_shapes=[pltpu.VMEM(shape, dtype) for shape, dtype in scratch],
        compiler_params=pltpu.CompilerParams(vmem_limit_bytes=48 * 2**20),
        cost_estimate=pl.CostEstimate(flops=flops, bytes_accessed=10**7, transcendentals=0),
        name=name,
    )(*scalars, *arrays)


def across(left, right):
    return lax.dot_general(left, right, (((1,), (1,)), ((), ())), preferred_element_type=jnp.float32)


def unit_rms(value):
    return lax.rsqrt(jnp.mean(value * value, axis=-1, keepdims=True) + EPSILON)


def put_rows(mine, pieces, target):
    shard = pieces[0].shape[0]
    for step, piece in enumerate(pieces):
        target[pl.ds(pl.multiple_of((mine[0] ^ step) * shard, 16), shard), :] = piece[...]


def turn(pair, cos, sin):
    half = HEAD // 2
    front, behind = pair[:half], pair[half:]
    return jnp.concatenate([front * cos - behind * sin, behind * cos + front * sin], axis=0).astype(jnp.bfloat16)


def turn_back(pair, cos, sin):
    return turn(pair, cos, -sin)


def project_keys_kernel(mine, x_ref, own, near, far, far_near, cos_ref, sin_ref, hat_ref, send_ref, w_ref):
    put_rows(mine, (own, near, far, far_near), w_ref)
    hidden = x_ref[...].astype(jnp.float32)
    hat = (hidden * unit_rms(hidden)).astype(jnp.bfloat16)
    hat_ref[...] = hat
    key_width = KV_HEADS * HEAD
    per = HEADS // KV_HEADS
    lin = jnp.dot(hat, w_ref[...], preferred_element_type=jnp.float32).T
    for head in range(KV_HEADS):
        key = turn(lin[head * HEAD:(head + 1) * HEAD], cos_ref[...], sin_ref[...])
        value = lin[key_width + head * HEAD:key_width + (head + 1) * HEAD].astype(jnp.bfloat16)
        for query in range(per):
            send_ref[head * per + query, :HEAD] = key
            send_ref[head * per + query, HEAD:] = value
    send_ref[HEADS:] = jnp.zeros((send_ref.shape[0] - HEADS,) + send_ref.shape[1:], jnp.bfloat16)


def project_keys(mine, x, pieces, cos, sin, groups):
    rows, width = x.shape
    columns = pieces[0].shape[1]
    return in_vmem(
        project_keys_kernel,
        ((x.shape, jnp.bfloat16), ((groups, 2 * HEAD, rows), jnp.bfloat16), ((width, columns), jnp.bfloat16)),
        (mine,),
        (x, *pieces, cos, sin),
        name="project_keys",
    )


def project_queries_kernel(mine, hat_ref, own, near, far, far_near, cos_ref, sin_ref, send_ref, w_ref):
    put_rows(mine, (own, near, far, far_near), w_ref)
    per = HEADS // KV_HEADS
    for group in range(KV_HEADS):
        columns = slice(group * per * HEAD, (group + 1) * per * HEAD)
        lin = jnp.dot(hat_ref[...], w_ref[:, columns], preferred_element_type=jnp.float32).T
        for query in range(per):
            send_ref[group * per + query] = turn(lin[query * HEAD:(query + 1) * HEAD], cos_ref[...], sin_ref[...])
    send_ref[HEADS:] = jnp.zeros((send_ref.shape[0] - HEADS,) + send_ref.shape[1:], jnp.bfloat16)


def project_queries(mine, hat, pieces, cos, sin, groups):
    rows, width = hat.shape
    columns = pieces[0].shape[1]
    return in_vmem(
        project_queries_kernel,
        (((groups, HEAD, rows), jnp.bfloat16), ((width, columns), jnp.bfloat16)),
        (mine,),
        (hat, *pieces, cos, sin),
        name="project_queries",
    )


def stack_rows_kernel(mine, own, near, far, far_near, out_ref):
    put_rows(mine, (own, near, far, far_near), out_ref)


def stack_rows(mine, pieces):
    shard, columns = pieces[0].shape
    return in_vmem(stack_rows_kernel, (((4 * shard, columns), jnp.bfloat16),), (mine,), pieces, flops=10**6, name="stack_rows")[0]


def merge_kernel(dq, dkv_own, dkv_received, out_ref):
    out_ref[:, :HEAD] = dq[...]
    out_ref[:, HEAD:] = (dkv_own[...] + dkv_received[...].astype(jnp.float32)).astype(jnp.bfloat16)


def merge(dq, dkv_own, dkv_received):
    groups, _, rows = dq.shape
    return in_vmem(merge_kernel, (((groups, 3 * HEAD, rows), jnp.bfloat16),), (), (dq, dkv_own, dkv_received), flops=10**6, name="merge")[0]


def finish_kernel(mine, home, x_ref, hat_ref, kv_ref, query_ref, mid_ref, cos_ref, sin_ref, keep_ref, give_ref, tokens_ref, turned, hat_t):
    shard = query_ref.shape[0] // 4
    cos, sin = cos_ref[...], sin_ref[...]
    key_width = KV_HEADS * HEAD
    per = HEADS // KV_HEADS

    for head in range(KV_HEADS):
        total = sum(home[head * per + query, HEAD:, :].astype(jnp.float32) for query in range(per))
        total = jnp.concatenate([total[:, :BLK].T, total[:, BLK:].T], axis=1)
        turned[head * HEAD:(head + 1) * HEAD, :] = turn_back(total[:HEAD], cos, sin)
        turned[key_width + head * HEAD:key_width + (head + 1) * HEAD, :] = total[HEAD:].astype(jnp.bfloat16)
        for query in range(per):
            start = 2 * key_width + (head * per + query) * HEAD
            turned[start:start + HEAD, :] = turn_back(home[head * per + query, :HEAD, :].astype(jnp.float32), cos, sin)
    hat_t[...] = hat_ref[...].T
    core = mine[0] & 1
    for target, at in ((keep_ref, core), (give_ref, 1 - core)):
        target[...] = jnp.zeros(target.shape, target.dtype)
        for part in range(2):
            rows = hat_t[pl.ds(pl.multiple_of((2 * part + at) * shard, 16), shard), :]
            grads = lax.dot_general(rows, turned[...], (((1,), (1,)), ((), ())), preferred_element_type=jnp.float32)
            target[part, :shard, : grads.shape[1]] = grads.astype(jnp.bfloat16)
    scaled = jnp.dot(kv_ref[...], turned[:2 * key_width, :], preferred_element_type=jnp.float32)
    scaled = (scaled + jnp.dot(query_ref[...], turned[2 * key_width:, :], preferred_element_type=jnp.float32)).T
    hidden = x_ref[...].astype(jnp.float32)
    tokens_ref[...] = (mid_ref[...] + norm_back(hidden, scaled)).astype(jnp.bfloat16)


def finish(mine, home, x, hat, w_kv, w_query, mid, cos, sin):
    rows, width = x.shape
    columns = w_kv.shape[1] + w_query.shape[1]
    half = ((2, 256, -(-columns // BLK) * BLK), jnp.bfloat16)
    return in_vmem(
        finish_kernel,
        (half, half, (x.shape, jnp.bfloat16)),
        (mine,),
        (home, x, hat, w_kv, w_query, mid, cos, sin),
        scratch=(((columns, rows), jnp.bfloat16), ((width, rows), jnp.bfloat16)),
        name="finish",
    )


def norm_back(value, grad):
    rms = unit_rms(value)
    hat = value * rms
    return rms * (grad - hat * jnp.mean(grad * hat, axis=-1, keepdims=True))


def out_kernel(attn, x_ref, w_ref, mid_ref, hat_ref):
    rows = attn[:HEADS].reshape(HEADS * HEAD, attn.shape[2]).T
    mid = x_ref[...].astype(jnp.float32) + jnp.dot(rows, w_ref[...], preferred_element_type=jnp.float32)
    mid_ref[...] = mid
    hat_ref[...] = (mid * unit_rms(mid)).astype(jnp.bfloat16)


def project_out(attn, x, w_out):
    return in_vmem(out_kernel, ((x.shape, jnp.float32), (x.shape, jnp.bfloat16)), (), (attn, x, w_out), name="project_out")


def feed_kernel(mine, *refs):
    hats, grads, weights, (w_down,) = refs[:4], refs[4:8], refs[8:12], refs[12:13]
    scaled_keep, scaled_send, out_keep, out_send, act_ref, gate_grad_ref, up_grad_ref, w_gate, w_up = refs[13:]
    shard = weights[0].shape[1]
    for step, piece in enumerate(weights):
        where = pl.ds(pl.multiple_of((mine[0] ^ step) * shard, 16), shard)
        w_gate[where, :] = piece[0]
        w_up[where, :] = piece[1]
    rows = hats[0].shape[0]
    for step in range(4):
        here = slice(step * rows, (step + 1) * rows)
        hat = hats[step][...]
        gate = jnp.dot(hat, w_gate[...], preferred_element_type=jnp.float32)
        up = jnp.dot(hat, w_up[...], preferred_element_type=jnp.float32)
        sigmoid = jax.nn.sigmoid(gate)
        silu = gate * sigmoid
        act = (silu * up).astype(jnp.bfloat16)
        act_ref[here, :] = act
        grad_act = across(grads[step][...], w_down[...]).astype(jnp.bfloat16).astype(jnp.float32)
        gate_grad = (grad_act * up * sigmoid * (1.0 + gate * (1.0 - sigmoid))).astype(jnp.bfloat16)
        up_grad = (grad_act * silu).astype(jnp.bfloat16)
        gate_grad_ref[here, :] = gate_grad
        up_grad_ref[here, :] = up_grad
        scaled = across(gate_grad, w_gate[...]) + across(up_grad, w_up[...])
        out = jnp.dot(act, w_down[...], preferred_element_type=jnp.float32)
        if step % 2:
            scaled_send[step // 2, :, : scaled.shape[1]] = scaled.astype(jnp.bfloat16)
            out_send[step // 2, :, : out.shape[1]] = out.astype(jnp.bfloat16)
            for target in (scaled_send, out_send):
                target[step // 2, :, scaled.shape[1]:] = jnp.zeros((rows, target.shape[2] - scaled.shape[1]), jnp.bfloat16)
        else:
            scaled_keep[step // 2] = scaled
            out_keep[step // 2] = out


def feed(mine, hats, grads, weights, w_down):
    rows, width = hats[0].shape
    part = w_down.shape[0]
    pair = (2, rows, width)
    sent = (2, rows, -(-width // 256) * 256)
    hidden = ((4 * rows, part), jnp.bfloat16)
    return in_vmem(
        feed_kernel,
        ((pair, jnp.float32), (sent, jnp.bfloat16), (pair, jnp.float32), (sent, jnp.bfloat16), hidden, hidden, hidden),
        (mine,),
        (*hats, *grads, *weights, w_down),
        scratch=(((width, part), jnp.bfloat16),) * 2,
        flops=10**10,
        name="feed",
    )


def feed_grads_kernel(*refs):
    hats, grads, (act, gate_grad, up_grad), (out_ref, hat_t, grad_t) = refs[:4], refs[4:8], refs[8:11], refs[11:]
    rows = hats[0].shape[0]
    for step in range(4):
        here = slice(step * rows, (step + 1) * rows)
        hat_t[:, here] = hats[step][...].T
        grad_t[:, here] = grads[step][...].T
    shard = hat_t.shape[0] // 4
    strips = shard // STRIP
    for index, (left, right) in enumerate(((hat_t, gate_grad), (hat_t, up_grad), (grad_t, act))):
        for part in range(4):
            product = jnp.dot(left[part * shard:(part + 1) * shard, :], right[...], preferred_element_type=jnp.float32)
            out_ref[:strips, 4 * index + part] = product.astype(jnp.bfloat16).reshape(strips, STRIP, product.shape[1])
    out_ref[strips:] = jnp.zeros((out_ref.shape[0] - strips,) + out_ref.shape[1:], jnp.bfloat16)


def feed_grads(hats, grads, act, gate_grad, up_grad, ring):
    rows, width = hats[0].shape
    turned = ((width, 4 * rows), jnp.bfloat16)
    return in_vmem(
        feed_grads_kernel,
        (((ring, 12, STRIP, act.shape[1]), jnp.bfloat16),),
        (),
        (*hats, *grads, act, gate_grad, up_grad),
        scratch=(turned, turned),
        flops=8 * 10**9,
        name="feed_grads",
    )[0]


def mid_kernel(keep, received, far, mid_ref, grad_ref, w_ref, total_ref, low_ref, send_ref):
    scaled = keep[0] + received[0, :, : keep.shape[2]].astype(jnp.float32) + far[...].astype(jnp.float32)
    total = grad_ref[...].astype(jnp.float32) + norm_back(mid_ref[...], scaled)
    total_ref[...] = total
    low = total.astype(jnp.bfloat16)
    low_ref[...] = low
    send_ref[:HEADS] = across(w_ref[...], low).astype(jnp.bfloat16).reshape(HEADS, HEAD, low.shape[0])
    send_ref[HEADS:] = jnp.zeros((send_ref.shape[0] - HEADS,) + send_ref.shape[1:], jnp.bfloat16)


def mid_back(keep, received, far, mid, grad, w_out, groups):
    shape = mid.shape
    return in_vmem(
        mid_kernel,
        ((shape, jnp.float32), (shape, jnp.bfloat16), ((groups, HEAD, shape[0]), jnp.bfloat16)),
        (),
        (keep, received, far, mid, grad, w_out),
        name="mid_back",
    )


def out_grad_kernel(mine, attn, low, keep_ref, give_ref, rows_ref):
    width = low.shape[1]
    shard = width // 4
    rows_ref[...] = attn[:HEADS].reshape(HEADS * HEAD, attn.shape[2])
    core = mine[0] & 1
    for target, at in ((keep_ref, core), (give_ref, 1 - core)):
        target[...] = jnp.zeros(target.shape, target.dtype)
        for part in range(2):
            rows = rows_ref[pl.ds(pl.multiple_of((2 * part + at) * shard, 16), shard), :]
            target[part, :shard, :width] = jnp.dot(rows, low[...], preferred_element_type=jnp.float32).astype(target.dtype)


def out_grad(mine, attn, low):
    rows, width = low.shape
    shape = (2, 256, 1024)
    return in_vmem(
        out_grad_kernel, ((shape, jnp.bfloat16), (shape, jnp.bfloat16)), (mine,), (attn, low), scratch=(((width, rows), jnp.bfloat16),), name="out_grad"
    )


def pack_kernel(key_t, value_t, query, gain, kv_ref, query_ref):
    width = key_t.shape[0]
    scale = gain[...]
    for index, piece in enumerate((key_t, value_t)):
        kv_ref[:, index * width:(index + 1) * width] = (piece[...].astype(jnp.float32).T * scale).astype(jnp.bfloat16)
    query_ref[...] = (query[...].astype(jnp.float32) * scale).astype(jnp.bfloat16)


def pack(w_key, w_value, w_query, gain):
    shard = w_key.shape[0]
    return in_vmem(
        pack_kernel,
        (((shard, 2 * w_key.shape[1]), jnp.bfloat16), (w_query.shape, jnp.bfloat16)),
        (),
        (w_key.T, w_value.T, w_query, gain),
        flops=10**6,
        name="pack",
    )


def as_row(column):
    return jnp.broadcast_to(column, (column.shape[0], BLK)).T[:1]


def last_kernel(total, w_kv, w_query, gain, query_ref, key_ref, value_ref, out_ref, gain_ref):
    shard, width = w_query.shape
    key_width = key_ref.shape[0]
    columns = 2 * key_width + width
    padded = -(-columns // BLK) * BLK
    rows = total[...].reshape(total.shape[0] * total.shape[1], total.shape[2])[:shard].astype(jnp.float32)
    kv, query = rows[:, : 2 * key_width], rows[:, 2 * key_width : columns]
    scale = gain[...]
    gain_sum = jnp.sum(kv * w_kv[...].astype(jnp.float32), axis=1, keepdims=True) + jnp.sum(query * w_query[...].astype(jnp.float32), axis=1, keepdims=True)
    gain_ref[...] = as_row(gain_sum / scale)
    kv = kv * scale
    key_ref[...] = kv[:, :key_width].T
    value_ref[...] = kv[:, key_width:].T
    query_ref[...] = query * scale
    out_ref[...] = rows[:, padded:padded + width]


def last(total, w_kv, w_query, gain):
    shard, width = w_query.shape
    square = (w_query.shape, jnp.float32)
    turned = ((w_kv.shape[1] // 2, shard), jnp.float32)
    query, key, value, out, gain_grad = in_vmem(
        last_kernel, (square, turned, turned, square, ((1, shard), jnp.float32)), (), (total, w_kv, w_query, gain), name="last"
    )
    return gain_grad.reshape(shard), query, key.T, value.T, out


def unpack_kernel(total, w_gate, w_up, gain, gate_ref, up_ref, down_ref, gain_ref):
    shard, part = w_gate.shape[0], total.shape[3]
    strips = shard // STRIP
    scale = gain[...]
    gain_sum = jnp.zeros((shard, 1), jnp.float32)
    for index, (weight, target) in enumerate(((w_gate, gate_ref), (w_up, up_ref))):
        for step in range(4):
            columns = slice(step * part, (step + 1) * part)
            grads = total[:strips, 4 * index + step].reshape(shard, part).astype(jnp.float32)
            gain_sum = gain_sum + jnp.sum(grads * weight[:, columns].astype(jnp.float32), axis=1, keepdims=True)
            target[:, columns] = grads * scale
    for step in range(4):
        down_ref[step * shard:(step + 1) * shard, :] = total[:strips, 8 + step].reshape(shard, part).astype(jnp.float32)
    gain_ref[...] = as_row(gain_sum)


def unpack(total, w_gate, w_up, gain):
    shard, columns = w_gate.shape
    part = total.shape[3]
    full = ((shard, columns), jnp.float32)
    gate, up, down, gain_grad = in_vmem(
        unpack_kernel, (full, full, ((4 * shard, part), jnp.float32), ((1, shard), jnp.float32)), (), (total, w_gate, w_up, gain), name="unpack"
    )
    return gain_grad.reshape(shard), gate, up, down.T


def over_core(value):
    return lax.ppermute(value, "core", SWAP)


def over_chip(value):
    return lax.ppermute(value, "xh", SWAP)


def over_both(value):
    return lax.ppermute(value, FSDP_AXES, ((0, 3), (3, 0), (1, 2), (2, 1)))


def trade(value):
    return lax.ppermute(value, ("xl", "core"), ((0, 0), (1, 2), (2, 1), (3, 3)))


def arrange(pieces, xh, core):
    low = jnp.where(core == 1, pieces[1], pieces[0]), jnp.where(core == 1, pieces[0], pieces[1])
    high = jnp.where(core == 1, pieces[3], pieces[2]), jnp.where(core == 1, pieces[2], pieces[3])
    return jnp.stack([jnp.where(xh == 1, h, l) for l, h in zip(low, high)] + [jnp.where(xh == 1, l, h) for l, h in zip(low, high)])


def gather_tokens(rows):
    far = over_chip(rows)
    return rows, over_core(rows), far, over_core(far)


def exchange(value, axes):
    return lax.all_to_all(value, axes, split_axis=0, concat_axis=0, tiled=True)


def per_device(
    tokens,
    block_order,
    gain_attn,
    w_query,
    w_key,
    w_value,
    w_out,
    gain_mlp,
    w_gate,
    w_up,
    w_down,
    cotangent,
):
    f32, bf16 = jnp.float32, jnp.bfloat16
    xh, core = lax.axis_index("xh"), lax.axis_index("core")
    mine = 2 * xh + core
    own_id = mine.reshape(1)
    row_total, width = tokens.shape[1:]
    shard = w_query.shape[0]
    ff_part = w_down.shape[0]
    groups = lax.axis_size(SEQ_AXES)
    key_width = KV_HEADS * HEAD
    gain_one = gain_attn.astype(f32)[:, None]
    gain_two = gain_mlp.astype(f32)[:, None]

    kv_shard, query_shard = pack(w_key, w_value, w_query, gain_one)
    far_kv, far_query = over_chip(kv_shard), over_chip(query_shard)
    near_kv, near_query = over_core(kv_shard), over_core(query_shard)
    hidden_low = trade(tokens[0])

    def gate_up(step):
        start = (mine ^ step) * ff_part
        both = [lax.dynamic_slice_in_dim(w, start, ff_part, 1).astype(f32) * gain_two for w in (w_gate, w_up)]
        return jnp.stack(both).astype(bf16)

    gate_up_parts = [gate_up(step) for step in range(4)]
    far_kv, hidden_low, gate_up_parts = lax.optimization_barrier((far_kv, hidden_low, gate_up_parts))

    own_order = lax.dynamic_slice_in_dim(block_order, 2 * groups * core, 2 * groups)
    other_order = lax.dynamic_slice_in_dim(block_order, 2 * groups * (1 - core), 2 * groups)
    key_pos = jnp.concatenate([own_order, other_order])
    query_rank = jnp.sum((own_order[None, :] < own_order[:, None]).astype(jnp.int32), axis=1)
    hit = query_rank[None, :] == jnp.arange(2 * groups, dtype=jnp.int32)[:, None]
    sorted_pos = jnp.sum(jnp.where(hit, own_order[None, :], 0), axis=1)
    sorted_id = jnp.sum(jnp.where(hit, jnp.arange(2 * groups, dtype=jnp.int32)[None, :], 0), axis=1)
    here = lax.axis_index(SEQ_AXES)
    own_blocks = lax.dynamic_slice_in_dim(own_order, 2 * here, 2)
    row = jnp.arange(row_total, dtype=jnp.int32)
    own_pos = jnp.where(row < BLK, own_blocks[0] * BLK + row, own_blocks[1] * BLK + row - BLK)
    inverse_freq = THETA ** (-jnp.arange(HEAD // 2, dtype=f32) / (HEAD // 2))
    angles = inverse_freq[:, None] * own_pos.astype(f32)[None, :]
    cos_table, sin_table = jnp.cos(angles), jnp.sin(angles)

    normed_one, kv_send, kv_full = project_keys(own_id, hidden_low, (kv_shard, near_kv, far_kv, over_core(far_kv)), cos_table, sin_table, groups)
    kv_own, upstream = lax.optimization_barrier((exchange(kv_send, SEQ_AXES), trade(cotangent[0])))
    query_send, query_full = project_queries(own_id, normed_one, (query_shard, near_query, far_query, over_core(far_query)), cos_table, sin_table, groups)
    query_in = exchange(query_send, SEQ_AXES)
    kv_other = over_core(kv_own)

    query_in, w_out, upstream, gate_up_parts = lax.optimization_barrier((query_in, w_out, upstream, gate_up_parts))
    far_out, far_upstream = over_chip(w_out), over_chip(upstream)
    far_weights = over_chip(gate_up_parts[2]), over_both(gate_up_parts[3])
    out_send, out_blocks, lse, kv_sorted, kv_turned = attend(key_pos, query_rank, sorted_pos, sorted_id, query_in, kv_own, kv_other)
    out_send, far_out, far_upstream, far_weights = lax.optimization_barrier((out_send, far_out, far_upstream, far_weights))
    out_full = stack_rows(own_id, (w_out, over_core(w_out), far_out, over_core(far_out)))
    weights = (gate_up_parts[0], over_core(gate_up_parts[1])) + far_weights
    upstream_all = (upstream, over_core(upstream), far_upstream, over_core(far_upstream))

    attn = exchange(out_send, SEQ_AXES)
    mid_state, second_hat = project_out(attn, hidden_low, out_full)
    normed_all = gather_tokens(second_hat)
    scaled_keep, scaled_send, result_keep, result_send, hidden_act, grad_gate_lin, grad_up_lin = feed(own_id, normed_all, upstream_all, weights, w_down)
    scaled_received = over_core(scaled_send)
    far_send = (scaled_keep[1] + scaled_received[1, :, :width].astype(f32)).astype(bf16)
    far_send, normed_all, hidden_act = lax.optimization_barrier((far_send, normed_all, hidden_act))
    scaled_far = over_chip(far_send)
    ring = lax.axis_size(SEQ_AXES)
    stacked = feed_grads(normed_all, upstream_all, hidden_act, grad_gate_lin, grad_up_lin, ring)
    scaled_far, stacked = lax.optimization_barrier((scaled_far, stacked))
    reduced = lax.psum_scatter(stacked.reshape(ring, 12 * STRIP, ff_part), SEQ_AXES, scatter_dimension=0, tiled=True)[0]

    grad_mid, mid_low, grad_send = mid_back(scaled_keep, scaled_received, scaled_far, mid_state, upstream, out_full, groups)
    grad_group = exchange(grad_send, SEQ_AXES)
    ctx = lax.axis_size(CTX_AXES)
    slab = 8
    out_grad_keep, out_grad_give = out_grad(own_id, attn, mid_low)
    out_chip = (out_grad_keep.astype(f32) + over_core(out_grad_give).astype(f32)).astype(bf16).reshape(2 * ctx, slab, -1)
    result_received = over_core(result_send)[:, :, :width]
    result_send = (result_keep[1] + result_received[1].astype(f32)).astype(bf16)
    grad_group, result_send, out_chip = lax.optimization_barrier((grad_group, result_send, out_chip))

    out_chips = exchange(out_chip, CHIP_AXES)
    result_far = over_chip(result_send)

    dq, dkv_own, dkv_other = attend_back(key_pos, query_rank, sorted_pos, sorted_id, query_in, grad_group, out_blocks, lse, kv_sorted, kv_turned)
    dkv_other, reduced, out_chips, result_far = lax.optimization_barrier((dkv_other, reduced, out_chips, result_far))
    result = mid_state + result_keep[0] + result_received[0].astype(f32) + result_far.astype(f32)
    block_out = trade(result.astype(bf16))
    out_sum = jnp.sum(out_chips.astype(f32), axis=0).astype(bf16)
    dkv_received = over_core(dkv_other)
    reduced = reduced.reshape(3, 4, STRIP, ff_part)
    cube = jnp.broadcast_to(reduced[:2].transpose(1, 0, 2, 3)[None], (2, 4, 2, STRIP, ff_part)).reshape(8, 2 * STRIP, ff_part)
    cube = exchange(cube, CUBE_AXES).reshape(2, 4, 2, STRIP, ff_part).astype(f32)
    down_piece = (reduced[2].astype(f32) + lax.ppermute(reduced[2], "xl", SWAP).astype(f32)).astype(bf16)
    pieces = jnp.concatenate([(cube[0] + cube[1]).astype(bf16).transpose(1, 0, 2, 3), down_piece[None]]).reshape(12, STRIP, ff_part)
    home_send, pieces = lax.optimization_barrier((merge(dq, dkv_own, dkv_received), pieces))
    home = exchange(home_send, SEQ_AXES)
    home, block_out = lax.optimization_barrier((home, block_out))
    whole = lax.all_gather(pieces, SEQ_AXES, axis=0, tiled=False)
    gain_two_shard, gate_shard, up_shard, down_shard = unpack(whole, w_gate, w_up, gain_two)

    keep, give, grad_tokens = finish(own_id, home, hidden_low, normed_one, kv_full, query_full, grad_mid, cos_table, sin_table)
    grad_tokens = trade(grad_tokens)
    columns = keep.shape[-1]
    chip_sum = (keep.astype(f32) + over_core(give).astype(f32)).astype(bf16).reshape(2 * ctx, slab, columns)
    qkv_chips, grad_tokens = lax.optimization_barrier((exchange(chip_sum, CHIP_AXES), grad_tokens))
    qkv_sum = jnp.sum(qkv_chips.astype(f32), axis=0).astype(bf16)
    summed = jnp.concatenate([qkv_sum, out_sum], axis=1)
    final = exchange(jnp.broadcast_to(summed[None], (ctx,) + summed.shape), CTX_AXES)
    final, gate_shard = lax.optimization_barrier((final, gate_shard))
    gain_one_shard, query_shard, key_shard, value_shard, out_shard = last(final, kv_shard, query_shard, gain_one)
    return (
        block_out[None],
        grad_tokens.astype(f32)[None],
        gain_one_shard,
        query_shard,
        key_shard,
        value_shard,
        out_shard,
        gain_two_shard,
        gate_shard,
        up_shard,
        down_shard,
    )


def solution(mesh):
    fine = Mesh(mesh.devices.reshape(2, 4, 4, 2, 2), ("xl", "z", "y", "xh", "core"))
    rows = P(FSDP_AXES, CTX_AXES, None)
    gain = P(FSDP_AXES)
    weight = P(FSDP_AXES, None)
    return jax.shard_map(
        per_device,
        mesh=fine,
        in_specs=(rows, P(), gain, weight, weight, weight, weight, gain, weight, weight, weight, rows),
        out_specs=(rows, rows, gain, weight, weight, weight, weight, gain, weight, weight, weight),
        check_vma=False,
    )
```

```python
import functools
import math

import jax
import jax.numpy as jnp
from jax import lax
from jax.experimental import pallas as pl
from jax.experimental.pallas import tpu as pltpu
from jax.sharding import Mesh
from jax.sharding import PartitionSpec as P

HEADS = 15
KV_HEADS = 5
EPSILON = 1e-05
THETA = 100000.0
SEQ_AXES = ("z", "y")
CTX_AXES = ("xl", "z", "y")
CHIP_AXES = ("xh", "xl", "z", "y")
FSDP_AXES = ("xh", "core")
CUBE_AXES = ("xl", "xh", "core")
SWAP = ((0, 1), (1, 0))
STRIP = 16
BLK = 128
HEAD = 64
EXP_SCALE = math.log2(math.e) / 8.0
MASKED = -1e30


def attend_kernel(key_pos, query_rank, sorted_pos, sorted_id, q_ref, own_in, other_in, send_ref, out_ref, lse_ref, kv_ref, kvt_ref, ones_v, q_sorted, *, big, small, edge_size, blocks):
    groups, width = own_in.shape[0], HEAD
    rows = blocks * BLK
    is_key = lax.broadcasted_iota(jnp.int32, (BLK, 2 * width), 1) < width

    def place(index, _):
        for side, source in enumerate((own_in, other_in)):
            for half in range(2):
                where = pl.multiple_of(key_pos[side * 2 * groups + 2 * index + half] * BLK, BLK)
                piece = source[index, :, half * BLK:(half + 1) * BLK]
                kvt_ref[:, pl.ds(where, BLK)] = piece
                turned = piece.T
                kv_ref[pl.ds(where, BLK), :] = turned
                ones_v[pl.ds(where, BLK), :] = jnp.where(is_key, jnp.ones_like(turned), turned)
        for half in range(2):
            query = q_ref[index, :, half * BLK:(half + 1) * BLK]
            query = jnp.concatenate([query, jnp.zeros_like(query)], axis=0)
            q_sorted[pl.ds(pl.multiple_of(query_rank[2 * index + half] * BLK, BLK), BLK), :] = query.T
        return 0

    lax.fori_loop(0, groups, place, 0, unroll=4)

    def tile(index, _):
        low, high = sorted_pos[blocks * index], sorted_pos[blocks * index + blocks - 1]
        query = q_sorted[pl.ds(pl.multiple_of(index * rows, rows), rows), :]
        row = lax.broadcasted_iota(jnp.int32, (rows, 1), 0)
        place_of = row + low * BLK
        for part in range(1, blocks):
            place_of = jnp.where(row >= part * BLK, row + (sorted_pos[blocks * index + part] - part) * BLK, place_of)

        def step(start, carry, size, masked):
            top, total = carry
            scores = lax.dot_general(query, kv_ref[pl.ds(start, size), :], (((1,), (1,)), ((), ())), preferred_element_type=jnp.float32)
            if masked:
                column = start + lax.broadcasted_iota(jnp.int32, scores.shape, 1)
                scores = jnp.where(column <= place_of, scores, MASKED)
            new_top = jnp.maximum(top, jnp.max(scores, axis=1, keepdims=True))
            weights = jnp.exp2((scores - new_top) * EXP_SCALE).astype(jnp.bfloat16)
            factor = jnp.exp2((top - new_top) * EXP_SCALE)
            added = jnp.dot(weights, ones_v[pl.ds(start, size), :], preferred_element_type=jnp.float32)
            return new_top, total * factor + added

        def full(count, carry):
            for part in range(big // small):
                carry = step(pl.multiple_of(count * big + part * small, small), carry, small, False)
            return carry

        def edge(count, carry):
            return step(pl.multiple_of(count * edge_size, edge_size), carry, edge_size, True)

        carry = (jnp.full((rows, 1), MASKED, jnp.float32), jnp.zeros((rows, 2 * width), jnp.float32))
        done = low * BLK // big
        carry = lax.fori_loop(0, done, full, carry)
        top, total = lax.fori_loop(done * (big // edge_size), (high * BLK + BLK + edge_size - 1) // edge_size, edge, carry)
        lse = (top * EXP_SCALE + jnp.log2(total)).T
        total = total.T
        result = total[width:] / total[:1]
        for part in range(blocks):
            ident = sorted_id[blocks * index + part]
            piece = result[:, part * BLK:(part + 1) * BLK]
            out_ref[ident] = piece
            send_ref[ident // 2, :, pl.ds(pl.multiple_of(ident % 2 * BLK, BLK), BLK)] = piece.astype(jnp.bfloat16)
            lse_ref[ident] = lse[:8, part * BLK:(part + 1) * BLK]
        return 0

    lax.fori_loop(0, 2 * groups // blocks, tile, 0)


def attend(key_pos, query_rank, sorted_pos, sorted_id, q, own_in, other_in, big=1024, small=1024, edge_size=512, blocks=4):
    groups, width = own_in.shape[0], HEAD
    total = 4 * groups * BLK
    vm = pl.BlockSpec(memory_space=pltpu.VMEM)
    sm = pl.BlockSpec(memory_space=pltpu.SMEM)
    return pl.pallas_call(
        functools.partial(attend_kernel, big=big, small=small, edge_size=edge_size, blocks=blocks),
        out_shape=(
            jax.ShapeDtypeStruct((groups, width, 2 * BLK), jnp.bfloat16),
            jax.ShapeDtypeStruct((2 * groups, width, BLK), jnp.float32),
            jax.ShapeDtypeStruct((2 * groups, 8, BLK), jnp.float32),
            jax.ShapeDtypeStruct((total, 2 * width), jnp.bfloat16),
            jax.ShapeDtypeStruct((2 * width, total), jnp.bfloat16),
        ),
        in_specs=[sm] * 4 + [vm] * 3,
        out_specs=(vm,) * 5,
        scratch_shapes=[
            pltpu.VMEM((total, 2 * width), jnp.bfloat16),
            pltpu.VMEM((2 * groups * BLK, 2 * width), jnp.bfloat16),
        ],
        compiler_params=pltpu.CompilerParams(vmem_limit_bytes=48 * 2**20),
        cost_estimate=pl.CostEstimate(flops=40 * 10**9, bytes_accessed=10**7, transcendentals=2 * 10**7),
        name="attend",
    )(key_pos, query_rank, sorted_pos, sorted_id, q, own_in, other_in)


def back_kernel(key_pos, query_rank, sorted_pos, sorted_id, q_ref, da_ref, out_ref, lse_ref, kv_ref, kvt_ref, dq_ref, own_ref, other_ref, dkv, q_sorted, da_sorted, *, big, small, edge_size, flip):
    groups, width = q_ref.shape[0], HEAD

    def place(index, _):
        for half in range(2):
            rank = query_rank[2 * index + half]
            q_sorted[rank] = q_ref[index, :, half * BLK:(half + 1) * BLK]
            da_sorted[rank] = da_ref[index, :, half * BLK:(half + 1) * BLK]
        return 0

    lax.fori_loop(0, groups, place, 0)

    def clear(index, _):
        dkv[pl.ds(pl.multiple_of(index * BLK, BLK), BLK), :] = jnp.zeros((BLK, 2 * width), jnp.float32)
        return 0

    lax.fori_loop(0, 4 * groups, clear, 0)

    def tile(index, _):
        low, high = sorted_pos[2 * index], sorted_pos[2 * index + 1]
        first_id, second_id = sorted_id[2 * index], sorted_id[2 * index + 1]
        query = jnp.concatenate([q_sorted[2 * index], q_sorted[2 * index + 1]], axis=1)
        grad = jnp.concatenate([da_sorted[2 * index], da_sorted[2 * index + 1]], axis=1)
        value = jnp.concatenate([out_ref[first_id], out_ref[second_id]], axis=1)
        lse = jnp.concatenate([lse_ref[first_id][:1], lse_ref[second_id][:1]], axis=1)
        delta = jnp.sum(grad.astype(jnp.float32) * value, axis=0, keepdims=True)
        none = jnp.zeros_like(query)
        both = jnp.concatenate([jnp.concatenate([query, none], axis=1), jnp.concatenate([none, grad], axis=1)], axis=0)
        both_t = both.T
        lane = lax.broadcasted_iota(jnp.int32, (1, 2 * BLK), 1)
        place_of = jnp.where(lane < BLK, low * BLK + lane, (high - 1) * BLK + lane)

        def step(start, total, size, masked):
            keys = kv_ref[pl.ds(start, size), :]
            pair = jnp.dot(keys, both, preferred_element_type=jnp.float32)
            weights = jnp.exp2(pair[:, :2 * BLK] * EXP_SCALE - lse)
            if masked:
                row = start + lax.broadcasted_iota(jnp.int32, weights.shape, 0)
                weights = jnp.where(row <= place_of, weights, 0.0)
            grad_scores = (weights * (pair[:, 2 * BLK:] - delta)).astype(jnp.bfloat16)
            weights = weights.astype(jnp.bfloat16)
            dkv[pl.ds(start, size), :] += jnp.dot(jnp.concatenate([grad_scores, weights], axis=1), both_t, preferred_element_type=jnp.float32)
            if flip:
                return total + lax.dot_general(grad_scores, keys, (((0,), (0,)), ((), ())), preferred_element_type=jnp.float32)
            return total + jnp.dot(kvt_ref[:width, pl.ds(start, size)], grad_scores, preferred_element_type=jnp.float32)

        def full(count, carry):
            for part in range(big // small):
                carry = step(pl.multiple_of(count * big + part * small, small), carry, small, False)
            return carry

        def edge(count, carry):
            return step(pl.multiple_of(count * edge_size, edge_size), carry, edge_size, True)

        done = low * BLK // big
        total = jnp.zeros((2 * BLK, 2 * width) if flip else (width, 2 * BLK), jnp.float32)
        total = lax.fori_loop(0, done, full, total)
        total = lax.fori_loop(done * (big // edge_size), (high * BLK + BLK + edge_size - 1) // edge_size, edge, total) * 0.125
        if flip:
            total = total.T[:width]
        for half, ident in enumerate((first_id, second_id)):
            dq_ref[ident // 2, :, pl.ds(pl.multiple_of(ident % 2 * BLK, BLK), BLK)] = total[:, half * BLK:(half + 1) * BLK].astype(jnp.bfloat16)
        return 0

    lax.fori_loop(0, groups, tile, 0)
    factor = jnp.where(lax.broadcasted_iota(jnp.int32, (1, 2 * width), 1) < width, 0.125, 1.0)

    def spread(index, _):
        for side, target in enumerate((own_ref, other_ref)):
            for half in range(2):
                where = pl.multiple_of(key_pos[side * 2 * groups + 2 * index + half] * BLK, BLK)
                target[index, :, half * BLK:(half + 1) * BLK] = (dkv[pl.ds(where, BLK), :] * factor).astype(target.dtype)
        return 0

    lax.fori_loop(0, groups, spread, 0)


def attend_back(key_pos, query_rank, sorted_pos, sorted_id, q, da, out, lse, kv, kvt, big=1024, small=1024, edge_size=512, flip=False):
    groups, width = q.shape[0], HEAD
    total = 4 * groups * BLK
    vm = pl.BlockSpec(memory_space=pltpu.VMEM)
    sm = pl.BlockSpec(memory_space=pltpu.SMEM)
    return pl.pallas_call(
        functools.partial(back_kernel, big=big, small=small, edge_size=edge_size, flip=flip),
        out_shape=(
            jax.ShapeDtypeStruct((groups, width, 2 * BLK), jnp.bfloat16),
            jax.ShapeDtypeStruct((groups, 2 * width, 2 * BLK), jnp.float32),
            jax.ShapeDtypeStruct((groups, 2 * width, 2 * BLK), jnp.bfloat16),
        ),
        in_specs=[sm] * 4 + [vm] * 6,
        out_specs=(vm,) * 3,
        scratch_shapes=[
            pltpu.VMEM((total, 2 * width), jnp.float32),
            pltpu.VMEM((2 * groups, width, BLK), jnp.bfloat16),
            pltpu.VMEM((2 * groups, width, BLK), jnp.bfloat16),
        ],
        compiler_params=pltpu.CompilerParams(vmem_limit_bytes=48 * 2**20),
        cost_estimate=pl.CostEstimate(flops=60 * 10**9, bytes_accessed=10**7, transcendentals=2 * 10**7),
        name="attend_back",
    )(key_pos, query_rank, sorted_pos, sorted_id, q, da, out, lse, kv, kvt)


def in_vmem(kernel, out_shape, scalars, arrays, scratch=(), flops=10**9, name=None):
    vm = pl.BlockSpec(memory_space=pltpu.VMEM)
    return pl.pallas_call(
        kernel,
        out_shape=tuple(jax.ShapeDtypeStruct(shape, dtype) for shape, dtype in out_shape),
        in_specs=[pl.BlockSpec(memory_space=pltpu.SMEM)] * len(scalars) + [vm] * len(arrays),
        out_specs=(vm,) * len(out_shape),
        scratch_shapes=[pltpu.VMEM(shape, dtype) for shape, dtype in scratch],
        compiler_params=pltpu.CompilerParams(vmem_limit_bytes=48 * 2**20),
        cost_estimate=pl.CostEstimate(flops=flops, bytes_accessed=10**7, transcendentals=0),
        name=name,
    )(*scalars, *arrays)


def across(left, right):
    return lax.dot_general(left, right, (((1,), (1,)), ((), ())), preferred_element_type=jnp.float32)


def unit_rms(value):
    return lax.rsqrt(jnp.mean(value * value, axis=-1, keepdims=True) + EPSILON)


def put_rows(mine, pieces, target):
    shard = pieces[0].shape[0]
    for step, piece in enumerate(pieces):
        target[pl.ds(pl.multiple_of((mine[0] ^ step) * shard, 16), shard), :] = piece[...]


def turn(pair, cos, sin):
    half = HEAD // 2
    front, behind = pair[:half], pair[half:]
    return jnp.concatenate([front * cos - behind * sin, behind * cos + front * sin], axis=0).astype(jnp.bfloat16)


def turn_back(pair, cos, sin):
    return turn(pair, cos, -sin)


def project_keys_kernel(mine, x_ref, own, near, far, far_near, cos_ref, sin_ref, hat_ref, send_ref, w_ref):
    put_rows(mine, (own, near, far, far_near), w_ref)
    hidden = x_ref[...].astype(jnp.float32)
    hat = (hidden * unit_rms(hidden)).astype(jnp.bfloat16)
    hat_ref[...] = hat
    key_width = KV_HEADS * HEAD
    per = HEADS // KV_HEADS
    lin = jnp.dot(hat, w_ref[...], preferred_element_type=jnp.float32).T
    for head in range(KV_HEADS):
        key = turn(lin[head * HEAD:(head + 1) * HEAD], cos_ref[...], sin_ref[...])
        value = lin[key_width + head * HEAD:key_width + (head + 1) * HEAD].astype(jnp.bfloat16)
        for query in range(per):
            send_ref[head * per + query, :HEAD] = key
            send_ref[head * per + query, HEAD:] = value
    send_ref[HEADS:] = jnp.zeros((send_ref.shape[0] - HEADS,) + send_ref.shape[1:], jnp.bfloat16)


def project_keys(mine, x, pieces, cos, sin, groups):
    rows, width = x.shape
    columns = pieces[0].shape[1]
    return in_vmem(
        project_keys_kernel,
        ((x.shape, jnp.bfloat16), ((groups, 2 * HEAD, rows), jnp.bfloat16), ((width, columns), jnp.bfloat16)),
        (mine,),
        (x, *pieces, cos, sin),
        name="project_keys",
    )


def project_queries_kernel(mine, hat_ref, own, near, far, far_near, cos_ref, sin_ref, send_ref, w_ref):
    put_rows(mine, (own, near, far, far_near), w_ref)
    per = HEADS // KV_HEADS
    for group in range(KV_HEADS):
        columns = slice(group * per * HEAD, (group + 1) * per * HEAD)
        lin = jnp.dot(hat_ref[...], w_ref[:, columns], preferred_element_type=jnp.float32).T
        for query in range(per):
            send_ref[group * per + query] = turn(lin[query * HEAD:(query + 1) * HEAD], cos_ref[...], sin_ref[...])
    send_ref[HEADS:] = jnp.zeros((send_ref.shape[0] - HEADS,) + send_ref.shape[1:], jnp.bfloat16)


def project_queries(mine, hat, pieces, cos, sin, groups):
    rows, width = hat.shape
    columns = pieces[0].shape[1]
    return in_vmem(
        project_queries_kernel,
        (((groups, HEAD, rows), jnp.bfloat16), ((width, columns), jnp.bfloat16)),
        (mine,),
        (hat, *pieces, cos, sin),
        name="project_queries",
    )


def stack_rows_kernel(mine, own, near, far, far_near, out_ref):
    put_rows(mine, (own, near, far, far_near), out_ref)


def stack_rows(mine, pieces):
    shard, columns = pieces[0].shape
    return in_vmem(stack_rows_kernel, (((4 * shard, columns), jnp.bfloat16),), (mine,), pieces, flops=10**6, name="stack_rows")[0]


def finish_kernel(mine, dq_ref, home, x_ref, hat_ref, kv_ref, query_ref, mid_ref, cos_ref, sin_ref, keep_ref, give_ref, tokens_ref, turned, hat_t):
    shard = query_ref.shape[0] // 4
    cos, sin = cos_ref[...], sin_ref[...]
    key_width = KV_HEADS * HEAD
    per = HEADS // KV_HEADS

    for head in range(KV_HEADS):
        total = sum(home[head * per + query].astype(jnp.float32) for query in range(per))
        total = jnp.concatenate([total[:, :BLK].T, total[:, BLK:].T], axis=1)
        turned[head * HEAD:(head + 1) * HEAD, :] = turn_back(total[:HEAD], cos, sin)
        turned[key_width + head * HEAD:key_width + (head + 1) * HEAD, :] = total[HEAD:].astype(jnp.bfloat16)
        for query in range(per):
            start = 2 * key_width + (head * per + query) * HEAD
            turned[start:start + HEAD, :] = turn_back(dq_ref[head * per + query].astype(jnp.float32), cos, sin)
    hat_t[...] = hat_ref[...].T
    core = mine[0] & 1
    for target, at in ((keep_ref, core), (give_ref, 1 - core)):
        target[...] = jnp.zeros(target.shape, target.dtype)
        for part in range(2):
            rows = hat_t[pl.ds(pl.multiple_of((2 * part + at) * shard, 16), shard), :]
            grads = lax.dot_general(rows, turned[...], (((1,), (1,)), ((), ())), preferred_element_type=jnp.float32)
            target[part, :shard, : grads.shape[1]] = grads.astype(jnp.bfloat16)
    scaled = jnp.dot(kv_ref[...], turned[:2 * key_width, :], preferred_element_type=jnp.float32)
    scaled = (scaled + jnp.dot(query_ref[...], turned[2 * key_width:, :], preferred_element_type=jnp.float32)).T
    hidden = x_ref[...].astype(jnp.float32)
    tokens_ref[...] = (mid_ref[...] + norm_back(hidden, scaled)).astype(jnp.bfloat16)


def finish(mine, dq, home, x, hat, w_kv, w_query, mid, cos, sin):
    rows, width = x.shape
    columns = w_kv.shape[1] + w_query.shape[1]
    half = ((2, 256, -(-columns // BLK) * BLK), jnp.bfloat16)
    return in_vmem(
        finish_kernel,
        (half, half, (x.shape, jnp.bfloat16)),
        (mine,),
        (dq, home, x, hat, w_kv, w_query, mid, cos, sin),
        scratch=(((columns, rows), jnp.bfloat16), ((width, rows), jnp.bfloat16)),
        name="finish",
    )


def norm_back(value, grad):
    rms = unit_rms(value)
    hat = value * rms
    return rms * (grad - hat * jnp.mean(grad * hat, axis=-1, keepdims=True))


def out_kernel(attn, x_ref, w_ref, mid_ref, hat_ref):
    rows = attn[:HEADS].reshape(HEADS * HEAD, attn.shape[2]).T
    mid = x_ref[...].astype(jnp.float32) + jnp.dot(rows, w_ref[...], preferred_element_type=jnp.float32)
    mid_ref[...] = mid
    hat_ref[...] = (mid * unit_rms(mid)).astype(jnp.bfloat16)


def project_out(attn, x, w_out):
    return in_vmem(out_kernel, ((x.shape, jnp.float32), (x.shape, jnp.bfloat16)), (), (attn, x, w_out), name="project_out")


def stack_pairs_kernel(mine, own, near, far, far_near, gate_ref, up_ref):
    pieces = (own, near, far, far_near)
    put_rows(mine, [piece.at[0] for piece in pieces], gate_ref)
    put_rows(mine, [piece.at[1] for piece in pieces], up_ref)


def stack_pairs(mine, pieces):
    _, shard, columns = pieces[0].shape
    whole = ((4 * shard, columns), jnp.bfloat16)
    return in_vmem(stack_pairs_kernel, (whole, whole), (mine,), pieces, flops=10**6, name="stack_pairs")


def feed_kernel(hat_own, hat_peer, grad_own, grad_peer, w_gate, w_up, w_down, scaled_keep, scaled_send, out_keep, out_send, act_ref, gate_grad_ref, up_grad_ref):
    rows, width = hat_own.shape
    for step, (hat_ref, grad_ref) in enumerate(((hat_own, grad_own), (hat_peer, grad_peer))):
        here = slice(step * rows, (step + 1) * rows)
        hat = hat_ref[...]
        gate = jnp.dot(hat, w_gate[...], preferred_element_type=jnp.float32)
        up = jnp.dot(hat, w_up[...], preferred_element_type=jnp.float32)
        sigmoid = jax.nn.sigmoid(gate)
        silu = gate * sigmoid
        act = (silu * up).astype(jnp.bfloat16)
        act_ref[here, :] = act
        grad_act = across(grad_ref[...], w_down[...]).astype(jnp.bfloat16).astype(jnp.float32)
        gate_grad = (grad_act * up * sigmoid * (1.0 + gate * (1.0 - sigmoid))).astype(jnp.bfloat16)
        up_grad = (grad_act * silu).astype(jnp.bfloat16)
        gate_grad_ref[here, :] = gate_grad
        up_grad_ref[here, :] = up_grad
        scaled = across(gate_grad, w_gate[...]) + across(up_grad, w_up[...])
        out = jnp.dot(act, w_down[...], preferred_element_type=jnp.float32)
        if step:
            for target, value in ((scaled_send, scaled), (out_send, out)):
                target[:, :width] = value.astype(jnp.bfloat16)
                target[:, width:] = jnp.zeros((rows, target.shape[1] - width), jnp.bfloat16)
        else:
            scaled_keep[...] = scaled
            out_keep[...] = out


def feed(hats, grads, w_gate, w_up, w_down):
    rows, width = hats[0].shape
    kept = ((rows, width), jnp.float32)
    sent = ((rows, -(-width // 256) * 256), jnp.bfloat16)
    hidden = ((2 * rows, w_down.shape[0]), jnp.bfloat16)
    return in_vmem(feed_kernel, (kept, sent, kept, sent, hidden, hidden, hidden), (), (*hats, *grads, w_gate, w_up, w_down), flops=6 * 10**9, name="feed")


def feed_grads_kernel(*refs):
    hats, grads, near, far, (out_ref, hat_t, grad_t) = refs[:4], refs[4:8], refs[8:11], refs[11:14], refs[14:]
    rows = hats[0].shape[0]
    for step in range(4):
        here = slice(step * rows, (step + 1) * rows)
        hat_t[:, here] = hats[step][...].T
        grad_t[:, here] = grads[step][...].T
    shard = hat_t.shape[0] // 4
    strips = shard // STRIP
    for index, (left, at) in enumerate(((hat_t, 1), (hat_t, 2), (grad_t, 0))):
        for part in range(4):
            some = left[part * shard:(part + 1) * shard, :]
            product = jnp.dot(some[:, : 2 * rows], near[at][...], preferred_element_type=jnp.float32)
            product = product + jnp.dot(some[:, 2 * rows:], far[at][...], preferred_element_type=jnp.float32)
            out_ref[:strips, 4 * index + part] = product.astype(jnp.bfloat16).reshape(strips, STRIP, product.shape[1])
    out_ref[strips:] = jnp.zeros((out_ref.shape[0] - strips,) + out_ref.shape[1:], jnp.bfloat16)


def feed_grads(hats, grads, near, far, ring):
    rows, width = hats[0].shape
    turned = ((width, 4 * rows), jnp.bfloat16)
    return in_vmem(
        feed_grads_kernel,
        (((ring, 12, STRIP, near[0].shape[1]), jnp.bfloat16),),
        (),
        (*hats, *grads, *near, *far),
        scratch=(turned, turned),
        flops=8 * 10**9,
        name="feed_grads",
    )[0]


def mid_kernel(keep, received, far, mid_ref, grad_ref, w_ref, total_ref, low_ref, send_ref):
    scaled = keep[...] + received[:, : keep.shape[1]].astype(jnp.float32) + far[...].astype(jnp.float32)
    total = grad_ref[...].astype(jnp.float32) + norm_back(mid_ref[...], scaled)
    total_ref[...] = total
    low = total.astype(jnp.bfloat16)
    low_ref[...] = low
    send_ref[:HEADS] = across(w_ref[...], low).astype(jnp.bfloat16).reshape(HEADS, HEAD, low.shape[0])
    send_ref[HEADS:] = jnp.zeros((send_ref.shape[0] - HEADS,) + send_ref.shape[1:], jnp.bfloat16)


def mid_back(keep, received, far, mid, grad, w_out, groups):
    shape = mid.shape
    return in_vmem(
        mid_kernel,
        ((shape, jnp.float32), (shape, jnp.bfloat16), ((groups, HEAD, shape[0]), jnp.bfloat16)),
        (),
        (keep, received, far, mid, grad, w_out),
        name="mid_back",
    )


def out_grad_kernel(mine, attn, low, keep_ref, give_ref, rows_ref):
    width = low.shape[1]
    shard = width // 4
    rows_ref[...] = attn[:HEADS].reshape(HEADS * HEAD, attn.shape[2])
    core = mine[0] & 1
    for target, at in ((keep_ref, core), (give_ref, 1 - core)):
        target[...] = jnp.zeros(target.shape, target.dtype)
        for part in range(2):
            rows = rows_ref[pl.ds(pl.multiple_of((2 * part + at) * shard, 16), shard), :]
            target[part, :shard, :width] = jnp.dot(rows, low[...], preferred_element_type=jnp.float32).astype(target.dtype)


def out_grad(mine, attn, low):
    rows, width = low.shape
    shape = (2, 256, 1024)
    return in_vmem(
        out_grad_kernel, ((shape, jnp.bfloat16), (shape, jnp.bfloat16)), (mine,), (attn, low), scratch=(((width, rows), jnp.bfloat16),), name="out_grad"
    )


def pack_kernel(key_t, value_t, query, gain, kv_ref, query_ref):
    width = key_t.shape[0]
    scale = gain[...]
    for index, piece in enumerate((key_t, value_t)):
        kv_ref[:, index * width:(index + 1) * width] = (piece[...].astype(jnp.float32).T * scale).astype(jnp.bfloat16)
    query_ref[...] = (query[...].astype(jnp.float32) * scale).astype(jnp.bfloat16)


def pack(w_key, w_value, w_query, gain):
    shard = w_key.shape[0]
    return in_vmem(
        pack_kernel,
        (((shard, 2 * w_key.shape[1]), jnp.bfloat16), (w_query.shape, jnp.bfloat16)),
        (),
        (w_key.T, w_value.T, w_query, gain),
        flops=10**6,
        name="pack",
    )


def as_row(column):
    return jnp.broadcast_to(column, (column.shape[0], BLK)).T[:1]


def last_kernel(total, w_kv, w_query, gain, query_ref, key_ref, value_ref, out_ref, gain_ref):
    shard, width = w_query.shape
    key_width = key_ref.shape[0]
    columns = 2 * key_width + width
    padded = -(-columns // BLK) * BLK
    rows = total[...].reshape(total.shape[0] * total.shape[1], total.shape[2])[:shard].astype(jnp.float32)
    kv, query = rows[:, : 2 * key_width], rows[:, 2 * key_width : columns]
    scale = gain[...]
    gain_sum = jnp.sum(kv * w_kv[...].astype(jnp.float32), axis=1, keepdims=True) + jnp.sum(query * w_query[...].astype(jnp.float32), axis=1, keepdims=True)
    gain_ref[...] = as_row(gain_sum / scale)
    kv = kv * scale
    key_ref[...] = kv[:, :key_width].T
    value_ref[...] = kv[:, key_width:].T
    query_ref[...] = query * scale
    out_ref[...] = rows[:, padded:padded + width]


def last(total, w_kv, w_query, gain):
    shard, width = w_query.shape
    square = (w_query.shape, jnp.float32)
    turned = ((w_kv.shape[1] // 2, shard), jnp.float32)
    query, key, value, out, gain_grad = in_vmem(
        last_kernel, (square, turned, turned, square, ((1, shard), jnp.float32)), (), (total, w_kv, w_query, gain), name="last"
    )
    return gain_grad.reshape(shard), query, key.T, value.T, out


def unpack_kernel(total, w_gate, w_up, gain, gate_ref, up_ref, down_ref, gain_ref):
    shard, part = w_gate.shape[0], total.shape[3]
    strips = shard // STRIP
    scale = gain[...]
    gain_sum = jnp.zeros((shard, 1), jnp.float32)
    for index, (weight, target) in enumerate(((w_gate, gate_ref), (w_up, up_ref))):
        for step in range(4):
            columns = slice(step * part, (step + 1) * part)
            grads = total[:strips, 4 * index + step].reshape(shard, part).astype(jnp.float32)
            gain_sum = gain_sum + jnp.sum(grads * weight[:, columns].astype(jnp.float32), axis=1, keepdims=True)
            target[:, columns] = grads * scale
    for step in range(4):
        down_ref[step * shard:(step + 1) * shard, :] = total[:strips, 8 + step].reshape(shard, part).astype(jnp.float32)
    gain_ref[...] = as_row(gain_sum)


def unpack(total, w_gate, w_up, gain):
    shard, columns = w_gate.shape
    part = total.shape[3]
    full = ((shard, columns), jnp.float32)
    gate, up, down, gain_grad = in_vmem(
        unpack_kernel, (full, full, ((4 * shard, part), jnp.float32), ((1, shard), jnp.float32)), (), (total, w_gate, w_up, gain), name="unpack"
    )
    return gain_grad.reshape(shard), gate, up, down.T


def over_core(value):
    return lax.ppermute(value, "core", SWAP)


def over_chip(value):
    return lax.ppermute(value, "xh", SWAP)


def over_both(value):
    return lax.ppermute(value, FSDP_AXES, ((0, 3), (3, 0), (1, 2), (2, 1)))


def trade(value):
    return lax.ppermute(value, ("xl", "core"), ((0, 0), (1, 2), (2, 1), (3, 3)))


def arrange(pieces, xh, core):
    low = jnp.where(core == 1, pieces[1], pieces[0]), jnp.where(core == 1, pieces[0], pieces[1])
    high = jnp.where(core == 1, pieces[3], pieces[2]), jnp.where(core == 1, pieces[2], pieces[3])
    return jnp.stack([jnp.where(xh == 1, h, l) for l, h in zip(low, high)] + [jnp.where(xh == 1, l, h) for l, h in zip(low, high)])


def exchange(value, axes):
    return lax.all_to_all(value, axes, split_axis=0, concat_axis=0, tiled=True)


def per_device(
    tokens,
    block_order,
    gain_attn,
    w_query,
    w_key,
    w_value,
    w_out,
    gain_mlp,
    w_gate,
    w_up,
    w_down,
    cotangent,
):
    f32, bf16 = jnp.float32, jnp.bfloat16
    xh, core = lax.axis_index("xh"), lax.axis_index("core")
    mine = 2 * xh + core
    own_id = mine.reshape(1)
    row_total, width = tokens.shape[1:]
    shard = w_query.shape[0]
    ff_part = w_down.shape[0]
    groups = lax.axis_size(SEQ_AXES)
    key_width = KV_HEADS * HEAD
    gain_one = gain_attn.astype(f32)[:, None]
    gain_two = gain_mlp.astype(f32)[:, None]

    kv_shard, query_shard = pack(w_key, w_value, w_query, gain_one)
    far_kv, far_query = over_chip(kv_shard), over_chip(query_shard)
    near_kv, near_query = over_core(kv_shard), over_core(query_shard)
    hidden_low = trade(tokens[0])

    def gate_up(step):
        start = (mine ^ step) * ff_part
        both = [lax.dynamic_slice_in_dim(w, start, ff_part, 1).astype(f32) * gain_two for w in (w_gate, w_up)]
        return jnp.stack(both).astype(bf16)

    gate_up_parts = [gate_up(step) for step in range(4)]
    far_kv, hidden_low, gate_up_parts = lax.optimization_barrier((far_kv, hidden_low, gate_up_parts))

    own_order = lax.dynamic_slice_in_dim(block_order, 2 * groups * core, 2 * groups)
    other_order = lax.dynamic_slice_in_dim(block_order, 2 * groups * (1 - core), 2 * groups)
    key_pos = jnp.concatenate([own_order, other_order])
    query_rank = jnp.sum((own_order[None, :] < own_order[:, None]).astype(jnp.int32), axis=1)
    hit = query_rank[None, :] == jnp.arange(2 * groups, dtype=jnp.int32)[:, None]
    sorted_pos = jnp.sum(jnp.where(hit, own_order[None, :], 0), axis=1)
    sorted_id = jnp.sum(jnp.where(hit, jnp.arange(2 * groups, dtype=jnp.int32)[None, :], 0), axis=1)
    here = lax.axis_index(SEQ_AXES)
    own_blocks = lax.dynamic_slice_in_dim(own_order, 2 * here, 2)
    row = jnp.arange(row_total, dtype=jnp.int32)
    own_pos = jnp.where(row < BLK, own_blocks[0] * BLK + row, own_blocks[1] * BLK + row - BLK)
    inverse_freq = THETA ** (-jnp.arange(HEAD // 2, dtype=f32) / (HEAD // 2))
    angles = inverse_freq[:, None] * own_pos.astype(f32)[None, :]
    cos_table, sin_table = jnp.cos(angles), jnp.sin(angles)

    normed_one, kv_send, kv_full = project_keys(own_id, hidden_low, (kv_shard, near_kv, far_kv, over_core(far_kv)), cos_table, sin_table, groups)
    kv_send, far_query = lax.optimization_barrier((kv_send, far_query))
    kv_own, upstream = lax.optimization_barrier((exchange(kv_send, SEQ_AXES), trade(cotangent[0])))
    query_send, query_full = project_queries(own_id, normed_one, (query_shard, near_query, far_query, over_core(far_query)), cos_table, sin_table, groups)
    query_in = exchange(query_send, SEQ_AXES)
    kv_other = over_core(kv_own)

    query_in, w_out, upstream, gate_up_parts = lax.optimization_barrier((query_in, w_out, upstream, gate_up_parts))
    far_out, far_upstream = over_chip(w_out), over_chip(upstream)
    far_weights = over_chip(gate_up_parts[2]), over_both(gate_up_parts[3])
    out_send, out_blocks, lse, kv_sorted, kv_turned = attend(key_pos, query_rank, sorted_pos, sorted_id, query_in, kv_own, kv_other)
    out_send, far_out, far_upstream, far_weights = lax.optimization_barrier((out_send, far_out, far_upstream, far_weights))
    out_full = stack_rows(own_id, (w_out, over_core(w_out), far_out, over_core(far_out)))
    weights = (gate_up_parts[0], over_core(gate_up_parts[1])) + far_weights
    upstream_all = (upstream, over_core(upstream), far_upstream, over_core(far_upstream))

    attn = exchange(out_send, SEQ_AXES)
    mid_state, second_hat = project_out(attn, hidden_low, out_full)
    far_hat = over_chip(second_hat)
    near_hat = over_core(second_hat)
    gate_part, up_part = stack_pairs(own_id, weights)
    near_side = feed((second_hat, near_hat), upstream_all[:2], gate_part, up_part, w_down)
    far_hat, near_side = lax.optimization_barrier((far_hat, near_side))
    normed_all = second_hat, near_hat, far_hat, over_core(far_hat)
    far_side = feed(normed_all[2:], upstream_all[2:], gate_part, up_part, w_down)
    scaled_received = over_core(near_side[1])
    far_send = (far_side[0] + over_core(far_side[1])[:, :width].astype(f32)).astype(bf16)
    far_send, normed_all = lax.optimization_barrier((far_send, normed_all))
    scaled_far = over_chip(far_send)
    ring = lax.axis_size(SEQ_AXES)
    stacked = feed_grads(normed_all, upstream_all, near_side[4:], far_side[4:], ring)
    scaled_far, stacked = lax.optimization_barrier((scaled_far, stacked))
    reduced = lax.psum_scatter(stacked.reshape(ring, 12 * STRIP, ff_part), SEQ_AXES, scatter_dimension=0, tiled=True)[0]

    grad_mid, mid_low, grad_send = mid_back(near_side[0], scaled_received, scaled_far, mid_state, upstream, out_full, groups)
    grad_group = exchange(grad_send, SEQ_AXES)
    ctx = lax.axis_size(CTX_AXES)
    slab = 8
    out_grad_keep, out_grad_give = out_grad(own_id, attn, mid_low)
    out_chip = (out_grad_keep.astype(f32) + over_core(out_grad_give).astype(f32)).astype(bf16).reshape(2 * ctx, slab, -1)
    result_received = over_core(near_side[3])
    result_send = (far_side[2] + over_core(far_side[3])[:, :width].astype(f32)).astype(bf16)
    grad_group, result_send, out_chip = lax.optimization_barrier((grad_group, result_send, out_chip))

    out_chips = exchange(out_chip, CHIP_AXES)
    result_far = over_chip(result_send)

    dq, dkv_own, dkv_other = attend_back(key_pos, query_rank, sorted_pos, sorted_id, query_in, grad_group, out_blocks, lse, kv_sorted, kv_turned)
    dkv_other, reduced, out_chips, result_far = lax.optimization_barrier((dkv_other, reduced, out_chips, result_far))
    result = mid_state + near_side[2] + result_received[:, :width].astype(f32) + result_far.astype(f32)
    block_out = trade(result.astype(bf16))
    out_sum = jnp.sum(out_chips.astype(f32), axis=0).astype(bf16)
    dq_home = exchange(dq, SEQ_AXES)
    dkv_received = over_core(dkv_other)
    reduced = (reduced.astype(f32) + lax.ppermute(reduced, "xl", SWAP).astype(f32)).astype(bf16).reshape(3, 4, STRIP, ff_part)
    dkv, reduced = lax.optimization_barrier(((dkv_own + dkv_received.astype(f32)).astype(bf16), reduced))
    part = lambda step: lax.dynamic_index_in_dim(reduced[:2], mine ^ step, 1, keepdims=False)
    pieces = arrange([part(0), over_core(part(1)), over_chip(part(2)), over_both(part(3))], xh, core).transpose(1, 0, 2, 3)
    pieces = jnp.concatenate([pieces, reduced[2:]]).reshape(12, STRIP, ff_part)
    home, pieces = lax.optimization_barrier((exchange(dkv, SEQ_AXES), pieces))
    home, block_out = lax.optimization_barrier((home, block_out))
    whole = lax.all_gather(pieces, SEQ_AXES, axis=0, tiled=False)
    gain_two_shard, gate_shard, up_shard, down_shard = unpack(whole, w_gate, w_up, gain_two)

    keep, give, grad_tokens = finish(own_id, dq_home, home, hidden_low, normed_one, kv_full, query_full, grad_mid, cos_table, sin_table)
    grad_tokens = trade(grad_tokens)
    columns = keep.shape[-1]
    chip_sum = (keep.astype(f32) + over_core(give).astype(f32)).astype(bf16).reshape(2 * ctx, slab, columns)
    qkv_chips, grad_tokens = lax.optimization_barrier((exchange(chip_sum, CHIP_AXES), grad_tokens))
    qkv_sum = jnp.sum(qkv_chips.astype(f32), axis=0).astype(bf16)
    summed = jnp.concatenate([qkv_sum, out_sum], axis=1)
    final = exchange(jnp.broadcast_to(summed[None], (ctx,) + summed.shape), CTX_AXES)
    final, gate_shard = lax.optimization_barrier((final, gate_shard))
    gain_one_shard, query_shard, key_shard, value_shard, out_shard = last(final, kv_shard, query_shard, gain_one)
    return (
        block_out[None],
        grad_tokens.astype(f32)[None],
        gain_one_shard,
        query_shard,
        key_shard,
        value_shard,
        out_shard,
        gain_two_shard,
        gate_shard,
        up_shard,
        down_shard,
    )


def solution(mesh):
    fine = Mesh(mesh.devices.reshape(2, 4, 4, 2, 2), ("xl", "z", "y", "xh", "core"))
    rows = P(FSDP_AXES, CTX_AXES, None)
    gain = P(FSDP_AXES)
    weight = P(FSDP_AXES, None)
    return jax.shard_map(
        per_device,
        mesh=fine,
        in_specs=(rows, P(), gain, weight, weight, weight, weight, gain, weight, weight, weight, rows),
        out_specs=(rows, rows, gain, weight, weight, weight, weight, gain, weight, weight, weight),
        check_vma=False,
    )
```

```python
import functools
import math

import jax
import jax.numpy as jnp
from jax import lax
from jax.experimental import pallas as pl
from jax.experimental.pallas import tpu as pltpu
from jax.sharding import Mesh
from jax.sharding import PartitionSpec as P

HEADS = 15
KV_HEADS = 5
EPSILON = 1e-05
THETA = 100000.0
SEQ_AXES = ("z", "y")
CTX_AXES = ("xl", "z", "y")
CHIP_AXES = ("xh", "xl", "z", "y")
FSDP_AXES = ("xh", "core")
CUBE_AXES = ("xl", "xh", "core")
SWAP = ((0, 1), (1, 0))
STRIP = 16
BLK = 128
HEAD = 64
EXP_SCALE = math.log2(math.e) / 8.0
MASKED = -1e30


def attend_kernel(key_pos, query_rank, sorted_pos, sorted_id, q_ref, own_in, other_in, send_ref, out_ref, lse_ref, kv_ref, kvt_ref, ones_v, q_sorted, *, big, small, edge_size, blocks):
    groups, width = own_in.shape[0], HEAD
    rows = blocks * BLK
    is_key = lax.broadcasted_iota(jnp.int32, (BLK, 2 * width), 1) < width

    def place(index, _):
        for side, source in enumerate((own_in, other_in)):
            for half in range(2):
                where = pl.multiple_of(key_pos[side * 2 * groups + 2 * index + half] * BLK, BLK)
                piece = source[index, :, half * BLK:(half + 1) * BLK]
                kvt_ref[:, pl.ds(where, BLK)] = piece
                turned = piece.T
                kv_ref[pl.ds(where, BLK), :] = turned
                ones_v[pl.ds(where, BLK), :] = jnp.where(is_key, jnp.ones_like(turned), turned)
        for half in range(2):
            query = q_ref[index, :, half * BLK:(half + 1) * BLK]
            query = jnp.concatenate([query, jnp.zeros_like(query)], axis=0)
            q_sorted[pl.ds(pl.multiple_of(query_rank[2 * index + half] * BLK, BLK), BLK), :] = query.T
        return 0

    lax.fori_loop(0, groups, place, 0, unroll=4)

    def tile(index, _):
        low, high = sorted_pos[blocks * index], sorted_pos[blocks * index + blocks - 1]
        query = q_sorted[pl.ds(pl.multiple_of(index * rows, rows), rows), :]
        row = lax.broadcasted_iota(jnp.int32, (rows, 1), 0)
        place_of = row + low * BLK
        for part in range(1, blocks):
            place_of = jnp.where(row >= part * BLK, row + (sorted_pos[blocks * index + part] - part) * BLK, place_of)

        def step(start, carry, size, masked):
            top, total = carry
            scores = lax.dot_general(query, kv_ref[pl.ds(start, size), :], (((1,), (1,)), ((), ())), preferred_element_type=jnp.float32)
            if masked:
                column = start + lax.broadcasted_iota(jnp.int32, scores.shape, 1)
                scores = jnp.where(column <= place_of, scores, MASKED)
            new_top = jnp.maximum(top, jnp.max(scores, axis=1, keepdims=True))
            weights = jnp.exp2((scores - new_top) * EXP_SCALE).astype(jnp.bfloat16)
            factor = jnp.exp2((top - new_top) * EXP_SCALE)
            added = jnp.dot(weights, ones_v[pl.ds(start, size), :], preferred_element_type=jnp.float32)
            return new_top, total * factor + added

        def full(count, carry):
            for part in range(big // small):
                carry = step(pl.multiple_of(count * big + part * small, small), carry, small, False)
            return carry

        def edge(count, carry):
            return step(pl.multiple_of(count * edge_size, edge_size), carry, edge_size, True)

        carry = (jnp.full((rows, 1), MASKED, jnp.float32), jnp.zeros((rows, 2 * width), jnp.float32))
        done = low * BLK // big
        carry = lax.fori_loop(0, done, full, carry)
        top, total = lax.fori_loop(done * (big // edge_size), (high * BLK + BLK + edge_size - 1) // edge_size, edge, carry)
        lse = (top * EXP_SCALE + jnp.log2(total)).T
        total = total.T
        result = total[width:] / total[:1]
        for part in range(blocks):
            ident = sorted_id[blocks * index + part]
            piece = result[:, part * BLK:(part + 1) * BLK]
            out_ref[ident] = piece
            send_ref[ident // 2, :, pl.ds(pl.multiple_of(ident % 2 * BLK, BLK), BLK)] = piece.astype(jnp.bfloat16)
            lse_ref[ident] = lse[:8, part * BLK:(part + 1) * BLK]
        return 0

    lax.fori_loop(0, 2 * groups // blocks, tile, 0)


def attend(key_pos, query_rank, sorted_pos, sorted_id, q, own_in, other_in, big=1024, small=1024, edge_size=512, blocks=4):
    groups, width = own_in.shape[0], HEAD
    total = 4 * groups * BLK
    vm = pl.BlockSpec(memory_space=pltpu.VMEM)
    sm = pl.BlockSpec(memory_space=pltpu.SMEM)
    return pl.pallas_call(
        functools.partial(attend_kernel, big=big, small=small, edge_size=edge_size, blocks=blocks),
        out_shape=(
            jax.ShapeDtypeStruct((groups, width, 2 * BLK), jnp.bfloat16),
            jax.ShapeDtypeStruct((2 * groups, width, BLK), jnp.float32),
            jax.ShapeDtypeStruct((2 * groups, 8, BLK), jnp.float32),
            jax.ShapeDtypeStruct((total, 2 * width), jnp.bfloat16),
            jax.ShapeDtypeStruct((2 * width, total), jnp.bfloat16),
        ),
        in_specs=[sm] * 4 + [vm] * 3,
        out_specs=(vm,) * 5,
        scratch_shapes=[
            pltpu.VMEM((total, 2 * width), jnp.bfloat16),
            pltpu.VMEM((2 * groups * BLK, 2 * width), jnp.bfloat16),
        ],
        compiler_params=pltpu.CompilerParams(vmem_limit_bytes=48 * 2**20),
        cost_estimate=pl.CostEstimate(flops=40 * 10**9, bytes_accessed=10**7, transcendentals=2 * 10**7),
        name="attend",
    )(key_pos, query_rank, sorted_pos, sorted_id, q, own_in, other_in)


def back_kernel(key_pos, query_rank, sorted_pos, sorted_id, q_ref, da_ref, out_ref, lse_ref, kv_ref, kvt_ref, dq_ref, own_ref, other_ref, dkv, q_sorted, da_sorted, *, big, small, edge_size, flip):
    groups, width = q_ref.shape[0], HEAD

    def place(index, _):
        for half in range(2):
            rank = query_rank[2 * index + half]
            q_sorted[rank] = q_ref[index, :, half * BLK:(half + 1) * BLK]
            da_sorted[rank] = da_ref[index, :, half * BLK:(half + 1) * BLK]
        return 0

    lax.fori_loop(0, groups, place, 0)

    def clear(index, _):
        dkv[pl.ds(pl.multiple_of(index * BLK, BLK), BLK), :] = jnp.zeros((BLK, 2 * width), jnp.float32)
        return 0

    lax.fori_loop(0, 4 * groups, clear, 0)

    def tile(index, _):
        low, high = sorted_pos[2 * index], sorted_pos[2 * index + 1]
        first_id, second_id = sorted_id[2 * index], sorted_id[2 * index + 1]
        query = jnp.concatenate([q_sorted[2 * index], q_sorted[2 * index + 1]], axis=1)
        grad = jnp.concatenate([da_sorted[2 * index], da_sorted[2 * index + 1]], axis=1)
        value = jnp.concatenate([out_ref[first_id], out_ref[second_id]], axis=1)
        lse = jnp.concatenate([lse_ref[first_id][:1], lse_ref[second_id][:1]], axis=1)
        delta = jnp.sum(grad.astype(jnp.float32) * value, axis=0, keepdims=True)
        none = jnp.zeros_like(query)
        both = jnp.concatenate([jnp.concatenate([query, none], axis=1), jnp.concatenate([none, grad], axis=1)], axis=0)
        both_t = both.T
        lane = lax.broadcasted_iota(jnp.int32, (1, 2 * BLK), 1)
        place_of = jnp.where(lane < BLK, low * BLK + lane, (high - 1) * BLK + lane)

        def step(start, total, size, masked):
            keys = kv_ref[pl.ds(start, size), :]
            pair = jnp.dot(keys, both, preferred_element_type=jnp.float32)
            weights = jnp.exp2(pair[:, :2 * BLK] * EXP_SCALE - lse)
            if masked:
                row = start + lax.broadcasted_iota(jnp.int32, weights.shape, 0)
                weights = jnp.where(row <= place_of, weights, 0.0)
            grad_scores = (weights * (pair[:, 2 * BLK:] - delta)).astype(jnp.bfloat16)
            weights = weights.astype(jnp.bfloat16)
            dkv[pl.ds(start, size), :] += jnp.dot(jnp.concatenate([grad_scores, weights], axis=1), both_t, preferred_element_type=jnp.float32)
            if flip:
                return total + lax.dot_general(grad_scores, keys, (((0,), (0,)), ((), ())), preferred_element_type=jnp.float32)
            return total + jnp.dot(kvt_ref[:width, pl.ds(start, size)], grad_scores, preferred_element_type=jnp.float32)

        def full(count, carry):
            for part in range(big // small):
                carry = step(pl.multiple_of(count * big + part * small, small), carry, small, False)
            return carry

        def edge(count, carry):
            return step(pl.multiple_of(count * edge_size, edge_size), carry, edge_size, True)

        done = low * BLK // big
        total = jnp.zeros((2 * BLK, 2 * width) if flip else (width, 2 * BLK), jnp.float32)
        total = lax.fori_loop(0, done, full, total)
        total = lax.fori_loop(done * (big // edge_size), (high * BLK + BLK + edge_size - 1) // edge_size, edge, total) * 0.125
        if flip:
            total = total.T[:width]
        for half, ident in enumerate((first_id, second_id)):
            dq_ref[ident // 2, :, pl.ds(pl.multiple_of(ident % 2 * BLK, BLK), BLK)] = total[:, half * BLK:(half + 1) * BLK].astype(jnp.bfloat16)
        return 0

    lax.fori_loop(0, groups, tile, 0)
    factor = jnp.where(lax.broadcasted_iota(jnp.int32, (1, 2 * width), 1) < width, 0.125, 1.0)

    def spread(index, _):
        for side, target in enumerate((own_ref, other_ref)):
            for half in range(2):
                where = pl.multiple_of(key_pos[side * 2 * groups + 2 * index + half] * BLK, BLK)
                target[index, :, half * BLK:(half + 1) * BLK] = (dkv[pl.ds(where, BLK), :] * factor).astype(target.dtype)
        return 0

    lax.fori_loop(0, groups, spread, 0)


def attend_back(key_pos, query_rank, sorted_pos, sorted_id, q, da, out, lse, kv, kvt, big=1024, small=1024, edge_size=512, flip=False):
    groups, width = q.shape[0], HEAD
    total = 4 * groups * BLK
    vm = pl.BlockSpec(memory_space=pltpu.VMEM)
    sm = pl.BlockSpec(memory_space=pltpu.SMEM)
    return pl.pallas_call(
        functools.partial(back_kernel, big=big, small=small, edge_size=edge_size, flip=flip),
        out_shape=(
            jax.ShapeDtypeStruct((groups, width, 2 * BLK), jnp.bfloat16),
            jax.ShapeDtypeStruct((groups, 2 * width, 2 * BLK), jnp.float32),
            jax.ShapeDtypeStruct((groups, 2 * width, 2 * BLK), jnp.bfloat16),
        ),
        in_specs=[sm] * 4 + [vm] * 6,
        out_specs=(vm,) * 3,
        scratch_shapes=[
            pltpu.VMEM((total, 2 * width), jnp.float32),
            pltpu.VMEM((2 * groups, width, BLK), jnp.bfloat16),
            pltpu.VMEM((2 * groups, width, BLK), jnp.bfloat16),
        ],
        compiler_params=pltpu.CompilerParams(vmem_limit_bytes=48 * 2**20),
        cost_estimate=pl.CostEstimate(flops=60 * 10**9, bytes_accessed=10**7, transcendentals=2 * 10**7),
        name="attend_back",
    )(key_pos, query_rank, sorted_pos, sorted_id, q, da, out, lse, kv, kvt)


def in_vmem(kernel, out_shape, scalars, arrays, scratch=(), flops=10**9, name=None):
    vm = pl.BlockSpec(memory_space=pltpu.VMEM)
    return pl.pallas_call(
        kernel,
        out_shape=tuple(jax.ShapeDtypeStruct(shape, dtype) for shape, dtype in out_shape),
        in_specs=[pl.BlockSpec(memory_space=pltpu.SMEM)] * len(scalars) + [vm] * len(arrays),
        out_specs=(vm,) * len(out_shape),
        scratch_shapes=[pltpu.VMEM(shape, dtype) for shape, dtype in scratch],
        compiler_params=pltpu.CompilerParams(vmem_limit_bytes=48 * 2**20),
        cost_estimate=pl.CostEstimate(flops=flops, bytes_accessed=10**7, transcendentals=0),
        name=name,
    )(*scalars, *arrays)


def across(left, right):
    return lax.dot_general(left, right, (((1,), (1,)), ((), ())), preferred_element_type=jnp.float32)


def unit_rms(value):
    return lax.rsqrt(jnp.mean(value * value, axis=-1, keepdims=True) + EPSILON)


def put_rows(mine, pieces, target):
    shard = pieces[0].shape[0]
    for step, piece in enumerate(pieces):
        target[pl.ds(pl.multiple_of((mine[0] ^ step) * shard, 16), shard), :] = piece[...]


def turn(pair, cos, sin):
    half = HEAD // 2
    front, behind = pair[:half], pair[half:]
    return jnp.concatenate([front * cos - behind * sin, behind * cos + front * sin], axis=0).astype(jnp.bfloat16)


def turn_back(pair, cos, sin):
    return turn(pair, cos, -sin)


def project_keys_kernel(mine, x_ref, own, near, far, far_near, cos_ref, sin_ref, hat_ref, send_ref, w_ref):
    put_rows(mine, (own, near, far, far_near), w_ref)
    hidden = x_ref[...].astype(jnp.float32)
    hat = (hidden * unit_rms(hidden)).astype(jnp.bfloat16)
    hat_ref[...] = hat
    key_width = KV_HEADS * HEAD
    per = HEADS // KV_HEADS
    lin = jnp.dot(hat, w_ref[...], preferred_element_type=jnp.float32).T
    for head in range(KV_HEADS):
        key = turn(lin[head * HEAD:(head + 1) * HEAD], cos_ref[...], sin_ref[...])
        value = lin[key_width + head * HEAD:key_width + (head + 1) * HEAD].astype(jnp.bfloat16)
        for query in range(per):
            send_ref[head * per + query, :HEAD] = key
            send_ref[head * per + query, HEAD:] = value
    send_ref[HEADS:] = jnp.zeros((send_ref.shape[0] - HEADS,) + send_ref.shape[1:], jnp.bfloat16)


def project_keys(mine, x, pieces, cos, sin, groups):
    rows, width = x.shape
    columns = pieces[0].shape[1]
    return in_vmem(
        project_keys_kernel,
        ((x.shape, jnp.bfloat16), ((groups, 2 * HEAD, rows), jnp.bfloat16), ((width, columns), jnp.bfloat16)),
        (mine,),
        (x, *pieces, cos, sin),
        name="project_keys",
    )


def project_queries_kernel(mine, hat_ref, own, near, far, far_near, cos_ref, sin_ref, send_ref, w_ref):
    put_rows(mine, (own, near, far, far_near), w_ref)
    per = HEADS // KV_HEADS
    for group in range(KV_HEADS):
        columns = slice(group * per * HEAD, (group + 1) * per * HEAD)
        lin = jnp.dot(hat_ref[...], w_ref[:, columns], preferred_element_type=jnp.float32).T
        for query in range(per):
            send_ref[group * per + query] = turn(lin[query * HEAD:(query + 1) * HEAD], cos_ref[...], sin_ref[...])
    send_ref[HEADS:] = jnp.zeros((send_ref.shape[0] - HEADS,) + send_ref.shape[1:], jnp.bfloat16)


def project_queries(mine, hat, pieces, cos, sin, groups):
    rows, width = hat.shape
    columns = pieces[0].shape[1]
    return in_vmem(
        project_queries_kernel,
        (((groups, HEAD, rows), jnp.bfloat16), ((width, columns), jnp.bfloat16)),
        (mine,),
        (hat, *pieces, cos, sin),
        name="project_queries",
    )


def stack_rows_kernel(mine, own, near, far, far_near, out_ref):
    put_rows(mine, (own, near, far, far_near), out_ref)


def stack_rows(mine, pieces):
    shard, columns = pieces[0].shape
    return in_vmem(stack_rows_kernel, (((4 * shard, columns), jnp.bfloat16),), (mine,), pieces, flops=10**6, name="stack_rows")[0]


def finish_kernel(mine, dq_ref, home, x_ref, hat_ref, kv_ref, query_ref, mid_ref, cos_ref, sin_ref, keep_ref, give_ref, tokens_ref, turned, hat_t):
    shard = query_ref.shape[0] // 4
    cos, sin = cos_ref[...], sin_ref[...]
    key_width = KV_HEADS * HEAD
    per = HEADS // KV_HEADS

    for head in range(KV_HEADS):
        total = sum(home[head * per + query].astype(jnp.float32) for query in range(per))
        total = jnp.concatenate([total[:, :BLK].T, total[:, BLK:].T], axis=1)
        turned[head * HEAD:(head + 1) * HEAD, :] = turn_back(total[:HEAD], cos, sin)
        turned[key_width + head * HEAD:key_width + (head + 1) * HEAD, :] = total[HEAD:].astype(jnp.bfloat16)
        for query in range(per):
            start = 2 * key_width + (head * per + query) * HEAD
            turned[start:start + HEAD, :] = turn_back(dq_ref[head * per + query].astype(jnp.float32), cos, sin)
    hat_t[...] = hat_ref[...].T
    core = mine[0] & 1
    for target, at in ((keep_ref, core), (give_ref, 1 - core)):
        target[...] = jnp.zeros(target.shape, target.dtype)
        for part in range(2):
            rows = hat_t[pl.ds(pl.multiple_of((2 * part + at) * shard, 16), shard), :]
            grads = lax.dot_general(rows, turned[...], (((1,), (1,)), ((), ())), preferred_element_type=jnp.float32)
            target[part, :shard, : grads.shape[1]] = grads.astype(jnp.bfloat16)
    scaled = jnp.dot(kv_ref[...], turned[:2 * key_width, :], preferred_element_type=jnp.float32)
    scaled = (scaled + jnp.dot(query_ref[...], turned[2 * key_width:, :], preferred_element_type=jnp.float32)).T
    hidden = x_ref[...].astype(jnp.float32)
    tokens_ref[...] = (mid_ref[...] + norm_back(hidden, scaled)).astype(jnp.bfloat16)


def finish(mine, dq, home, x, hat, w_kv, w_query, mid, cos, sin):
    rows, width = x.shape
    columns = w_kv.shape[1] + w_query.shape[1]
    half = ((2, 256, -(-columns // BLK) * BLK), jnp.bfloat16)
    return in_vmem(
        finish_kernel,
        (half, half, (x.shape, jnp.bfloat16)),
        (mine,),
        (dq, home, x, hat, w_kv, w_query, mid, cos, sin),
        scratch=(((columns, rows), jnp.bfloat16), ((width, rows), jnp.bfloat16)),
        name="finish",
    )


def norm_back(value, grad):
    rms = unit_rms(value)
    hat = value * rms
    return rms * (grad - hat * jnp.mean(grad * hat, axis=-1, keepdims=True))


def out_kernel(attn, x_ref, w_ref, mid_ref, hat_ref):
    rows = attn[:HEADS].reshape(HEADS * HEAD, attn.shape[2]).T
    mid = x_ref[...].astype(jnp.float32) + jnp.dot(rows, w_ref[...], preferred_element_type=jnp.float32)
    mid_ref[...] = mid
    hat_ref[...] = (mid * unit_rms(mid)).astype(jnp.bfloat16)


def project_out(attn, x, w_out):
    return in_vmem(out_kernel, ((x.shape, jnp.float32), (x.shape, jnp.bfloat16)), (), (attn, x, w_out), name="project_out")


def stack_pairs_kernel(mine, own, near, far, far_near, gate_ref, up_ref):
    pieces = (own, near, far, far_near)
    put_rows(mine, [piece.at[0] for piece in pieces], gate_ref)
    put_rows(mine, [piece.at[1] for piece in pieces], up_ref)


def stack_pairs(mine, pieces):
    _, shard, columns = pieces[0].shape
    whole = ((4 * shard, columns), jnp.bfloat16)
    return in_vmem(stack_pairs_kernel, (whole, whole), (mine,), pieces, flops=10**6, name="stack_pairs")


def feed_kernel(hat_own, hat_peer, grad_own, grad_peer, w_gate, w_up, down_t, scaled_keep, scaled_send, out_keep, out_send, act_ref, gate_grad_ref, up_grad_ref, hat_ref, grad_ref):
    rows, width = hat_own.shape
    for step, (hat, grad) in enumerate(((hat_own, grad_own), (hat_peer, grad_peer))):
        hat_ref[step * rows:(step + 1) * rows, :] = hat[...]
        grad_ref[step * rows:(step + 1) * rows, :] = grad[...]
    gate = jnp.dot(hat_ref[...], w_gate[...], preferred_element_type=jnp.float32)
    up = jnp.dot(hat_ref[...], w_up[...], preferred_element_type=jnp.float32)
    sigmoid = jax.nn.sigmoid(gate)
    silu = gate * sigmoid
    act_ref[...] = (silu * up).astype(jnp.bfloat16)
    grad_act = jnp.dot(grad_ref[...], down_t[...], preferred_element_type=jnp.float32).astype(jnp.bfloat16).astype(jnp.float32)
    gate_grad_ref[...] = (grad_act * up * sigmoid * (1.0 + gate * (1.0 - sigmoid))).astype(jnp.bfloat16)
    up_grad_ref[...] = (grad_act * silu).astype(jnp.bfloat16)
    scaled = across(gate_grad_ref[...], w_gate[...]) + across(up_grad_ref[...], w_up[...])
    out = across(act_ref[...], down_t[...])
    scaled_keep[...] = scaled[:rows]
    out_keep[...] = out[:rows]
    for target, value in ((scaled_send, scaled), (out_send, out)):
        target[:, :width] = value[rows:].astype(jnp.bfloat16)
        target[:, width:] = jnp.zeros((rows, target.shape[1] - width), jnp.bfloat16)


def feed(hats, grads, w_gate, w_up, down_t):
    rows, width = hats[0].shape
    kept = ((rows, width), jnp.float32)
    sent = ((rows, -(-width // 256) * 256), jnp.bfloat16)
    hidden = ((2 * rows, down_t.shape[1]), jnp.bfloat16)
    both = ((2 * rows, width), jnp.bfloat16)
    return in_vmem(
        feed_kernel,
        (kept, sent, kept, sent, hidden, hidden, hidden),
        (),
        (*hats, *grads, w_gate, w_up, down_t),
        scratch=(both, both),
        flops=6 * 10**9,
        name="feed",
    )


def feed_grads_kernel(*refs):
    hats, grads, near, far, (out_ref, hat_t, grad_t) = refs[:4], refs[4:8], refs[8:11], refs[11:14], refs[14:]
    rows = hats[0].shape[0]
    for step in range(4):
        here = slice(step * rows, (step + 1) * rows)
        hat_t[:, here] = hats[step][...].T
        grad_t[:, here] = grads[step][...].T
    shard = hat_t.shape[0] // 4
    strips = shard // STRIP
    for index, (left, at) in enumerate(((hat_t, 1), (hat_t, 2), (grad_t, 0))):
        for part in range(4):
            some = left[part * shard:(part + 1) * shard, :]
            product = jnp.dot(some[:, : 2 * rows], near[at][...], preferred_element_type=jnp.float32)
            product = product + jnp.dot(some[:, 2 * rows:], far[at][...], preferred_element_type=jnp.float32)
            out_ref[:strips, 4 * index + part] = product.astype(jnp.bfloat16).reshape(strips, STRIP, product.shape[1])
    out_ref[strips:] = jnp.zeros((out_ref.shape[0] - strips,) + out_ref.shape[1:], jnp.bfloat16)


def feed_grads(hats, grads, near, far, ring):
    rows, width = hats[0].shape
    turned = ((width, 4 * rows), jnp.bfloat16)
    return in_vmem(
        feed_grads_kernel,
        (((ring, 12, STRIP, near[0].shape[1]), jnp.bfloat16),),
        (),
        (*hats, *grads, *near, *far),
        scratch=(turned, turned),
        flops=8 * 10**9,
        name="feed_grads",
    )[0]


def mid_kernel(keep, received, far, mid_ref, grad_ref, w_ref, total_ref, low_ref, send_ref):
    scaled = keep[...] + received[:, : keep.shape[1]].astype(jnp.float32) + far[...].astype(jnp.float32)
    total = grad_ref[...].astype(jnp.float32) + norm_back(mid_ref[...], scaled)
    total_ref[...] = total
    low = total.astype(jnp.bfloat16)
    low_ref[...] = low
    send_ref[:HEADS] = across(w_ref[...], low).astype(jnp.bfloat16).reshape(HEADS, HEAD, low.shape[0])
    send_ref[HEADS:] = jnp.zeros((send_ref.shape[0] - HEADS,) + send_ref.shape[1:], jnp.bfloat16)


def mid_back(keep, received, far, mid, grad, w_out, groups):
    shape = mid.shape
    return in_vmem(
        mid_kernel,
        ((shape, jnp.float32), (shape, jnp.bfloat16), ((groups, HEAD, shape[0]), jnp.bfloat16)),
        (),
        (keep, received, far, mid, grad, w_out),
        name="mid_back",
    )


def out_grad_kernel(mine, attn, low, keep_ref, give_ref, rows_ref):
    width = low.shape[1]
    shard = width // 4
    rows_ref[...] = attn[:HEADS].reshape(HEADS * HEAD, attn.shape[2])
    core = mine[0] & 1
    for target, at in ((keep_ref, core), (give_ref, 1 - core)):
        target[...] = jnp.zeros(target.shape, target.dtype)
        for part in range(2):
            rows = rows_ref[pl.ds(pl.multiple_of((2 * part + at) * shard, 16), shard), :]
            target[part, :shard, :width] = jnp.dot(rows, low[...], preferred_element_type=jnp.float32).astype(target.dtype)


def out_grad(mine, attn, low):
    rows, width = low.shape
    shape = (2, 256, 1024)
    return in_vmem(
        out_grad_kernel, ((shape, jnp.bfloat16), (shape, jnp.bfloat16)), (mine,), (attn, low), scratch=(((width, rows), jnp.bfloat16),), name="out_grad"
    )


def pack_kernel(key_t, value_t, query, gain, kv_ref, query_ref):
    width = key_t.shape[0]
    scale = gain[...]
    for index, piece in enumerate((key_t, value_t)):
        kv_ref[:, index * width:(index + 1) * width] = (piece[...].astype(jnp.float32).T * scale).astype(jnp.bfloat16)
    query_ref[...] = (query[...].astype(jnp.float32) * scale).astype(jnp.bfloat16)


def pack(w_key, w_value, w_query, gain):
    shard = w_key.shape[0]
    return in_vmem(
        pack_kernel,
        (((shard, 2 * w_key.shape[1]), jnp.bfloat16), (w_query.shape, jnp.bfloat16)),
        (),
        (w_key.T, w_value.T, w_query, gain),
        flops=10**6,
        name="pack",
    )


def as_row(column):
    return jnp.broadcast_to(column, (column.shape[0], BLK)).T[:1]


def last_kernel(total, w_kv, w_query, gain, query_ref, key_ref, value_ref, out_ref, gain_ref):
    shard, width = w_query.shape
    key_width = key_ref.shape[0]
    columns = 2 * key_width + width
    padded = -(-columns // BLK) * BLK
    rows = total[...].reshape(total.shape[0] * total.shape[1], total.shape[2])[:shard].astype(jnp.float32)
    kv, query = rows[:, : 2 * key_width], rows[:, 2 * key_width : columns]
    scale = gain[...]
    gain_sum = jnp.sum(kv * w_kv[...].astype(jnp.float32), axis=1, keepdims=True) + jnp.sum(query * w_query[...].astype(jnp.float32), axis=1, keepdims=True)
    gain_ref[...] = as_row(gain_sum / scale)
    kv = kv * scale
    key_ref[...] = kv[:, :key_width].T
    value_ref[...] = kv[:, key_width:].T
    query_ref[...] = query * scale
    out_ref[...] = rows[:, padded:padded + width]


def last(total, w_kv, w_query, gain):
    shard, width = w_query.shape
    square = (w_query.shape, jnp.float32)
    turned = ((w_kv.shape[1] // 2, shard), jnp.float32)
    query, key, value, out, gain_grad = in_vmem(
        last_kernel, (square, turned, turned, square, ((1, shard), jnp.float32)), (), (total, w_kv, w_query, gain), name="last"
    )
    return gain_grad.reshape(shard), query, key.T, value.T, out


def unpack_kernel(total, w_gate, w_up, gain, gate_ref, up_ref, down_ref, gain_ref):
    shard, part = w_gate.shape[0], total.shape[3]
    strips = shard // STRIP
    scale = gain[...]
    gain_sum = jnp.zeros((shard, 1), jnp.float32)
    for index, (weight, target) in enumerate(((w_gate, gate_ref), (w_up, up_ref))):
        for step in range(4):
            columns = slice(step * part, (step + 1) * part)
            grads = total[:strips, 4 * index + step].reshape(shard, part).astype(jnp.float32)
            gain_sum = gain_sum + jnp.sum(grads * weight[:, columns].astype(jnp.float32), axis=1, keepdims=True)
            target[:, columns] = grads * scale
    for step in range(4):
        down_ref[step * shard:(step + 1) * shard, :] = total[:strips, 8 + step].reshape(shard, part).astype(jnp.float32)
    gain_ref[...] = as_row(gain_sum)


def unpack(total, w_gate, w_up, gain):
    shard, columns = w_gate.shape
    part = total.shape[3]
    full = ((shard, columns), jnp.float32)
    gate, up, down, gain_grad = in_vmem(
        unpack_kernel, (full, full, ((4 * shard, part), jnp.float32), ((1, shard), jnp.float32)), (), (total, w_gate, w_up, gain), name="unpack"
    )
    return gain_grad.reshape(shard), gate, up, down.T


def over_core(value):
    return lax.ppermute(value, "core", SWAP)


def over_chip(value):
    return lax.ppermute(value, "xh", SWAP)


def over_both(value):
    return lax.ppermute(value, FSDP_AXES, ((0, 3), (3, 0), (1, 2), (2, 1)))


def trade(value):
    return lax.ppermute(value, ("xl", "core"), ((0, 0), (1, 2), (2, 1), (3, 3)))


def arrange(pieces, xh, core):
    low = jnp.where(core == 1, pieces[1], pieces[0]), jnp.where(core == 1, pieces[0], pieces[1])
    high = jnp.where(core == 1, pieces[3], pieces[2]), jnp.where(core == 1, pieces[2], pieces[3])
    return jnp.stack([jnp.where(xh == 1, h, l) for l, h in zip(low, high)] + [jnp.where(xh == 1, l, h) for l, h in zip(low, high)])


def exchange(value, axes):
    return lax.all_to_all(value, axes, split_axis=0, concat_axis=0, tiled=True)


def per_device(
    tokens,
    block_order,
    gain_attn,
    w_query,
    w_key,
    w_value,
    w_out,
    gain_mlp,
    w_gate,
    w_up,
    w_down,
    cotangent,
):
    f32, bf16 = jnp.float32, jnp.bfloat16
    xh, core = lax.axis_index("xh"), lax.axis_index("core")
    mine = 2 * xh + core
    own_id = mine.reshape(1)
    row_total, width = tokens.shape[1:]
    shard = w_query.shape[0]
    ff_part = w_down.shape[0]
    groups = lax.axis_size(SEQ_AXES)
    key_width = KV_HEADS * HEAD
    gain_one = gain_attn.astype(f32)[:, None]
    gain_two = gain_mlp.astype(f32)[:, None]

    kv_shard, query_shard = pack(w_key, w_value, w_query, gain_one)
    far_kv, far_query = over_chip(kv_shard), over_chip(query_shard)
    near_kv, near_query = over_core(kv_shard), over_core(query_shard)
    hidden_low = trade(tokens[0])

    def gate_up(step):
        start = (mine ^ step) * ff_part
        both = [lax.dynamic_slice_in_dim(w, start, ff_part, 1).astype(f32) * gain_two for w in (w_gate, w_up)]
        return jnp.stack(both).astype(bf16)

    gate_up_parts = [gate_up(step) for step in range(4)]
    far_kv, hidden_low, gate_up_parts = lax.optimization_barrier((far_kv, hidden_low, gate_up_parts))

    own_order = lax.dynamic_slice_in_dim(block_order, 2 * groups * core, 2 * groups)
    other_order = lax.dynamic_slice_in_dim(block_order, 2 * groups * (1 - core), 2 * groups)
    key_pos = jnp.concatenate([own_order, other_order])
    query_rank = jnp.sum((own_order[None, :] < own_order[:, None]).astype(jnp.int32), axis=1)
    hit = query_rank[None, :] == jnp.arange(2 * groups, dtype=jnp.int32)[:, None]
    sorted_pos = jnp.sum(jnp.where(hit, own_order[None, :], 0), axis=1)
    sorted_id = jnp.sum(jnp.where(hit, jnp.arange(2 * groups, dtype=jnp.int32)[None, :], 0), axis=1)
    here = lax.axis_index(SEQ_AXES)
    own_blocks = lax.dynamic_slice_in_dim(own_order, 2 * here, 2)
    row = jnp.arange(row_total, dtype=jnp.int32)
    own_pos = jnp.where(row < BLK, own_blocks[0] * BLK + row, own_blocks[1] * BLK + row - BLK)
    inverse_freq = THETA ** (-jnp.arange(HEAD // 2, dtype=f32) / (HEAD // 2))
    angles = inverse_freq[:, None] * own_pos.astype(f32)[None, :]
    cos_table, sin_table = jnp.cos(angles), jnp.sin(angles)

    normed_one, kv_send, kv_full = project_keys(own_id, hidden_low, (kv_shard, near_kv, far_kv, over_core(far_kv)), cos_table, sin_table, groups)
    kv_send, far_query = lax.optimization_barrier((kv_send, far_query))
    query_send, query_full = project_queries(own_id, normed_one, (query_shard, near_query, far_query, over_core(far_query)), cos_table, sin_table, groups)
    kv_own, query_send, upstream = lax.optimization_barrier((exchange(kv_send, SEQ_AXES), query_send, trade(cotangent[0])))
    query_in = exchange(query_send, SEQ_AXES)
    kv_other = over_core(kv_own)

    kv_other, w_out, upstream, gate_up_parts = lax.optimization_barrier((kv_other, w_out, upstream, gate_up_parts))
    far_out, far_upstream = over_chip(w_out), over_chip(upstream)
    far_weights = over_chip(gate_up_parts[2]), over_both(gate_up_parts[3])
    out_send, out_blocks, lse, kv_sorted, kv_turned = attend(key_pos, query_rank, sorted_pos, sorted_id, query_in, kv_own, kv_other)
    out_send, far_out, far_upstream, far_weights = lax.optimization_barrier((out_send, far_out, far_upstream, far_weights))
    out_full = stack_rows(own_id, (w_out, over_core(w_out), far_out, over_core(far_out)))
    weights = (gate_up_parts[0], over_core(gate_up_parts[1])) + far_weights
    upstream_all = (upstream, over_core(upstream), far_upstream, over_core(far_upstream))

    gate_part, up_part = stack_pairs(own_id, weights)
    attn, out_full, gate_part, up_part = lax.optimization_barrier((exchange(out_send, SEQ_AXES), out_full, gate_part, up_part))
    mid_state, second_hat = project_out(attn, hidden_low, out_full)
    far_hat = over_chip(second_hat)
    near_hat = over_core(second_hat)
    down_turned = w_down.T
    near_side = feed((second_hat, near_hat), upstream_all[:2], gate_part, up_part, down_turned)
    far_hat, near_side = lax.optimization_barrier((far_hat, near_side))
    normed_all = second_hat, near_hat, far_hat, over_core(far_hat)
    far_side = feed(normed_all[2:], upstream_all[2:], gate_part, up_part, down_turned)
    scaled_received = over_core(near_side[1])
    far_send = (far_side[0] + over_core(far_side[1])[:, :width].astype(f32)).astype(bf16)
    far_send, normed_all, scaled_received = lax.optimization_barrier((far_send, normed_all, scaled_received))
    scaled_far = over_chip(far_send)
    ring = lax.axis_size(SEQ_AXES)
    stacked = feed_grads(normed_all, upstream_all, near_side[4:], far_side[4:], ring)
    scaled_far, stacked = lax.optimization_barrier((scaled_far, stacked))
    reduced = lax.psum_scatter(stacked.reshape(ring, 12 * STRIP, ff_part), SEQ_AXES, scatter_dimension=0, tiled=True)[0]

    grad_mid, mid_low, grad_send = mid_back(near_side[0], scaled_received, scaled_far, mid_state, upstream, out_full, groups)
    grad_group = exchange(grad_send, SEQ_AXES)
    ctx = lax.axis_size(CTX_AXES)
    slab = 8
    out_grad_keep, out_grad_give = out_grad(own_id, attn, mid_low)
    out_chip = (out_grad_keep.astype(f32) + over_core(out_grad_give).astype(f32)).astype(bf16).reshape(2 * ctx, slab, -1)
    result_received = over_core(near_side[3])
    result_send = (far_side[2] + over_core(far_side[3])[:, :width].astype(f32)).astype(bf16)
    grad_group, result_send, out_chip = lax.optimization_barrier((grad_group, result_send, out_chip))

    out_chips = exchange(out_chip, CHIP_AXES)
    result_far = over_chip(result_send)

    dq, dkv_own, dkv_other = attend_back(key_pos, query_rank, sorted_pos, sorted_id, query_in, grad_group, out_blocks, lse, kv_sorted, kv_turned)
    dkv_other, reduced, out_chips, result_far = lax.optimization_barrier((dkv_other, reduced, out_chips, result_far))
    result = mid_state + near_side[2] + result_received[:, :width].astype(f32) + result_far.astype(f32)
    block_out = trade(result.astype(bf16))
    out_sum = jnp.sum(out_chips.astype(f32), axis=0).astype(bf16)
    dq_home = exchange(dq, SEQ_AXES)
    dkv_received = over_core(dkv_other)
    reduced = (reduced.astype(f32) + lax.ppermute(reduced, "xl", SWAP).astype(f32)).astype(bf16).reshape(3, 4, STRIP, ff_part)
    reduced = reduced.reshape(3, 4, STRIP, ff_part)
    part = lambda step: lax.dynamic_index_in_dim(reduced[:2], mine ^ step, 1, keepdims=False)
    pieces = arrange([part(0), over_core(part(1)), over_chip(part(2)), over_both(part(3))], xh, core).transpose(1, 0, 2, 3)
    pieces = jnp.concatenate([pieces, reduced[2:]]).reshape(12, STRIP, ff_part)
    dkv = (dkv_own + dkv_received.astype(f32)).astype(bf16)
    dq_home, dkv, pieces = lax.optimization_barrier((dq_home, dkv, pieces))
    home = exchange(dkv, SEQ_AXES)
    home, block_out = lax.optimization_barrier((home, block_out))
    whole = lax.all_gather(pieces, SEQ_AXES, axis=0, tiled=False)
    gain_two_shard, gate_shard, up_shard, down_shard = unpack(whole, w_gate, w_up, gain_two)

    keep, give, grad_tokens = finish(own_id, dq_home, home, hidden_low, normed_one, kv_full, query_full, grad_mid, cos_table, sin_table)
    grad_tokens = trade(grad_tokens)
    columns = keep.shape[-1]
    chip_sum = (keep.astype(f32) + over_core(give).astype(f32)).astype(bf16).reshape(2 * ctx, slab, columns)
    qkv_chips, grad_tokens = lax.optimization_barrier((exchange(chip_sum, CHIP_AXES), grad_tokens))
    qkv_sum = jnp.sum(qkv_chips.astype(f32), axis=0).astype(bf16)
    summed = jnp.concatenate([qkv_sum, out_sum], axis=1)
    final = exchange(jnp.broadcast_to(summed[None], (ctx,) + summed.shape), CTX_AXES)
    final, gate_shard = lax.optimization_barrier((final, gate_shard))
    gain_one_shard, query_shard, key_shard, value_shard, out_shard = last(final, kv_shard, query_shard, gain_one)
    return (
        block_out[None],
        grad_tokens.astype(f32)[None],
        gain_one_shard,
        query_shard,
        key_shard,
        value_shard,
        out_shard,
        gain_two_shard,
        gate_shard,
        up_shard,
        down_shard,
    )


def solution(mesh):
    fine = Mesh(mesh.devices.reshape(2, 4, 4, 2, 2), ("xl", "z", "y", "xh", "core"))
    rows = P(FSDP_AXES, CTX_AXES, None)
    gain = P(FSDP_AXES)
    weight = P(FSDP_AXES, None)
    return jax.shard_map(
        per_device,
        mesh=fine,
        in_specs=(rows, P(), gain, weight, weight, weight, weight, gain, weight, weight, weight, rows),
        out_specs=(rows, rows, gain, weight, weight, weight, weight, gain, weight, weight, weight),
        check_vma=False,
    )
```

```python
import functools
import math

import jax
import jax.numpy as jnp
from jax import lax
from jax.experimental import pallas as pl
from jax.experimental.pallas import tpu as pltpu
from jax.sharding import Mesh
from jax.sharding import PartitionSpec as P

HEADS = 15
KV_HEADS = 5
EPSILON = 1e-05
THETA = 100000.0
SEQ_AXES = ("z", "y")
CTX_AXES = ("xl", "z", "y")
CHIP_AXES = ("xh", "xl", "z", "y")
FSDP_AXES = ("xh", "core")
CUBE_AXES = ("xl", "xh", "core")
SWAP = ((0, 1), (1, 0))
STRIP = 16
BLK = 128
HEAD = 64
EXP_SCALE = math.log2(math.e) / 8.0
MASKED = -1e30


def attend_kernel(key_pos, query_rank, sorted_pos, sorted_id, q_ref, own_in, other_in, send_ref, out_ref, lse_ref, kv_ref, kvt_ref, ones_v, q_sorted, *, big, small, edge_size, blocks):
    groups, width = own_in.shape[0], HEAD
    rows = blocks * BLK
    is_key = lax.broadcasted_iota(jnp.int32, (BLK, 2 * width), 1) < width

    def place(index, _):
        for side, source in enumerate((own_in, other_in)):
            for half in range(2):
                where = pl.multiple_of(key_pos[side * 2 * groups + 2 * index + half] * BLK, BLK)
                piece = source[index, :, half * BLK:(half + 1) * BLK]
                kvt_ref[:, pl.ds(where, BLK)] = piece
                turned = piece.T
                kv_ref[pl.ds(where, BLK), :] = turned
                ones_v[pl.ds(where, BLK), :] = jnp.where(is_key, jnp.ones_like(turned), turned)
        for half in range(2):
            query = q_ref[index, :, half * BLK:(half + 1) * BLK]
            query = jnp.concatenate([query, jnp.zeros_like(query)], axis=0)
            q_sorted[pl.ds(pl.multiple_of(query_rank[2 * index + half] * BLK, BLK), BLK), :] = query.T
        return 0

    lax.fori_loop(0, groups, place, 0, unroll=4)

    def tile(index, _):
        low, high = sorted_pos[blocks * index], sorted_pos[blocks * index + blocks - 1]
        query = q_sorted[pl.ds(pl.multiple_of(index * rows, rows), rows), :]
        row = lax.broadcasted_iota(jnp.int32, (rows, 1), 0)
        place_of = row + low * BLK
        for part in range(1, blocks):
            place_of = jnp.where(row >= part * BLK, row + (sorted_pos[blocks * index + part] - part) * BLK, place_of)

        def step(start, carry, size, masked):
            top, total = carry
            scores = lax.dot_general(query, kv_ref[pl.ds(start, size), :], (((1,), (1,)), ((), ())), preferred_element_type=jnp.float32)
            if masked:
                column = start + lax.broadcasted_iota(jnp.int32, scores.shape, 1)
                scores = jnp.where(column <= place_of, scores, MASKED)
            new_top = jnp.maximum(top, jnp.max(scores, axis=1, keepdims=True))
            weights = jnp.exp2((scores - new_top) * EXP_SCALE).astype(jnp.bfloat16)
            factor = jnp.exp2((top - new_top) * EXP_SCALE)
            added = jnp.dot(weights, ones_v[pl.ds(start, size), :], preferred_element_type=jnp.float32)
            return new_top, total * factor + added

        def full(count, carry):
            for part in range(big // small):
                carry = step(pl.multiple_of(count * big + part * small, small), carry, small, False)
            return carry

        def edge(count, carry):
            return step(pl.multiple_of(count * edge_size, edge_size), carry, edge_size, True)

        carry = (jnp.full((rows, 1), MASKED, jnp.float32), jnp.zeros((rows, 2 * width), jnp.float32))
        done = low * BLK // big
        carry = lax.fori_loop(0, done, full, carry)
        top, total = lax.fori_loop(done * (big // edge_size), (high * BLK + BLK + edge_size - 1) // edge_size, edge, carry)
        lse = (top * EXP_SCALE + jnp.log2(total)).T
        total = total.T
        result = total[width:] / total[:1]
        for part in range(blocks):
            ident = sorted_id[blocks * index + part]
            piece = result[:, part * BLK:(part + 1) * BLK]
            out_ref[ident] = piece
            send_ref[ident // 2, :, pl.ds(pl.multiple_of(ident % 2 * BLK, BLK), BLK)] = piece.astype(jnp.bfloat16)
            lse_ref[ident] = lse[:8, part * BLK:(part + 1) * BLK]
        return 0

    lax.fori_loop(0, 2 * groups // blocks, tile, 0)


def attend(key_pos, query_rank, sorted_pos, sorted_id, q, own_in, other_in, big=1024, small=1024, edge_size=512, blocks=4):
    groups, width = own_in.shape[0], HEAD
    total = 4 * groups * BLK
    vm = pl.BlockSpec(memory_space=pltpu.VMEM)
    sm = pl.BlockSpec(memory_space=pltpu.SMEM)
    return pl.pallas_call(
        functools.partial(attend_kernel, big=big, small=small, edge_size=edge_size, blocks=blocks),
        out_shape=(
            jax.ShapeDtypeStruct((groups, width, 2 * BLK), jnp.bfloat16),
            jax.ShapeDtypeStruct((2 * groups, width, BLK), jnp.float32),
            jax.ShapeDtypeStruct((2 * groups, 8, BLK), jnp.float32),
            jax.ShapeDtypeStruct((total, 2 * width), jnp.bfloat16),
            jax.ShapeDtypeStruct((2 * width, total), jnp.bfloat16),
        ),
        in_specs=[sm] * 4 + [vm] * 3,
        out_specs=(vm,) * 5,
        scratch_shapes=[
            pltpu.VMEM((total, 2 * width), jnp.bfloat16),
            pltpu.VMEM((2 * groups * BLK, 2 * width), jnp.bfloat16),
        ],
        compiler_params=pltpu.CompilerParams(vmem_limit_bytes=48 * 2**20),
        cost_estimate=pl.CostEstimate(flops=40 * 10**9, bytes_accessed=10**7, transcendentals=2 * 10**7),
        name="attend",
    )(key_pos, query_rank, sorted_pos, sorted_id, q, own_in, other_in)


def back_kernel(key_pos, query_rank, sorted_pos, sorted_id, q_ref, da_ref, out_ref, lse_ref, kv_ref, kvt_ref, dq_ref, own_ref, other_ref, dkv, q_sorted, da_sorted, *, big, small, edge_size, flip):
    groups, width = q_ref.shape[0], HEAD

    def place(index, _):
        for half in range(2):
            rank = query_rank[2 * index + half]
            q_sorted[rank] = q_ref[index, :, half * BLK:(half + 1) * BLK]
            da_sorted[rank] = da_ref[index, :, half * BLK:(half + 1) * BLK]
        return 0

    lax.fori_loop(0, groups, place, 0)

    def clear(index, _):
        dkv[pl.ds(pl.multiple_of(index * BLK, BLK), BLK), :] = jnp.zeros((BLK, 2 * width), jnp.float32)
        return 0

    lax.fori_loop(0, 4 * groups, clear, 0)

    def tile(index, _):
        low, high = sorted_pos[2 * index], sorted_pos[2 * index + 1]
        first_id, second_id = sorted_id[2 * index], sorted_id[2 * index + 1]
        query = jnp.concatenate([q_sorted[2 * index], q_sorted[2 * index + 1]], axis=1)
        grad = jnp.concatenate([da_sorted[2 * index], da_sorted[2 * index + 1]], axis=1)
        value = jnp.concatenate([out_ref[first_id], out_ref[second_id]], axis=1)
        lse = jnp.concatenate([lse_ref[first_id][:1], lse_ref[second_id][:1]], axis=1)
        delta = jnp.sum(grad.astype(jnp.float32) * value, axis=0, keepdims=True)
        none = jnp.zeros_like(query)
        both = jnp.concatenate([jnp.concatenate([query, none], axis=1), jnp.concatenate([none, grad], axis=1)], axis=0)
        both_t = both.T
        lane = lax.broadcasted_iota(jnp.int32, (1, 2 * BLK), 1)
        place_of = jnp.where(lane < BLK, low * BLK + lane, (high - 1) * BLK + lane)

        def step(start, total, size, masked):
            keys = kv_ref[pl.ds(start, size), :]
            pair = jnp.dot(keys, both, preferred_element_type=jnp.float32)
            weights = jnp.exp2(pair[:, :2 * BLK] * EXP_SCALE - lse)
            if masked:
                row = start + lax.broadcasted_iota(jnp.int32, weights.shape, 0)
                weights = jnp.where(row <= place_of, weights, 0.0)
            grad_scores = (weights * (pair[:, 2 * BLK:] - delta)).astype(jnp.bfloat16)
            weights = weights.astype(jnp.bfloat16)
            dkv[pl.ds(start, size), :] += jnp.dot(jnp.concatenate([grad_scores, weights], axis=1), both_t, preferred_element_type=jnp.float32)
            if flip:
                return total + lax.dot_general(grad_scores, keys, (((0,), (0,)), ((), ())), preferred_element_type=jnp.float32)
            return total + jnp.dot(kvt_ref[:width, pl.ds(start, size)], grad_scores, preferred_element_type=jnp.float32)

        def full(count, carry):
            for part in range(big // small):
                carry = step(pl.multiple_of(count * big + part * small, small), carry, small, False)
            return carry

        def edge(count, carry):
            return step(pl.multiple_of(count * edge_size, edge_size), carry, edge_size, True)

        done = low * BLK // big
        total = jnp.zeros((2 * BLK, 2 * width) if flip else (width, 2 * BLK), jnp.float32)
        total = lax.fori_loop(0, done, full, total)
        total = lax.fori_loop(done * (big // edge_size), (high * BLK + BLK + edge_size - 1) // edge_size, edge, total) * 0.125
        if flip:
            total = total.T[:width]
        for half, ident in enumerate((first_id, second_id)):
            dq_ref[ident // 2, :, pl.ds(pl.multiple_of(ident % 2 * BLK, BLK), BLK)] = total[:, half * BLK:(half + 1) * BLK].astype(jnp.bfloat16)
        return 0

    lax.fori_loop(0, groups, tile, 0)
    factor = jnp.where(lax.broadcasted_iota(jnp.int32, (1, 2 * width), 1) < width, 0.125, 1.0)

    def spread(index, _):
        for side, target in enumerate((own_ref, other_ref)):
            for half in range(2):
                where = pl.multiple_of(key_pos[side * 2 * groups + 2 * index + half] * BLK, BLK)
                target[index, :, half * BLK:(half + 1) * BLK] = (dkv[pl.ds(where, BLK), :] * factor).astype(target.dtype)
        return 0

    lax.fori_loop(0, groups, spread, 0)


def attend_back(key_pos, query_rank, sorted_pos, sorted_id, q, da, out, lse, kv, kvt, big=1024, small=1024, edge_size=512, flip=False):
    groups, width = q.shape[0], HEAD
    total = 4 * groups * BLK
    vm = pl.BlockSpec(memory_space=pltpu.VMEM)
    sm = pl.BlockSpec(memory_space=pltpu.SMEM)
    return pl.pallas_call(
        functools.partial(back_kernel, big=big, small=small, edge_size=edge_size, flip=flip),
        out_shape=(
            jax.ShapeDtypeStruct((groups, width, 2 * BLK), jnp.bfloat16),
            jax.ShapeDtypeStruct((groups, 2 * width, 2 * BLK), jnp.float32),
            jax.ShapeDtypeStruct((groups, 2 * width, 2 * BLK), jnp.bfloat16),
        ),
        in_specs=[sm] * 4 + [vm] * 6,
        out_specs=(vm,) * 3,
        scratch_shapes=[
            pltpu.VMEM((total, 2 * width), jnp.float32),
            pltpu.VMEM((2 * groups, width, BLK), jnp.bfloat16),
            pltpu.VMEM((2 * groups, width, BLK), jnp.bfloat16),
        ],
        compiler_params=pltpu.CompilerParams(vmem_limit_bytes=48 * 2**20),
        cost_estimate=pl.CostEstimate(flops=60 * 10**9, bytes_accessed=10**7, transcendentals=2 * 10**7),
        name="attend_back",
    )(key_pos, query_rank, sorted_pos, sorted_id, q, da, out, lse, kv, kvt)


def in_vmem(kernel, out_shape, scalars, arrays, scratch=(), flops=10**9, name=None):
    vm = pl.BlockSpec(memory_space=pltpu.VMEM)
    return pl.pallas_call(
        kernel,
        out_shape=tuple(jax.ShapeDtypeStruct(shape, dtype) for shape, dtype in out_shape),
        in_specs=[pl.BlockSpec(memory_space=pltpu.SMEM)] * len(scalars) + [vm] * len(arrays),
        out_specs=(vm,) * len(out_shape),
        scratch_shapes=[pltpu.VMEM(shape, dtype) for shape, dtype in scratch],
        compiler_params=pltpu.CompilerParams(vmem_limit_bytes=48 * 2**20),
        cost_estimate=pl.CostEstimate(flops=flops, bytes_accessed=10**7, transcendentals=0),
        name=name,
    )(*scalars, *arrays)


def across(left, right):
    return lax.dot_general(left, right, (((1,), (1,)), ((), ())), preferred_element_type=jnp.float32)


def unit_rms(value):
    return lax.rsqrt(jnp.mean(value * value, axis=-1, keepdims=True) + EPSILON)


def put_rows(mine, pieces, target):
    shard = pieces[0].shape[0]
    for step, piece in enumerate(pieces):
        target[pl.ds(pl.multiple_of((mine[0] ^ step) * shard, 16), shard), :] = piece[...]


def turn(pair, cos, sin):
    half = HEAD // 2
    front, behind = pair[:half], pair[half:]
    return jnp.concatenate([front * cos - behind * sin, behind * cos + front * sin], axis=0).astype(jnp.bfloat16)


def turn_back(pair, cos, sin):
    return turn(pair, cos, -sin)


def project_keys_kernel(mine, x_ref, own, near, far, far_near, cos_ref, sin_ref, hat_ref, send_ref, w_ref):
    put_rows(mine, (own, near, far, far_near), w_ref)
    hidden = x_ref[...].astype(jnp.float32)
    hat = (hidden * unit_rms(hidden)).astype(jnp.bfloat16)
    hat_ref[...] = hat
    key_width = KV_HEADS * HEAD
    per = HEADS // KV_HEADS
    lin = jnp.dot(hat, w_ref[...], preferred_element_type=jnp.float32).T
    for head in range(KV_HEADS):
        key = turn(lin[head * HEAD:(head + 1) * HEAD], cos_ref[...], sin_ref[...])
        value = lin[key_width + head * HEAD:key_width + (head + 1) * HEAD].astype(jnp.bfloat16)
        for query in range(per):
            send_ref[head * per + query, :HEAD] = key
            send_ref[head * per + query, HEAD:] = value
    send_ref[HEADS:] = jnp.zeros((send_ref.shape[0] - HEADS,) + send_ref.shape[1:], jnp.bfloat16)


def project_keys(mine, x, pieces, cos, sin, groups):
    rows, width = x.shape
    columns = pieces[0].shape[1]
    return in_vmem(
        project_keys_kernel,
        ((x.shape, jnp.bfloat16), ((groups, 2 * HEAD, rows), jnp.bfloat16), ((width, columns), jnp.bfloat16)),
        (mine,),
        (x, *pieces, cos, sin),
        name="project_keys",
    )


def project_queries_kernel(mine, hat_ref, own, near, far, far_near, cos_ref, sin_ref, send_ref, w_ref):
    put_rows(mine, (own, near, far, far_near), w_ref)
    per = HEADS // KV_HEADS
    for group in range(KV_HEADS):
        columns = slice(group * per * HEAD, (group + 1) * per * HEAD)
        lin = jnp.dot(hat_ref[...], w_ref[:, columns], preferred_element_type=jnp.float32).T
        for query in range(per):
            send_ref[group * per + query] = turn(lin[query * HEAD:(query + 1) * HEAD], cos_ref[...], sin_ref[...])
    send_ref[HEADS:] = jnp.zeros((send_ref.shape[0] - HEADS,) + send_ref.shape[1:], jnp.bfloat16)


def project_queries(mine, hat, pieces, cos, sin, groups):
    rows, width = hat.shape
    columns = pieces[0].shape[1]
    return in_vmem(
        project_queries_kernel,
        (((groups, HEAD, rows), jnp.bfloat16), ((width, columns), jnp.bfloat16)),
        (mine,),
        (hat, *pieces, cos, sin),
        name="project_queries",
    )


def stack_rows_kernel(mine, own, near, far, far_near, out_ref):
    put_rows(mine, (own, near, far, far_near), out_ref)


def stack_rows(mine, pieces):
    shard, columns = pieces[0].shape
    return in_vmem(stack_rows_kernel, (((4 * shard, columns), jnp.bfloat16),), (mine,), pieces, flops=10**6, name="stack_rows")[0]


def finish_kernel(mine, dq_ref, home, x_ref, hat_ref, kv_ref, query_ref, mid_ref, cos_ref, sin_ref, keep_ref, give_ref, tokens_ref, turned, hat_t):
    shard = query_ref.shape[0] // 4
    cos, sin = cos_ref[...], sin_ref[...]
    key_width = KV_HEADS * HEAD
    per = HEADS // KV_HEADS

    for head in range(KV_HEADS):
        total = sum(home[head * per + query].astype(jnp.float32) for query in range(per))
        total = jnp.concatenate([total[:, :BLK].T, total[:, BLK:].T], axis=1)
        turned[head * HEAD:(head + 1) * HEAD, :] = turn_back(total[:HEAD], cos, sin)
        turned[key_width + head * HEAD:key_width + (head + 1) * HEAD, :] = total[HEAD:].astype(jnp.bfloat16)
        for query in range(per):
            start = 2 * key_width + (head * per + query) * HEAD
            turned[start:start + HEAD, :] = turn_back(dq_ref[head * per + query].astype(jnp.float32), cos, sin)
    hat_t[...] = hat_ref[...].T
    core = mine[0] & 1
    for target, at in ((keep_ref, core), (give_ref, 1 - core)):
        target[...] = jnp.zeros(target.shape, target.dtype)
        for part in range(2):
            rows = hat_t[pl.ds(pl.multiple_of((2 * part + at) * shard, 16), shard), :]
            grads = lax.dot_general(rows, turned[...], (((1,), (1,)), ((), ())), preferred_element_type=jnp.float32)
            target[part, :shard, : grads.shape[1]] = grads.astype(jnp.bfloat16)
    scaled = jnp.dot(kv_ref[...], turned[:2 * key_width, :], preferred_element_type=jnp.float32)
    scaled = (scaled + jnp.dot(query_ref[...], turned[2 * key_width:, :], preferred_element_type=jnp.float32)).T
    hidden = x_ref[...].astype(jnp.float32)
    tokens_ref[...] = (mid_ref[...] + norm_back(hidden, scaled)).astype(jnp.bfloat16)


def finish(mine, dq, home, x, hat, w_kv, w_query, mid, cos, sin):
    rows, width = x.shape
    columns = w_kv.shape[1] + w_query.shape[1]
    half = ((2, 256, -(-columns // BLK) * BLK), jnp.bfloat16)
    return in_vmem(
        finish_kernel,
        (half, half, (x.shape, jnp.bfloat16)),
        (mine,),
        (dq, home, x, hat, w_kv, w_query, mid, cos, sin),
        scratch=(((columns, rows), jnp.bfloat16), ((width, rows), jnp.bfloat16)),
        name="finish",
    )


def norm_back(value, grad):
    rms = unit_rms(value)
    hat = value * rms
    return rms * (grad - hat * jnp.mean(grad * hat, axis=-1, keepdims=True))


def out_kernel(attn, x_ref, w_ref, mid_ref, hat_ref):
    rows = attn[:HEADS].reshape(HEADS * HEAD, attn.shape[2]).T
    mid = x_ref[...].astype(jnp.float32) + jnp.dot(rows, w_ref[...], preferred_element_type=jnp.float32)
    mid_ref[...] = mid
    hat_ref[...] = (mid * unit_rms(mid)).astype(jnp.bfloat16)


def project_out(attn, x, w_out):
    return in_vmem(out_kernel, ((x.shape, jnp.float32), (x.shape, jnp.bfloat16)), (), (attn, x, w_out), name="project_out")


def stack_pairs_kernel(mine, own, near, far, far_near, gate_ref, up_ref):
    pieces = (own, near, far, far_near)
    put_rows(mine, [piece.at[0] for piece in pieces], gate_ref)
    put_rows(mine, [piece.at[1] for piece in pieces], up_ref)


def stack_pairs(mine, pieces):
    _, shard, columns = pieces[0].shape
    whole = ((4 * shard, columns), jnp.bfloat16)
    return in_vmem(stack_pairs_kernel, (whole, whole), (mine,), pieces, flops=10**6, name="stack_pairs")


def feed_kernel(hat_own, hat_peer, grad_own, grad_peer, w_gate, w_up, down_t, scaled_keep, scaled_send, out_keep, out_send, act_ref, gate_grad_ref, up_grad_ref, hat_ref, grad_ref):
    rows, width = hat_own.shape
    for step, (hat, grad) in enumerate(((hat_own, grad_own), (hat_peer, grad_peer))):
        hat_ref[step * rows:(step + 1) * rows, :] = hat[...]
        grad_ref[step * rows:(step + 1) * rows, :] = grad[...]
    gate = jnp.dot(hat_ref[...], w_gate[...], preferred_element_type=jnp.float32)
    up = jnp.dot(hat_ref[...], w_up[...], preferred_element_type=jnp.float32)
    sigmoid = jax.nn.sigmoid(gate)
    silu = gate * sigmoid
    act_ref[...] = (silu * up).astype(jnp.bfloat16)
    grad_act = jnp.dot(grad_ref[...], down_t[...], preferred_element_type=jnp.float32).astype(jnp.bfloat16).astype(jnp.float32)
    gate_grad_ref[...] = (grad_act * up * sigmoid * (1.0 + gate * (1.0 - sigmoid))).astype(jnp.bfloat16)
    up_grad_ref[...] = (grad_act * silu).astype(jnp.bfloat16)
    scaled = across(gate_grad_ref[...], w_gate[...]) + across(up_grad_ref[...], w_up[...])
    out = across(act_ref[...], down_t[...])
    scaled_keep[...] = scaled[:rows]
    out_keep[...] = out[:rows]
    for target, value in ((scaled_send, scaled), (out_send, out)):
        target[:, :width] = value[rows:].astype(jnp.bfloat16)
        target[:, width:] = jnp.zeros((rows, target.shape[1] - width), jnp.bfloat16)


def feed(hats, grads, w_gate, w_up, down_t):
    rows, width = hats[0].shape
    kept = ((rows, width), jnp.float32)
    sent = ((rows, -(-width // 256) * 256), jnp.bfloat16)
    hidden = ((2 * rows, down_t.shape[1]), jnp.bfloat16)
    both = ((2 * rows, width), jnp.bfloat16)
    return in_vmem(
        feed_kernel,
        (kept, sent, kept, sent, hidden, hidden, hidden),
        (),
        (*hats, *grads, w_gate, w_up, down_t),
        scratch=(both, both),
        flops=6 * 10**9,
        name="feed",
    )


def feed_grads_kernel(*refs):
    hats, grads, near, far, (out_ref, hat_t, grad_t) = refs[:4], refs[4:8], refs[8:11], refs[11:14], refs[14:]
    rows = hats[0].shape[0]
    for step in range(4):
        here = slice(step * rows, (step + 1) * rows)
        hat_t[:, here] = hats[step][...].T
        grad_t[:, here] = grads[step][...].T
    shard = hat_t.shape[0] // 4
    strips = shard // STRIP
    for index, (left, at) in enumerate(((hat_t, 1), (hat_t, 2), (grad_t, 0))):
        for part in range(4):
            some = left[part * shard:(part + 1) * shard, :]
            product = jnp.dot(some[:, : 2 * rows], near[at][...], preferred_element_type=jnp.float32)
            product = product + jnp.dot(some[:, 2 * rows:], far[at][...], preferred_element_type=jnp.float32)
            out_ref[:strips, 4 * index + part] = product.astype(jnp.bfloat16).reshape(strips, STRIP, product.shape[1])
    out_ref[strips:] = jnp.zeros((out_ref.shape[0] - strips,) + out_ref.shape[1:], jnp.bfloat16)


def feed_grads(hats, grads, near, far, ring):
    rows, width = hats[0].shape
    turned = ((width, 4 * rows), jnp.bfloat16)
    return in_vmem(
        feed_grads_kernel,
        (((ring, 12, STRIP, near[0].shape[1]), jnp.bfloat16),),
        (),
        (*hats, *grads, *near, *far),
        scratch=(turned, turned),
        flops=8 * 10**9,
        name="feed_grads",
    )[0]


def mid_kernel(mine, keep, received, far, mid_ref, grad_ref, w_ref, attn, total_ref, send_ref, keep_ref, give_ref, rows_ref):
    width = keep.shape[1]
    shard = width // 4
    scaled = keep[...] + received[:, :width].astype(jnp.float32) + far[...].astype(jnp.float32)
    total = grad_ref[...].astype(jnp.float32) + norm_back(mid_ref[...], scaled)
    total_ref[...] = total
    low = total.astype(jnp.bfloat16)
    send_ref[:HEADS] = across(w_ref[...], low).astype(jnp.bfloat16).reshape(HEADS, HEAD, low.shape[0])
    send_ref[HEADS:] = jnp.zeros((send_ref.shape[0] - HEADS,) + send_ref.shape[1:], jnp.bfloat16)
    rows_ref[...] = attn[:HEADS].reshape(HEADS * HEAD, attn.shape[2])
    core = mine[0] & 1
    for target, at in ((keep_ref, core), (give_ref, 1 - core)):
        target[...] = jnp.zeros(target.shape, target.dtype)
        for part in range(2):
            rows = rows_ref[pl.ds(pl.multiple_of((2 * part + at) * shard, 16), shard), :]
            target[part, :shard, :width] = jnp.dot(rows, low, preferred_element_type=jnp.float32).astype(target.dtype)


def mid_back(mine, keep, received, far, mid, grad, w_out, attn):
    half = ((2, 256, 1024), jnp.bfloat16)
    return in_vmem(
        mid_kernel,
        ((mid.shape, jnp.float32), (attn.shape, jnp.bfloat16), half, half),
        (mine,),
        (keep, received, far, mid, grad, w_out, attn),
        scratch=((mid.shape[::-1], jnp.bfloat16),),
        name="mid_back",
    )


def pack_kernel(key_t, value_t, query, gain, kv_ref, query_ref):
    width = key_t.shape[0]
    scale = gain[...]
    for index, piece in enumerate((key_t, value_t)):
        kv_ref[:, index * width:(index + 1) * width] = (piece[...].astype(jnp.float32).T * scale).astype(jnp.bfloat16)
    query_ref[...] = (query[...].astype(jnp.float32) * scale).astype(jnp.bfloat16)


def pack(w_key, w_value, w_query, gain):
    shard = w_key.shape[0]
    return in_vmem(
        pack_kernel,
        (((shard, 2 * w_key.shape[1]), jnp.bfloat16), (w_query.shape, jnp.bfloat16)),
        (),
        (w_key.T, w_value.T, w_query, gain),
        flops=10**6,
        name="pack",
    )


def as_row(column):
    return jnp.broadcast_to(column, (column.shape[0], BLK)).T[:1]


def last_kernel(total, w_kv, w_query, gain, query_ref, key_ref, value_ref, out_ref, gain_ref):
    shard, width = w_query.shape
    key_width = key_ref.shape[0]
    columns = 2 * key_width + width
    padded = -(-columns // BLK) * BLK
    rows = total[...].reshape(total.shape[0] * total.shape[1], total.shape[2])[:shard].astype(jnp.float32)
    kv, query = rows[:, : 2 * key_width], rows[:, 2 * key_width : columns]
    scale = gain[...]
    gain_sum = jnp.sum(kv * w_kv[...].astype(jnp.float32), axis=1, keepdims=True) + jnp.sum(query * w_query[...].astype(jnp.float32), axis=1, keepdims=True)
    gain_ref[...] = as_row(gain_sum / scale)
    kv = kv * scale
    key_ref[...] = kv[:, :key_width].T
    value_ref[...] = kv[:, key_width:].T
    query_ref[...] = query * scale
    out_ref[...] = rows[:, padded:padded + width]


def last(total, w_kv, w_query, gain):
    shard, width = w_query.shape
    square = (w_query.shape, jnp.float32)
    turned = ((w_kv.shape[1] // 2, shard), jnp.float32)
    query, key, value, out, gain_grad = in_vmem(
        last_kernel, (square, turned, turned, square, ((1, shard), jnp.float32)), (), (total, w_kv, w_query, gain), name="last"
    )
    return gain_grad.reshape(shard), query, key.T, value.T, out


def unpack_kernel(total, w_gate, w_up, gain, gate_ref, up_ref, down_ref, gain_ref):
    shard, part = w_gate.shape[0], total.shape[3]
    strips = shard // STRIP
    scale = gain[...]
    gain_sum = jnp.zeros((shard, 1), jnp.float32)
    for index, (weight, target) in enumerate(((w_gate, gate_ref), (w_up, up_ref))):
        for step in range(4):
            columns = slice(step * part, (step + 1) * part)
            grads = total[:strips, 4 * index + step].reshape(shard, part).astype(jnp.float32)
            gain_sum = gain_sum + jnp.sum(grads * weight[:, columns].astype(jnp.float32), axis=1, keepdims=True)
            target[:, columns] = grads * scale
    for step in range(4):
        down_ref[step * shard:(step + 1) * shard, :] = total[:strips, 8 + step].reshape(shard, part).astype(jnp.float32)
    gain_ref[...] = as_row(gain_sum)


def unpack(total, w_gate, w_up, gain):
    shard, columns = w_gate.shape
    part = total.shape[3]
    full = ((shard, columns), jnp.float32)
    gate, up, down, gain_grad = in_vmem(
        unpack_kernel, (full, full, ((4 * shard, part), jnp.float32), ((1, shard), jnp.float32)), (), (total, w_gate, w_up, gain), name="unpack"
    )
    return gain_grad.reshape(shard), gate, up, down.T


def over_core(value):
    return lax.ppermute(value, "core", SWAP)


def over_chip(value):
    return lax.ppermute(value, "xh", SWAP)


def over_both(value):
    return lax.ppermute(value, FSDP_AXES, ((0, 3), (3, 0), (1, 2), (2, 1)))


def trade(value):
    return lax.ppermute(value, ("xl", "core"), ((0, 0), (1, 2), (2, 1), (3, 3)))


def arrange(pieces, xh, core):
    low = jnp.where(core == 1, pieces[1], pieces[0]), jnp.where(core == 1, pieces[0], pieces[1])
    high = jnp.where(core == 1, pieces[3], pieces[2]), jnp.where(core == 1, pieces[2], pieces[3])
    return jnp.stack([jnp.where(xh == 1, h, l) for l, h in zip(low, high)] + [jnp.where(xh == 1, l, h) for l, h in zip(low, high)])


def exchange(value, axes):
    return lax.all_to_all(value, axes, split_axis=0, concat_axis=0, tiled=True)


def per_device(
    tokens,
    block_order,
    gain_attn,
    w_query,
    w_key,
    w_value,
    w_out,
    gain_mlp,
    w_gate,
    w_up,
    w_down,
    cotangent,
):
    f32, bf16 = jnp.float32, jnp.bfloat16
    xh, core = lax.axis_index("xh"), lax.axis_index("core")
    mine = 2 * xh + core
    own_id = mine.reshape(1)
    row_total, width = tokens.shape[1:]
    shard = w_query.shape[0]
    ff_part = w_down.shape[0]
    groups = lax.axis_size(SEQ_AXES)
    key_width = KV_HEADS * HEAD
    gain_one = gain_attn.astype(f32)[:, None]
    gain_two = gain_mlp.astype(f32)[:, None]

    kv_shard, query_shard = pack(w_key, w_value, w_query, gain_one)
    far_kv, far_query = over_chip(kv_shard), over_chip(query_shard)
    near_kv, near_query = over_core(kv_shard), over_core(query_shard)
    hidden_low = trade(tokens[0])

    def gate_up(step):
        start = (mine ^ step) * ff_part
        both = [lax.dynamic_slice_in_dim(w, start, ff_part, 1).astype(f32) * gain_two for w in (w_gate, w_up)]
        return jnp.stack(both).astype(bf16)

    gate_up_parts = [gate_up(step) for step in range(4)]
    far_kv, hidden_low, gate_up_parts = lax.optimization_barrier((far_kv, hidden_low, gate_up_parts))

    own_order = lax.dynamic_slice_in_dim(block_order, 2 * groups * core, 2 * groups)
    other_order = lax.dynamic_slice_in_dim(block_order, 2 * groups * (1 - core), 2 * groups)
    key_pos = jnp.concatenate([own_order, other_order])
    query_rank = jnp.sum((own_order[None, :] < own_order[:, None]).astype(jnp.int32), axis=1)
    hit = query_rank[None, :] == jnp.arange(2 * groups, dtype=jnp.int32)[:, None]
    sorted_pos = jnp.sum(jnp.where(hit, own_order[None, :], 0), axis=1)
    sorted_id = jnp.sum(jnp.where(hit, jnp.arange(2 * groups, dtype=jnp.int32)[None, :], 0), axis=1)
    here = lax.axis_index(SEQ_AXES)
    own_blocks = lax.dynamic_slice_in_dim(own_order, 2 * here, 2)
    row = jnp.arange(row_total, dtype=jnp.int32)
    own_pos = jnp.where(row < BLK, own_blocks[0] * BLK + row, own_blocks[1] * BLK + row - BLK)
    inverse_freq = THETA ** (-jnp.arange(HEAD // 2, dtype=f32) / (HEAD // 2))
    angles = inverse_freq[:, None] * own_pos.astype(f32)[None, :]
    cos_table, sin_table = jnp.cos(angles), jnp.sin(angles)

    normed_one, kv_send, kv_full = project_keys(own_id, hidden_low, (kv_shard, near_kv, far_kv, over_core(far_kv)), cos_table, sin_table, groups)
    query_send, query_full = project_queries(own_id, normed_one, (query_shard, near_query, far_query, over_core(far_query)), cos_table, sin_table, groups)
    kv_own, query_send, upstream = lax.optimization_barrier((exchange(kv_send, SEQ_AXES), query_send, trade(cotangent[0])))
    query_in = exchange(query_send, SEQ_AXES)
    kv_other = over_core(kv_own)

    kv_other, w_out, upstream, gate_up_parts = lax.optimization_barrier((kv_other, w_out, upstream, gate_up_parts))
    far_out, far_upstream = over_chip(w_out), over_chip(upstream)
    far_weights = over_chip(gate_up_parts[2]), over_both(gate_up_parts[3])
    out_send, out_blocks, lse, kv_sorted, kv_turned = attend(key_pos, query_rank, sorted_pos, sorted_id, query_in, kv_own, kv_other)
    out_send, far_out, far_upstream, far_weights = lax.optimization_barrier((out_send, far_out, far_upstream, far_weights))
    out_full = stack_rows(own_id, (w_out, over_core(w_out), far_out, over_core(far_out)))
    weights = (gate_up_parts[0], over_core(gate_up_parts[1])) + far_weights
    upstream_all = (upstream, over_core(upstream), far_upstream, over_core(far_upstream))

    gate_part, up_part = stack_pairs(own_id, weights)
    attn, out_full, gate_part, up_part = lax.optimization_barrier((exchange(out_send, SEQ_AXES), out_full, gate_part, up_part))
    mid_state, second_hat = project_out(attn, hidden_low, out_full)
    far_hat = over_chip(second_hat)
    near_hat = over_core(second_hat)
    down_turned = w_down.T
    near_side = feed((second_hat, near_hat), upstream_all[:2], gate_part, up_part, down_turned)
    far_hat, near_side = lax.optimization_barrier((far_hat, near_side))
    normed_all = second_hat, near_hat, far_hat, over_core(far_hat)
    far_side = feed(normed_all[2:], upstream_all[2:], gate_part, up_part, down_turned)
    scaled_received = over_core(near_side[1])
    far_send = (far_side[0] + over_core(far_side[1])[:, :width].astype(f32)).astype(bf16)
    far_send, normed_all, scaled_received = lax.optimization_barrier((far_send, normed_all, scaled_received))
    scaled_far = over_chip(far_send)
    ring = lax.axis_size(SEQ_AXES)
    stacked = feed_grads(normed_all, upstream_all, near_side[4:], far_side[4:], ring)
    scaled_far, stacked = lax.optimization_barrier((scaled_far, stacked))
    reduced = lax.psum_scatter(stacked.reshape(ring, 12 * STRIP, ff_part), SEQ_AXES, scatter_dimension=0, tiled=True)[0]

    grad_mid, grad_send, out_grad_keep, out_grad_give = mid_back(own_id, near_side[0], scaled_received, scaled_far, mid_state, upstream, out_full, attn)
    grad_group = exchange(grad_send, SEQ_AXES)
    ctx = lax.axis_size(CTX_AXES)
    slab = 8
    out_chip = (out_grad_keep.astype(f32) + over_core(out_grad_give).astype(f32)).astype(bf16).reshape(2 * ctx, slab, -1)
    result_received = over_core(near_side[3])
    result_send = (far_side[2] + over_core(far_side[3])[:, :width].astype(f32)).astype(bf16)
    grad_group, out_chip = lax.optimization_barrier((grad_group, out_chip))

    out_chips = exchange(out_chip, CHIP_AXES)

    dq, dkv_own, dkv_other = attend_back(key_pos, query_rank, sorted_pos, sorted_id, query_in, grad_group, out_blocks, lse, kv_sorted, kv_turned)
    dkv_other, reduced, out_chips, result_send = lax.optimization_barrier((dkv_other, reduced, out_chips, result_send))
    result_far = over_chip(result_send)
    out_sum = jnp.sum(out_chips.astype(f32), axis=0).astype(bf16)
    dq_home = exchange(dq, SEQ_AXES)
    dkv_received = over_core(dkv_other)
    reduced = (reduced.astype(f32) + lax.ppermute(reduced, "xl", SWAP).astype(f32)).astype(bf16).reshape(3, 4, STRIP, ff_part)
    dkv = (dkv_own + dkv_received.astype(f32)).astype(bf16)
    dq_home, dkv, reduced = lax.optimization_barrier((dq_home, dkv, reduced))
    part = lambda step: lax.dynamic_index_in_dim(reduced[:2], mine ^ step, 1, keepdims=False)
    pieces = arrange([part(0), over_core(part(1)), over_chip(part(2)), over_both(part(3))], xh, core).transpose(1, 0, 2, 3)
    pieces = jnp.concatenate([pieces, reduced[2:]]).reshape(12, STRIP, ff_part)
    result = mid_state + near_side[2] + result_received[:, :width].astype(f32) + result_far.astype(f32)
    home, pieces, result = lax.optimization_barrier((exchange(dkv, SEQ_AXES), pieces, result.astype(bf16)))
    block_out = trade(result)
    whole = lax.all_gather(pieces, SEQ_AXES, axis=0, tiled=False)
    gain_two_shard, gate_shard, up_shard, down_shard = unpack(whole, w_gate, w_up, gain_two)

    keep, give, grad_tokens = finish(own_id, dq_home, home, hidden_low, normed_one, kv_full, query_full, grad_mid, cos_table, sin_table)
    grad_tokens = trade(grad_tokens)
    columns = keep.shape[-1]
    chip_sum = (keep.astype(f32) + over_core(give).astype(f32)).astype(bf16).reshape(2 * ctx, slab, columns)
    qkv_chips, grad_tokens, block_out = lax.optimization_barrier((exchange(chip_sum, CHIP_AXES), grad_tokens, block_out))
    qkv_sum = jnp.sum(qkv_chips.astype(f32), axis=0).astype(bf16)
    summed = jnp.concatenate([qkv_sum, out_sum], axis=1)
    final = exchange(jnp.broadcast_to(summed[None], (ctx,) + summed.shape), CTX_AXES)
    final, gate_shard = lax.optimization_barrier((final, gate_shard))
    gain_one_shard, query_shard, key_shard, value_shard, out_shard = last(final, kv_shard, query_shard, gain_one)
    return (
        block_out[None],
        grad_tokens.astype(f32)[None],
        gain_one_shard,
        query_shard,
        key_shard,
        value_shard,
        out_shard,
        gain_two_shard,
        gate_shard,
        up_shard,
        down_shard,
    )


def solution(mesh):
    fine = Mesh(mesh.devices.reshape(2, 4, 4, 2, 2), ("xl", "z", "y", "xh", "core"))
    rows = P(FSDP_AXES, CTX_AXES, None)
    gain = P(FSDP_AXES)
    weight = P(FSDP_AXES, None)
    return jax.shard_map(
        per_device,
        mesh=fine,
        in_specs=(rows, P(), gain, weight, weight, weight, weight, gain, weight, weight, weight, rows),
        out_specs=(rows, rows, gain, weight, weight, weight, weight, gain, weight, weight, weight),
        check_vma=False,
    )
```

```python
import functools
import math

import jax
import jax.numpy as jnp
from jax import lax
from jax.experimental import pallas as pl
from jax.experimental.pallas import tpu as pltpu
from jax.sharding import Mesh
from jax.sharding import PartitionSpec as P

HEADS = 15
KV_HEADS = 5
EPSILON = 1e-05
THETA = 100000.0
SEQ_AXES = ("z", "y")
CTX_AXES = ("xl", "z", "y")
CHIP_AXES = ("xh", "xl", "z", "y")
FSDP_AXES = ("xh", "core")
CUBE_AXES = ("xl", "xh", "core")
SWAP = ((0, 1), (1, 0))
STRIP = 16
BLK = 128
HEAD = 64
EXP_SCALE = math.log2(math.e) / 8.0
MASKED = -1e30


def attend_kernel(key_pos, query_rank, sorted_pos, sorted_id, q_ref, own_in, other_in, send_ref, out_ref, lse_ref, kv_ref, kvt_ref, ones_v, q_sorted, *, big, small, edge_size, blocks):
    groups, width = own_in.shape[0], HEAD
    rows = blocks * BLK
    is_key = lax.broadcasted_iota(jnp.int32, (BLK, 2 * width), 1) < width

    def place(index, _):
        for side, source in enumerate((own_in, other_in)):
            for half in range(2):
                where = pl.multiple_of(key_pos[side * 2 * groups + 2 * index + half] * BLK, BLK)
                piece = source[index, :, half * BLK:(half + 1) * BLK]
                kvt_ref[:, pl.ds(where, BLK)] = piece
                turned = piece.T
                kv_ref[pl.ds(where, BLK), :] = turned
                ones_v[pl.ds(where, BLK), :] = jnp.where(is_key, jnp.ones_like(turned), turned)
        for half in range(2):
            query = q_ref[index, :, half * BLK:(half + 1) * BLK]
            query = jnp.concatenate([query, jnp.zeros_like(query)], axis=0)
            q_sorted[pl.ds(pl.multiple_of(query_rank[2 * index + half] * BLK, BLK), BLK), :] = query.T
        return 0

    lax.fori_loop(0, groups, place, 0, unroll=4)

    def tile(index, _):
        low, high = sorted_pos[blocks * index], sorted_pos[blocks * index + blocks - 1]
        query = q_sorted[pl.ds(pl.multiple_of(index * rows, rows), rows), :]
        row = lax.broadcasted_iota(jnp.int32, (rows, 1), 0)
        place_of = row + low * BLK
        for part in range(1, blocks):
            place_of = jnp.where(row >= part * BLK, row + (sorted_pos[blocks * index + part] - part) * BLK, place_of)

        def step(start, carry, size, masked):
            top, total = carry
            scores = lax.dot_general(query, kv_ref[pl.ds(start, size), :], (((1,), (1,)), ((), ())), preferred_element_type=jnp.float32)
            if masked:
                column = start + lax.broadcasted_iota(jnp.int32, scores.shape, 1)
                scores = jnp.where(column <= place_of, scores, MASKED)
            new_top = jnp.maximum(top, jnp.max(scores, axis=1, keepdims=True))
            weights = jnp.exp2((scores - new_top) * EXP_SCALE).astype(jnp.bfloat16)
            factor = jnp.exp2((top - new_top) * EXP_SCALE)
            added = jnp.dot(weights, ones_v[pl.ds(start, size), :], preferred_element_type=jnp.float32)
            return new_top, total * factor + added

        def full(count, carry):
            for part in range(big // small):
                carry = step(pl.multiple_of(count * big + part * small, small), carry, small, False)
            return carry

        def edge(count, carry):
            return step(pl.multiple_of(count * edge_size, edge_size), carry, edge_size, True)

        carry = (jnp.full((rows, 1), MASKED, jnp.float32), jnp.zeros((rows, 2 * width), jnp.float32))
        done = low * BLK // big
        carry = lax.fori_loop(0, done, full, carry)
        top, total = lax.fori_loop(done * (big // edge_size), (high * BLK + BLK + edge_size - 1) // edge_size, edge, carry)
        lse = (top * EXP_SCALE + jnp.log2(total)).T
        total = total.T
        result = total[width:] / total[:1]
        for part in range(blocks):
            ident = sorted_id[blocks * index + part]
            piece = result[:, part * BLK:(part + 1) * BLK]
            out_ref[ident] = piece
            send_ref[ident // 2, :, pl.ds(pl.multiple_of(ident % 2 * BLK, BLK), BLK)] = piece.astype(jnp.bfloat16)
            lse_ref[ident] = lse[:8, part * BLK:(part + 1) * BLK]
        return 0

    lax.fori_loop(0, 2 * groups // blocks, tile, 0)


def attend(key_pos, query_rank, sorted_pos, sorted_id, q, own_in, other_in, big=1024, small=1024, edge_size=512, blocks=4):
    groups, width = own_in.shape[0], HEAD
    total = 4 * groups * BLK
    vm = pl.BlockSpec(memory_space=pltpu.VMEM)
    sm = pl.BlockSpec(memory_space=pltpu.SMEM)
    return pl.pallas_call(
        functools.partial(attend_kernel, big=big, small=small, edge_size=edge_size, blocks=blocks),
        out_shape=(
            jax.ShapeDtypeStruct((groups, width, 2 * BLK), jnp.bfloat16),
            jax.ShapeDtypeStruct((2 * groups, width, BLK), jnp.float32),
            jax.ShapeDtypeStruct((2 * groups, 8, BLK), jnp.float32),
            jax.ShapeDtypeStruct((total, 2 * width), jnp.bfloat16),
            jax.ShapeDtypeStruct((2 * width, total), jnp.bfloat16),
        ),
        in_specs=[sm] * 4 + [vm] * 3,
        out_specs=(vm,) * 5,
        scratch_shapes=[
            pltpu.VMEM((total, 2 * width), jnp.bfloat16),
            pltpu.VMEM((2 * groups * BLK, 2 * width), jnp.bfloat16),
        ],
        compiler_params=pltpu.CompilerParams(vmem_limit_bytes=24 * 2**20),
        cost_estimate=pl.CostEstimate(flops=40 * 10**9, bytes_accessed=10**7, transcendentals=2 * 10**7),
        name="attend",
    )(key_pos, query_rank, sorted_pos, sorted_id, q, own_in, other_in)


def back_kernel(key_pos, query_rank, sorted_pos, sorted_id, q_ref, da_ref, out_ref, lse_ref, kv_ref, kvt_ref, dq_ref, own_ref, other_ref, dkv, q_sorted, da_sorted, *, big, small, edge_size, flip):
    groups, width = q_ref.shape[0], HEAD

    def place(index, _):
        for half in range(2):
            rank = query_rank[2 * index + half]
            q_sorted[rank] = q_ref[index, :, half * BLK:(half + 1) * BLK]
            da_sorted[rank] = da_ref[index, :, half * BLK:(half + 1) * BLK]
        return 0

    lax.fori_loop(0, groups, place, 0)

    def clear(index, _):
        dkv[pl.ds(pl.multiple_of(index * BLK, BLK), BLK), :] = jnp.zeros((BLK, 2 * width), jnp.float32)
        return 0

    lax.fori_loop(0, 4 * groups, clear, 0)

    def tile(index, _):
        low, high = sorted_pos[2 * index], sorted_pos[2 * index + 1]
        first_id, second_id = sorted_id[2 * index], sorted_id[2 * index + 1]
        query = jnp.concatenate([q_sorted[2 * index], q_sorted[2 * index + 1]], axis=1)
        grad = jnp.concatenate([da_sorted[2 * index], da_sorted[2 * index + 1]], axis=1)
        value = jnp.concatenate([out_ref[first_id], out_ref[second_id]], axis=1)
        lse = jnp.concatenate([lse_ref[first_id][:1], lse_ref[second_id][:1]], axis=1)
        delta = jnp.sum(grad.astype(jnp.float32) * value, axis=0, keepdims=True)
        none = jnp.zeros_like(query)
        both = jnp.concatenate([jnp.concatenate([query, none], axis=1), jnp.concatenate([none, grad], axis=1)], axis=0)
        both_t = both.T
        lane = lax.broadcasted_iota(jnp.int32, (1, 2 * BLK), 1)
        place_of = jnp.where(lane < BLK, low * BLK + lane, (high - 1) * BLK + lane)

        def step(start, total, size, masked):
            keys = kv_ref[pl.ds(start, size), :]
            pair = jnp.dot(keys, both, preferred_element_type=jnp.float32)
            weights = jnp.exp2(pair[:, :2 * BLK] * EXP_SCALE - lse)
            if masked:
                row = start + lax.broadcasted_iota(jnp.int32, weights.shape, 0)
                weights = jnp.where(row <= place_of, weights, 0.0)
            grad_scores = (weights * (pair[:, 2 * BLK:] - delta)).astype(jnp.bfloat16)
            weights = weights.astype(jnp.bfloat16)
            dkv[pl.ds(start, size), :] += jnp.dot(jnp.concatenate([grad_scores, weights], axis=1), both_t, preferred_element_type=jnp.float32)
            if flip:
                return total + lax.dot_general(grad_scores, keys, (((0,), (0,)), ((), ())), preferred_element_type=jnp.float32)
            return total + jnp.dot(kvt_ref[:width, pl.ds(start, size)], grad_scores, preferred_element_type=jnp.float32)

        def full(count, carry):
            for part in range(big // small):
                carry = step(pl.multiple_of(count * big + part * small, small), carry, small, False)
            return carry

        def edge(count, carry):
            return step(pl.multiple_of(count * edge_size, edge_size), carry, edge_size, True)

        done = low * BLK // big
        total = jnp.zeros((2 * BLK, 2 * width) if flip else (width, 2 * BLK), jnp.float32)
        total = lax.fori_loop(0, done, full, total)
        total = lax.fori_loop(done * (big // edge_size), (high * BLK + BLK + edge_size - 1) // edge_size, edge, total) * 0.125
        if flip:
            total = total.T[:width]
        for half, ident in enumerate((first_id, second_id)):
            dq_ref[ident // 2, :, pl.ds(pl.multiple_of(ident % 2 * BLK, BLK), BLK)] = total[:, half * BLK:(half + 1) * BLK].astype(jnp.bfloat16)
        return 0

    lax.fori_loop(0, groups, tile, 0)
    factor = jnp.where(lax.broadcasted_iota(jnp.int32, (1, 2 * width), 1) < width, 0.125, 1.0)

    def spread(index, _):
        for side, target in enumerate((own_ref, other_ref)):
            for half in range(2):
                where = pl.multiple_of(key_pos[side * 2 * groups + 2 * index + half] * BLK, BLK)
                target[index, :, half * BLK:(half + 1) * BLK] = (dkv[pl.ds(where, BLK), :] * factor).astype(target.dtype)
        return 0

    lax.fori_loop(0, groups, spread, 0)


def attend_back(key_pos, query_rank, sorted_pos, sorted_id, q, da, out, lse, kv, kvt, big=1024, small=1024, edge_size=512, flip=False):
    groups, width = q.shape[0], HEAD
    total = 4 * groups * BLK
    vm = pl.BlockSpec(memory_space=pltpu.VMEM)
    sm = pl.BlockSpec(memory_space=pltpu.SMEM)
    return pl.pallas_call(
        functools.partial(back_kernel, big=big, small=small, edge_size=edge_size, flip=flip),
        out_shape=(
            jax.ShapeDtypeStruct((groups, width, 2 * BLK), jnp.bfloat16),
            jax.ShapeDtypeStruct((groups, 2 * width, 2 * BLK), jnp.float32),
            jax.ShapeDtypeStruct((groups, 2 * width, 2 * BLK), jnp.bfloat16),
        ),
        in_specs=[sm] * 4 + [vm] * 6,
        out_specs=(vm,) * 3,
        scratch_shapes=[
            pltpu.VMEM((total, 2 * width), jnp.float32),
            pltpu.VMEM((2 * groups, width, BLK), jnp.bfloat16),
            pltpu.VMEM((2 * groups, width, BLK), jnp.bfloat16),
        ],
        compiler_params=pltpu.CompilerParams(vmem_limit_bytes=28 * 2**20),
        cost_estimate=pl.CostEstimate(flops=60 * 10**9, bytes_accessed=10**7, transcendentals=2 * 10**7),
        name="attend_back",
    )(key_pos, query_rank, sorted_pos, sorted_id, q, da, out, lse, kv, kvt)


def in_vmem(kernel, out_shape, scalars, arrays, scratch=(), flops=10**9, vmem=24, name=None):
    vm = pl.BlockSpec(memory_space=pltpu.VMEM)
    return pl.pallas_call(
        kernel,
        out_shape=tuple(jax.ShapeDtypeStruct(shape, dtype) for shape, dtype in out_shape),
        in_specs=[pl.BlockSpec(memory_space=pltpu.SMEM)] * len(scalars) + [vm] * len(arrays),
        out_specs=(vm,) * len(out_shape),
        scratch_shapes=[pltpu.VMEM(shape, dtype) for shape, dtype in scratch],
        compiler_params=pltpu.CompilerParams(vmem_limit_bytes=vmem * 2**20),
        cost_estimate=pl.CostEstimate(flops=flops, bytes_accessed=10**7, transcendentals=0),
        name=name,
    )(*scalars, *arrays)


def across(left, right):
    return lax.dot_general(left, right, (((1,), (1,)), ((), ())), preferred_element_type=jnp.float32)


def unit_rms(value):
    return lax.rsqrt(jnp.mean(value * value, axis=-1, keepdims=True) + EPSILON)


def put_rows(mine, pieces, target):
    shard = pieces[0].shape[0]
    for step, piece in enumerate(pieces):
        target[pl.ds(pl.multiple_of((mine[0] ^ step) * shard, 16), shard), :] = piece[...]


def turn(pair, cos, sin):
    half = HEAD // 2
    front, behind = pair[:half], pair[half:]
    return jnp.concatenate([front * cos - behind * sin, behind * cos + front * sin], axis=0).astype(jnp.bfloat16)


def turn_back(pair, cos, sin):
    return turn(pair, cos, -sin)


def project_keys_kernel(mine, x_ref, own, near, far, far_near, cos_ref, sin_ref, hat_ref, send_ref, w_ref):
    put_rows(mine, (own, near, far, far_near), w_ref)
    hidden = x_ref[...].astype(jnp.float32)
    hat = (hidden * unit_rms(hidden)).astype(jnp.bfloat16)
    hat_ref[...] = hat
    key_width = KV_HEADS * HEAD
    per = HEADS // KV_HEADS
    lin = jnp.dot(hat, w_ref[...], preferred_element_type=jnp.float32).T
    for head in range(KV_HEADS):
        key = turn(lin[head * HEAD:(head + 1) * HEAD], cos_ref[...], sin_ref[...])
        value = lin[key_width + head * HEAD:key_width + (head + 1) * HEAD].astype(jnp.bfloat16)
        for query in range(per):
            send_ref[head * per + query, :HEAD] = key
            send_ref[head * per + query, HEAD:] = value
    send_ref[HEADS:] = jnp.zeros((send_ref.shape[0] - HEADS,) + send_ref.shape[1:], jnp.bfloat16)


def project_keys(mine, x, pieces, cos, sin, groups):
    rows, width = x.shape
    columns = pieces[0].shape[1]
    return in_vmem(
        project_keys_kernel,
        ((x.shape, jnp.bfloat16), ((groups, 2 * HEAD, rows), jnp.bfloat16), ((width, columns), jnp.bfloat16)),
        (mine,),
        (x, *pieces, cos, sin),
        name="project_keys",
    )


def project_queries_kernel(mine, hat_ref, own, near, far, far_near, cos_ref, sin_ref, send_ref, w_ref):
    put_rows(mine, (own, near, far, far_near), w_ref)
    per = HEADS // KV_HEADS
    for group in range(KV_HEADS):
        columns = slice(group * per * HEAD, (group + 1) * per * HEAD)
        lin = jnp.dot(hat_ref[...], w_ref[:, columns], preferred_element_type=jnp.float32).T
        for query in range(per):
            send_ref[group * per + query] = turn(lin[query * HEAD:(query + 1) * HEAD], cos_ref[...], sin_ref[...])
    send_ref[HEADS:] = jnp.zeros((send_ref.shape[0] - HEADS,) + send_ref.shape[1:], jnp.bfloat16)


def project_queries(mine, hat, pieces, cos, sin, groups):
    rows, width = hat.shape
    columns = pieces[0].shape[1]
    return in_vmem(
        project_queries_kernel,
        (((groups, HEAD, rows), jnp.bfloat16), ((width, columns), jnp.bfloat16)),
        (mine,),
        (hat, *pieces, cos, sin),
        name="project_queries",
    )


def stack_rows_kernel(mine, own, near, far, far_near, out_ref):
    put_rows(mine, (own, near, far, far_near), out_ref)


def stack_rows(mine, pieces):
    shard, columns = pieces[0].shape
    return in_vmem(stack_rows_kernel, (((4 * shard, columns), jnp.bfloat16),), (mine,), pieces, flops=10**6, name="stack_rows")[0]


def finish_kernel(mine, dq_ref, home, x_ref, hat_ref, kv_ref, query_ref, mid_ref, cos_ref, sin_ref, keep_ref, give_ref, tokens_ref, turned, hat_t):
    shard = query_ref.shape[0] // 4
    cos, sin = cos_ref[...], sin_ref[...]
    key_width = KV_HEADS * HEAD
    per = HEADS // KV_HEADS

    for head in range(KV_HEADS):
        total = sum(home[head * per + query].astype(jnp.float32) for query in range(per))
        total = jnp.concatenate([total[:, :BLK].T, total[:, BLK:].T], axis=1)
        turned[head * HEAD:(head + 1) * HEAD, :] = turn_back(total[:HEAD], cos, sin)
        turned[key_width + head * HEAD:key_width + (head + 1) * HEAD, :] = total[HEAD:].astype(jnp.bfloat16)
        for query in range(per):
            start = 2 * key_width + (head * per + query) * HEAD
            turned[start:start + HEAD, :] = turn_back(dq_ref[head * per + query].astype(jnp.float32), cos, sin)
    hat_t[...] = hat_ref[...].T
    core = mine[0] & 1
    for target, at in ((keep_ref, core), (give_ref, 1 - core)):
        target[...] = jnp.zeros(target.shape, target.dtype)
        for part in range(2):
            rows = hat_t[pl.ds(pl.multiple_of((2 * part + at) * shard, 16), shard), :]
            grads = lax.dot_general(rows, turned[...], (((1,), (1,)), ((), ())), preferred_element_type=jnp.float32)
            target[part, :shard, : grads.shape[1]] = grads.astype(jnp.bfloat16)
    scaled = jnp.dot(kv_ref[...], turned[:2 * key_width, :], preferred_element_type=jnp.float32)
    scaled = (scaled + jnp.dot(query_ref[...], turned[2 * key_width:, :], preferred_element_type=jnp.float32)).T
    hidden = x_ref[...].astype(jnp.float32)
    tokens_ref[...] = (mid_ref[...] + norm_back(hidden, scaled)).astype(jnp.bfloat16)


def finish(mine, dq, home, x, hat, w_kv, w_query, mid, cos, sin):
    rows, width = x.shape
    columns = w_kv.shape[1] + w_query.shape[1]
    half = ((2, 256, -(-columns // BLK) * BLK), jnp.bfloat16)
    return in_vmem(
        finish_kernel,
        (half, half, (x.shape, jnp.bfloat16)),
        (mine,),
        (dq, home, x, hat, w_kv, w_query, mid, cos, sin),
        scratch=(((columns, rows), jnp.bfloat16), ((width, rows), jnp.bfloat16)),
        name="finish",
    )


def norm_back(value, grad):
    rms = unit_rms(value)
    hat = value * rms
    return rms * (grad - hat * jnp.mean(grad * hat, axis=-1, keepdims=True))


def out_kernel(attn, x_ref, w_ref, mid_ref, hat_ref):
    rows = attn[:HEADS].reshape(HEADS * HEAD, attn.shape[2]).T
    mid = x_ref[...].astype(jnp.float32) + jnp.dot(rows, w_ref[...], preferred_element_type=jnp.float32)
    mid_ref[...] = mid
    hat_ref[...] = (mid * unit_rms(mid)).astype(jnp.bfloat16)


def project_out(attn, x, w_out):
    return in_vmem(out_kernel, ((x.shape, jnp.float32), (x.shape, jnp.bfloat16)), (), (attn, x, w_out), name="project_out")


def stack_pairs_kernel(mine, own, near, far, far_near, gate_ref, up_ref):
    pieces = (own, near, far, far_near)
    put_rows(mine, [piece.at[0] for piece in pieces], gate_ref)
    put_rows(mine, [piece.at[1] for piece in pieces], up_ref)


def stack_pairs(mine, pieces):
    _, shard, columns = pieces[0].shape
    whole = ((4 * shard, columns), jnp.bfloat16)
    return in_vmem(stack_pairs_kernel, (whole, whole), (mine,), pieces, flops=10**6, name="stack_pairs")


def feed_kernel(hat_own, hat_peer, grad_own, grad_peer, w_gate, w_up, down_t, scaled_keep, scaled_send, out_keep, out_send, act_ref, gate_grad_ref, up_grad_ref, hat_ref, grad_ref):
    rows, width = hat_own.shape
    for step, (hat, grad) in enumerate(((hat_own, grad_own), (hat_peer, grad_peer))):
        hat_ref[step * rows:(step + 1) * rows, :] = hat[...]
        grad_ref[step * rows:(step + 1) * rows, :] = grad[...]
    scaled = out = None
    for start, stop in ((0, 256), (256, 640)):
        cut = slice(start, stop)
        gate = jnp.dot(hat_ref[...], w_gate[:, cut], preferred_element_type=jnp.float32)
        up = jnp.dot(hat_ref[...], w_up[:, cut], preferred_element_type=jnp.float32)
        sigmoid = jax.nn.sigmoid(gate)
        silu = gate * sigmoid
        act = (silu * up).astype(jnp.bfloat16)
        grad_act = jnp.dot(grad_ref[...], down_t[:, cut], preferred_element_type=jnp.float32).astype(jnp.bfloat16).astype(jnp.float32)
        gate_grad = (grad_act * up * sigmoid * (1.0 + gate * (1.0 - sigmoid))).astype(jnp.bfloat16)
        up_grad = (grad_act * silu).astype(jnp.bfloat16)
        act_ref[:, cut], gate_grad_ref[:, cut], up_grad_ref[:, cut] = act, gate_grad, up_grad
        scaled_cut = across(gate_grad, w_gate[:, cut]) + across(up_grad, w_up[:, cut])
        out_cut = across(act, down_t[:, cut])
        scaled, out = (scaled_cut, out_cut) if scaled is None else (scaled + scaled_cut, out + out_cut)
    scaled_keep[...] = scaled[:rows]
    out_keep[...] = out[:rows]
    for target, value in ((scaled_send, scaled), (out_send, out)):
        target[:, :width] = value[rows:].astype(jnp.bfloat16)
        target[:, width:] = jnp.zeros((rows, target.shape[1] - width), jnp.bfloat16)


def feed(hats, grads, w_gate, w_up, down_t):
    rows, width = hats[0].shape
    kept = ((rows, width), jnp.float32)
    sent = ((rows, -(-width // 256) * 256), jnp.bfloat16)
    hidden = ((2 * rows, down_t.shape[1]), jnp.bfloat16)
    both = ((2 * rows, width), jnp.bfloat16)
    return in_vmem(
        feed_kernel,
        (kept, sent, kept, sent, hidden, hidden, hidden),
        (),
        (*hats, *grads, w_gate, w_up, down_t),
        scratch=(both, both),
        flops=6 * 10**9,
        vmem=28, name="feed",
    )


def feed_grads_kernel(*refs):
    hats, grads, near, far, (out_ref, hat_t, grad_t) = refs[:4], refs[4:8], refs[8:11], refs[11:14], refs[14:]
    rows = hats[0].shape[0]
    for step in range(4):
        here = slice(step * rows, (step + 1) * rows)
        hat_t[:, here] = hats[step][...].T
        grad_t[:, here] = grads[step][...].T
    shard = hat_t.shape[0] // 4
    strips = shard // STRIP
    for index, (left, at) in enumerate(((hat_t, 1), (hat_t, 2), (grad_t, 0))):
        for part in range(4):
            some = left[part * shard:(part + 1) * shard, :]
            product = jnp.dot(some[:, : 2 * rows], near[at][...], preferred_element_type=jnp.float32)
            product = product + jnp.dot(some[:, 2 * rows:], far[at][...], preferred_element_type=jnp.float32)
            out_ref[:strips, 4 * index + part] = product.astype(jnp.bfloat16).reshape(strips, STRIP, product.shape[1])
    out_ref[strips:] = jnp.zeros((out_ref.shape[0] - strips,) + out_ref.shape[1:], jnp.bfloat16)


def feed_grads(hats, grads, near, far, ring):
    rows, width = hats[0].shape
    turned = ((width, 4 * rows), jnp.bfloat16)
    return in_vmem(
        feed_grads_kernel,
        (((ring, 12, STRIP, near[0].shape[1]), jnp.bfloat16),),
        (),
        (*hats, *grads, *near, *far),
        scratch=(turned, turned),
        flops=8 * 10**9,
        vmem=28, name="feed_grads",
    )[0]


def mid_kernel(mine, keep, received, far, mid_ref, grad_ref, w_ref, attn, total_ref, send_ref, keep_ref, give_ref, rows_ref):
    width = keep.shape[1]
    shard = width // 4
    scaled = keep[...] + received[:, :width].astype(jnp.float32) + far[...].astype(jnp.float32)
    total = grad_ref[...].astype(jnp.float32) + norm_back(mid_ref[...], scaled)
    total_ref[...] = total
    low = total.astype(jnp.bfloat16)
    send_ref[:HEADS] = across(w_ref[...], low).astype(jnp.bfloat16).reshape(HEADS, HEAD, low.shape[0])
    send_ref[HEADS:] = jnp.zeros((send_ref.shape[0] - HEADS,) + send_ref.shape[1:], jnp.bfloat16)
    rows_ref[...] = attn[:HEADS].reshape(HEADS * HEAD, attn.shape[2])
    core = mine[0] & 1
    for target, at in ((keep_ref, core), (give_ref, 1 - core)):
        target[...] = jnp.zeros(target.shape, target.dtype)
        for part in range(2):
            rows = rows_ref[pl.ds(pl.multiple_of((2 * part + at) * shard, 16), shard), :]
            target[part, :shard, :width] = jnp.dot(rows, low, preferred_element_type=jnp.float32).astype(target.dtype)


def mid_back(mine, keep, received, far, mid, grad, w_out, attn):
    half = ((2, 256, 1024), jnp.bfloat16)
    return in_vmem(
        mid_kernel,
        ((mid.shape, jnp.float32), (attn.shape, jnp.bfloat16), half, half),
        (mine,),
        (keep, received, far, mid, grad, w_out, attn),
        scratch=((mid.shape[::-1], jnp.bfloat16),),
        name="mid_back",
    )


def pack_kernel(key_t, value_t, query, gain, kv_ref, query_ref):
    width = key_t.shape[0]
    scale = gain[...]
    for index, piece in enumerate((key_t, value_t)):
        kv_ref[:, index * width:(index + 1) * width] = (piece[...].astype(jnp.float32).T * scale).astype(jnp.bfloat16)
    query_ref[...] = (query[...].astype(jnp.float32) * scale).astype(jnp.bfloat16)


def pack(w_key, w_value, w_query, gain):
    shard = w_key.shape[0]
    return in_vmem(
        pack_kernel,
        (((shard, 2 * w_key.shape[1]), jnp.bfloat16), (w_query.shape, jnp.bfloat16)),
        (),
        (w_key.T, w_value.T, w_query, gain),
        flops=10**6,
        name="pack",
    )


def as_row(column):
    return jnp.broadcast_to(column, (column.shape[0], BLK)).T[:1]


def last_kernel(total, w_kv, w_query, gain, query_ref, key_ref, value_ref, out_ref, gain_ref):
    shard, width = w_query.shape
    key_width = key_ref.shape[0]
    columns = 2 * key_width + width
    padded = -(-columns // BLK) * BLK
    rows = total[...].reshape(total.shape[0] * total.shape[1], total.shape[2])[:shard].astype(jnp.float32)
    kv, query = rows[:, : 2 * key_width], rows[:, 2 * key_width : columns]
    scale = gain[...]
    gain_sum = jnp.sum(kv * w_kv[...].astype(jnp.float32), axis=1, keepdims=True) + jnp.sum(query * w_query[...].astype(jnp.float32), axis=1, keepdims=True)
    gain_ref[...] = as_row(gain_sum / scale)
    kv = kv * scale
    key_ref[...] = kv[:, :key_width].T
    value_ref[...] = kv[:, key_width:].T
    query_ref[...] = query * scale
    out_ref[...] = rows[:, padded:padded + width]


def last(total, w_kv, w_query, gain):
    shard, width = w_query.shape
    square = (w_query.shape, jnp.float32)
    turned = ((w_kv.shape[1] // 2, shard), jnp.float32)
    query, key, value, out, gain_grad = in_vmem(
        last_kernel, (square, turned, turned, square, ((1, shard), jnp.float32)), (), (total, w_kv, w_query, gain), name="last"
    )
    return gain_grad.reshape(shard), query, key.T, value.T, out


def unpack_kernel(total, w_gate, w_up, gain, gate_ref, up_ref, down_ref, gain_ref):
    shard, part = w_gate.shape[0], total.shape[3]
    strips = shard // STRIP
    scale = gain[...]
    gain_sum = jnp.zeros((shard, 1), jnp.float32)
    for index, (weight, target) in enumerate(((w_gate, gate_ref), (w_up, up_ref))):
        for step in range(4):
            columns = slice(step * part, (step + 1) * part)
            grads = total[:strips, 4 * index + step].reshape(shard, part).astype(jnp.float32)
            gain_sum = gain_sum + jnp.sum(grads * weight[:, columns].astype(jnp.float32), axis=1, keepdims=True)
            target[:, columns] = grads * scale
    for step in range(4):
        down_ref[step * shard:(step + 1) * shard, :] = total[:strips, 8 + step].reshape(shard, part).astype(jnp.float32)
    gain_ref[...] = as_row(gain_sum)


def unpack(total, w_gate, w_up, gain):
    shard, columns = w_gate.shape
    part = total.shape[3]
    full = ((shard, columns), jnp.float32)
    gate, up, down, gain_grad = in_vmem(
        unpack_kernel, (full, full, ((4 * shard, part), jnp.float32), ((1, shard), jnp.float32)), (), (total, w_gate, w_up, gain), vmem=28, name="unpack"
    )
    return gain_grad.reshape(shard), gate, up, down.T


def over_core(value):
    return lax.ppermute(value, "core", SWAP)


def over_chip(value):
    return lax.ppermute(value, "xh", SWAP)


def over_both(value):
    return lax.ppermute(value, FSDP_AXES, ((0, 3), (3, 0), (1, 2), (2, 1)))


def trade(value):
    return lax.ppermute(value, ("xl", "core"), ((0, 0), (1, 2), (2, 1), (3, 3)))


def arrange(pieces, xh, core):
    low = jnp.where(core == 1, pieces[1], pieces[0]), jnp.where(core == 1, pieces[0], pieces[1])
    high = jnp.where(core == 1, pieces[3], pieces[2]), jnp.where(core == 1, pieces[2], pieces[3])
    return jnp.stack([jnp.where(xh == 1, h, l) for l, h in zip(low, high)] + [jnp.where(xh == 1, l, h) for l, h in zip(low, high)])


def exchange(value, axes):
    return lax.all_to_all(value, axes, split_axis=0, concat_axis=0, tiled=True)


def per_device(
    tokens,
    block_order,
    gain_attn,
    w_query,
    w_key,
    w_value,
    w_out,
    gain_mlp,
    w_gate,
    w_up,
    w_down,
    cotangent,
):
    f32, bf16 = jnp.float32, jnp.bfloat16
    xh, core = lax.axis_index("xh"), lax.axis_index("core")
    mine = 2 * xh + core
    own_id = mine.reshape(1)
    row_total, width = tokens.shape[1:]
    shard = w_query.shape[0]
    ff_part = w_down.shape[0]
    groups = lax.axis_size(SEQ_AXES)
    key_width = KV_HEADS * HEAD
    gain_one = gain_attn.astype(f32)[:, None]
    gain_two = gain_mlp.astype(f32)[:, None]

    kv_shard, query_shard = pack(w_key, w_value, w_query, gain_one)
    far_kv, near_kv = over_chip(kv_shard), over_core(kv_shard)
    hidden_low, query_shard = lax.optimization_barrier((trade(tokens[0]), query_shard))
    far_query, near_query = over_chip(query_shard), over_core(query_shard)

    def gate_up(step):
        start = (mine ^ step) * ff_part
        both = [lax.dynamic_slice_in_dim(w, start, ff_part, 1).astype(f32) * gain_two for w in (w_gate, w_up)]
        return jnp.stack(both).astype(bf16)

    gate_up_parts = [gate_up(step) for step in range(4)]
    far_kv, hidden_low, gate_up_parts = lax.optimization_barrier((far_kv, hidden_low, gate_up_parts))

    own_order = lax.dynamic_slice_in_dim(block_order, 2 * groups * core, 2 * groups)
    other_order = lax.dynamic_slice_in_dim(block_order, 2 * groups * (1 - core), 2 * groups)
    key_pos = jnp.concatenate([own_order, other_order])
    query_rank = jnp.sum((own_order[None, :] < own_order[:, None]).astype(jnp.int32), axis=1)
    hit = query_rank[None, :] == jnp.arange(2 * groups, dtype=jnp.int32)[:, None]
    sorted_pos = jnp.sum(jnp.where(hit, own_order[None, :], 0), axis=1)
    sorted_id = jnp.sum(jnp.where(hit, jnp.arange(2 * groups, dtype=jnp.int32)[None, :], 0), axis=1)
    here = lax.axis_index(SEQ_AXES)
    own_blocks = lax.dynamic_slice_in_dim(own_order, 2 * here, 2)
    row = jnp.arange(row_total, dtype=jnp.int32)
    own_pos = jnp.where(row < BLK, own_blocks[0] * BLK + row, own_blocks[1] * BLK + row - BLK)
    inverse_freq = THETA ** (-jnp.arange(HEAD // 2, dtype=f32) / (HEAD // 2))
    angles = inverse_freq[:, None] * own_pos.astype(f32)[None, :]
    cos_table, sin_table = jnp.cos(angles), jnp.sin(angles)

    normed_one, kv_send, kv_full = project_keys(own_id, hidden_low, (kv_shard, near_kv, far_kv, over_core(far_kv)), cos_table, sin_table, groups)
    query_send, query_full = project_queries(own_id, normed_one, (query_shard, near_query, far_query, over_core(far_query)), cos_table, sin_table, groups)
    kv_own, query_send, upstream = lax.optimization_barrier((exchange(kv_send, SEQ_AXES), query_send, trade(cotangent[0])))
    query_in = exchange(query_send, SEQ_AXES)
    kv_other = over_core(kv_own)

    kv_other, w_out, upstream, gate_up_parts = lax.optimization_barrier((kv_other, w_out, upstream, gate_up_parts))
    far_out, far_upstream = over_chip(w_out), over_chip(upstream)
    far_weights = over_chip(gate_up_parts[2]), over_both(gate_up_parts[3])
    out_send, out_blocks, lse, kv_sorted, kv_turned = attend(key_pos, query_rank, sorted_pos, sorted_id, query_in, kv_own, kv_other)
    out_send, far_out, far_upstream, far_weights = lax.optimization_barrier((out_send, far_out, far_upstream, far_weights))
    out_full = stack_rows(own_id, (w_out, over_core(w_out), far_out, over_core(far_out)))
    weights = (gate_up_parts[0], over_core(gate_up_parts[1])) + far_weights
    upstream_all = (upstream, over_core(upstream), far_upstream, over_core(far_upstream))

    gate_part, up_part = stack_pairs(own_id, weights)
    attn, out_full, gate_part, up_part = lax.optimization_barrier((exchange(out_send, SEQ_AXES), out_full, gate_part, up_part))
    mid_state, second_hat = project_out(attn, hidden_low, out_full)
    far_hat = over_chip(second_hat)
    near_hat = over_core(second_hat)
    down_turned = w_down.T
    near_side = feed((second_hat, near_hat), upstream_all[:2], gate_part, up_part, down_turned)
    far_hat, near_side = lax.optimization_barrier((far_hat, near_side))
    normed_all = second_hat, near_hat, far_hat, over_core(far_hat)
    far_side = feed(normed_all[2:], upstream_all[2:], gate_part, up_part, down_turned)
    scaled_received = over_core(near_side[1])
    far_send = (far_side[0] + over_core(far_side[1])[:, :width].astype(f32)).astype(bf16)
    far_send, normed_all, scaled_received = lax.optimization_barrier((far_send, normed_all, scaled_received))
    scaled_far = over_chip(far_send)
    ring = lax.axis_size(SEQ_AXES)
    stacked = feed_grads(normed_all, upstream_all, near_side[4:], far_side[4:], ring)
    scaled_far, stacked = lax.optimization_barrier((scaled_far, stacked))
    reduced = lax.psum_scatter(stacked.reshape(ring, 12 * STRIP, ff_part), SEQ_AXES, scatter_dimension=0, tiled=True)[0]

    grad_mid, grad_send, out_grad_keep, out_grad_give = mid_back(own_id, near_side[0], scaled_received, scaled_far, mid_state, upstream, out_full, attn)
    grad_group = exchange(grad_send, SEQ_AXES)
    ctx = lax.axis_size(CTX_AXES)
    slab = 8
    out_chip = (out_grad_keep.astype(f32) + over_core(out_grad_give).astype(f32)).astype(bf16).reshape(2 * ctx, slab, -1)
    result_received = over_core(near_side[3])
    result_send = (far_side[2] + over_core(far_side[3])[:, :width].astype(f32)).astype(bf16)
    grad_group, out_chip = lax.optimization_barrier((grad_group, out_chip))

    out_chips = exchange(out_chip, CHIP_AXES)

    dq, dkv_own, dkv_other = attend_back(key_pos, query_rank, sorted_pos, sorted_id, query_in, grad_group, out_blocks, lse, kv_sorted, kv_turned)
    dkv_other, reduced, out_chips, result_send = lax.optimization_barrier((dkv_other, reduced, out_chips, result_send))
    result_far = over_chip(result_send)
    out_sum = jnp.sum(out_chips.astype(f32), axis=0).astype(bf16)
    dq_home = exchange(dq, SEQ_AXES)
    dkv_received = over_core(dkv_other)
    reduced = (reduced.astype(f32) + lax.ppermute(reduced, "xl", SWAP).astype(f32)).astype(bf16).reshape(3, 4, STRIP, ff_part)
    dkv = (dkv_own + dkv_received.astype(f32)).astype(bf16)
    dq_home, dkv, reduced = lax.optimization_barrier((dq_home, dkv, reduced))
    part = lambda step: lax.dynamic_index_in_dim(reduced[:2], mine ^ step, 1, keepdims=False)
    pieces = arrange([part(0), over_core(part(1)), over_chip(part(2)), over_both(part(3))], xh, core).transpose(1, 0, 2, 3)
    pieces = jnp.concatenate([pieces, reduced[2:]]).reshape(12, STRIP, ff_part)
    result = mid_state + near_side[2] + result_received[:, :width].astype(f32) + result_far.astype(f32)
    home, pieces, result = lax.optimization_barrier((exchange(dkv, SEQ_AXES), pieces, result.astype(bf16)))
    block_out = trade(result)
    whole = lax.all_gather(pieces, SEQ_AXES, axis=0, tiled=False)
    gain_two_shard, gate_shard, up_shard, down_shard = unpack(whole, w_gate, w_up, gain_two)

    keep, give, grad_tokens = finish(own_id, dq_home, home, hidden_low, normed_one, kv_full, query_full, grad_mid, cos_table, sin_table)
    grad_tokens = trade(grad_tokens)
    columns = keep.shape[-1]
    chip_sum = (keep.astype(f32) + over_core(give).astype(f32)).astype(bf16).reshape(2 * ctx, slab, columns)
    qkv_chips, grad_tokens, block_out = lax.optimization_barrier((exchange(chip_sum, CHIP_AXES), grad_tokens, block_out))
    qkv_sum = jnp.sum(qkv_chips.astype(f32), axis=0).astype(bf16)
    summed = jnp.concatenate([qkv_sum, out_sum], axis=1)
    final = exchange(jnp.broadcast_to(summed[None], (ctx,) + summed.shape), CTX_AXES)
    final, gate_shard = lax.optimization_barrier((final, gate_shard))
    gain_one_shard, query_shard, key_shard, value_shard, out_shard = last(final, kv_shard, query_shard, gain_one)
    return (
        block_out[None],
        grad_tokens.astype(f32)[None],
        gain_one_shard,
        query_shard,
        key_shard,
        value_shard,
        out_shard,
        gain_two_shard,
        gate_shard,
        up_shard,
        down_shard,
    )


def solution(mesh):
    fine = Mesh(mesh.devices.reshape(2, 4, 4, 2, 2), ("xl", "z", "y", "xh", "core"))
    rows = P(FSDP_AXES, CTX_AXES, None)
    gain = P(FSDP_AXES)
    weight = P(FSDP_AXES, None)
    return jax.shard_map(
        per_device,
        mesh=fine,
        in_specs=(rows, P(), gain, weight, weight, weight, weight, gain, weight, weight, weight, rows),
        out_specs=(rows, rows, gain, weight, weight, weight, weight, gain, weight, weight, weight),
        check_vma=False,
    )
```

```python
import functools
import math

import jax
import jax.numpy as jnp
from jax import lax
from jax.experimental import pallas as pl
from jax.experimental.pallas import tpu as pltpu
from jax.sharding import Mesh
from jax.sharding import PartitionSpec as P

HEADS = 15
KV_HEADS = 5
EPSILON = 1e-05
THETA = 100000.0
SEQ_AXES = ("z", "y")
CTX_AXES = ("xl", "z", "y")
CHIP_AXES = ("xh", "xl", "z", "y")
FSDP_AXES = ("xh", "core")
CUBE_AXES = ("xl", "xh", "core")
SWAP = ((0, 1), (1, 0))
STRIP = 16
BLK = 128
HEAD = 64
EXP_SCALE = math.log2(math.e) / 8.0
MASKED = -1e30


def attend_kernel(key_pos, query_rank, sorted_pos, sorted_id, q_ref, own_in, other_in, send_ref, out_ref, lse_ref, kv_ref, kvt_ref, ones_v, q_sorted, *, big, small, edge_size, blocks):
    groups, width = own_in.shape[0], HEAD
    rows = blocks * BLK
    is_key = lax.broadcasted_iota(jnp.int32, (BLK, 2 * width), 1) < width

    def place(index, _):
        for side, source in enumerate((own_in, other_in)):
            for half in range(2):
                where = pl.multiple_of(key_pos[side * 2 * groups + 2 * index + half] * BLK, BLK)
                piece = source[index, :, half * BLK:(half + 1) * BLK]
                kvt_ref[:, pl.ds(where, BLK)] = piece
                turned = piece.T
                kv_ref[pl.ds(where, BLK), :] = turned
                ones_v[pl.ds(where, BLK), :] = jnp.where(is_key, jnp.ones_like(turned), turned)
        for half in range(2):
            query = q_ref[index, :, half * BLK:(half + 1) * BLK]
            query = jnp.concatenate([query, jnp.zeros_like(query)], axis=0)
            q_sorted[pl.ds(pl.multiple_of(query_rank[2 * index + half] * BLK, BLK), BLK), :] = query.T
        return 0

    lax.fori_loop(0, groups, place, 0, unroll=4)

    def tile(index, _):
        low, high = sorted_pos[blocks * index], sorted_pos[blocks * index + blocks - 1]
        query = q_sorted[pl.ds(pl.multiple_of(index * rows, rows), rows), :]
        row = lax.broadcasted_iota(jnp.int32, (rows, 1), 0)
        place_of = row + low * BLK
        for part in range(1, blocks):
            place_of = jnp.where(row >= part * BLK, row + (sorted_pos[blocks * index + part] - part) * BLK, place_of)

        def step(start, carry, size, masked):
            top, total = carry
            scores = lax.dot_general(query, kv_ref[pl.ds(start, size), :], (((1,), (1,)), ((), ())), preferred_element_type=jnp.float32)
            if masked:
                column = start + lax.broadcasted_iota(jnp.int32, scores.shape, 1)
                scores = jnp.where(column <= place_of, scores, MASKED)
            new_top = jnp.maximum(top, jnp.max(scores, axis=1, keepdims=True))
            weights = jnp.exp2((scores - new_top) * EXP_SCALE).astype(jnp.bfloat16)
            factor = jnp.exp2((top - new_top) * EXP_SCALE)
            added = jnp.dot(weights, ones_v[pl.ds(start, size), :], preferred_element_type=jnp.float32)
            return new_top, total * factor + added

        def full(count, carry):
            for part in range(big // small):
                carry = step(pl.multiple_of(count * big + part * small, small), carry, small, False)
            return carry

        def edge(count, carry):
            return step(pl.multiple_of(count * edge_size, edge_size), carry, edge_size, True)

        carry = (jnp.full((rows, 1), MASKED, jnp.float32), jnp.zeros((rows, 2 * width), jnp.float32))
        done = low * BLK // big
        carry = lax.fori_loop(0, done, full, carry)
        top, total = lax.fori_loop(done * (big // edge_size), (high * BLK + BLK + edge_size - 1) // edge_size, edge, carry)
        lse = (top * EXP_SCALE + jnp.log2(total)).T
        total = total.T
        result = total[width:] / total[:1]
        for part in range(blocks):
            ident = sorted_id[blocks * index + part]
            piece = result[:, part * BLK:(part + 1) * BLK]
            out_ref[ident] = piece
            send_ref[ident // 2, :, pl.ds(pl.multiple_of(ident % 2 * BLK, BLK), BLK)] = piece.astype(jnp.bfloat16)
            lse_ref[ident] = lse[:8, part * BLK:(part + 1) * BLK]
        return 0

    lax.fori_loop(0, 2 * groups // blocks, tile, 0)


def attend(key_pos, query_rank, sorted_pos, sorted_id, q, own_in, other_in, big=1024, small=1024, edge_size=512, blocks=4):
    groups, width = own_in.shape[0], HEAD
    total = 4 * groups * BLK
    vm = pl.BlockSpec(memory_space=pltpu.VMEM)
    sm = pl.BlockSpec(memory_space=pltpu.SMEM)
    return pl.pallas_call(
        functools.partial(attend_kernel, big=big, small=small, edge_size=edge_size, blocks=blocks),
        out_shape=(
            jax.ShapeDtypeStruct((groups, width, 2 * BLK), jnp.bfloat16),
            jax.ShapeDtypeStruct((2 * groups, width, BLK), jnp.float32),
            jax.ShapeDtypeStruct((2 * groups, 8, BLK), jnp.float32),
            jax.ShapeDtypeStruct((total, 2 * width), jnp.bfloat16),
            jax.ShapeDtypeStruct((2 * width, total), jnp.bfloat16),
        ),
        in_specs=[sm] * 4 + [vm] * 3,
        out_specs=(vm,) * 5,
        scratch_shapes=[
            pltpu.VMEM((total, 2 * width), jnp.bfloat16),
            pltpu.VMEM((2 * groups * BLK, 2 * width), jnp.bfloat16),
        ],
        compiler_params=pltpu.CompilerParams(vmem_limit_bytes=60 * 2**20),
        cost_estimate=pl.CostEstimate(flops=40 * 10**9, bytes_accessed=10**7, transcendentals=2 * 10**7),
        name="attend",
    )(key_pos, query_rank, sorted_pos, sorted_id, q, own_in, other_in)


def back_kernel(key_pos, query_rank, sorted_pos, sorted_id, q_ref, da_ref, out_ref, lse_ref, kv_ref, kvt_ref, dq_ref, own_ref, other_ref, dkv, q_sorted, da_sorted, *, big, small, edge_size, flip):
    groups, width = q_ref.shape[0], HEAD

    def place(index, _):
        for half in range(2):
            rank = query_rank[2 * index + half]
            q_sorted[rank] = q_ref[index, :, half * BLK:(half + 1) * BLK]
            da_sorted[rank] = da_ref[index, :, half * BLK:(half + 1) * BLK]
        return 0

    lax.fori_loop(0, groups, place, 0)

    def clear(index, _):
        dkv[pl.ds(pl.multiple_of(index * BLK, BLK), BLK), :] = jnp.zeros((BLK, 2 * width), jnp.float32)
        return 0

    lax.fori_loop(0, 4 * groups, clear, 0)

    def tile(index, _):
        low, high = sorted_pos[2 * index], sorted_pos[2 * index + 1]
        first_id, second_id = sorted_id[2 * index], sorted_id[2 * index + 1]
        query = jnp.concatenate([q_sorted[2 * index], q_sorted[2 * index + 1]], axis=1)
        grad = jnp.concatenate([da_sorted[2 * index], da_sorted[2 * index + 1]], axis=1)
        value = jnp.concatenate([out_ref[first_id], out_ref[second_id]], axis=1)
        lse = jnp.concatenate([lse_ref[first_id][:1], lse_ref[second_id][:1]], axis=1)
        delta = jnp.sum(grad.astype(jnp.float32) * value, axis=0, keepdims=True)
        none = jnp.zeros_like(query)
        both = jnp.concatenate([jnp.concatenate([query, none], axis=1), jnp.concatenate([none, grad], axis=1)], axis=0)
        both_t = both.T
        lane = lax.broadcasted_iota(jnp.int32, (1, 2 * BLK), 1)
        place_of = jnp.where(lane < BLK, low * BLK + lane, (high - 1) * BLK + lane)

        def step(start, total, size, masked):
            keys = kv_ref[pl.ds(start, size), :]
            pair = jnp.dot(keys, both, preferred_element_type=jnp.float32)
            weights = jnp.exp2(pair[:, :2 * BLK] * EXP_SCALE - lse)
            if masked:
                row = start + lax.broadcasted_iota(jnp.int32, weights.shape, 0)
                weights = jnp.where(row <= place_of, weights, 0.0)
            grad_scores = (weights * (pair[:, 2 * BLK:] - delta)).astype(jnp.bfloat16)
            weights = weights.astype(jnp.bfloat16)
            dkv[pl.ds(start, size), :] += jnp.dot(jnp.concatenate([grad_scores, weights], axis=1), both_t, preferred_element_type=jnp.float32)
            if flip:
                return total + lax.dot_general(grad_scores, keys, (((0,), (0,)), ((), ())), preferred_element_type=jnp.float32)
            return total + jnp.dot(kvt_ref[:width, pl.ds(start, size)], grad_scores, preferred_element_type=jnp.float32)

        def full(count, carry):
            for part in range(big // small):
                carry = step(pl.multiple_of(count * big + part * small, small), carry, small, False)
            return carry

        def edge(count, carry):
            return step(pl.multiple_of(count * edge_size, edge_size), carry, edge_size, True)

        done = low * BLK // big
        total = jnp.zeros((2 * BLK, 2 * width) if flip else (width, 2 * BLK), jnp.float32)
        total = lax.fori_loop(0, done, full, total)
        total = lax.fori_loop(done * (big // edge_size), (high * BLK + BLK + edge_size - 1) // edge_size, edge, total) * 0.125
        if flip:
            total = total.T[:width]
        for half, ident in enumerate((first_id, second_id)):
            dq_ref[ident // 2, :, pl.ds(pl.multiple_of(ident % 2 * BLK, BLK), BLK)] = total[:, half * BLK:(half + 1) * BLK].astype(jnp.bfloat16)
        return 0

    lax.fori_loop(0, groups, tile, 0)
    factor = jnp.where(lax.broadcasted_iota(jnp.int32, (1, 2 * width), 1) < width, 0.125, 1.0)

    def spread(index, _):
        for side, target in enumerate((own_ref, other_ref)):
            for half in range(2):
                where = pl.multiple_of(key_pos[side * 2 * groups + 2 * index + half] * BLK, BLK)
                target[index, :, half * BLK:(half + 1) * BLK] = (dkv[pl.ds(where, BLK), :] * factor).astype(target.dtype)
        return 0

    lax.fori_loop(0, groups, spread, 0)


def attend_back(key_pos, query_rank, sorted_pos, sorted_id, q, da, out, lse, kv, kvt, big=1024, small=1024, edge_size=512, flip=False):
    groups, width = q.shape[0], HEAD
    total = 4 * groups * BLK
    vm = pl.BlockSpec(memory_space=pltpu.VMEM)
    sm = pl.BlockSpec(memory_space=pltpu.SMEM)
    return pl.pallas_call(
        functools.partial(back_kernel, big=big, small=small, edge_size=edge_size, flip=flip),
        out_shape=(
            jax.ShapeDtypeStruct((groups, width, 2 * BLK), jnp.bfloat16),
            jax.ShapeDtypeStruct((groups, 2 * width, 2 * BLK), jnp.float32),
            jax.ShapeDtypeStruct((groups, 2 * width, 2 * BLK), jnp.bfloat16),
        ),
        in_specs=[sm] * 4 + [vm] * 6,
        out_specs=(vm,) * 3,
        scratch_shapes=[
            pltpu.VMEM((total, 2 * width), jnp.float32),
            pltpu.VMEM((2 * groups, width, BLK), jnp.bfloat16),
            pltpu.VMEM((2 * groups, width, BLK), jnp.bfloat16),
        ],
        compiler_params=pltpu.CompilerParams(vmem_limit_bytes=60 * 2**20),
        cost_estimate=pl.CostEstimate(flops=60 * 10**9, bytes_accessed=10**7, transcendentals=2 * 10**7),
        name="attend_back",
    )(key_pos, query_rank, sorted_pos, sorted_id, q, da, out, lse, kv, kvt)


def in_vmem(kernel, out_shape, scalars, arrays, scratch=(), flops=10**9, name=None):
    vm = pl.BlockSpec(memory_space=pltpu.VMEM)
    return pl.pallas_call(
        kernel,
        out_shape=tuple(jax.ShapeDtypeStruct(shape, dtype) for shape, dtype in out_shape),
        in_specs=[pl.BlockSpec(memory_space=pltpu.SMEM)] * len(scalars) + [vm] * len(arrays),
        out_specs=(vm,) * len(out_shape),
        scratch_shapes=[pltpu.VMEM(shape, dtype) for shape, dtype in scratch],
        compiler_params=pltpu.CompilerParams(vmem_limit_bytes=60 * 2**20),
        cost_estimate=pl.CostEstimate(flops=flops, bytes_accessed=10**7, transcendentals=0),
        name=name,
    )(*scalars, *arrays)


def across(left, right):
    return lax.dot_general(left, right, (((1,), (1,)), ((), ())), preferred_element_type=jnp.float32)


def unit_rms(value):
    return lax.rsqrt(jnp.mean(value * value, axis=-1, keepdims=True) + EPSILON)


def put_rows(mine, pieces, target):
    shard = pieces[0].shape[0]
    for step, piece in enumerate(pieces):
        target[pl.ds(pl.multiple_of((mine[0] ^ step) * shard, 16), shard), :] = piece[...]


def turn(pair, cos, sin):
    half = HEAD // 2
    front, behind = pair[:half], pair[half:]
    return jnp.concatenate([front * cos - behind * sin, behind * cos + front * sin], axis=0).astype(jnp.bfloat16)


def turn_back(pair, cos, sin):
    return turn(pair, cos, -sin)


def project_keys_kernel(mine, x_ref, own, near, far, far_near, cos_ref, sin_ref, hat_ref, send_ref, w_ref):
    put_rows(mine, (own, near, far, far_near), w_ref)
    hidden = x_ref[...].astype(jnp.float32)
    hat = (hidden * unit_rms(hidden)).astype(jnp.bfloat16)
    hat_ref[...] = hat
    key_width = KV_HEADS * HEAD
    per = HEADS // KV_HEADS
    lin = jnp.dot(hat, w_ref[...], preferred_element_type=jnp.float32).T
    for head in range(KV_HEADS):
        key = turn(lin[head * HEAD:(head + 1) * HEAD], cos_ref[...], sin_ref[...])
        value = lin[key_width + head * HEAD:key_width + (head + 1) * HEAD].astype(jnp.bfloat16)
        for query in range(per):
            send_ref[head * per + query, :HEAD] = key
            send_ref[head * per + query, HEAD:] = value
    send_ref[HEADS:] = jnp.zeros((send_ref.shape[0] - HEADS,) + send_ref.shape[1:], jnp.bfloat16)


def project_keys(mine, x, pieces, cos, sin, groups):
    rows, width = x.shape
    columns = pieces[0].shape[1]
    return in_vmem(
        project_keys_kernel,
        ((x.shape, jnp.bfloat16), ((groups, 2 * HEAD, rows), jnp.bfloat16), ((width, columns), jnp.bfloat16)),
        (mine,),
        (x, *pieces, cos, sin),
        name="project_keys",
    )


def project_queries_kernel(mine, hat_ref, own, near, far, far_near, cos_ref, sin_ref, send_ref, w_ref):
    put_rows(mine, (own, near, far, far_near), w_ref)
    per = HEADS // KV_HEADS
    for group in range(KV_HEADS):
        columns = slice(group * per * HEAD, (group + 1) * per * HEAD)
        lin = jnp.dot(hat_ref[...], w_ref[:, columns], preferred_element_type=jnp.float32).T
        for query in range(per):
            send_ref[group * per + query] = turn(lin[query * HEAD:(query + 1) * HEAD], cos_ref[...], sin_ref[...])
    send_ref[HEADS:] = jnp.zeros((send_ref.shape[0] - HEADS,) + send_ref.shape[1:], jnp.bfloat16)


def project_queries(mine, hat, pieces, cos, sin, groups):
    rows, width = hat.shape
    columns = pieces[0].shape[1]
    return in_vmem(
        project_queries_kernel,
        (((groups, HEAD, rows), jnp.bfloat16), ((width, columns), jnp.bfloat16)),
        (mine,),
        (hat, *pieces, cos, sin),
        name="project_queries",
    )


def stack_rows_kernel(mine, own, near, far, far_near, out_ref):
    put_rows(mine, (own, near, far, far_near), out_ref)


def stack_rows(mine, pieces):
    shard, columns = pieces[0].shape
    return in_vmem(stack_rows_kernel, (((4 * shard, columns), jnp.bfloat16),), (mine,), pieces, flops=10**6, name="stack_rows")[0]


def finish_kernel(mine, dq_ref, home, x_ref, hat_ref, kv_ref, query_ref, mid_ref, cos_ref, sin_ref, keep_ref, give_ref, tokens_ref, turned, hat_t):
    shard = query_ref.shape[0] // 4
    cos, sin = cos_ref[...], sin_ref[...]
    key_width = KV_HEADS * HEAD
    per = HEADS // KV_HEADS

    for head in range(KV_HEADS):
        total = sum(home[head * per + query].astype(jnp.float32) for query in range(per))
        total = jnp.concatenate([total[:, :BLK].T, total[:, BLK:].T], axis=1)
        turned[head * HEAD:(head + 1) * HEAD, :] = turn_back(total[:HEAD], cos, sin)
        turned[key_width + head * HEAD:key_width + (head + 1) * HEAD, :] = total[HEAD:].astype(jnp.bfloat16)
        for query in range(per):
            start = 2 * key_width + (head * per + query) * HEAD
            turned[start:start + HEAD, :] = turn_back(dq_ref[head * per + query].astype(jnp.float32), cos, sin)
    hat_t[...] = hat_ref[...].T
    core = mine[0] & 1
    for target, at in ((keep_ref, core), (give_ref, 1 - core)):
        target[...] = jnp.zeros(target.shape, target.dtype)
        for part in range(2):
            rows = hat_t[pl.ds(pl.multiple_of((2 * part + at) * shard, 16), shard), :]
            grads = lax.dot_general(rows, turned[...], (((1,), (1,)), ((), ())), preferred_element_type=jnp.float32)
            target[part, :shard, : grads.shape[1]] = grads.astype(jnp.bfloat16)
    scaled = jnp.dot(kv_ref[...], turned[:2 * key_width, :], preferred_element_type=jnp.float32)
    scaled = (scaled + jnp.dot(query_ref[...], turned[2 * key_width:, :], preferred_element_type=jnp.float32)).T
    hidden = x_ref[...].astype(jnp.float32)
    tokens_ref[...] = (mid_ref[...] + norm_back(hidden, scaled)).astype(jnp.bfloat16)


def finish(mine, dq, home, x, hat, w_kv, w_query, mid, cos, sin):
    rows, width = x.shape
    columns = w_kv.shape[1] + w_query.shape[1]
    half = ((2, 256, -(-columns // BLK) * BLK), jnp.bfloat16)
    return in_vmem(
        finish_kernel,
        (half, half, (x.shape, jnp.bfloat16)),
        (mine,),
        (dq, home, x, hat, w_kv, w_query, mid, cos, sin),
        scratch=(((columns, rows), jnp.bfloat16), ((width, rows), jnp.bfloat16)),
        name="finish",
    )


def norm_back(value, grad):
    rms = unit_rms(value)
    hat = value * rms
    return rms * (grad - hat * jnp.mean(grad * hat, axis=-1, keepdims=True))


def out_kernel(attn, x_ref, w_ref, mid_ref, hat_ref):
    rows = attn[:HEADS].reshape(HEADS * HEAD, attn.shape[2]).T
    mid = x_ref[...].astype(jnp.float32) + jnp.dot(rows, w_ref[...], preferred_element_type=jnp.float32)
    mid_ref[...] = mid
    hat_ref[...] = (mid * unit_rms(mid)).astype(jnp.bfloat16)


def project_out(attn, x, w_out):
    return in_vmem(out_kernel, ((x.shape, jnp.float32), (x.shape, jnp.bfloat16)), (), (attn, x, w_out), name="project_out")


def stack_pairs_kernel(mine, own, near, far, far_near, gate_ref, up_ref):
    pieces = (own, near, far, far_near)
    put_rows(mine, [piece.at[0] for piece in pieces], gate_ref)
    put_rows(mine, [piece.at[1] for piece in pieces], up_ref)


def stack_pairs(mine, pieces):
    _, shard, columns = pieces[0].shape
    whole = ((4 * shard, columns), jnp.bfloat16)
    return in_vmem(stack_pairs_kernel, (whole, whole), (mine,), pieces, flops=10**6, name="stack_pairs")


def feed_kernel(hat_own, hat_peer, grad_own, grad_peer, w_gate, w_up, down_t, scaled_keep, scaled_send, out_keep, out_send, act_ref, gate_grad_ref, up_grad_ref, hat_ref, grad_ref):
    rows, width = hat_own.shape
    for step, (hat, grad) in enumerate(((hat_own, grad_own), (hat_peer, grad_peer))):
        hat_ref[step * rows:(step + 1) * rows, :] = hat[...]
        grad_ref[step * rows:(step + 1) * rows, :] = grad[...]
    scaled = out = None
    for start, stop in ((0, 256), (256, 640)):
        cut = slice(start, stop)
        gate = jnp.dot(hat_ref[...], w_gate[:, cut], preferred_element_type=jnp.float32)
        up = jnp.dot(hat_ref[...], w_up[:, cut], preferred_element_type=jnp.float32)
        sigmoid = jax.nn.sigmoid(gate)
        silu = gate * sigmoid
        act = (silu * up).astype(jnp.bfloat16)
        grad_act = jnp.dot(grad_ref[...], down_t[:, cut], preferred_element_type=jnp.float32).astype(jnp.bfloat16).astype(jnp.float32)
        gate_grad = (grad_act * up * sigmoid * (1.0 + gate * (1.0 - sigmoid))).astype(jnp.bfloat16)
        up_grad = (grad_act * silu).astype(jnp.bfloat16)
        act_ref[:, cut], gate_grad_ref[:, cut], up_grad_ref[:, cut] = act, gate_grad, up_grad
        scaled_cut = across(gate_grad, w_gate[:, cut]) + across(up_grad, w_up[:, cut])
        out_cut = across(act, down_t[:, cut])
        scaled, out = (scaled_cut, out_cut) if scaled is None else (scaled + scaled_cut, out + out_cut)
    scaled_keep[...] = scaled[:rows]
    out_keep[...] = out[:rows]
    for target, value in ((scaled_send, scaled), (out_send, out)):
        target[:, :width] = value[rows:].astype(jnp.bfloat16)
        target[:, width:] = jnp.zeros((rows, target.shape[1] - width), jnp.bfloat16)


def feed(hats, grads, w_gate, w_up, down_t):
    rows, width = hats[0].shape
    kept = ((rows, width), jnp.float32)
    sent = ((rows, -(-width // 256) * 256), jnp.bfloat16)
    hidden = ((2 * rows, down_t.shape[1]), jnp.bfloat16)
    both = ((2 * rows, width), jnp.bfloat16)
    return in_vmem(
        feed_kernel,
        (kept, sent, kept, sent, hidden, hidden, hidden),
        (),
        (*hats, *grads, w_gate, w_up, down_t),
        scratch=(both, both),
        flops=6 * 10**9,
        name="feed",
    )


def feed_grads_kernel(*refs):
    hats, grads, near, far, (out_ref, hat_t, grad_t) = refs[:4], refs[4:8], refs[8:11], refs[11:14], refs[14:]
    rows = hats[0].shape[0]
    for step in range(4):
        here = slice(step * rows, (step + 1) * rows)
        hat_t[:, here] = hats[step][...].T
        grad_t[:, here] = grads[step][...].T
    shard = hat_t.shape[0] // 4
    strips = shard // STRIP
    for index, (left, at) in enumerate(((hat_t, 1), (hat_t, 2), (grad_t, 0))):
        for part in range(4):
            some = left[part * shard:(part + 1) * shard, :]
            product = jnp.dot(some[:, : 2 * rows], near[at][...], preferred_element_type=jnp.float32)
            product = product + jnp.dot(some[:, 2 * rows:], far[at][...], preferred_element_type=jnp.float32)
            out_ref[:strips, 4 * index + part] = product.astype(jnp.bfloat16).reshape(strips, STRIP, product.shape[1])
    out_ref[strips:] = jnp.zeros((out_ref.shape[0] - strips,) + out_ref.shape[1:], jnp.bfloat16)


def feed_grads(hats, grads, near, far, ring):
    rows, width = hats[0].shape
    turned = ((width, 4 * rows), jnp.bfloat16)
    return in_vmem(
        feed_grads_kernel,
        (((ring, 12, STRIP, near[0].shape[1]), jnp.bfloat16),),
        (),
        (*hats, *grads, *near, *far),
        scratch=(turned, turned),
        flops=8 * 10**9,
        name="feed_grads",
    )[0]


def mid_kernel(mine, keep, received, far, mid_ref, grad_ref, w_ref, attn, total_ref, send_ref, keep_ref, give_ref, rows_ref):
    width = keep.shape[1]
    shard = width // 4
    scaled = keep[...] + received[:, :width].astype(jnp.float32) + far[...].astype(jnp.float32)
    total = grad_ref[...].astype(jnp.float32) + norm_back(mid_ref[...], scaled)
    total_ref[...] = total
    low = total.astype(jnp.bfloat16)
    send_ref[:HEADS] = across(w_ref[...], low).astype(jnp.bfloat16).reshape(HEADS, HEAD, low.shape[0])
    send_ref[HEADS:] = jnp.zeros((send_ref.shape[0] - HEADS,) + send_ref.shape[1:], jnp.bfloat16)
    rows_ref[...] = attn[:HEADS].reshape(HEADS * HEAD, attn.shape[2])
    core = mine[0] & 1
    for target, at in ((keep_ref, core), (give_ref, 1 - core)):
        target[...] = jnp.zeros(target.shape, target.dtype)
        for part in range(2):
            rows = rows_ref[pl.ds(pl.multiple_of((2 * part + at) * shard, 16), shard), :]
            target[part, :shard, :width] = jnp.dot(rows, low, preferred_element_type=jnp.float32).astype(target.dtype)


def mid_back(mine, keep, received, far, mid, grad, w_out, attn):
    half = ((2, 256, 1024), jnp.bfloat16)
    return in_vmem(
        mid_kernel,
        ((mid.shape, jnp.float32), (attn.shape, jnp.bfloat16), half, half),
        (mine,),
        (keep, received, far, mid, grad, w_out, attn),
        scratch=((mid.shape[::-1], jnp.bfloat16),),
        name="mid_back",
    )


def pack_kernel(key_t, value_t, query, gain, kv_ref, query_ref):
    width = key_t.shape[0]
    scale = gain[...]
    for index, piece in enumerate((key_t, value_t)):
        kv_ref[:, index * width:(index + 1) * width] = (piece[...].astype(jnp.float32).T * scale).astype(jnp.bfloat16)
    query_ref[...] = (query[...].astype(jnp.float32) * scale).astype(jnp.bfloat16)


def pack(w_key, w_value, w_query, gain):
    shard = w_key.shape[0]
    return in_vmem(
        pack_kernel,
        (((shard, 2 * w_key.shape[1]), jnp.bfloat16), (w_query.shape, jnp.bfloat16)),
        (),
        (w_key.T, w_value.T, w_query, gain),
        flops=10**6,
        name="pack",
    )


def as_row(column):
    return jnp.broadcast_to(column, (column.shape[0], BLK)).T[:1]


def last_kernel(total, w_kv, w_query, gain, query_ref, key_ref, value_ref, out_ref, gain_ref):
    shard, width = w_query.shape
    key_width = key_ref.shape[0]
    columns = 2 * key_width + width
    padded = -(-columns // BLK) * BLK
    rows = total[...].reshape(total.shape[0] * total.shape[1], total.shape[2])[:shard].astype(jnp.float32)
    kv, query = rows[:, : 2 * key_width], rows[:, 2 * key_width : columns]
    scale = gain[...]
    gain_sum = jnp.sum(kv * w_kv[...].astype(jnp.float32), axis=1, keepdims=True) + jnp.sum(query * w_query[...].astype(jnp.float32), axis=1, keepdims=True)
    gain_ref[...] = as_row(gain_sum / scale)
    kv = kv * scale
    key_ref[...] = kv[:, :key_width].T
    value_ref[...] = kv[:, key_width:].T
    query_ref[...] = query * scale
    out_ref[...] = rows[:, padded:padded + width]


def last(total, w_kv, w_query, gain):
    shard, width = w_query.shape
    square = (w_query.shape, jnp.float32)
    turned = ((w_kv.shape[1] // 2, shard), jnp.float32)
    query, key, value, out, gain_grad = in_vmem(
        last_kernel, (square, turned, turned, square, ((1, shard), jnp.float32)), (), (total, w_kv, w_query, gain), name="last"
    )
    return gain_grad.reshape(shard), query, key.T, value.T, out


def unpack_kernel(total, w_gate, w_up, gain, gate_ref, up_ref, down_ref, gain_ref):
    shard, part = w_gate.shape[0], total.shape[3]
    strips = shard // STRIP
    scale = gain[...]
    gain_sum = jnp.zeros((shard, 1), jnp.float32)
    for index, (weight, target) in enumerate(((w_gate, gate_ref), (w_up, up_ref))):
        for step in range(4):
            columns = slice(step * part, (step + 1) * part)
            grads = total[:strips, 4 * index + step].reshape(shard, part).astype(jnp.float32)
            gain_sum = gain_sum + jnp.sum(grads * weight[:, columns].astype(jnp.float32), axis=1, keepdims=True)
            target[:, columns] = grads * scale
    for step in range(4):
        down_ref[step * shard:(step + 1) * shard, :] = total[:strips, 8 + step].reshape(shard, part).astype(jnp.float32)
    gain_ref[...] = as_row(gain_sum)


def unpack(total, w_gate, w_up, gain):
    shard, columns = w_gate.shape
    part = total.shape[3]
    full = ((shard, columns), jnp.float32)
    gate, up, down, gain_grad = in_vmem(
        unpack_kernel, (full, full, ((4 * shard, part), jnp.float32), ((1, shard), jnp.float32)), (), (total, w_gate, w_up, gain), name="unpack"
    )
    return gain_grad.reshape(shard), gate, up, down.T


def over_core(value):
    return lax.ppermute(value, "core", SWAP)


def over_chip(value):
    return lax.ppermute(value, "xh", SWAP)


def over_both(value):
    return lax.ppermute(value, FSDP_AXES, ((0, 3), (3, 0), (1, 2), (2, 1)))


def trade(value):
    return lax.ppermute(value, ("xl", "core"), ((0, 0), (1, 2), (2, 1), (3, 3)))


def arrange(pieces, xh, core):
    low = jnp.where(core == 1, pieces[1], pieces[0]), jnp.where(core == 1, pieces[0], pieces[1])
    high = jnp.where(core == 1, pieces[3], pieces[2]), jnp.where(core == 1, pieces[2], pieces[3])
    return jnp.stack([jnp.where(xh == 1, h, l) for l, h in zip(low, high)] + [jnp.where(xh == 1, l, h) for l, h in zip(low, high)])


def exchange(value, axes):
    return lax.all_to_all(value, axes, split_axis=0, concat_axis=0, tiled=True)


def per_device(
    tokens,
    block_order,
    gain_attn,
    w_query,
    w_key,
    w_value,
    w_out,
    gain_mlp,
    w_gate,
    w_up,
    w_down,
    cotangent,
):
    f32, bf16 = jnp.float32, jnp.bfloat16
    xh, core = lax.axis_index("xh"), lax.axis_index("core")
    mine = 2 * xh + core
    own_id = mine.reshape(1)
    row_total, width = tokens.shape[1:]
    shard = w_query.shape[0]
    ff_part = w_down.shape[0]
    groups = lax.axis_size(SEQ_AXES)
    key_width = KV_HEADS * HEAD
    gain_one = gain_attn.astype(f32)[:, None]
    gain_two = gain_mlp.astype(f32)[:, None]

    kv_shard, query_shard = pack(w_key, w_value, w_query, gain_one)
    far_kv, near_kv = over_chip(kv_shard), over_core(kv_shard)
    hidden_low, query_shard = lax.optimization_barrier((trade(tokens[0]), query_shard))
    far_query, near_query = over_chip(query_shard), over_core(query_shard)

    def gate_up(step):
        start = (mine ^ step) * ff_part
        both = [lax.dynamic_slice_in_dim(w, start, ff_part, 1).astype(f32) * gain_two for w in (w_gate, w_up)]
        return jnp.stack(both).astype(bf16)

    gate_up_parts = [gate_up(step) for step in range(4)]
    far_kv, hidden_low, gate_up_parts = lax.optimization_barrier((far_kv, hidden_low, gate_up_parts))

    own_order = lax.dynamic_slice_in_dim(block_order, 2 * groups * core, 2 * groups)
    other_order = lax.dynamic_slice_in_dim(block_order, 2 * groups * (1 - core), 2 * groups)
    key_pos = jnp.concatenate([own_order, other_order])
    query_rank = jnp.sum((own_order[None, :] < own_order[:, None]).astype(jnp.int32), axis=1)
    hit = query_rank[None, :] == jnp.arange(2 * groups, dtype=jnp.int32)[:, None]
    sorted_pos = jnp.sum(jnp.where(hit, own_order[None, :], 0), axis=1)
    sorted_id = jnp.sum(jnp.where(hit, jnp.arange(2 * groups, dtype=jnp.int32)[None, :], 0), axis=1)
    here = lax.axis_index(SEQ_AXES)
    own_blocks = lax.dynamic_slice_in_dim(own_order, 2 * here, 2)
    row = jnp.arange(row_total, dtype=jnp.int32)
    own_pos = jnp.where(row < BLK, own_blocks[0] * BLK + row, own_blocks[1] * BLK + row - BLK)
    inverse_freq = THETA ** (-jnp.arange(HEAD // 2, dtype=f32) / (HEAD // 2))
    angles = inverse_freq[:, None] * own_pos.astype(f32)[None, :]
    cos_table, sin_table = jnp.cos(angles), jnp.sin(angles)

    normed_one, kv_send, kv_full = project_keys(own_id, hidden_low, (kv_shard, near_kv, far_kv, over_core(far_kv)), cos_table, sin_table, groups)
    query_send, query_full = project_queries(own_id, normed_one, (query_shard, near_query, far_query, over_core(far_query)), cos_table, sin_table, groups)
    kv_own, query_send, upstream = lax.optimization_barrier((exchange(kv_send, SEQ_AXES), query_send, trade(cotangent[0])))
    query_in = exchange(query_send, SEQ_AXES)
    kv_other = over_core(kv_own)

    kv_other, w_out, upstream, gate_up_parts = lax.optimization_barrier((kv_other, w_out, upstream, gate_up_parts))
    far_out, far_upstream = over_chip(w_out), over_chip(upstream)
    far_weights = over_chip(gate_up_parts[2]), over_both(gate_up_parts[3])
    out_send, out_blocks, lse, kv_sorted, kv_turned = attend(key_pos, query_rank, sorted_pos, sorted_id, query_in, kv_own, kv_other)
    out_send, far_out, far_upstream, far_weights = lax.optimization_barrier((out_send, far_out, far_upstream, far_weights))
    out_full = stack_rows(own_id, (w_out, over_core(w_out), far_out, over_core(far_out)))
    weights = (gate_up_parts[0], over_core(gate_up_parts[1])) + far_weights
    upstream_all = (upstream, over_core(upstream), far_upstream, over_core(far_upstream))

    gate_part, up_part = stack_pairs(own_id, weights)
    attn, out_full, gate_part, up_part = lax.optimization_barrier((exchange(out_send, SEQ_AXES), out_full, gate_part, up_part))
    mid_state, second_hat = project_out(attn, hidden_low, out_full)
    far_hat = over_chip(second_hat)
    near_hat = over_core(second_hat)
    down_turned = w_down.T
    near_side = feed((second_hat, near_hat), upstream_all[:2], gate_part, up_part, down_turned)
    far_hat, near_side = lax.optimization_barrier((far_hat, near_side))
    normed_all = second_hat, near_hat, far_hat, over_core(far_hat)
    far_side = feed(normed_all[2:], upstream_all[2:], gate_part, up_part, down_turned)
    scaled_received = over_core(near_side[1])
    far_send = (far_side[0] + over_core(far_side[1])[:, :width].astype(f32)).astype(bf16)
    far_send, normed_all, scaled_received = lax.optimization_barrier((far_send, normed_all, scaled_received))
    scaled_far = over_chip(far_send)
    ring = lax.axis_size(SEQ_AXES)
    stacked = feed_grads(normed_all, upstream_all, near_side[4:], far_side[4:], ring)
    scaled_far, stacked = lax.optimization_barrier((scaled_far, stacked))
    reduced = lax.psum_scatter(stacked.reshape(ring, 12 * STRIP, ff_part), SEQ_AXES, scatter_dimension=0, tiled=True)[0]

    grad_mid, grad_send, out_grad_keep, out_grad_give = mid_back(own_id, near_side[0], scaled_received, scaled_far, mid_state, upstream, out_full, attn)
    grad_group = exchange(grad_send, SEQ_AXES)
    ctx = lax.axis_size(CTX_AXES)
    slab = 8
    out_chip = (out_grad_keep.astype(f32) + over_core(out_grad_give).astype(f32)).astype(bf16).reshape(2 * ctx, slab, -1)
    result_received = over_core(near_side[3])
    result_send = (far_side[2] + over_core(far_side[3])[:, :width].astype(f32)).astype(bf16)
    grad_group, out_chip = lax.optimization_barrier((grad_group, out_chip))

    out_chips = exchange(out_chip, CHIP_AXES)

    dq, dkv_own, dkv_other = attend_back(key_pos, query_rank, sorted_pos, sorted_id, query_in, grad_group, out_blocks, lse, kv_sorted, kv_turned)
    dkv_other, reduced, out_chips, result_send = lax.optimization_barrier((dkv_other, reduced, out_chips, result_send))
    result_far = over_chip(result_send)
    out_sum = jnp.sum(out_chips.astype(f32), axis=0).astype(bf16)
    dq_home = exchange(dq, SEQ_AXES)
    dkv_received = over_core(dkv_other)
    reduced = (reduced.astype(f32) + lax.ppermute(reduced, "xl", SWAP).astype(f32)).astype(bf16).reshape(3, 4, STRIP, ff_part)
    dkv = (dkv_own + dkv_received.astype(f32)).astype(bf16)
    dq_home, dkv, reduced = lax.optimization_barrier((dq_home, dkv, reduced))
    part = lambda step: lax.dynamic_index_in_dim(reduced[:2], mine ^ step, 1, keepdims=False)
    pieces = arrange([part(0), over_core(part(1)), over_chip(part(2)), over_both(part(3))], xh, core).transpose(1, 0, 2, 3)
    pieces = jnp.concatenate([pieces, reduced[2:]]).reshape(12, STRIP, ff_part)
    result = mid_state + near_side[2] + result_received[:, :width].astype(f32) + result_far.astype(f32)
    home, pieces, result = lax.optimization_barrier((exchange(dkv, SEQ_AXES), pieces, result.astype(bf16)))
    block_out = trade(result)
    whole = lax.all_gather(pieces, SEQ_AXES, axis=0, tiled=False)
    gain_two_shard, gate_shard, up_shard, down_shard = unpack(whole, w_gate, w_up, gain_two)

    keep, give, grad_tokens = finish(own_id, dq_home, home, hidden_low, normed_one, kv_full, query_full, grad_mid, cos_table, sin_table)
    grad_tokens = trade(grad_tokens)
    columns = keep.shape[-1]
    chip_sum = (keep.astype(f32) + over_core(give).astype(f32)).astype(bf16).reshape(2 * ctx, slab, columns)
    qkv_chips, grad_tokens, block_out = lax.optimization_barrier((exchange(chip_sum, CHIP_AXES), grad_tokens, block_out))
    qkv_sum = jnp.sum(qkv_chips.astype(f32), axis=0).astype(bf16)
    summed = jnp.concatenate([qkv_sum, out_sum], axis=1)
    final = exchange(jnp.broadcast_to(summed[None], (ctx,) + summed.shape), CTX_AXES)
    final, gate_shard = lax.optimization_barrier((final, gate_shard))
    gain_one_shard, query_shard, key_shard, value_shard, out_shard = last(final, kv_shard, query_shard, gain_one)
    return (
        block_out[None],
        grad_tokens.astype(f32)[None],
        gain_one_shard,
        query_shard,
        key_shard,
        value_shard,
        out_shard,
        gain_two_shard,
        gate_shard,
        up_shard,
        down_shard,
    )


def solution(mesh):
    fine = Mesh(mesh.devices.reshape(2, 4, 4, 2, 2), ("xl", "z", "y", "xh", "core"))
    rows = P(FSDP_AXES, CTX_AXES, None)
    gain = P(FSDP_AXES)
    weight = P(FSDP_AXES, None)
    return jax.shard_map(
        per_device,
        mesh=fine,
        in_specs=(rows, P(), gain, weight, weight, weight, weight, gain, weight, weight, weight, rows),
        out_specs=(rows, rows, gain, weight, weight, weight, weight, gain, weight, weight, weight),
        check_vma=False,
    )
```

```python
import functools
import math

import jax
import jax.numpy as jnp
from jax import lax
from jax.experimental import pallas as pl
from jax.experimental.pallas import tpu as pltpu
from jax.sharding import Mesh
from jax.sharding import PartitionSpec as P

HEADS = 15
KV_HEADS = 5
EPSILON = 1e-05
THETA = 100000.0
SEQ_AXES = ("z", "y")
CTX_AXES = ("xl", "z", "y")
CHIP_AXES = ("xh", "xl", "z", "y")
FSDP_AXES = ("xh", "core")
CUBE_AXES = ("xl", "xh", "core")
SWAP = ((0, 1), (1, 0))
STRIP = 16
BLK = 128
HEAD = 64
EXP_SCALE = math.log2(math.e) / 8.0
MASKED = -1e30


def attend_kernel(key_pos, query_rank, sorted_pos, sorted_id, q_ref, own_in, other_in, send_ref, out_ref, lse_ref, kv_ref, kvt_ref, ones_v, q_sorted, *, big, small, edge_size, blocks):
    groups, width = own_in.shape[0], HEAD
    rows = blocks * BLK
    is_key = lax.broadcasted_iota(jnp.int32, (BLK, 2 * width), 1) < width

    def place(index, _):
        for side, source in enumerate((own_in, other_in)):
            for half in range(2):
                where = pl.multiple_of(key_pos[side * 2 * groups + 2 * index + half] * BLK, BLK)
                piece = source[index, :, half * BLK:(half + 1) * BLK]
                kvt_ref[:, pl.ds(where, BLK)] = piece
                turned = piece.T
                kv_ref[pl.ds(where, BLK), :] = turned
                ones_v[pl.ds(where, BLK), :] = jnp.where(is_key, jnp.ones_like(turned), turned)
        for half in range(2):
            query = q_ref[index, :, half * BLK:(half + 1) * BLK]
            query = jnp.concatenate([query, jnp.zeros_like(query)], axis=0)
            q_sorted[pl.ds(pl.multiple_of(query_rank[2 * index + half] * BLK, BLK), BLK), :] = query.T
        return 0

    lax.fori_loop(0, groups, place, 0, unroll=4)

    def tile(index, _):
        low, high = sorted_pos[blocks * index], sorted_pos[blocks * index + blocks - 1]
        query = q_sorted[pl.ds(pl.multiple_of(index * rows, rows), rows), :]
        row = lax.broadcasted_iota(jnp.int32, (rows, 1), 0)
        place_of = row + low * BLK
        for part in range(1, blocks):
            place_of = jnp.where(row >= part * BLK, row + (sorted_pos[blocks * index + part] - part) * BLK, place_of)

        def step(start, carry, size, masked):
            top, total = carry
            scores = lax.dot_general(query, kv_ref[pl.ds(start, size), :], (((1,), (1,)), ((), ())), preferred_element_type=jnp.float32)
            if masked:
                column = start + lax.broadcasted_iota(jnp.int32, scores.shape, 1)
                scores = jnp.where(column <= place_of, scores, MASKED)
            new_top = jnp.maximum(top, jnp.max(scores, axis=1, keepdims=True))
            weights = jnp.exp2((scores - new_top) * EXP_SCALE).astype(jnp.bfloat16)
            factor = jnp.exp2((top - new_top) * EXP_SCALE)
            added = jnp.dot(weights, ones_v[pl.ds(start, size), :], preferred_element_type=jnp.float32)
            return new_top, total * factor + added

        def full(count, carry):
            for part in range(big // small):
                carry = step(pl.multiple_of(count * big + part * small, small), carry, small, False)
            return carry

        def edge(count, carry):
            return step(pl.multiple_of(count * edge_size, edge_size), carry, edge_size, True)

        carry = (jnp.full((rows, 1), MASKED, jnp.float32), jnp.zeros((rows, 2 * width), jnp.float32))
        done = low * BLK // big
        carry = lax.fori_loop(0, done, full, carry)
        top, total = lax.fori_loop(done * (big // edge_size), (high * BLK + BLK + edge_size - 1) // edge_size, edge, carry)
        lse = (top * EXP_SCALE + jnp.log2(total)).T
        total = total.T
        result = total[width:] / total[:1]
        for part in range(blocks):
            ident = sorted_id[blocks * index + part]
            piece = result[:, part * BLK:(part + 1) * BLK]
            out_ref[ident] = piece
            send_ref[ident // 2, :, pl.ds(pl.multiple_of(ident % 2 * BLK, BLK), BLK)] = piece.astype(jnp.bfloat16)
            lse_ref[ident] = lse[:8, part * BLK:(part + 1) * BLK]
        return 0

    lax.fori_loop(0, 2 * groups // blocks, tile, 0)


def attend(key_pos, query_rank, sorted_pos, sorted_id, q, own_in, other_in, big=1024, small=1024, edge_size=512, blocks=4):
    groups, width = own_in.shape[0], HEAD
    total = 4 * groups * BLK
    vm = pl.BlockSpec(memory_space=pltpu.VMEM)
    sm = pl.BlockSpec(memory_space=pltpu.SMEM)
    return pl.pallas_call(
        functools.partial(attend_kernel, big=big, small=small, edge_size=edge_size, blocks=blocks),
        out_shape=(
            jax.ShapeDtypeStruct((groups, width, 2 * BLK), jnp.bfloat16),
            jax.ShapeDtypeStruct((2 * groups, width, BLK), jnp.float32),
            jax.ShapeDtypeStruct((2 * groups, 8, BLK), jnp.float32),
            jax.ShapeDtypeStruct((total, 2 * width), jnp.bfloat16),
            jax.ShapeDtypeStruct((2 * width, total), jnp.bfloat16),
        ),
        in_specs=[sm] * 4 + [vm] * 3,
        out_specs=(vm,) * 5,
        scratch_shapes=[
            pltpu.VMEM((total, 2 * width), jnp.bfloat16),
            pltpu.VMEM((2 * groups * BLK, 2 * width), jnp.bfloat16),
        ],
        compiler_params=pltpu.CompilerParams(vmem_limit_bytes=60 * 2**20),
        cost_estimate=pl.CostEstimate(flops=40 * 10**9, bytes_accessed=10**7, transcendentals=2 * 10**7),
        name="attend",
    )(key_pos, query_rank, sorted_pos, sorted_id, q, own_in, other_in)


def back_kernel(key_pos, query_rank, sorted_pos, sorted_id, q_ref, da_ref, out_ref, lse_ref, kv_ref, kvt_ref, dq_ref, own_ref, other_ref, dkv, q_sorted, da_sorted, *, big, small, edge_size, flip):
    groups, width = q_ref.shape[0], HEAD

    def place(index, _):
        for half in range(2):
            rank = query_rank[2 * index + half]
            q_sorted[rank] = q_ref[index, :, half * BLK:(half + 1) * BLK]
            da_sorted[rank] = da_ref[index, :, half * BLK:(half + 1) * BLK]
        return 0

    lax.fori_loop(0, groups, place, 0)

    def clear(index, _):
        dkv[pl.ds(pl.multiple_of(index * BLK, BLK), BLK), :] = jnp.zeros((BLK, 2 * width), jnp.float32)
        return 0

    lax.fori_loop(0, 4 * groups, clear, 0)

    def tile(index, _):
        low, high = sorted_pos[2 * index], sorted_pos[2 * index + 1]
        first_id, second_id = sorted_id[2 * index], sorted_id[2 * index + 1]
        query = jnp.concatenate([q_sorted[2 * index], q_sorted[2 * index + 1]], axis=1)
        grad = jnp.concatenate([da_sorted[2 * index], da_sorted[2 * index + 1]], axis=1)
        value = jnp.concatenate([out_ref[first_id], out_ref[second_id]], axis=1)
        lse = jnp.concatenate([lse_ref[first_id][:1], lse_ref[second_id][:1]], axis=1)
        delta = jnp.sum(grad.astype(jnp.float32) * value, axis=0, keepdims=True)
        none = jnp.zeros_like(query)
        both = jnp.concatenate([jnp.concatenate([query, none], axis=1), jnp.concatenate([none, grad], axis=1)], axis=0)
        both_t = both.T
        lane = lax.broadcasted_iota(jnp.int32, (1, 2 * BLK), 1)
        place_of = jnp.where(lane < BLK, low * BLK + lane, (high - 1) * BLK + lane)

        def step(start, total, size, masked):
            keys = kv_ref[pl.ds(start, size), :]
            pair = jnp.dot(keys, both, preferred_element_type=jnp.float32)
            weights = jnp.exp2(pair[:, :2 * BLK] * EXP_SCALE - lse)
            if masked:
                row = start + lax.broadcasted_iota(jnp.int32, weights.shape, 0)
                weights = jnp.where(row <= place_of, weights, 0.0)
            grad_scores = (weights * (pair[:, 2 * BLK:] - delta)).astype(jnp.bfloat16)
            weights = weights.astype(jnp.bfloat16)
            dkv[pl.ds(start, size), :] += jnp.dot(jnp.concatenate([grad_scores, weights], axis=1), both_t, preferred_element_type=jnp.float32)
            if flip:
                return total + lax.dot_general(grad_scores, keys, (((0,), (0,)), ((), ())), preferred_element_type=jnp.float32)
            return total + jnp.dot(kvt_ref[:width, pl.ds(start, size)], grad_scores, preferred_element_type=jnp.float32)

        def full(count, carry):
            for part in range(big // small):
                carry = step(pl.multiple_of(count * big + part * small, small), carry, small, False)
            return carry

        def edge(count, carry):
            return step(pl.multiple_of(count * edge_size, edge_size), carry, edge_size, True)

        done = low * BLK // big
        total = jnp.zeros((2 * BLK, 2 * width) if flip else (width, 2 * BLK), jnp.float32)
        total = lax.fori_loop(0, done, full, total)
        total = lax.fori_loop(done * (big // edge_size), (high * BLK + BLK + edge_size - 1) // edge_size, edge, total) * 0.125
        if flip:
            total = total.T[:width]
        for half, ident in enumerate((first_id, second_id)):
            dq_ref[ident // 2, :, pl.ds(pl.multiple_of(ident % 2 * BLK, BLK), BLK)] = total[:, half * BLK:(half + 1) * BLK].astype(jnp.bfloat16)
        return 0

    lax.fori_loop(0, groups, tile, 0)
    factor = jnp.where(lax.broadcasted_iota(jnp.int32, (1, 2 * width), 1) < width, 0.125, 1.0)

    def spread(index, _):
        for side, target in enumerate((own_ref, other_ref)):
            for half in range(2):
                where = pl.multiple_of(key_pos[side * 2 * groups + 2 * index + half] * BLK, BLK)
                target[index, :, half * BLK:(half + 1) * BLK] = (dkv[pl.ds(where, BLK), :] * factor).astype(target.dtype)
        return 0

    lax.fori_loop(0, groups, spread, 0)


def attend_back(key_pos, query_rank, sorted_pos, sorted_id, q, da, out, lse, kv, kvt, big=1024, small=1024, edge_size=512, flip=False):
    groups, width = q.shape[0], HEAD
    total = 4 * groups * BLK
    vm = pl.BlockSpec(memory_space=pltpu.VMEM)
    sm = pl.BlockSpec(memory_space=pltpu.SMEM)
    return pl.pallas_call(
        functools.partial(back_kernel, big=big, small=small, edge_size=edge_size, flip=flip),
        out_shape=(
            jax.ShapeDtypeStruct((groups, width, 2 * BLK), jnp.bfloat16),
            jax.ShapeDtypeStruct((groups, 2 * width, 2 * BLK), jnp.float32),
            jax.ShapeDtypeStruct((groups, 2 * width, 2 * BLK), jnp.bfloat16),
        ),
        in_specs=[sm] * 4 + [vm] * 6,
        out_specs=(vm,) * 3,
        scratch_shapes=[
            pltpu.VMEM((total, 2 * width), jnp.float32),
            pltpu.VMEM((2 * groups, width, BLK), jnp.bfloat16),
            pltpu.VMEM((2 * groups, width, BLK), jnp.bfloat16),
        ],
        compiler_params=pltpu.CompilerParams(vmem_limit_bytes=60 * 2**20),
        cost_estimate=pl.CostEstimate(flops=60 * 10**9, bytes_accessed=10**7, transcendentals=2 * 10**7),
        name="attend_back",
    )(key_pos, query_rank, sorted_pos, sorted_id, q, da, out, lse, kv, kvt)


def in_vmem(kernel, out_shape, scalars, arrays, scratch=(), flops=10**9, name=None):
    vm = pl.BlockSpec(memory_space=pltpu.VMEM)
    return pl.pallas_call(
        kernel,
        out_shape=tuple(jax.ShapeDtypeStruct(shape, dtype) for shape, dtype in out_shape),
        in_specs=[pl.BlockSpec(memory_space=pltpu.SMEM)] * len(scalars) + [vm] * len(arrays),
        out_specs=(vm,) * len(out_shape),
        scratch_shapes=[pltpu.VMEM(shape, dtype) for shape, dtype in scratch],
        compiler_params=pltpu.CompilerParams(vmem_limit_bytes=60 * 2**20),
        cost_estimate=pl.CostEstimate(flops=flops, bytes_accessed=10**7, transcendentals=0),
        name=name,
    )(*scalars, *arrays)


def across(left, right):
    return lax.dot_general(left, right, (((1,), (1,)), ((), ())), preferred_element_type=jnp.float32)


def unit_rms(value):
    return lax.rsqrt(jnp.mean(value * value, axis=-1, keepdims=True) + EPSILON)


def put_rows(mine, pieces, target):
    shard = pieces[0].shape[0]
    for step, piece in enumerate(pieces):
        target[pl.ds(pl.multiple_of((mine[0] ^ step) * shard, 16), shard), :] = piece[...]


def turn(pair, cos, sin):
    half = HEAD // 2
    front, behind = pair[:half], pair[half:]
    return jnp.concatenate([front * cos - behind * sin, behind * cos + front * sin], axis=0).astype(jnp.bfloat16)


def turn_back(pair, cos, sin):
    return turn(pair, cos, -sin)


def project_keys_kernel(mine, x_ref, own, near, far, far_near, cos_ref, sin_ref, hat_ref, send_ref, w_ref):
    put_rows(mine, (own, near, far, far_near), w_ref)
    hidden = x_ref[...].astype(jnp.float32)
    hat = (hidden * unit_rms(hidden)).astype(jnp.bfloat16)
    hat_ref[...] = hat
    key_width = KV_HEADS * HEAD
    per = HEADS // KV_HEADS
    lin = jnp.dot(hat, w_ref[...], preferred_element_type=jnp.float32).T
    for head in range(KV_HEADS):
        key = turn(lin[head * HEAD:(head + 1) * HEAD], cos_ref[...], sin_ref[...])
        value = lin[key_width + head * HEAD:key_width + (head + 1) * HEAD].astype(jnp.bfloat16)
        for query in range(per):
            send_ref[head * per + query, :HEAD] = key
            send_ref[head * per + query, HEAD:] = value
    send_ref[HEADS:] = jnp.zeros((send_ref.shape[0] - HEADS,) + send_ref.shape[1:], jnp.bfloat16)


def project_keys(mine, x, pieces, cos, sin, groups):
    rows, width = x.shape
    columns = pieces[0].shape[1]
    return in_vmem(
        project_keys_kernel,
        ((x.shape, jnp.bfloat16), ((groups, 2 * HEAD, rows), jnp.bfloat16), ((width, columns), jnp.bfloat16)),
        (mine,),
        (x, *pieces, cos, sin),
        name="project_keys",
    )


def project_queries_kernel(mine, hat_ref, own, near, far, far_near, cos_ref, sin_ref, send_ref, w_ref):
    put_rows(mine, (own, near, far, far_near), w_ref)
    per = HEADS // KV_HEADS
    for group in range(KV_HEADS):
        columns = slice(group * per * HEAD, (group + 1) * per * HEAD)
        lin = jnp.dot(hat_ref[...], w_ref[:, columns], preferred_element_type=jnp.float32).T
        for query in range(per):
            send_ref[group * per + query] = turn(lin[query * HEAD:(query + 1) * HEAD], cos_ref[...], sin_ref[...])
    send_ref[HEADS:] = jnp.zeros((send_ref.shape[0] - HEADS,) + send_ref.shape[1:], jnp.bfloat16)


def project_queries(mine, hat, pieces, cos, sin, groups):
    rows, width = hat.shape
    columns = pieces[0].shape[1]
    return in_vmem(
        project_queries_kernel,
        (((groups, HEAD, rows), jnp.bfloat16), ((width, columns), jnp.bfloat16)),
        (mine,),
        (hat, *pieces, cos, sin),
        name="project_queries",
    )


def stack_rows_kernel(mine, own, near, far, far_near, out_ref):
    put_rows(mine, (own, near, far, far_near), out_ref)


def stack_rows(mine, pieces):
    shard, columns = pieces[0].shape
    return in_vmem(stack_rows_kernel, (((4 * shard, columns), jnp.bfloat16),), (mine,), pieces, flops=10**6, name="stack_rows")[0]


def finish_grads_kernel(mine, dq_ref, home, hat_ref, cos_ref, sin_ref, keep_ref, give_ref, turned, hat_t):
    shard = hat_ref.shape[1] // 4
    cos, sin = cos_ref[...], sin_ref[...]
    key_width = KV_HEADS * HEAD
    per = HEADS // KV_HEADS
    for head in range(KV_HEADS):
        total = sum(home[head * per + query].astype(jnp.float32) for query in range(per))
        total = jnp.concatenate([total[:, :BLK].T, total[:, BLK:].T], axis=1)
        turned[head * HEAD:(head + 1) * HEAD, :] = turn_back(total[:HEAD], cos, sin)
        turned[key_width + head * HEAD:key_width + (head + 1) * HEAD, :] = total[HEAD:].astype(jnp.bfloat16)
        for query in range(per):
            start = 2 * key_width + (head * per + query) * HEAD
            turned[start:start + HEAD, :] = turn_back(dq_ref[head * per + query].astype(jnp.float32), cos, sin)
    hat_t[...] = hat_ref[...].T
    core = mine[0] & 1
    for target, at in ((keep_ref, core), (give_ref, 1 - core)):
        target[...] = jnp.zeros(target.shape, target.dtype)
        for part in range(2):
            rows = hat_t[pl.ds(pl.multiple_of((2 * part + at) * shard, 16), shard), :]
            grads = across(rows, turned[...])
            target[part, :shard, : grads.shape[1]] = grads.astype(jnp.bfloat16)


def finish_grads(mine, dq, home, hat, cos, sin):
    rows, width = hat.shape
    columns = 2 * KV_HEADS * HEAD + HEADS * HEAD
    half = ((2, 256, -(-columns // BLK) * BLK), jnp.bfloat16)
    return in_vmem(
        finish_grads_kernel,
        (half, half, ((columns, rows), jnp.bfloat16)),
        (mine,),
        (dq, home, hat, cos, sin),
        scratch=(((width, rows), jnp.bfloat16),),
        name="finish_grads",
    )


def finish_tokens_kernel(turned, x_ref, kv_ref, query_ref, mid_ref, tokens_ref):
    key_width = KV_HEADS * HEAD
    scaled = jnp.dot(kv_ref[...], turned[: 2 * key_width, :], preferred_element_type=jnp.float32)
    scaled = (scaled + jnp.dot(query_ref[...], turned[2 * key_width :, :], preferred_element_type=jnp.float32)).T
    tokens_ref[...] = (mid_ref[...] + norm_back(x_ref[...].astype(jnp.float32), scaled)).T.astype(jnp.bfloat16)


def finish_tokens(turned, x, w_kv, w_query, mid):
    return in_vmem(finish_tokens_kernel, ((x.shape[::-1], jnp.bfloat16),), (), (turned, x, w_kv, w_query, mid), name="finish_tokens")[0]


def total_out_kernel(mid, keep, received, far, out_ref):
    total = mid[...] + keep[...] + received[:, : mid.shape[1]].astype(jnp.float32) + far[...].astype(jnp.float32)
    out_ref[...] = total.T.astype(jnp.bfloat16)


def total_out(mid, keep, received, far):
    return in_vmem(total_out_kernel, ((mid.shape[::-1], jnp.bfloat16),), (), (mid, keep, received, far), flops=10**6, name="total_out")[0]


def norm_back(value, grad):
    rms = unit_rms(value)
    hat = value * rms
    return rms * (grad - hat * jnp.mean(grad * hat, axis=-1, keepdims=True))


def out_kernel(attn, x_ref, w_ref, mid_ref, hat_ref):
    rows = attn[:HEADS].reshape(HEADS * HEAD, attn.shape[2]).T
    mid = x_ref[...].astype(jnp.float32) + jnp.dot(rows, w_ref[...], preferred_element_type=jnp.float32)
    mid_ref[...] = mid
    hat_ref[...] = (mid * unit_rms(mid)).astype(jnp.bfloat16)


def project_out(attn, x, w_out):
    return in_vmem(out_kernel, ((x.shape, jnp.float32), (x.shape, jnp.bfloat16)), (), (attn, x, w_out), name="project_out")


def stack_pairs_kernel(mine, own, near, far, far_near, gate_ref, up_ref):
    pieces = (own, near, far, far_near)
    put_rows(mine, [piece.at[0] for piece in pieces], gate_ref)
    put_rows(mine, [piece.at[1] for piece in pieces], up_ref)


def stack_pairs(mine, pieces):
    _, shard, columns = pieces[0].shape
    whole = ((4 * shard, columns), jnp.bfloat16)
    return in_vmem(stack_pairs_kernel, (whole, whole), (mine,), pieces, flops=10**6, name="stack_pairs")


def feed_kernel(hat_own, hat_peer, grad_own, grad_peer, w_gate, w_up, down_t, scaled_keep, scaled_send, out_keep, out_send, act_ref, gate_grad_ref, up_grad_ref, hat_ref, grad_ref):
    rows, width = hat_own.shape
    for step, (hat, grad) in enumerate(((hat_own, grad_own), (hat_peer, grad_peer))):
        hat_ref[step * rows:(step + 1) * rows, :] = hat[...]
        grad_ref[step * rows:(step + 1) * rows, :] = grad[...]
    scaled = out = None
    for start, stop in ((0, 256), (256, 640)):
        cut = slice(start, stop)
        gate = jnp.dot(hat_ref[...], w_gate[:, cut], preferred_element_type=jnp.float32)
        up = jnp.dot(hat_ref[...], w_up[:, cut], preferred_element_type=jnp.float32)
        sigmoid = jax.nn.sigmoid(gate)
        silu = gate * sigmoid
        act = (silu * up).astype(jnp.bfloat16)
        grad_act = jnp.dot(grad_ref[...], down_t[:, cut], preferred_element_type=jnp.float32).astype(jnp.bfloat16).astype(jnp.float32)
        gate_grad = (grad_act * up * sigmoid * (1.0 + gate * (1.0 - sigmoid))).astype(jnp.bfloat16)
        up_grad = (grad_act * silu).astype(jnp.bfloat16)
        act_ref[:, cut], gate_grad_ref[:, cut], up_grad_ref[:, cut] = act, gate_grad, up_grad
        scaled_cut = across(gate_grad, w_gate[:, cut]) + across(up_grad, w_up[:, cut])
        out_cut = across(act, down_t[:, cut])
        scaled, out = (scaled_cut, out_cut) if scaled is None else (scaled + scaled_cut, out + out_cut)
    scaled_keep[...] = scaled[:rows]
    out_keep[...] = out[:rows]
    for target, value in ((scaled_send, scaled), (out_send, out)):
        target[:, :width] = value[rows:].astype(jnp.bfloat16)
        target[:, width:] = jnp.zeros((rows, target.shape[1] - width), jnp.bfloat16)


def feed(hats, grads, w_gate, w_up, down_t):
    rows, width = hats[0].shape
    kept = ((rows, width), jnp.float32)
    sent = ((rows, -(-width // 256) * 256), jnp.bfloat16)
    hidden = ((2 * rows, down_t.shape[1]), jnp.bfloat16)
    both = ((2 * rows, width), jnp.bfloat16)
    return in_vmem(
        feed_kernel,
        (kept, sent, kept, sent, hidden, hidden, hidden),
        (),
        (*hats, *grads, w_gate, w_up, down_t),
        scratch=(both, both),
        flops=6 * 10**9,
        name="feed",
    )


def feed_grads_kernel(*refs):
    hats, grads, near, far, (out_ref, hat_t, grad_t) = refs[:4], refs[4:8], refs[8:11], refs[11:14], refs[14:]
    rows = hats[0].shape[0]
    for step in range(4):
        here = slice(step * rows, (step + 1) * rows)
        hat_t[:, here] = hats[step][...].T
        grad_t[:, here] = grads[step][...].T
    shard = hat_t.shape[0] // 4
    strips = shard // STRIP
    for index, (left, at) in enumerate(((hat_t, 1), (hat_t, 2), (grad_t, 0))):
        for part in range(4):
            some = left[part * shard:(part + 1) * shard, :]
            product = jnp.dot(some[:, : 2 * rows], near[at][...], preferred_element_type=jnp.float32)
            product = product + jnp.dot(some[:, 2 * rows:], far[at][...], preferred_element_type=jnp.float32)
            out_ref[:strips, 4 * index + part] = product.astype(jnp.bfloat16).reshape(strips, STRIP, product.shape[1])
    out_ref[strips:] = jnp.zeros((out_ref.shape[0] - strips,) + out_ref.shape[1:], jnp.bfloat16)


def feed_grads(hats, grads, near, far, ring):
    rows, width = hats[0].shape
    turned = ((width, 4 * rows), jnp.bfloat16)
    return in_vmem(
        feed_grads_kernel,
        (((ring, 12, STRIP, near[0].shape[1]), jnp.bfloat16),),
        (),
        (*hats, *grads, *near, *far),
        scratch=(turned, turned),
        flops=8 * 10**9,
        name="feed_grads",
    )[0]


def mid_kernel(mine, keep, received, far, mid_ref, grad_ref, w_ref, attn, total_ref, send_ref, keep_ref, give_ref, rows_ref):
    width = keep.shape[1]
    shard = width // 4
    scaled = keep[...] + received[:, :width].astype(jnp.float32) + far[...].astype(jnp.float32)
    total = grad_ref[...].astype(jnp.float32) + norm_back(mid_ref[...], scaled)
    total_ref[...] = total
    low = total.astype(jnp.bfloat16)
    send_ref[:HEADS] = across(w_ref[...], low).astype(jnp.bfloat16).reshape(HEADS, HEAD, low.shape[0])
    send_ref[HEADS:] = jnp.zeros((send_ref.shape[0] - HEADS,) + send_ref.shape[1:], jnp.bfloat16)
    rows_ref[...] = attn[:HEADS].reshape(HEADS * HEAD, attn.shape[2])
    core = mine[0] & 1
    for target, at in ((keep_ref, core), (give_ref, 1 - core)):
        target[...] = jnp.zeros(target.shape, target.dtype)
        for part in range(2):
            rows = rows_ref[pl.ds(pl.multiple_of((2 * part + at) * shard, 16), shard), :]
            target[part, :shard, :width] = jnp.dot(rows, low, preferred_element_type=jnp.float32).astype(target.dtype)


def mid_back(mine, keep, received, far, mid, grad, w_out, attn):
    half = ((2, 256, 1024), jnp.bfloat16)
    return in_vmem(
        mid_kernel,
        ((mid.shape, jnp.float32), (attn.shape, jnp.bfloat16), half, half),
        (mine,),
        (keep, received, far, mid, grad, w_out, attn),
        scratch=((mid.shape[::-1], jnp.bfloat16),),
        name="mid_back",
    )


def pack_kernel(key_t, value_t, query, gain, kv_ref, query_ref):
    width = key_t.shape[0]
    scale = gain[...]
    for index, piece in enumerate((key_t, value_t)):
        kv_ref[:, index * width:(index + 1) * width] = (piece[...].astype(jnp.float32).T * scale).astype(jnp.bfloat16)
    query_ref[...] = (query[...].astype(jnp.float32) * scale).astype(jnp.bfloat16)


def pack(w_key, w_value, w_query, gain):
    shard = w_key.shape[0]
    return in_vmem(
        pack_kernel,
        (((shard, 2 * w_key.shape[1]), jnp.bfloat16), (w_query.shape, jnp.bfloat16)),
        (),
        (w_key.T, w_value.T, w_query, gain),
        flops=10**6,
        name="pack",
    )


def as_row(column):
    return jnp.broadcast_to(column, (column.shape[0], BLK)).T[:1]


def last_kernel(total, w_kv, w_query, gain, query_ref, key_ref, value_ref, out_ref, gain_ref):
    shard, width = w_query.shape
    key_width = key_ref.shape[0]
    columns = 2 * key_width + width
    padded = -(-columns // BLK) * BLK
    rows = total[...].reshape(total.shape[0] * total.shape[1], total.shape[2])[:shard].astype(jnp.float32)
    kv, query = rows[:, : 2 * key_width], rows[:, 2 * key_width : columns]
    scale = gain[...]
    gain_sum = jnp.sum(kv * w_kv[...].astype(jnp.float32), axis=1, keepdims=True) + jnp.sum(query * w_query[...].astype(jnp.float32), axis=1, keepdims=True)
    gain_ref[...] = as_row(gain_sum / scale)
    kv = kv * scale
    key_ref[...] = kv[:, :key_width].T
    value_ref[...] = kv[:, key_width:].T
    query_ref[...] = query * scale
    out_ref[...] = rows[:, padded:padded + width]


def last(total, w_kv, w_query, gain):
    shard, width = w_query.shape
    square = (w_query.shape, jnp.float32)
    turned = ((w_kv.shape[1] // 2, shard), jnp.float32)
    query, key, value, out, gain_grad = in_vmem(
        last_kernel, (square, turned, turned, square, ((1, shard), jnp.float32)), (), (total, w_kv, w_query, gain), name="last"
    )
    return gain_grad.reshape(shard), query, key.T, value.T, out


def unpack_kernel(total, w_gate, w_up, gain, gate_ref, up_ref, down_ref, gain_ref):
    shard, part = w_gate.shape[0], total.shape[3]
    strips = shard // STRIP
    scale = gain[...]
    gain_sum = jnp.zeros((shard, 1), jnp.float32)
    for index, (weight, target) in enumerate(((w_gate, gate_ref), (w_up, up_ref))):
        for step in range(4):
            columns = slice(step * part, (step + 1) * part)
            grads = total[:strips, 4 * index + step].reshape(shard, part).astype(jnp.float32)
            gain_sum = gain_sum + jnp.sum(grads * weight[:, columns].astype(jnp.float32), axis=1, keepdims=True)
            target[:, columns] = grads * scale
    for step in range(4):
        down_ref[step * shard:(step + 1) * shard, :] = total[:strips, 8 + step].reshape(shard, part).astype(jnp.float32)
    gain_ref[...] = as_row(gain_sum)


def unpack(total, w_gate, w_up, gain):
    shard, columns = w_gate.shape
    part = total.shape[3]
    full = ((shard, columns), jnp.float32)
    gate, up, down, gain_grad = in_vmem(
        unpack_kernel, (full, full, ((4 * shard, part), jnp.float32), ((1, shard), jnp.float32)), (), (total, w_gate, w_up, gain), name="unpack"
    )
    return gain_grad.reshape(shard), gate, up, down.T


def over_core(value):
    return lax.ppermute(value, "core", SWAP)


def over_chip(value):
    return lax.ppermute(value, "xh", SWAP)


def over_both(value):
    return lax.ppermute(value, FSDP_AXES, ((0, 3), (3, 0), (1, 2), (2, 1)))


def trade(value):
    return lax.ppermute(value, ("xl", "core"), ((0, 0), (1, 2), (2, 1), (3, 3)))


def arrange(pieces, xh, core):
    low = jnp.where(core == 1, pieces[1], pieces[0]), jnp.where(core == 1, pieces[0], pieces[1])
    high = jnp.where(core == 1, pieces[3], pieces[2]), jnp.where(core == 1, pieces[2], pieces[3])
    return jnp.stack([jnp.where(xh == 1, h, l) for l, h in zip(low, high)] + [jnp.where(xh == 1, l, h) for l, h in zip(low, high)])


def exchange(value, axes):
    return lax.all_to_all(value, axes, split_axis=0, concat_axis=0, tiled=True)


def per_device(
    tokens,
    block_order,
    gain_attn,
    w_query,
    w_key,
    w_value,
    w_out,
    gain_mlp,
    w_gate,
    w_up,
    w_down,
    cotangent,
):
    f32, bf16 = jnp.float32, jnp.bfloat16
    xh, core = lax.axis_index("xh"), lax.axis_index("core")
    mine = 2 * xh + core
    own_id = mine.reshape(1)
    row_total, width = tokens.shape[1:]
    shard = w_query.shape[0]
    ff_part = w_down.shape[0]
    groups = lax.axis_size(SEQ_AXES)
    key_width = KV_HEADS * HEAD
    gain_one = gain_attn.astype(f32)[:, None]
    gain_two = gain_mlp.astype(f32)[:, None]

    kv_shard, query_shard = pack(w_key, w_value, w_query, gain_one)
    far_kv, near_kv = over_chip(kv_shard), over_core(kv_shard)
    hidden_low, query_shard = lax.optimization_barrier((trade(tokens[0]), query_shard))
    far_query, near_query = over_chip(query_shard), over_core(query_shard)

    def gate_up(step):
        start = (mine ^ step) * ff_part
        both = [lax.dynamic_slice_in_dim(w, start, ff_part, 1).astype(f32) * gain_two for w in (w_gate, w_up)]
        return jnp.stack(both).astype(bf16)

    gate_up_parts = [gate_up(step) for step in range(4)]
    far_kv, hidden_low, gate_up_parts = lax.optimization_barrier((far_kv, hidden_low, gate_up_parts))

    own_order = lax.dynamic_slice_in_dim(block_order, 2 * groups * core, 2 * groups)
    other_order = lax.dynamic_slice_in_dim(block_order, 2 * groups * (1 - core), 2 * groups)
    key_pos = jnp.concatenate([own_order, other_order])
    query_rank = jnp.sum((own_order[None, :] < own_order[:, None]).astype(jnp.int32), axis=1)
    hit = query_rank[None, :] == jnp.arange(2 * groups, dtype=jnp.int32)[:, None]
    sorted_pos = jnp.sum(jnp.where(hit, own_order[None, :], 0), axis=1)
    sorted_id = jnp.sum(jnp.where(hit, jnp.arange(2 * groups, dtype=jnp.int32)[None, :], 0), axis=1)
    here = lax.axis_index(SEQ_AXES)
    own_blocks = lax.dynamic_slice_in_dim(own_order, 2 * here, 2)
    row = jnp.arange(row_total, dtype=jnp.int32)
    own_pos = jnp.where(row < BLK, own_blocks[0] * BLK + row, own_blocks[1] * BLK + row - BLK)
    inverse_freq = THETA ** (-jnp.arange(HEAD // 2, dtype=f32) / (HEAD // 2))
    angles = inverse_freq[:, None] * own_pos.astype(f32)[None, :]
    cos_table, sin_table = jnp.cos(angles), jnp.sin(angles)

    normed_one, kv_send, kv_full = project_keys(own_id, hidden_low, (kv_shard, near_kv, far_kv, over_core(far_kv)), cos_table, sin_table, groups)
    query_send, query_full = project_queries(own_id, normed_one, (query_shard, near_query, far_query, over_core(far_query)), cos_table, sin_table, groups)
    kv_own, query_send, upstream = lax.optimization_barrier((exchange(kv_send, SEQ_AXES), query_send, trade(cotangent[0])))
    query_in = exchange(query_send, SEQ_AXES)
    kv_other = over_core(kv_own)

    kv_other, w_out, upstream, gate_up_parts = lax.optimization_barrier((kv_other, w_out, upstream, gate_up_parts))
    far_out, far_upstream = over_chip(w_out), over_chip(upstream)
    far_weights = over_chip(gate_up_parts[2]), over_both(gate_up_parts[3])
    out_send, out_blocks, lse, kv_sorted, kv_turned = attend(key_pos, query_rank, sorted_pos, sorted_id, query_in, kv_own, kv_other)
    out_send, far_out, far_upstream, far_weights = lax.optimization_barrier((out_send, far_out, far_upstream, far_weights))
    out_full = stack_rows(own_id, (w_out, over_core(w_out), far_out, over_core(far_out)))
    weights = (gate_up_parts[0], over_core(gate_up_parts[1])) + far_weights
    upstream_all = (upstream, over_core(upstream), far_upstream, over_core(far_upstream))

    gate_part, up_part = stack_pairs(own_id, weights)
    attn, out_full, gate_part, up_part = lax.optimization_barrier((exchange(out_send, SEQ_AXES), out_full, gate_part, up_part))
    mid_state, second_hat = project_out(attn, hidden_low, out_full)
    far_hat = over_chip(second_hat)
    near_hat = over_core(second_hat)
    down_turned = w_down.T
    near_side = feed((second_hat, near_hat), upstream_all[:2], gate_part, up_part, down_turned)
    far_hat, near_side = lax.optimization_barrier((far_hat, near_side))
    normed_all = second_hat, near_hat, far_hat, over_core(far_hat)
    far_side = feed(normed_all[2:], upstream_all[2:], gate_part, up_part, down_turned)
    scaled_received = over_core(near_side[1])
    far_send = (far_side[0] + over_core(far_side[1])[:, :width].astype(f32)).astype(bf16)
    far_send, normed_all, scaled_received = lax.optimization_barrier((far_send, normed_all, scaled_received))
    scaled_far = over_chip(far_send)
    ring = lax.axis_size(SEQ_AXES)
    stacked = feed_grads(normed_all, upstream_all, near_side[4:], far_side[4:], ring)
    scaled_far, stacked = lax.optimization_barrier((scaled_far, stacked))
    reduced = lax.psum_scatter(stacked.reshape(ring, 12 * STRIP, ff_part), SEQ_AXES, scatter_dimension=0, tiled=True)[0]

    grad_mid, grad_send, out_grad_keep, out_grad_give = mid_back(own_id, near_side[0], scaled_received, scaled_far, mid_state, upstream, out_full, attn)
    grad_group = exchange(grad_send, SEQ_AXES)
    ctx = lax.axis_size(CTX_AXES)
    slab = 8
    out_chip = (out_grad_keep.astype(f32) + over_core(out_grad_give).astype(f32)).astype(bf16).reshape(2 * ctx, slab, -1)
    result_received = over_core(near_side[3])
    result_send = (far_side[2] + over_core(far_side[3])[:, :width].astype(f32)).astype(bf16)
    grad_group, out_chip = lax.optimization_barrier((grad_group, out_chip))

    out_chips = exchange(out_chip, CHIP_AXES)

    dq, dkv_own, dkv_other = attend_back(key_pos, query_rank, sorted_pos, sorted_id, query_in, grad_group, out_blocks, lse, kv_sorted, kv_turned)
    dkv_other, reduced, out_chips, result_send = lax.optimization_barrier((dkv_other, reduced, out_chips, result_send))
    result_far = over_chip(result_send)
    out_sum = jnp.sum(out_chips.astype(f32), axis=0).astype(bf16)
    dq_home = exchange(dq, SEQ_AXES)
    dkv_received = over_core(dkv_other)
    reduced = (reduced.astype(f32) + lax.ppermute(reduced, "xl", SWAP).astype(f32)).astype(bf16).reshape(3, 4, STRIP, ff_part)
    dkv = (dkv_own + dkv_received.astype(f32)).astype(bf16)
    dq_home, dkv, reduced = lax.optimization_barrier((dq_home, dkv, reduced))
    part = lambda step: lax.dynamic_index_in_dim(reduced[:2], mine ^ step, 1, keepdims=False)
    pieces = arrange([part(0), over_core(part(1)), over_chip(part(2)), over_both(part(3))], xh, core).transpose(1, 0, 2, 3)
    pieces = jnp.concatenate([pieces, reduced[2:]]).reshape(12, STRIP, ff_part)
    result = total_out(mid_state, near_side[2], result_received, result_far)
    home, pieces, result = lax.optimization_barrier((exchange(dkv, SEQ_AXES), pieces, result))
    block_out = trade(result)
    whole = lax.all_gather(pieces, SEQ_AXES, axis=0, tiled=False)
    gain_two_shard, gate_shard, up_shard, down_shard = unpack(whole, w_gate, w_up, gain_two)

    keep, give, turned_grads = finish_grads(own_id, dq_home, home, normed_one, cos_table, sin_table)
    grad_tokens = finish_tokens(turned_grads, hidden_low, kv_full, query_full, grad_mid)
    grad_tokens = trade(grad_tokens)
    columns = keep.shape[-1]
    chip_sum = (keep.astype(f32) + over_core(give).astype(f32)).astype(bf16).reshape(2 * ctx, slab, columns)
    qkv_chips, grad_tokens = lax.optimization_barrier((exchange(chip_sum, CHIP_AXES), grad_tokens))
    qkv_sum = jnp.sum(qkv_chips.astype(f32), axis=0).astype(bf16)
    summed = jnp.concatenate([qkv_sum, out_sum], axis=1)
    final = exchange(jnp.broadcast_to(summed[None], (ctx,) + summed.shape), CTX_AXES)
    final, gate_shard, block_out = lax.optimization_barrier((final, gate_shard, block_out))
    gain_one_shard, query_shard, key_shard, value_shard, out_shard = last(final, kv_shard, query_shard, gain_one)
    return (
        block_out.T[None],
        grad_tokens.astype(f32).T[None],
        gain_one_shard,
        query_shard,
        key_shard,
        value_shard,
        out_shard,
        gain_two_shard,
        gate_shard,
        up_shard,
        down_shard,
    )


def solution(mesh):
    fine = Mesh(mesh.devices.reshape(2, 4, 4, 2, 2), ("xl", "z", "y", "xh", "core"))
    rows = P(FSDP_AXES, CTX_AXES, None)
    gain = P(FSDP_AXES)
    weight = P(FSDP_AXES, None)
    return jax.shard_map(
        per_device,
        mesh=fine,
        in_specs=(rows, P(), gain, weight, weight, weight, weight, gain, weight, weight, weight, rows),
        out_specs=(rows, rows, gain, weight, weight, weight, weight, gain, weight, weight, weight),
        check_vma=False,
    )
```

```python
import functools
import math

import jax
import jax.numpy as jnp
from jax import lax
from jax.experimental import pallas as pl
from jax.experimental.pallas import tpu as pltpu
from jax.sharding import Mesh
from jax.sharding import PartitionSpec as P

HEADS = 15
KV_HEADS = 5
EPSILON = 1e-05
THETA = 100000.0
SEQ_AXES = ("z", "y")
CTX_AXES = ("xl", "z", "y")
CHIP_AXES = ("xh", "xl", "z", "y")
FSDP_AXES = ("xh", "core")
CUBE_AXES = ("xl", "xh", "core")
SWAP = ((0, 1), (1, 0))
STRIP = 16
BLK = 128
HEAD = 64
EXP_SCALE = math.log2(math.e) / 8.0
MASKED = -1e30


def attend_kernel(key_pos, query_rank, sorted_pos, sorted_id, q_ref, own_in, other_in, send_ref, out_ref, lse_ref, kv_ref, kvt_ref, ones_v, q_sorted, *, big, small, edge_size, blocks):
    groups, width = own_in.shape[0], HEAD
    rows = blocks * BLK
    is_key = lax.broadcasted_iota(jnp.int32, (BLK, 2 * width), 1) < width

    def place(index, _):
        for side, source in enumerate((own_in, other_in)):
            for half in range(2):
                where = pl.multiple_of(key_pos[side * 2 * groups + 2 * index + half] * BLK, BLK)
                piece = source[index, :, half * BLK:(half + 1) * BLK]
                kvt_ref[:, pl.ds(where, BLK)] = piece
                turned = piece.T
                kv_ref[pl.ds(where, BLK), :] = turned
                ones_v[pl.ds(where, BLK), :] = jnp.where(is_key, jnp.ones_like(turned), turned)
        for half in range(2):
            query = q_ref[index, :, half * BLK:(half + 1) * BLK]
            query = jnp.concatenate([query, jnp.zeros_like(query)], axis=0)
            q_sorted[pl.ds(pl.multiple_of(query_rank[2 * index + half] * BLK, BLK), BLK), :] = query.T
        return 0

    lax.fori_loop(0, groups, place, 0, unroll=4)

    def tile(index, _):
        low, high = sorted_pos[blocks * index], sorted_pos[blocks * index + blocks - 1]
        query = q_sorted[pl.ds(pl.multiple_of(index * rows, rows), rows), :]
        row = lax.broadcasted_iota(jnp.int32, (rows, 1), 0)
        place_of = row + low * BLK
        for part in range(1, blocks):
            place_of = jnp.where(row >= part * BLK, row + (sorted_pos[blocks * index + part] - part) * BLK, place_of)

        def step(start, carry, size, masked):
            top, total = carry
            scores = lax.dot_general(query, kv_ref[pl.ds(start, size), :], (((1,), (1,)), ((), ())), preferred_element_type=jnp.float32)
            if masked:
                column = start + lax.broadcasted_iota(jnp.int32, scores.shape, 1)
                scores = jnp.where(column <= place_of, scores, MASKED)
            new_top = jnp.maximum(top, jnp.max(scores, axis=1, keepdims=True))
            weights = jnp.exp2((scores - new_top) * EXP_SCALE).astype(jnp.bfloat16)
            factor = jnp.exp2((top - new_top) * EXP_SCALE)
            added = jnp.dot(weights, ones_v[pl.ds(start, size), :], preferred_element_type=jnp.float32)
            return new_top, total * factor + added

        def full(count, carry):
            for part in range(big // small):
                carry = step(pl.multiple_of(count * big + part * small, small), carry, small, False)
            return carry

        def edge(count, carry):
            return step(pl.multiple_of(count * edge_size, edge_size), carry, edge_size, True)

        carry = (jnp.full((rows, 1), MASKED, jnp.float32), jnp.zeros((rows, 2 * width), jnp.float32))
        done = low * BLK // big
        carry = lax.fori_loop(0, done, full, carry)
        top, total = lax.fori_loop(done * (big // edge_size), (high * BLK + BLK + edge_size - 1) // edge_size, edge, carry)
        lse = (top * EXP_SCALE + jnp.log2(total)).T
        total = total.T
        result = total[width:] / total[:1]
        for part in range(blocks):
            ident = sorted_id[blocks * index + part]
            piece = result[:, part * BLK:(part + 1) * BLK]
            out_ref[ident] = piece
            send_ref[ident // 2, :, pl.ds(pl.multiple_of(ident % 2 * BLK, BLK), BLK)] = piece.astype(jnp.bfloat16)
            lse_ref[ident] = lse[:8, part * BLK:(part + 1) * BLK]
        return 0

    lax.fori_loop(0, 2 * groups // blocks, tile, 0)


def attend(key_pos, query_rank, sorted_pos, sorted_id, q, own_in, other_in, big=1024, small=1024, edge_size=512, blocks=4):
    groups, width = own_in.shape[0], HEAD
    total = 4 * groups * BLK
    vm = pl.BlockSpec(memory_space=pltpu.VMEM)
    sm = pl.BlockSpec(memory_space=pltpu.SMEM)
    return pl.pallas_call(
        functools.partial(attend_kernel, big=big, small=small, edge_size=edge_size, blocks=blocks),
        out_shape=(
            jax.ShapeDtypeStruct((groups, width, 2 * BLK), jnp.bfloat16),
            jax.ShapeDtypeStruct((2 * groups, width, BLK), jnp.float32),
            jax.ShapeDtypeStruct((2 * groups, 8, BLK), jnp.float32),
            jax.ShapeDtypeStruct((total, 2 * width), jnp.bfloat16),
            jax.ShapeDtypeStruct((2 * width, total), jnp.bfloat16),
        ),
        in_specs=[sm] * 4 + [vm] * 3,
        out_specs=(vm,) * 5,
        scratch_shapes=[
            pltpu.VMEM((total, 2 * width), jnp.bfloat16),
            pltpu.VMEM((2 * groups * BLK, 2 * width), jnp.bfloat16),
        ],
        compiler_params=pltpu.CompilerParams(vmem_limit_bytes=60 * 2**20),
        cost_estimate=pl.CostEstimate(flops=40 * 10**9, bytes_accessed=10**7, transcendentals=2 * 10**7),
        name="attend",
    )(key_pos, query_rank, sorted_pos, sorted_id, q, own_in, other_in)


def back_kernel(key_pos, query_rank, sorted_pos, sorted_id, q_ref, da_ref, out_ref, lse_ref, kv_ref, kvt_ref, dq_ref, own_ref, other_ref, dkv, q_sorted, da_sorted, *, big, small, edge_size, flip):
    groups, width = q_ref.shape[0], HEAD

    def place(index, _):
        for half in range(2):
            rank = query_rank[2 * index + half]
            q_sorted[rank] = q_ref[index, :, half * BLK:(half + 1) * BLK]
            da_sorted[rank] = da_ref[index, :, half * BLK:(half + 1) * BLK]
        return 0

    lax.fori_loop(0, groups, place, 0)

    def clear(index, _):
        dkv[pl.ds(pl.multiple_of(index * BLK, BLK), BLK), :] = jnp.zeros((BLK, 2 * width), jnp.float32)
        return 0

    lax.fori_loop(0, 4 * groups, clear, 0)

    def tile(index, _):
        low, high = sorted_pos[2 * index], sorted_pos[2 * index + 1]
        first_id, second_id = sorted_id[2 * index], sorted_id[2 * index + 1]
        query = jnp.concatenate([q_sorted[2 * index], q_sorted[2 * index + 1]], axis=1)
        grad = jnp.concatenate([da_sorted[2 * index], da_sorted[2 * index + 1]], axis=1)
        value = jnp.concatenate([out_ref[first_id], out_ref[second_id]], axis=1)
        lse = jnp.concatenate([lse_ref[first_id][:1], lse_ref[second_id][:1]], axis=1)
        delta = jnp.sum(grad.astype(jnp.float32) * value, axis=0, keepdims=True)
        none = jnp.zeros_like(query)
        both = jnp.concatenate([jnp.concatenate([query, none], axis=1), jnp.concatenate([none, grad], axis=1)], axis=0)
        both_t = both.T
        lane = lax.broadcasted_iota(jnp.int32, (1, 2 * BLK), 1)
        place_of = jnp.where(lane < BLK, low * BLK + lane, (high - 1) * BLK + lane)

        def step(start, total, size, masked):
            keys = kv_ref[pl.ds(start, size), :]
            pair = jnp.dot(keys, both, preferred_element_type=jnp.float32)
            weights = jnp.exp2(pair[:, :2 * BLK] * EXP_SCALE - lse)
            if masked:
                row = start + lax.broadcasted_iota(jnp.int32, weights.shape, 0)
                weights = jnp.where(row <= place_of, weights, 0.0)
            grad_scores = (weights * (pair[:, 2 * BLK:] - delta)).astype(jnp.bfloat16)
            weights = weights.astype(jnp.bfloat16)
            dkv[pl.ds(start, size), :] += jnp.dot(jnp.concatenate([grad_scores, weights], axis=1), both_t, preferred_element_type=jnp.float32)
            if flip:
                return total + lax.dot_general(grad_scores, keys, (((0,), (0,)), ((), ())), preferred_element_type=jnp.float32)
            return total + jnp.dot(kvt_ref[:width, pl.ds(start, size)], grad_scores, preferred_element_type=jnp.float32)

        def full(count, carry):
            for part in range(big // small):
                carry = step(pl.multiple_of(count * big + part * small, small), carry, small, False)
            return carry

        def edge(count, carry):
            return step(pl.multiple_of(count * edge_size, edge_size), carry, edge_size, True)

        done = low * BLK // big
        total = jnp.zeros((2 * BLK, 2 * width) if flip else (width, 2 * BLK), jnp.float32)
        total = lax.fori_loop(0, done, full, total)
        total = lax.fori_loop(done * (big // edge_size), (high * BLK + BLK + edge_size - 1) // edge_size, edge, total) * 0.125
        if flip:
            total = total.T[:width]
        for half, ident in enumerate((first_id, second_id)):
            dq_ref[ident // 2, :, pl.ds(pl.multiple_of(ident % 2 * BLK, BLK), BLK)] = total[:, half * BLK:(half + 1) * BLK].astype(jnp.bfloat16)
        return 0

    lax.fori_loop(0, groups, tile, 0)
    factor = jnp.where(lax.broadcasted_iota(jnp.int32, (1, 2 * width), 1) < width, 0.125, 1.0)

    def spread(index, _):
        for side, target in enumerate((own_ref, other_ref)):
            for half in range(2):
                where = pl.multiple_of(key_pos[side * 2 * groups + 2 * index + half] * BLK, BLK)
                target[index, :, half * BLK:(half + 1) * BLK] = (dkv[pl.ds(where, BLK), :] * factor).astype(target.dtype)
        return 0

    lax.fori_loop(0, groups, spread, 0)


def attend_back(key_pos, query_rank, sorted_pos, sorted_id, q, da, out, lse, kv, kvt, big=1024, small=1024, edge_size=512, flip=False):
    groups, width = q.shape[0], HEAD
    total = 4 * groups * BLK
    vm = pl.BlockSpec(memory_space=pltpu.VMEM)
    sm = pl.BlockSpec(memory_space=pltpu.SMEM)
    return pl.pallas_call(
        functools.partial(back_kernel, big=big, small=small, edge_size=edge_size, flip=flip),
        out_shape=(
            jax.ShapeDtypeStruct((groups, width, 2 * BLK), jnp.bfloat16),
            jax.ShapeDtypeStruct((groups, 2 * width, 2 * BLK), jnp.float32),
            jax.ShapeDtypeStruct((groups, 2 * width, 2 * BLK), jnp.bfloat16),
        ),
        in_specs=[sm] * 4 + [vm] * 6,
        out_specs=(vm,) * 3,
        scratch_shapes=[
            pltpu.VMEM((total, 2 * width), jnp.float32),
            pltpu.VMEM((2 * groups, width, BLK), jnp.bfloat16),
            pltpu.VMEM((2 * groups, width, BLK), jnp.bfloat16),
        ],
        compiler_params=pltpu.CompilerParams(vmem_limit_bytes=60 * 2**20),
        cost_estimate=pl.CostEstimate(flops=60 * 10**9, bytes_accessed=10**7, transcendentals=2 * 10**7),
        name="attend_back",
    )(key_pos, query_rank, sorted_pos, sorted_id, q, da, out, lse, kv, kvt)


def in_vmem(kernel, out_shape, scalars, arrays, scratch=(), flops=10**9, vmem=60, name=None):
    vm = pl.BlockSpec(memory_space=pltpu.VMEM)
    return pl.pallas_call(
        kernel,
        out_shape=tuple(jax.ShapeDtypeStruct(shape, dtype) for shape, dtype in out_shape),
        in_specs=[pl.BlockSpec(memory_space=pltpu.SMEM)] * len(scalars) + [vm] * len(arrays),
        out_specs=(vm,) * len(out_shape),
        scratch_shapes=[pltpu.VMEM(shape, dtype) for shape, dtype in scratch],
        compiler_params=pltpu.CompilerParams(vmem_limit_bytes=vmem * 2**20),
        cost_estimate=pl.CostEstimate(flops=flops, bytes_accessed=10**7, transcendentals=0),
        name=name,
    )(*scalars, *arrays)


def across(left, right):
    return lax.dot_general(left, right, (((1,), (1,)), ((), ())), preferred_element_type=jnp.float32)


def unit_rms(value):
    return lax.rsqrt(jnp.mean(value * value, axis=-1, keepdims=True) + EPSILON)


def put_rows(mine, pieces, target):
    shard = pieces[0].shape[0]
    for step, piece in enumerate(pieces):
        target[pl.ds(pl.multiple_of((mine[0] ^ step) * shard, 16), shard), :] = piece[...]


def turn(pair, cos, sin):
    half = HEAD // 2
    front, behind = pair[:half], pair[half:]
    return jnp.concatenate([front * cos - behind * sin, behind * cos + front * sin], axis=0).astype(jnp.bfloat16)


def turn_back(pair, cos, sin):
    return turn(pair, cos, -sin)


def project_keys_kernel(mine, x_ref, own, near, far, far_near, cos_ref, sin_ref, hat_ref, send_ref, w_ref):
    put_rows(mine, (own, near, far, far_near), w_ref)
    hidden = x_ref[...].astype(jnp.float32)
    hat = (hidden * unit_rms(hidden)).astype(jnp.bfloat16)
    hat_ref[...] = hat
    key_width = KV_HEADS * HEAD
    per = HEADS // KV_HEADS
    lin = jnp.dot(hat, w_ref[...], preferred_element_type=jnp.float32).T
    for head in range(KV_HEADS):
        key = turn(lin[head * HEAD:(head + 1) * HEAD], cos_ref[...], sin_ref[...])
        value = lin[key_width + head * HEAD:key_width + (head + 1) * HEAD].astype(jnp.bfloat16)
        for query in range(per):
            send_ref[head * per + query, :HEAD] = key
            send_ref[head * per + query, HEAD:] = value
    send_ref[HEADS:] = jnp.zeros((send_ref.shape[0] - HEADS,) + send_ref.shape[1:], jnp.bfloat16)


def project_keys(mine, x, pieces, cos, sin, groups):
    rows, width = x.shape
    columns = pieces[0].shape[1]
    return in_vmem(
        project_keys_kernel,
        ((x.shape, jnp.bfloat16), ((groups, 2 * HEAD, rows), jnp.bfloat16), ((width, columns), jnp.bfloat16)),
        (mine,),
        (x, *pieces, cos, sin),
        name="project_keys",
    )


def project_queries_kernel(mine, hat_ref, own, near, far, far_near, cos_ref, sin_ref, send_ref, w_ref):
    put_rows(mine, (own, near, far, far_near), w_ref)
    per = HEADS // KV_HEADS
    for group in range(KV_HEADS):
        columns = slice(group * per * HEAD, (group + 1) * per * HEAD)
        lin = jnp.dot(hat_ref[...], w_ref[:, columns], preferred_element_type=jnp.float32).T
        for query in range(per):
            send_ref[group * per + query] = turn(lin[query * HEAD:(query + 1) * HEAD], cos_ref[...], sin_ref[...])
    send_ref[HEADS:] = jnp.zeros((send_ref.shape[0] - HEADS,) + send_ref.shape[1:], jnp.bfloat16)


def project_queries(mine, hat, pieces, cos, sin, groups):
    rows, width = hat.shape
    columns = pieces[0].shape[1]
    return in_vmem(
        project_queries_kernel,
        (((groups, HEAD, rows), jnp.bfloat16), ((width, columns), jnp.bfloat16)),
        (mine,),
        (hat, *pieces, cos, sin),
        name="project_queries",
    )


def stack_rows_kernel(mine, own, near, far, far_near, out_ref):
    put_rows(mine, (own, near, far, far_near), out_ref)


def stack_rows(mine, pieces):
    shard, columns = pieces[0].shape
    return in_vmem(stack_rows_kernel, (((4 * shard, columns), jnp.bfloat16),), (mine,), pieces, flops=10**6, name="stack_rows")[0]


def finish_grads_kernel(mine, dq_ref, home, hat_ref, cos_ref, sin_ref, keep_ref, give_ref, turned, hat_t):
    shard = hat_ref.shape[1] // 4
    cos, sin = cos_ref[...], sin_ref[...]
    key_width = KV_HEADS * HEAD
    per = HEADS // KV_HEADS
    for head in range(KV_HEADS):
        total = sum(home[head * per + query].astype(jnp.float32) for query in range(per))
        total = jnp.concatenate([total[:, :BLK].T, total[:, BLK:].T], axis=1)
        turned[head * HEAD:(head + 1) * HEAD, :] = turn_back(total[:HEAD], cos, sin)
        turned[key_width + head * HEAD:key_width + (head + 1) * HEAD, :] = total[HEAD:].astype(jnp.bfloat16)
        for query in range(per):
            start = 2 * key_width + (head * per + query) * HEAD
            turned[start:start + HEAD, :] = turn_back(dq_ref[head * per + query].astype(jnp.float32), cos, sin)
    hat_t[...] = hat_ref[...].T
    core = mine[0] & 1
    for target, at in ((keep_ref, core), (give_ref, 1 - core)):
        target[...] = jnp.zeros(target.shape, target.dtype)
        for part in range(2):
            rows = hat_t[pl.ds(pl.multiple_of((2 * part + at) * shard, 16), shard), :]
            grads = across(rows, turned[...])
            target[part, :shard, : grads.shape[1]] = grads.astype(jnp.bfloat16)


def finish_grads(mine, dq, home, hat, cos, sin):
    rows, width = hat.shape
    columns = 2 * KV_HEADS * HEAD + HEADS * HEAD
    half = ((2, 256, -(-columns // BLK) * BLK), jnp.bfloat16)
    return in_vmem(
        finish_grads_kernel,
        (half, half, ((columns, rows), jnp.bfloat16)),
        (mine,),
        (dq, home, hat, cos, sin),
        scratch=(((width, rows), jnp.bfloat16),),
        name="finish_grads",
    )


def finish_tokens_kernel(turned, x_ref, kv_ref, query_ref, mid_ref, tokens_ref):
    key_width = KV_HEADS * HEAD
    scaled = jnp.dot(kv_ref[...], turned[: 2 * key_width, :], preferred_element_type=jnp.float32)
    scaled = (scaled + jnp.dot(query_ref[...], turned[2 * key_width :, :], preferred_element_type=jnp.float32)).T
    tokens_ref[...] = (mid_ref[...] + norm_back(x_ref[...].astype(jnp.float32), scaled)).astype(jnp.bfloat16)


def finish_tokens(turned, x, w_kv, w_query, mid):
    return in_vmem(finish_tokens_kernel, ((x.shape, jnp.bfloat16),), (), (turned, x, w_kv, w_query, mid), name="finish_tokens")[0]


def norm_back(value, grad):
    rms = unit_rms(value)
    hat = value * rms
    return rms * (grad - hat * jnp.mean(grad * hat, axis=-1, keepdims=True))


def out_kernel(attn, x_ref, w_ref, mid_ref, hat_ref):
    rows = attn[:HEADS].reshape(HEADS * HEAD, attn.shape[2]).T
    mid = x_ref[...].astype(jnp.float32) + jnp.dot(rows, w_ref[...], preferred_element_type=jnp.float32)
    mid_ref[...] = mid
    hat_ref[...] = (mid * unit_rms(mid)).astype(jnp.bfloat16)


def project_out(attn, x, w_out):
    return in_vmem(out_kernel, ((x.shape, jnp.float32), (x.shape, jnp.bfloat16)), (), (attn, x, w_out), name="project_out")


def stack_pairs_kernel(mine, own, near, far, far_near, gate_ref, up_ref):
    pieces = (own, near, far, far_near)
    put_rows(mine, [piece.at[0] for piece in pieces], gate_ref)
    put_rows(mine, [piece.at[1] for piece in pieces], up_ref)


def stack_pairs(mine, pieces):
    _, shard, columns = pieces[0].shape
    whole = ((4 * shard, columns), jnp.bfloat16)
    return in_vmem(stack_pairs_kernel, (whole, whole), (mine,), pieces, flops=10**6, name="stack_pairs")


def feed_kernel(hat_own, hat_peer, grad_own, grad_peer, w_gate, w_up, down_t, scaled_keep, scaled_send, out_keep, out_send, act_ref, gate_grad_ref, up_grad_ref, hat_ref, grad_ref):
    rows, width = hat_own.shape
    for step, (hat, grad) in enumerate(((hat_own, grad_own), (hat_peer, grad_peer))):
        hat_ref[step * rows:(step + 1) * rows, :] = hat[...]
        grad_ref[step * rows:(step + 1) * rows, :] = grad[...]
    scaled = out = None
    for start, stop in ((0, 256), (256, 640)):
        cut = slice(start, stop)
        gate = jnp.dot(hat_ref[...], w_gate[:, cut], preferred_element_type=jnp.float32)
        up = jnp.dot(hat_ref[...], w_up[:, cut], preferred_element_type=jnp.float32)
        sigmoid = jax.nn.sigmoid(gate)
        silu = gate * sigmoid
        act = (silu * up).astype(jnp.bfloat16)
        grad_act = jnp.dot(grad_ref[...], down_t[:, cut], preferred_element_type=jnp.float32).astype(jnp.bfloat16).astype(jnp.float32)
        gate_grad = (grad_act * up * sigmoid * (1.0 + gate * (1.0 - sigmoid))).astype(jnp.bfloat16)
        up_grad = (grad_act * silu).astype(jnp.bfloat16)
        act_ref[:, cut], gate_grad_ref[:, cut], up_grad_ref[:, cut] = act, gate_grad, up_grad
        scaled_cut = across(gate_grad, w_gate[:, cut]) + across(up_grad, w_up[:, cut])
        out_cut = across(act, down_t[:, cut])
        scaled, out = (scaled_cut, out_cut) if scaled is None else (scaled + scaled_cut, out + out_cut)
    scaled_keep[...] = scaled[:rows]
    out_keep[...] = out[:rows]
    for target, value in ((scaled_send, scaled), (out_send, out)):
        target[:, :width] = value[rows:].astype(jnp.bfloat16)
        target[:, width:] = jnp.zeros((rows, target.shape[1] - width), jnp.bfloat16)


def feed(hats, grads, w_gate, w_up, down_t, vmem=60):
    rows, width = hats[0].shape
    kept = ((rows, width), jnp.float32)
    sent = ((rows, -(-width // 256) * 256), jnp.bfloat16)
    hidden = ((2 * rows, down_t.shape[1]), jnp.bfloat16)
    both = ((2 * rows, width), jnp.bfloat16)
    return in_vmem(
        feed_kernel,
        (kept, sent, kept, sent, hidden, hidden, hidden),
        (),
        (*hats, *grads, w_gate, w_up, down_t),
        scratch=(both, both),
        flops=6 * 10**9,
        vmem=vmem,
        name="feed",
    )


def feed_grads_kernel(*refs):
    hats, grads, near, far, (out_ref, hat_t, grad_t) = refs[:4], refs[4:8], refs[8:11], refs[11:14], refs[14:]
    rows = hats[0].shape[0]
    for step in range(4):
        here = slice(step * rows, (step + 1) * rows)
        hat_t[:, here] = hats[step][...].T
        grad_t[:, here] = grads[step][...].T
    shard = hat_t.shape[0] // 4
    strips = shard // STRIP
    for index, (left, at) in enumerate(((hat_t, 1), (hat_t, 2), (grad_t, 0))):
        for part in range(4):
            some = left[part * shard:(part + 1) * shard, :]
            product = jnp.dot(some[:, : 2 * rows], near[at][...], preferred_element_type=jnp.float32)
            product = product + jnp.dot(some[:, 2 * rows:], far[at][...], preferred_element_type=jnp.float32)
            out_ref[:strips, 4 * index + part] = product.astype(jnp.bfloat16).reshape(strips, STRIP, product.shape[1])
    out_ref[strips:] = jnp.zeros((out_ref.shape[0] - strips,) + out_ref.shape[1:], jnp.bfloat16)


def feed_grads(hats, grads, near, far, ring):
    rows, width = hats[0].shape
    turned = ((width, 4 * rows), jnp.bfloat16)
    return in_vmem(
        feed_grads_kernel,
        (((ring, 12, STRIP, near[0].shape[1]), jnp.bfloat16),),
        (),
        (*hats, *grads, *near, *far),
        scratch=(turned, turned),
        flops=8 * 10**9,
        name="feed_grads",
    )[0]


def mid_kernel(mine, keep, received, far, mid_ref, grad_ref, w_ref, attn, total_ref, send_ref, keep_ref, give_ref, rows_ref):
    width = keep.shape[1]
    shard = width // 4
    scaled = keep[...] + received[:, :width].astype(jnp.float32) + far[...].astype(jnp.float32)
    total = grad_ref[...].astype(jnp.float32) + norm_back(mid_ref[...], scaled)
    total_ref[...] = total
    low = total.astype(jnp.bfloat16)
    send_ref[:HEADS] = across(w_ref[...], low).astype(jnp.bfloat16).reshape(HEADS, HEAD, low.shape[0])
    send_ref[HEADS:] = jnp.zeros((send_ref.shape[0] - HEADS,) + send_ref.shape[1:], jnp.bfloat16)
    rows_ref[...] = attn[:HEADS].reshape(HEADS * HEAD, attn.shape[2])
    core = mine[0] & 1
    for target, at in ((keep_ref, core), (give_ref, 1 - core)):
        target[...] = jnp.zeros(target.shape, target.dtype)
        for part in range(2):
            rows = rows_ref[pl.ds(pl.multiple_of((2 * part + at) * shard, 16), shard), :]
            target[part, :shard, :width] = jnp.dot(rows, low, preferred_element_type=jnp.float32).astype(target.dtype)


def mid_back(mine, keep, received, far, mid, grad, w_out, attn):
    half = ((2, 256, 1024), jnp.bfloat16)
    return in_vmem(
        mid_kernel,
        ((mid.shape, jnp.float32), (attn.shape, jnp.bfloat16), half, half),
        (mine,),
        (keep, received, far, mid, grad, w_out, attn),
        scratch=((mid.shape[::-1], jnp.bfloat16),),
        name="mid_back",
    )


def pack_kernel(key_t, value_t, query, gain, kv_ref, query_ref):
    width = key_t.shape[0]
    scale = gain[...]
    for index, piece in enumerate((key_t, value_t)):
        kv_ref[:, index * width:(index + 1) * width] = (piece[...].astype(jnp.float32).T * scale).astype(jnp.bfloat16)
    query_ref[...] = (query[...].astype(jnp.float32) * scale).astype(jnp.bfloat16)


def pack(w_key, w_value, w_query, gain):
    shard = w_key.shape[0]
    return in_vmem(
        pack_kernel,
        (((shard, 2 * w_key.shape[1]), jnp.bfloat16), (w_query.shape, jnp.bfloat16)),
        (),
        (w_key.T, w_value.T, w_query, gain),
        flops=10**6,
        name="pack",
    )


def as_row(column):
    return jnp.broadcast_to(column, (column.shape[0], BLK)).T[:1]


def last_kernel(total, w_kv, w_query, gain, query_ref, key_ref, value_ref, out_ref, gain_ref):
    shard, width = w_query.shape
    key_width = key_ref.shape[0]
    columns = 2 * key_width + width
    padded = -(-columns // BLK) * BLK
    rows = total[...].reshape(total.shape[0] * total.shape[1], total.shape[2])[:shard].astype(jnp.float32)
    kv, query = rows[:, : 2 * key_width], rows[:, 2 * key_width : columns]
    scale = gain[...]
    gain_sum = jnp.sum(kv * w_kv[...].astype(jnp.float32), axis=1, keepdims=True) + jnp.sum(query * w_query[...].astype(jnp.float32), axis=1, keepdims=True)
    gain_ref[...] = as_row(gain_sum / scale)
    kv = kv * scale
    key_ref[...] = kv[:, :key_width].T
    value_ref[...] = kv[:, key_width:].T
    query_ref[...] = query * scale
    out_ref[...] = rows[:, padded:padded + width]


def last(total, w_kv, w_query, gain):
    shard, width = w_query.shape
    square = (w_query.shape, jnp.float32)
    turned = ((w_kv.shape[1] // 2, shard), jnp.float32)
    query, key, value, out, gain_grad = in_vmem(
        last_kernel, (square, turned, turned, square, ((1, shard), jnp.float32)), (), (total, w_kv, w_query, gain), name="last"
    )
    return gain_grad.reshape(shard), query, key.T, value.T, out


def unpack_kernel(total, w_gate, w_up, gain, gate_ref, up_ref, down_ref, gain_ref):
    shard, part = w_gate.shape[0], total.shape[3]
    strips = shard // STRIP
    scale = gain[...]
    gain_sum = jnp.zeros((shard, 1), jnp.float32)
    for index, (weight, target) in enumerate(((w_gate, gate_ref), (w_up, up_ref))):
        for step in range(4):
            columns = slice(step * part, (step + 1) * part)
            grads = total[:strips, 4 * index + step].reshape(shard, part).astype(jnp.float32)
            gain_sum = gain_sum + jnp.sum(grads * weight[:, columns].astype(jnp.float32), axis=1, keepdims=True)
            target[:, columns] = grads * scale
    for step in range(4):
        down_ref[step * shard:(step + 1) * shard, :] = total[:strips, 8 + step].reshape(shard, part).astype(jnp.float32)
    gain_ref[...] = as_row(gain_sum)


def unpack(total, w_gate, w_up, gain):
    shard, columns = w_gate.shape
    part = total.shape[3]
    full = ((shard, columns), jnp.float32)
    gate, up, down, gain_grad = in_vmem(
        unpack_kernel, (full, full, ((4 * shard, part), jnp.float32), ((1, shard), jnp.float32)), (), (total, w_gate, w_up, gain), name="unpack"
    )
    return gain_grad.reshape(shard), gate, up, down.T


def over_core(value):
    return lax.ppermute(value, "core", SWAP)


def over_chip(value):
    return lax.ppermute(value, "xh", SWAP)


def over_both(value):
    return lax.ppermute(value, FSDP_AXES, ((0, 3), (3, 0), (1, 2), (2, 1)))


def trade(value):
    return lax.ppermute(value, ("xl", "core"), ((0, 0), (1, 2), (2, 1), (3, 3)))


def arrange(pieces, xh, core):
    low = jnp.where(core == 1, pieces[1], pieces[0]), jnp.where(core == 1, pieces[0], pieces[1])
    high = jnp.where(core == 1, pieces[3], pieces[2]), jnp.where(core == 1, pieces[2], pieces[3])
    return jnp.stack([jnp.where(xh == 1, h, l) for l, h in zip(low, high)] + [jnp.where(xh == 1, l, h) for l, h in zip(low, high)])


def exchange(value, axes):
    return lax.all_to_all(value, axes, split_axis=0, concat_axis=0, tiled=True)


def per_device(
    tokens,
    block_order,
    gain_attn,
    w_query,
    w_key,
    w_value,
    w_out,
    gain_mlp,
    w_gate,
    w_up,
    w_down,
    cotangent,
):
    f32, bf16 = jnp.float32, jnp.bfloat16
    xh, core = lax.axis_index("xh"), lax.axis_index("core")
    mine = 2 * xh + core
    own_id = mine.reshape(1)
    row_total, width = tokens.shape[1:]
    shard = w_query.shape[0]
    ff_part = w_down.shape[0]
    groups = lax.axis_size(SEQ_AXES)
    key_width = KV_HEADS * HEAD
    gain_one = gain_attn.astype(f32)[:, None]
    gain_two = gain_mlp.astype(f32)[:, None]

    kv_shard, query_shard = pack(w_key, w_value, w_query, gain_one)
    far_kv, near_kv = over_chip(kv_shard), over_core(kv_shard)
    hidden_low, query_shard = lax.optimization_barrier((trade(tokens[0]), query_shard))
    far_query, near_query = over_chip(query_shard), over_core(query_shard)

    def gate_up(step):
        start = (mine ^ step) * ff_part
        both = [lax.dynamic_slice_in_dim(w, start, ff_part, 1).astype(f32) * gain_two for w in (w_gate, w_up)]
        return jnp.stack(both).astype(bf16)

    gate_up_parts = [gate_up(step) for step in range(4)]
    far_kv, hidden_low, gate_up_parts = lax.optimization_barrier((far_kv, hidden_low, gate_up_parts))

    own_order = lax.dynamic_slice_in_dim(block_order, 2 * groups * core, 2 * groups)
    other_order = lax.dynamic_slice_in_dim(block_order, 2 * groups * (1 - core), 2 * groups)
    key_pos = jnp.concatenate([own_order, other_order])
    query_rank = jnp.sum((own_order[None, :] < own_order[:, None]).astype(jnp.int32), axis=1)
    hit = query_rank[None, :] == jnp.arange(2 * groups, dtype=jnp.int32)[:, None]
    sorted_pos = jnp.sum(jnp.where(hit, own_order[None, :], 0), axis=1)
    sorted_id = jnp.sum(jnp.where(hit, jnp.arange(2 * groups, dtype=jnp.int32)[None, :], 0), axis=1)
    here = lax.axis_index(SEQ_AXES)
    own_blocks = lax.dynamic_slice_in_dim(own_order, 2 * here, 2)
    row = jnp.arange(row_total, dtype=jnp.int32)
    own_pos = jnp.where(row < BLK, own_blocks[0] * BLK + row, own_blocks[1] * BLK + row - BLK)
    inverse_freq = THETA ** (-jnp.arange(HEAD // 2, dtype=f32) / (HEAD // 2))
    angles = inverse_freq[:, None] * own_pos.astype(f32)[None, :]
    cos_table, sin_table = jnp.cos(angles), jnp.sin(angles)

    normed_one, kv_send, kv_full = project_keys(own_id, hidden_low, (kv_shard, near_kv, far_kv, over_core(far_kv)), cos_table, sin_table, groups)
    query_send, query_full = project_queries(own_id, normed_one, (query_shard, near_query, far_query, over_core(far_query)), cos_table, sin_table, groups)
    kv_own, query_send, upstream = lax.optimization_barrier((exchange(kv_send, SEQ_AXES), query_send, trade(cotangent[0])))
    query_in = exchange(query_send, SEQ_AXES)
    kv_other = over_core(kv_own)

    kv_other, w_out, upstream, gate_up_parts = lax.optimization_barrier((kv_other, w_out, upstream, gate_up_parts))
    far_out, far_upstream = over_chip(w_out), over_chip(upstream)
    far_weights = over_chip(gate_up_parts[2]), over_both(gate_up_parts[3])
    out_send, out_blocks, lse, kv_sorted, kv_turned = attend(key_pos, query_rank, sorted_pos, sorted_id, query_in, kv_own, kv_other)
    out_send, far_out, far_upstream, far_weights = lax.optimization_barrier((out_send, far_out, far_upstream, far_weights))
    out_full = stack_rows(own_id, (w_out, over_core(w_out), far_out, over_core(far_out)))
    weights = (gate_up_parts[0], over_core(gate_up_parts[1])) + far_weights
    upstream_all = (upstream, over_core(upstream), far_upstream, over_core(far_upstream))

    gate_part, up_part = stack_pairs(own_id, weights)
    attn, out_full, gate_part, up_part = lax.optimization_barrier((exchange(out_send, SEQ_AXES), out_full, gate_part, up_part))
    mid_state, second_hat = project_out(attn, hidden_low, out_full)
    far_hat = over_chip(second_hat)
    near_hat = over_core(second_hat)
    down_turned = w_down.T
    near_side = feed((second_hat, near_hat), upstream_all[:2], gate_part, up_part, down_turned)
    far_hat, near_side = lax.optimization_barrier((far_hat, near_side))
    normed_all = second_hat, near_hat, far_hat, over_core(far_hat)
    far_side = feed(normed_all[2:], upstream_all[2:], gate_part, up_part, down_turned, vmem=60)
    scaled_received = over_core(near_side[1])
    far_send = (far_side[0] + over_core(far_side[1])[:, :width].astype(f32)).astype(bf16)
    far_send, normed_all, scaled_received = lax.optimization_barrier((far_send, normed_all, scaled_received))
    scaled_far = over_chip(far_send)
    ring = lax.axis_size(SEQ_AXES)
    stacked = feed_grads(normed_all, upstream_all, near_side[4:], far_side[4:], ring)
    scaled_far, stacked = lax.optimization_barrier((scaled_far, stacked))
    reduced = lax.psum_scatter(stacked.reshape(ring, 12 * STRIP, ff_part), SEQ_AXES, scatter_dimension=0, tiled=True)[0]

    grad_mid, grad_send, out_grad_keep, out_grad_give = mid_back(own_id, near_side[0], scaled_received, scaled_far, mid_state, upstream, out_full, attn)
    grad_group = exchange(grad_send, SEQ_AXES)
    ctx = lax.axis_size(CTX_AXES)
    slab = 8
    out_chip = (out_grad_keep.astype(f32) + over_core(out_grad_give).astype(f32)).astype(bf16).reshape(2 * ctx, slab, -1)
    result_received = over_core(near_side[3])
    result_send = (far_side[2] + over_core(far_side[3])[:, :width].astype(f32)).astype(bf16)
    grad_group, out_chip = lax.optimization_barrier((grad_group, out_chip))

    out_chips = exchange(out_chip, CHIP_AXES)

    dq, dkv_own, dkv_other = attend_back(key_pos, query_rank, sorted_pos, sorted_id, query_in, grad_group, out_blocks, lse, kv_sorted, kv_turned)
    dkv_other, reduced, out_chips, result_send = lax.optimization_barrier((dkv_other, reduced, out_chips, result_send))
    result_far = over_chip(result_send)
    out_sum = jnp.sum(out_chips.astype(f32), axis=0).astype(bf16)
    dq_home = exchange(dq, SEQ_AXES)
    dkv_received = over_core(dkv_other)
    reduced = (reduced.astype(f32) + lax.ppermute(reduced, "xl", SWAP).astype(f32)).astype(bf16).reshape(3, 4, STRIP, ff_part)
    dkv = (dkv_own + dkv_received.astype(f32)).astype(bf16)
    dq_home, dkv, reduced = lax.optimization_barrier((dq_home, dkv, reduced))
    part = lambda step: lax.dynamic_index_in_dim(reduced[:2], mine ^ step, 1, keepdims=False)
    pieces = arrange([part(0), over_core(part(1)), over_chip(part(2)), over_both(part(3))], xh, core).transpose(1, 0, 2, 3)
    pieces = jnp.concatenate([pieces, reduced[2:]]).reshape(12, STRIP, ff_part)
    result = mid_state + near_side[2] + result_received[:, :width].astype(f32) + result_far.astype(f32)
    home, pieces, result = lax.optimization_barrier((exchange(dkv, SEQ_AXES), pieces, result.astype(bf16)))
    block_out = trade(result)
    whole = lax.all_gather(pieces, SEQ_AXES, axis=0, tiled=False)
    gain_two_shard, gate_shard, up_shard, down_shard = unpack(whole, w_gate, w_up, gain_two)

    keep, give, turned_grads = finish_grads(own_id, dq_home, home, normed_one, cos_table, sin_table)
    grad_tokens = finish_tokens(turned_grads, hidden_low, kv_full, query_full, grad_mid)
    grad_tokens = trade(grad_tokens)
    columns = keep.shape[-1]
    chip_sum = (keep.astype(f32) + over_core(give).astype(f32)).astype(bf16).reshape(2 * ctx, slab, columns)
    qkv_chips, grad_tokens, block_out = lax.optimization_barrier((exchange(chip_sum, CHIP_AXES), grad_tokens, block_out))
    qkv_sum = jnp.sum(qkv_chips.astype(f32), axis=0).astype(bf16)
    summed = jnp.concatenate([qkv_sum, out_sum], axis=1)
    final = exchange(jnp.broadcast_to(summed[None], (ctx,) + summed.shape), CTX_AXES)
    final, gate_shard = lax.optimization_barrier((final, gate_shard))
    gain_one_shard, query_shard, key_shard, value_shard, out_shard = last(final, kv_shard, query_shard, gain_one)
    return (
        block_out[None],
        grad_tokens.astype(f32)[None],
        gain_one_shard,
        query_shard,
        key_shard,
        value_shard,
        out_shard,
        gain_two_shard,
        gate_shard,
        up_shard,
        down_shard,
    )


def solution(mesh):
    fine = Mesh(mesh.devices.reshape(2, 4, 4, 2, 2), ("xl", "z", "y", "xh", "core"))
    rows = P(FSDP_AXES, CTX_AXES, None)
    gain = P(FSDP_AXES)
    weight = P(FSDP_AXES, None)
    return jax.shard_map(
        per_device,
        mesh=fine,
        in_specs=(rows, P(), gain, weight, weight, weight, weight, gain, weight, weight, weight, rows),
        out_specs=(rows, rows, gain, weight, weight, weight, weight, gain, weight, weight, weight),
        check_vma=False,
    )
```
